128 devices in a mesh: dp: 64 (over x, y_lo, z, core), tensor: 2 (over y_hi).
Axes of the slice: x: 4, y: 4 (y_hi: 2, y_lo: 2; y = y_hi * 2 + y_lo), z: 4, core: 2. Of those that a mesh axis runs over, the one named last changes fastest.
Arguments:
- tokens: bfloat16 [32768, 768], P(('dp', 'tensor')), may hold values from -24 to 24
- cotangent: bfloat16 [32768, 768], P(('dp', 'tensor')), may hold values from -24 to 24
- segments: int32 [64, 512], P('dp'), may hold values from 0 to 2, as said below
- input_weight: bfloat16 [768, 3, 768], P('dp', None, 'tensor'), may hold values from -0.21875 to 0.21875
- output_weight: bfloat16 [768, 768], P('tensor', 'dp'), may hold values from -1.75 to 1.75
- up_weight: bfloat16 [768, 3072], P('dp', 'tensor'), may hold values from -0.21875 to 0.21875
- down_weight: bfloat16 [3072, 768], P('tensor', 'dp'), may hold values from -0.109375 to 0.109375
- head_bias: bfloat16 [2, 768], P(None, 'tensor'), may hold values from -3 to 3
- hidden_bias: bfloat16 [3072], P('tensor'), may hold values from -3 to 3
- norm_gains: bfloat16 [2, 768], P(None, 'dp'), may hold values from 0.25 to 1.75
- shifts: bfloat16 [4, 768], P(None, 'dp'), may hold values from -3 to 3
Outputs:
- block_out: bfloat16 [32768, 768], P(('dp', 'tensor'))
- token_grad: bfloat16 [32768, 768], P(('dp', 'tensor'))
- input_weight_grad: float32 [768, 3, 768], P('dp', None, 'tensor')
- output_weight_grad: float32 [768, 768], P('tensor', 'dp')
- up_weight_grad: float32 [768, 3072], P('dp', 'tensor')
- down_weight_grad: float32 [3072, 768], P('tensor', 'dp')
- head_bias_grad: float32 [2, 768], P(None, ('tensor', 'dp'))
- hidden_bias_grad: float32 [3072], P(('tensor', 'dp'))
- gain_grad: float32 [2, 768], P(None, ('dp', 'tensor'))
- shift_grad: float32 [4, 768], P(None, ('dp', 'tensor'))
The draws below stay inside these ranges and needn't reach their ends.
Inputs may be any that keep to these rules, and one draw needn't show every extreme that they name: `segments`: each sequence holds exactly three documents, numbered 0, 1, 2 in order of position; the first and the last have min(200, 64) positions or more, and positions 192 to 319 lie in the middle one.
All inputs are finite; a program needn't handle non-finite values.
Results may differ from the reference program's by a relative error of at most 0.019.
Values may be sent and summed in bfloat16 or wider, within the bound.
No kernel may reach another device: no remote copies, remote signals or barrier semaphores. Data moves between devices by JAX's collectives and lax.ppermute only.
A program may use at most 128 MiB of HBM per device.

```python
import math
import jax
import jax.numpy as jnp
from jax import lax

D = 768
FF = 3072
HEADS = 12
HEAD_DIM = 64
LEN = 512
SEQS = 64
TOKENS = 32768


def draw_segments(key, part):
    key = jax.random.fold_in(key, 11)
    spacing = min(200, LEN // 8)
    first_key, second_key = jax.random.split(key)
    first = jax.random.randint(first_key, (SEQS, 1), spacing, 3 * LEN // 8 + 1)
    second = jax.random.randint(second_key, (SEQS, 1), 5 * LEN // 8, LEN - spacing + 1)
    places = jnp.arange(LEN)[None, :]
    return ((places >= first).astype(jnp.int32) + (places >= second).astype(jnp.int32)).astype(jnp.int32)


def strengthened(array, key, source, target, shards_of, factor):
    def block_of(position):
        return (jnp.arange(array.shape[position]) // (array.shape[position] // shards_of)).reshape((-1,) + (1,) * (array.ndim - 1 - position))

    near = jax.random.permutation(key, shards_of)[block_of(target)]
    second = (block_of(target) + shards_of // 2) % shards_of
    return jnp.where((block_of(source) == near) | (block_of(source) == second), factor * array, array)


def block_scale(key, extent, shards, least, top_value):
    factor_of, own = 1.0, jax.random.fold_in(key, 6)
    for axis_at, blocks in shards:
        draws = jnp.exp(jax.random.uniform(jax.random.fold_in(own, axis_at), (blocks,), jnp.float32, least / len(shards), top_value / len(shards)))
        factor_of = factor_of * jnp.repeat(draws, extent[axis_at] // blocks).reshape([-1 if axis == axis_at else 1 for axis in range(len(extent))])
    return factor_of


def gaussian(stream_key, dims, scale, bound, cuts=(), kind=jnp.bfloat16):
    factor_of = block_scale(stream_key, dims, cuts, -0.22, 0.18) if cuts else 1.0
    array = jax.random.normal(stream_key, dims, jnp.float32) * scale * factor_of
    return jnp.minimum(jnp.maximum(array, -bound), bound).astype(kind)


def gaussian_with(own_key, dims, spread, most, pieces, heavy, kind=jnp.bfloat16):
    entries = spread * jax.random.normal(own_key, dims, jnp.float32)
    if pieces:
        entries = entries * block_scale(own_key, dims, pieces, -0.22, 0.18)
    return jnp.clip(strengthened(entries, jax.random.fold_in(own_key, 3), *heavy), -most, most).astype(kind)


def setup_inputs(seed: int = 0) -> dict:
    keys = jax.random.split(jax.random.key(seed), 12)
    return {
        "tokens": gaussian_with(keys[0], (TOKENS, D), 1.0, 24.0, ((0, 128),), (0, 1, 128, 5.5)),
        "cotangent": gaussian_with(keys[1], (TOKENS, D), 1.0, 24.0, ((0, 128),), (0, 1, 128, 5.5)),
        "segments": draw_segments(jax.random.fold_in(keys[11], 71), 0),
        "input_weight": gaussian(keys[3], (D, 3, D), D ** -0.5, 0.21875, ((0, 64), (2, 2))),
        "output_weight": gaussian(keys[4], (D, D), (D // 64) ** -0.5, 1.75, ((0, 2), (1, 64))),
        "up_weight": gaussian(keys[5], (D, FF), D ** -0.5, 0.21875, ((0, 64), (1, 2))),
        "down_weight": gaussian(keys[6], (FF, D), FF ** -0.5, 0.109375, ((0, 2), (1, 64))),
        "head_bias": gaussian(keys[7], (2, D), 0.3, 3.0, ((1, 2),)),
        "hidden_bias": gaussian(keys[8], (FF,), 0.3, 3.0, ((0, 2),)),
        "norm_gains": jnp.clip(1.0 + 0.15 * jax.random.normal(keys[9], (2, D), jnp.float32), 0.25, 1.75).astype(jnp.bfloat16),
        "shifts": gaussian(keys[10], (4, D), 0.3, 3.0, ((1, 64),)),
    }


norm_epsilon = 1e-05
masked_value = -1e+30
gelu_factor = 0.7978845608028654
highest = lax.Precision.HIGHEST

@jax.custom_vjp
def low(v):
    return lax.optimization_barrier(v.astype(jnp.bfloat16)).astype(jnp.float32)

@jax.custom_vjp
def low_back(v):
    return v

def low_keep(v):
    return (low(v), None)

def low_pass(kept, grad):
    return (grad,)

def back_keep(v):
    return (v, None)

def back_low(kept, grad):
    return (low(grad),)
low.defvjp(low_keep, low_pass)
low_back.defvjp(back_keep, back_low)

def layer_norm(values, gain_row, shift_row):
    mean_val = lax.optimization_barrier(jnp.mean(values, axis=-1, keepdims=True))
    centered = values - mean_val
    variance = lax.optimization_barrier(jnp.mean(centered * centered, axis=-1, keepdims=True))
    return centered * lax.rsqrt(variance + norm_epsilon) * gain_row + shift_row

def gelu_tanh(values):
    return 0.5 * values * (1.0 + jnp.tanh(gelu_factor * (values + 0.044715 * values * values * values)))

def attend_sequence(queries, key_heads, value_heads, segment_ids):
    length = segment_ids.shape[0]
    scores = jnp.einsum('qhd,khd->hqk', queries, key_heads, precision=highest) * (1.0 / math.sqrt(HEAD_DIM))
    scores = low_back(scores)
    places = jnp.arange(length)
    allowed = (segment_ids[:, None] == segment_ids[None, :]) & (places[:, None] >= places[None, :])
    scores = jnp.where(allowed[None], scores, masked_value)
    soft_weights = jax.nn.softmax(scores, axis=-1)
    return jnp.einsum('hqk,khd->qhd', low(soft_weights), value_heads, precision=highest)

def forward(residual, input_weight, output_weight, up_weight, down_weight, head_bias, hidden_bias, norm_gains, shifts, segment_block):
    group = segment_block.shape[0]
    row_total = residual.shape[0]
    normed_one = low(layer_norm(residual, norm_gains[0], shifts[0]))
    mixed_all = jnp.einsum('td,dcf->tcf', normed_one, input_weight, precision=highest)
    head_shape = (group, LEN, HEADS, HEAD_DIM)
    queries = low(low_back(mixed_all[:, 0] + head_bias[0])).reshape(head_shape)
    key_heads = low(low_back(mixed_all[:, 1])).reshape(head_shape)
    value_heads = low(low_back(mixed_all[:, 2] + head_bias[1])).reshape(head_shape)
    checked = jax.checkpoint(attend_sequence)
    context = lax.map(lambda element: checked(*element), (queries, key_heads, value_heads, segment_block))
    context = low(low_back(context.reshape(row_total, D)))
    branch_one = low_back(jnp.dot(context, output_weight, precision=highest))
    middle = residual + branch_one + shifts[2]
    normed_two = low(layer_norm(middle, norm_gains[1], shifts[1]))
    before = low_back(jnp.dot(normed_two, up_weight, precision=highest) + hidden_bias)
    hidden = low(gelu_tanh(before))
    branch_two = low_back(jnp.dot(hidden, down_weight, precision=highest))
    return middle + branch_two + shifts[3]

def reference(tokens, cotangent, segments, input_weight, output_weight, up_weight, down_weight, head_bias, hidden_bias, norm_gains, shifts):
    group = min(SEQS, max(1, 4096 // LEN))
    steps_count = SEQS // group
    params = tuple((param.astype(jnp.float32) for param in (input_weight, output_weight, up_weight, down_weight, head_bias, hidden_bias, norm_gains, shifts)))
    token_groups = tokens.astype(jnp.float32).reshape(steps_count, group * LEN, D)
    cot_groups = cotangent.astype(jnp.float32).reshape(steps_count, group * LEN, D)
    segment_groups = segments.reshape(steps_count, group, LEN)

    def step(totals, element):
        token_block, cot_block, segment_block = element

        def run(token_in, *weights):
            return forward(token_in, *weights, segment_block)
        result, pullback = jax.vjp(run, token_block, *params)
        grads = pullback(cot_block)
        totals = tuple((total + grad for total, grad in zip(totals, grads[1:])))
        return (totals, (result.astype(jnp.bfloat16), grads[0].astype(jnp.bfloat16)))
    zeros = tuple((jnp.zeros(param.shape, jnp.float32) for param in params))
    totals, (results, token_grads) = lax.scan(step, zeros, (token_groups, cot_groups, segment_groups))
    return (results.reshape(TOKENS, D), token_grads.reshape(TOKENS, D), totals[0], totals[1], totals[2], totals[3], totals[4], totals[5], totals[6], totals[7])
```

```python
import itertools
import math

import jax
import jax.numpy as jnp
from jax import lax
from jax.sharding import Mesh
from jax.sharding import PartitionSpec as P

HEAD_DIM = 64


norm_epsilon = 1e-05
masked_value = -1e30
gelu_factor = 0.7978845608028654


def gelu_tanh(values):
    return (
        0.5
        * values
        * (1.0 + jnp.tanh(gelu_factor * (values + 0.044715 * values * values * values)))
    )


def norm_forward(values, gain_row, shift_row):
    mean_val = jnp.mean(values, axis=-1, keepdims=True)
    centered = values - mean_val
    variance = jnp.mean(centered * centered, axis=-1, keepdims=True)
    inverse = lax.rsqrt(variance + norm_epsilon)
    unit_rows = centered * inverse
    return (unit_rows * gain_row + shift_row, unit_rows, inverse)


def norm_backward(grad_rows, unit_rows, inverse, gain_row):
    scaled = grad_rows * gain_row
    mean_grad = jnp.mean(scaled, axis=-1, keepdims=True)
    mean_cross = jnp.mean(scaled * unit_rows, axis=-1, keepdims=True)
    return inverse * (scaled - mean_grad - unit_rows * mean_cross)


def inner_rows(left_side, right_side):
    return lax.dot_general(
        left_side, right_side, (((0,), (0,)), ((), ())), preferred_element_type=jnp.float32
    )


def inner_cols(left_side, right_side):
    return lax.dot_general(
        left_side, right_side, (((1,), (1,)), ((), ())), preferred_element_type=jnp.float32
    )


AXES = ("xh", "xl", "yl", "zh", "zl", "c", "h")
DP = AXES[:6]
NEAR = ("xh", "zh", "h")
RING = {"x": ("xh", "xl"), "y": ("h", "yl"), "z": ("zh", "zl")}
PLACE = {"z": 0, "y": 1, "x": 2}
TURNS = (("x", "y", "z"), ("y", "z", "x"), ("z", "x", "y"))


def swap_roles(values):
    return lax.ppermute(values, ("c", "h"), [(0, 0), (1, 2), (2, 1), (3, 3)])


def pair(values):
    return lax.ppermute(values, "c", [(0, 1), (1, 0)])


def step_along(values, axis):
    high, low = RING[axis]
    order = [name for name in AXES if name in (high, low, "c")]
    moves = []
    for place in itertools.product(range(2), repeat=3):
        target = dict(zip(order, place))
        target[low] ^= 1
        target[high] ^= target["c"]
        moves.append(
            (place[0] * 4 + place[1] * 2 + place[2], sum(target[n] << (2 - i) for i, n in enumerate(order)))
        )
    return lax.ppermute(values, tuple(order), moves)


def gather_near(shard):
    copies = jnp.broadcast_to(shard[None], (8,) + shard.shape)
    return lax.all_to_all(copies, NEAR, split_axis=0, concat_axis=0, tiled=True).reshape(
        8 * shard.shape[0], shard.shape[1]
    )


def gather_far(pieces):
    pieces = [piece.reshape((1, 1, 1) + piece.shape) for piece in pieces]
    for turn in range(3):
        others = [step_along(piece, TURNS[i][turn]) for i, piece in enumerate(pieces)]
        pieces = [
            jnp.concatenate((piece, other), axis=PLACE[TURNS[i][turn]])
            for i, (piece, other) in enumerate(zip(pieces, others))
        ]
    return [piece.reshape(8 * piece.shape[3], piece.shape[4]) for piece in pieces]


def scatter_far(piece, turns):
    rows = piece.shape[0] // 8
    piece = piece.reshape(2, 2, 2, rows, piece.shape[1])
    for axis in turns[::-1]:
        place = PLACE[axis]
        mine = lax.slice_in_dim(piece, 0, 1, axis=place)
        other = step_along(lax.slice_in_dim(piece, 1, 2, axis=place), axis)
        piece = (mine.astype(jnp.float32) + other.astype(jnp.float32)).astype(jnp.bfloat16)
    return piece.reshape(rows, piece.shape[4])


def scatter_near(block):
    parts = block.reshape(8, block.shape[0] // 8, block.shape[1])
    parts = lax.all_to_all(parts, NEAR, split_axis=0, concat_axis=0, tiled=True)
    return jnp.sum(parts.astype(jnp.float32), axis=0)


def feature_order(width):
    block = width // 64
    place = lax.broadcasted_iota(jnp.int32, (width, width), 1)
    inner = place % block
    near = (place // block) % 8
    far = place // (8 * block)
    xl = lax.axis_index("xl") ^ (far & 1)
    yl = lax.axis_index("yl") ^ ((far >> 1) & 1)
    zl = lax.axis_index("zl") ^ (far >> 2)
    xh, zh, h = near >> 2, (near >> 1) & 1, near & 1
    source = (xh * 32 + xl * 16 + yl * 8 + zh * 4 + zl * 2 + h) * block + inner
    return (lax.broadcasted_iota(jnp.int32, (width, width), 0) == source).astype(jnp.bfloat16)


def mask_scores(scores, segment_ids, score_scale):
    length = segment_ids.shape[0]
    position = lax.iota(jnp.int32, length)
    allowed = (segment_ids[:, None] == segment_ids[None, :]) & (
        position[:, None] >= position[None, :]
    )
    return jnp.where(allowed[None], scores * score_scale, masked_value)


def dot(left, right):
    return jnp.dot(left, right, preferred_element_type=jnp.float32)


def local(
    tokens,
    cotangent,
    segments,
    input_weight,
    output_weight,
    up_weight,
    down_weight,
    head_bias,
    hidden_bias,
    norm_gains,
    shifts,
):
    bf16, f32 = jnp.bfloat16, jnp.float32
    half, width = tokens.shape
    length = segments.shape[1]
    block = input_weight.shape[0]
    heads_width = input_weight.shape[2]
    hidden_width = up_weight.shape[1]
    local_heads = heads_width // HEAD_DIM
    score_scale = 1.0 / math.sqrt(HEAD_DIM)
    core = lax.axis_index("c")

    spare = jnp.zeros((block, 122), bf16)
    shard = jnp.concatenate(
        (
            input_weight.reshape(block, 3 * heads_width),
            output_weight.T,
            norm_gains.T,
            shifts.T,
            spare,
            up_weight,
            down_weight.T,
        ),
        axis=1,
    )
    near_block = gather_near(swap_roles(shard))
    first_end = 4 * heads_width + 128
    second_end = first_end + hidden_width
    first, up_full, down_full = gather_far(
        (near_block[:, :first_end], near_block[:, first_end:second_end], near_block[:, second_end:])
    )
    input_full = first[:, : 3 * heads_width]
    output_full = first[:, 3 * heads_width : 4 * heads_width]
    vectors = first[:, 4 * heads_width : 4 * heads_width + 8].T.astype(f32)
    gains_full, shifts_full = vectors[:2], vectors[2:6]

    small = swap_roles(
        jnp.concatenate(
            (head_bias.reshape(-1), hidden_bias, segments[0].astype(bf16))
        )
    )
    bias_rows = small[: 2 * heads_width].reshape(2, heads_width).astype(f32)
    hidden_row = small[2 * heads_width : 2 * heads_width + hidden_width].astype(f32)
    segment_ids = small[2 * heads_width + hidden_width :].astype(jnp.int32)

    order = feature_order(width)

    def arrange(rows):
        return dot(rows, order)

    def restore(rows):
        return inner_cols(rows, order).astype(bf16)

    def own_half(rows):
        return lax.dynamic_slice_in_dim(rows, core * half, half, axis=0)

    def other_half(rows):
        return lax.dynamic_slice_in_dim(rows, (1 - core) * half, half, axis=0)

    residual = arrange(lax.all_gather(swap_roles(tokens), "c", axis=0, tiled=True))
    grad_out = arrange(lax.all_gather(swap_roles(cotangent), "c", axis=0, tiled=True))
    grad_rows = grad_out.astype(bf16)

    normed_one, unit_one, inverse_one = norm_forward(residual, gains_full[0], shifts_full[0])
    rows_one = normed_one.astype(bf16)
    mixed = dot(rows_one, input_full)

    def split(rows):
        return jnp.transpose(rows.reshape(length, local_heads, HEAD_DIM), (1, 0, 2))

    def merge(rows):
        return jnp.transpose(rows, (1, 0, 2)).reshape(length, heads_width)

    queries = split((mixed[:, :heads_width] + bias_rows[0]).astype(bf16))
    key_heads = split(mixed[:, heads_width : 2 * heads_width].astype(bf16))
    value_heads = split((mixed[:, 2 * heads_width :] + bias_rows[1]).astype(bf16))
    scores = mask_scores(
        jnp.einsum("hqd,hkd->hqk", queries, key_heads, preferred_element_type=f32),
        segment_ids,
        score_scale,
    )
    exponent = jnp.exp(scores - jnp.max(scores, axis=-1, keepdims=True))
    soft = exponent / jnp.sum(exponent, axis=-1, keepdims=True)
    soft_low = soft.astype(bf16)
    context = merge(
        jnp.einsum("hqk,hkd->hqd", soft_low, value_heads, preferred_element_type=f32).astype(bf16)
    )
    attended = inner_cols(context, output_full).astype(bf16)
    middle = residual + attended.astype(f32) + pair(attended).astype(f32) + shifts_full[2]

    normed_two, unit_two, inverse_two = norm_forward(middle, gains_full[1], shifts_full[1])
    rows_two = normed_two.astype(bf16)
    before = dot(rows_two, up_full) + hidden_row
    hidden = gelu_tanh(before).astype(bf16)
    down_grad = inner_rows(grad_rows, hidden).astype(bf16)
    down_block = scatter_far(down_grad, TURNS[2])
    grad_hidden = dot(grad_rows, down_full)
    _, gelu_pull = jax.vjp(gelu_tanh, before)
    grad_before = gelu_pull(grad_hidden)[0].astype(bf16)
    up_grad = inner_rows(rows_two, grad_before).astype(bf16)
    up_block = scatter_far(up_grad, TURNS[1])
    hidden_bias_grad = jnp.sum(grad_before, axis=0, dtype=f32)
    grad_two = inner_cols(grad_before, up_full).astype(bf16)
    grad_norm_two = grad_two.astype(f32) + pair(grad_two).astype(f32)
    grad_middle = grad_out + norm_backward(grad_norm_two, unit_two, inverse_two, gains_full[1])
    middle_rows = grad_middle.astype(bf16)

    feed = inner_cols(hidden, down_full).astype(bf16)
    outcome = (
        own_half(middle)
        + own_half(feed).astype(f32)
        + pair(other_half(feed)).astype(f32)
        + shifts_full[3]
    )
    block_out = swap_roles(restore(outcome.astype(bf16)))

    output_grad = inner_rows(middle_rows, context).astype(bf16)
    grad_context = split(dot(middle_rows, output_full).astype(bf16))
    grad_soft = jnp.einsum("hqd,hkd->hqk", grad_context, value_heads, preferred_element_type=f32)
    grad_scores = (
        soft * (grad_soft - jnp.sum(soft * grad_soft, axis=-1, keepdims=True))
    ).astype(bf16)
    grad_queries = merge(
        (
            jnp.einsum("hqk,hkd->hqd", grad_scores, key_heads, preferred_element_type=f32)
            * score_scale
        ).astype(bf16)
    )
    grad_keys = merge(
        (
            jnp.einsum("hqk,hqd->hkd", grad_scores, queries, preferred_element_type=f32)
            * score_scale
        ).astype(bf16)
    )
    grad_values = merge(
        jnp.einsum("hqk,hqd->hkd", soft_low, grad_context, preferred_element_type=f32).astype(bf16)
    )
    grad_mixed = jnp.concatenate((grad_queries, grad_keys, grad_values), axis=1)
    grad_one = inner_cols(grad_mixed, input_full).astype(bf16)
    grad_norm_one = grad_one.astype(f32) + pair(grad_one).astype(f32)
    input_grad = inner_rows(rows_one, grad_mixed).astype(bf16)
    token_grad = grad_middle + norm_backward(grad_norm_one, unit_one, inverse_one, gains_full[0])
    token_grad = swap_roles(restore(own_half(token_grad).astype(bf16)))

    head_rows = jnp.stack(
        (jnp.sum(grad_queries, axis=0, dtype=f32), jnp.sum(grad_values, axis=0, dtype=f32))
    )
    bias_terms = jnp.concatenate(
        (
            jnp.transpose(hidden_bias_grad.reshape(width, 2)),
            jnp.transpose(head_rows.reshape(2, 64, block // 2), (1, 0, 2)).reshape(1, width),
        )
    )
    bias_terms = jnp.dot(
        bias_terms, order.astype(f32), precision=lax.Precision.HIGHEST, preferred_element_type=f32
    )
    terms = jnp.concatenate(
        (
            jnp.stack(
                (
                    jnp.sum(grad_norm_one * unit_one, axis=0),
                    jnp.sum(grad_norm_two * unit_two, axis=0),
                    jnp.sum(grad_norm_one, axis=0),
                    jnp.sum(grad_norm_two, axis=0),
                    jnp.sum(grad_middle, axis=0),
                    jnp.sum(grad_out, axis=0),
                )
            ),
            bias_terms,
            jnp.zeros((119, width), f32),
        )
    )
    first_grad = jnp.concatenate((input_grad, output_grad, terms.astype(bf16).T), axis=1)
    first_block = scatter_far(first_grad, TURNS[0])
    grads = swap_roles(
        scatter_near(jnp.concatenate((first_block, up_block, down_block), axis=1)).astype(bf16)
    ).astype(f32)

    vector_part = grads[:, 4 * heads_width : first_end]
    tensor_half = lax.axis_index("h")
    six = block // 2
    norm_terms = lax.dynamic_slice_in_dim(vector_part[:, :6], tensor_half * six, six, axis=0).T
    return (
        block_out,
        token_grad,
        grads[:, : 3 * heads_width].reshape(block, 3, heads_width),
        grads[:, 3 * heads_width : 4 * heads_width].T,
        grads[:, first_end:second_end],
        grads[:, second_end:].T,
        vector_part[:, 8].reshape(2, six),
        vector_part[:, 6:8].reshape(2 * block),
        norm_terms[:2],
        norm_terms[2:6],
    )


def solution(mesh):
    fine = Mesh(mesh.devices.reshape((2,) * 7), AXES)
    in_specs = (
        P(AXES, None),
        P(AXES, None),
        P(DP, None),
        P(DP, None, "h"),
        P("h", DP),
        P(DP, "h"),
        P("h", DP),
        P(None, "h"),
        P("h"),
        P(None, DP),
        P(None, DP),
    )
    out_specs = (
        P(AXES, None),
        P(AXES, None),
        P(DP, None, "h"),
        P("h", DP),
        P(DP, "h"),
        P("h", DP),
        P(None, ("h",) + DP),
        P(("h",) + DP),
        P(None, AXES),
        P(None, AXES),
    )
    return jax.shard_map(local, mesh=fine, in_specs=in_specs, out_specs=out_specs, check_vma=False)
```

```python
import itertools
import math

import jax
import jax.numpy as jnp
from jax import lax
from jax.sharding import Mesh
from jax.sharding import PartitionSpec as P

HEAD_DIM = 64


norm_epsilon = 1e-05
masked_value = -1e30
gelu_factor = 0.7978845608028654


def gelu_tanh(values):
    return (
        0.5
        * values
        * (1.0 + jnp.tanh(gelu_factor * (values + 0.044715 * values * values * values)))
    )


def norm_forward(values, gain_row, shift_row):
    mean_val = jnp.mean(values, axis=-1, keepdims=True)
    centered = values - mean_val
    variance = jnp.mean(centered * centered, axis=-1, keepdims=True)
    inverse = lax.rsqrt(variance + norm_epsilon)
    unit_rows = centered * inverse
    return (unit_rows * gain_row + shift_row, unit_rows, inverse)


def norm_backward(grad_rows, unit_rows, inverse, gain_row):
    scaled = grad_rows * gain_row
    mean_grad = jnp.mean(scaled, axis=-1, keepdims=True)
    mean_cross = jnp.mean(scaled * unit_rows, axis=-1, keepdims=True)
    return inverse * (scaled - mean_grad - unit_rows * mean_cross)


def inner_rows(left_side, right_side):
    return lax.dot_general(
        left_side, right_side, (((0,), (0,)), ((), ())), preferred_element_type=jnp.float32
    )


def inner_cols(left_side, right_side):
    return lax.dot_general(
        left_side, right_side, (((1,), (1,)), ((), ())), preferred_element_type=jnp.float32
    )


AXES = ("xh", "xl", "yl", "zh", "zl", "c", "h")
DP = AXES[:6]
NEAR = ("xh", "zh", "h")
RING = {"x": ("xh", "xl"), "y": ("h", "yl"), "z": ("zh", "zl")}
PLACE = {"z": 0, "y": 1, "x": 2}
TURNS = (("x", "y", "z"), ("y", "z", "x"), ("z", "x", "y"))


def swap_roles(values):
    return lax.ppermute(values, ("c", "h"), [(0, 0), (1, 2), (2, 1), (3, 3)])


def pair(values):
    return lax.ppermute(values, "c", [(0, 1), (1, 0)])


def step_along(values, axis):
    high, low = RING[axis]
    order = [name for name in AXES if name in (high, low, "c")]
    moves = []
    for place in itertools.product(range(2), repeat=3):
        target = dict(zip(order, place))
        target[low] ^= 1
        target[high] ^= target["c"]
        moves.append(
            (place[0] * 4 + place[1] * 2 + place[2], sum(target[n] << (2 - i) for i, n in enumerate(order)))
        )
    return lax.ppermute(values, tuple(order), moves)


def gather_near(shard):
    copies = jnp.broadcast_to(shard[None], (8,) + shard.shape)
    return lax.all_to_all(copies, NEAR, split_axis=0, concat_axis=0, tiled=True).reshape(
        8 * shard.shape[0], shard.shape[1]
    )


def doubled(pieces, turn):
    others = [step_along(piece, TURNS[i][turn]) for i, piece in enumerate(pieces)]
    return [
        jnp.concatenate((piece, other), axis=PLACE[TURNS[i][turn]])
        for i, (piece, other) in enumerate(zip(pieces, others))
    ]


def open_blocks(piece):
    return piece.reshape((1, 1, 1) + piece.shape)


def close_blocks(piece):
    return piece.reshape(8 * piece.shape[3], piece.shape[4])


def scatter_far(pieces):
    rows = pieces[0].shape[0] // 8
    pieces = [piece.reshape(2, 2, 2, rows, piece.shape[1]) for piece in pieces]
    for turn in range(3):
        places = [PLACE[TURNS[i][turn]] for i in range(3)]
        sent = [lax.slice_in_dim(piece, 1, 2, axis=place) for piece, place in zip(pieces, places)]
        others = [step_along(part, TURNS[i][turn]) for i, part in enumerate(sent)]
        pieces = [
            (
                lax.slice_in_dim(piece, 0, 1, axis=place).astype(jnp.float32)
                + other.astype(jnp.float32)
            ).astype(jnp.bfloat16)
            for piece, place, other in zip(pieces, places, others)
        ]
    return jnp.concatenate([piece.reshape(rows, piece.shape[4]) for piece in pieces], axis=1)


def scatter_near(block):
    parts = block.reshape(8, block.shape[0] // 8, block.shape[1])
    parts = lax.all_to_all(parts, NEAR, split_axis=0, concat_axis=0, tiled=True)
    return jnp.sum(parts.astype(jnp.float32), axis=0)


def feature_order(width):
    block = width // 64
    place = lax.broadcasted_iota(jnp.int32, (width, width), 1)
    inner = place % block
    near = (place // block) % 8
    far = place // (8 * block)
    xl = lax.axis_index("xl") ^ (far & 1)
    yl = lax.axis_index("yl") ^ ((far >> 1) & 1)
    zl = lax.axis_index("zl") ^ (far >> 2)
    xh, zh, h = near >> 2, (near >> 1) & 1, near & 1
    source = (xh * 32 + xl * 16 + yl * 8 + zh * 4 + zl * 2 + h) * block + inner
    return (lax.broadcasted_iota(jnp.int32, (width, width), 0) == source).astype(jnp.bfloat16)


def mask_scores(scores, segment_ids, score_scale):
    length = segment_ids.shape[0]
    position = lax.iota(jnp.int32, length)
    allowed = (segment_ids[:, None] == segment_ids[None, :]) & (
        position[:, None] >= position[None, :]
    )
    return jnp.where(allowed[None], scores * score_scale, masked_value)


def dot(left, right):
    return jnp.dot(left, right, preferred_element_type=jnp.float32)


def local(
    tokens,
    cotangent,
    segments,
    input_weight,
    output_weight,
    up_weight,
    down_weight,
    head_bias,
    hidden_bias,
    norm_gains,
    shifts,
):
    bf16, f32 = jnp.bfloat16, jnp.float32
    half, width = tokens.shape
    length = segments.shape[1]
    block = input_weight.shape[0]
    heads_width = input_weight.shape[2]
    hidden_width = up_weight.shape[1]
    local_heads = heads_width // HEAD_DIM
    score_scale = 1.0 / math.sqrt(HEAD_DIM)
    core = lax.axis_index("c")

    third = hidden_width // 3
    down_rows = down_weight.T
    feed_parts = []
    for i in range(3):
        feed_parts += [
            up_weight[:, i * third : (i + 1) * third],
            down_rows[:, i * third : (i + 1) * third],
        ]
    shard = jnp.concatenate(
        [
            input_weight.reshape(block, 3 * heads_width),
            output_weight.T,
            norm_gains.T,
            shifts.T,
            jnp.zeros((block, 122), bf16),
        ]
        + feed_parts,
        axis=1,
    )
    near_block = gather_near(swap_roles(shard))
    first_end = 4 * heads_width + 128
    cuts = (0, 512, 1024, first_end)
    firsts = [open_blocks(near_block[:, cuts[i] : cuts[i + 1]]) for i in range(3)]
    feeds = [
        open_blocks(near_block[:, first_end + 2 * i * third : first_end + 2 * (i + 1) * third])
        for i in range(3)
    ]
    firsts = doubled(doubled(firsts, 0), 1)
    firsts, feeds = lax.optimization_barrier((firsts, feeds))
    first = jnp.concatenate([close_blocks(piece) for piece in doubled(firsts, 2)], axis=1)
    for turn in range(3):
        feeds = doubled(feeds, turn)
    feeds = [close_blocks(piece) for piece in feeds]
    up_full = jnp.concatenate([piece[:, :third] for piece in feeds], axis=1)
    down_full = jnp.concatenate([piece[:, third:] for piece in feeds], axis=1)
    input_full = first[:, : 3 * heads_width]
    output_full = first[:, 3 * heads_width : 4 * heads_width]
    vectors = first[:, 4 * heads_width : 4 * heads_width + 8].T.astype(f32)
    gains_full, shifts_full = vectors[:2], vectors[2:6]

    small = swap_roles(
        jnp.concatenate(
            (head_bias.reshape(-1), hidden_bias, segments[0].astype(bf16))
        )
    )
    bias_rows = small[: 2 * heads_width].reshape(2, heads_width).astype(f32)
    hidden_row = small[2 * heads_width : 2 * heads_width + hidden_width].astype(f32)
    segment_ids = small[2 * heads_width + hidden_width :].astype(jnp.int32)

    order = feature_order(width)

    def arrange(rows):
        return dot(rows, order)

    def restore(rows):
        return inner_cols(rows, order).astype(bf16)

    def own_half(rows):
        return lax.dynamic_slice_in_dim(rows, core * half, half, axis=0)

    def other_half(rows):
        return lax.dynamic_slice_in_dim(rows, (1 - core) * half, half, axis=0)

    residual = arrange(lax.all_gather(swap_roles(tokens), "c", axis=0, tiled=True))
    grad_out = arrange(lax.all_gather(swap_roles(cotangent), "c", axis=0, tiled=True))
    grad_rows = grad_out.astype(bf16)

    normed_one, unit_one, inverse_one = norm_forward(residual, gains_full[0], shifts_full[0])
    rows_one = normed_one.astype(bf16)
    mixed = dot(rows_one, input_full)

    def split(rows):
        return jnp.transpose(rows.reshape(length, local_heads, HEAD_DIM), (1, 0, 2))

    def merge(rows):
        return jnp.transpose(rows, (1, 0, 2)).reshape(length, heads_width)

    queries = split((mixed[:, :heads_width] + bias_rows[0]).astype(bf16))
    key_heads = split(mixed[:, heads_width : 2 * heads_width].astype(bf16))
    value_heads = split((mixed[:, 2 * heads_width :] + bias_rows[1]).astype(bf16))
    scores = mask_scores(
        jnp.einsum("hqd,hkd->hqk", queries, key_heads, preferred_element_type=f32),
        segment_ids,
        score_scale,
    )
    exponent = jnp.exp(scores - jnp.max(scores, axis=-1, keepdims=True))
    soft = exponent / jnp.sum(exponent, axis=-1, keepdims=True)
    soft_low = soft.astype(bf16)
    context = merge(
        jnp.einsum("hqk,hkd->hqd", soft_low, value_heads, preferred_element_type=f32).astype(bf16)
    )
    attended = inner_cols(context, output_full).astype(bf16)
    middle = residual + attended.astype(f32) + pair(attended).astype(f32) + shifts_full[2]

    normed_two, unit_two, inverse_two = norm_forward(middle, gains_full[1], shifts_full[1])
    rows_two = normed_two.astype(bf16)
    before = dot(rows_two, up_full) + hidden_row
    hidden = gelu_tanh(before).astype(bf16)
    down_grad = inner_rows(grad_rows, hidden).astype(bf16)
    grad_hidden = dot(grad_rows, down_full)
    _, gelu_pull = jax.vjp(gelu_tanh, before)
    grad_before = gelu_pull(grad_hidden)[0].astype(bf16)
    up_grad = inner_rows(rows_two, grad_before).astype(bf16)
    feed_grads = scatter_far(
        [
            jnp.concatenate(
                (
                    up_grad[:, i * third : (i + 1) * third],
                    down_grad[:, i * third : (i + 1) * third],
                ),
                axis=1,
            )
            for i in range(3)
        ]
    )
    feed_grads = swap_roles(scatter_near(feed_grads).astype(bf16)).astype(f32)
    hidden_bias_grad = jnp.sum(grad_before, axis=0, dtype=f32)
    grad_two = inner_cols(grad_before, up_full).astype(bf16)
    grad_norm_two = grad_two.astype(f32) + pair(grad_two).astype(f32)
    grad_middle = grad_out + norm_backward(grad_norm_two, unit_two, inverse_two, gains_full[1])
    middle_rows = grad_middle.astype(bf16)

    feed = inner_cols(hidden, down_full).astype(bf16)
    outcome = (
        own_half(middle)
        + own_half(feed).astype(f32)
        + pair(other_half(feed)).astype(f32)
        + shifts_full[3]
    )
    block_out = swap_roles(restore(outcome.astype(bf16)))

    output_grad = inner_rows(middle_rows, context).astype(bf16)
    grad_context = split(dot(middle_rows, output_full).astype(bf16))
    grad_soft = jnp.einsum("hqd,hkd->hqk", grad_context, value_heads, preferred_element_type=f32)
    grad_scores = (
        soft * (grad_soft - jnp.sum(soft * grad_soft, axis=-1, keepdims=True))
    ).astype(bf16)
    grad_queries = merge(
        (
            jnp.einsum("hqk,hkd->hqd", grad_scores, key_heads, preferred_element_type=f32)
            * score_scale
        ).astype(bf16)
    )
    grad_keys = merge(
        (
            jnp.einsum("hqk,hqd->hkd", grad_scores, queries, preferred_element_type=f32)
            * score_scale
        ).astype(bf16)
    )
    grad_values = merge(
        jnp.einsum("hqk,hqd->hkd", soft_low, grad_context, preferred_element_type=f32).astype(bf16)
    )
    grad_mixed = jnp.concatenate((grad_queries, grad_keys, grad_values), axis=1)
    grad_one = inner_cols(grad_mixed, input_full).astype(bf16)
    grad_norm_one = grad_one.astype(f32) + pair(grad_one).astype(f32)
    input_grad = inner_rows(rows_one, grad_mixed).astype(bf16)
    token_grad = grad_middle + norm_backward(grad_norm_one, unit_one, inverse_one, gains_full[0])
    token_grad = swap_roles(restore(own_half(token_grad).astype(bf16)))

    head_rows = jnp.stack(
        (jnp.sum(grad_queries, axis=0, dtype=f32), jnp.sum(grad_values, axis=0, dtype=f32))
    )
    bias_terms = jnp.concatenate(
        (
            jnp.transpose(hidden_bias_grad.reshape(width, 2)),
            jnp.transpose(head_rows.reshape(2, 64, block // 2), (1, 0, 2)).reshape(1, width),
        )
    )
    bias_terms = jnp.dot(
        bias_terms, order.astype(f32), precision=lax.Precision.HIGHEST, preferred_element_type=f32
    )
    terms = jnp.concatenate(
        (
            jnp.stack(
                (
                    jnp.sum(grad_norm_one * unit_one, axis=0),
                    jnp.sum(grad_norm_two * unit_two, axis=0),
                    jnp.sum(grad_norm_one, axis=0),
                    jnp.sum(grad_norm_two, axis=0),
                    jnp.sum(grad_middle, axis=0),
                    jnp.sum(grad_out, axis=0),
                )
            ),
            bias_terms,
            jnp.zeros((119, width), f32),
        )
    )
    first_grad = jnp.concatenate((input_grad, output_grad, terms.astype(bf16).T), axis=1)
    first_block = scatter_far([first_grad[:, cuts[i] : cuts[i + 1]] for i in range(3)])
    grads = swap_roles(scatter_near(first_block).astype(bf16)).astype(f32)
    up_out = jnp.concatenate(
        [feed_grads[:, 2 * i * third : (2 * i + 1) * third] for i in range(3)], axis=1
    )
    down_out = jnp.concatenate(
        [feed_grads[:, (2 * i + 1) * third : (2 * i + 2) * third] for i in range(3)], axis=1
    )

    vector_part = grads[:, 4 * heads_width : first_end]
    tensor_half = lax.axis_index("h")
    six = block // 2
    norm_terms = lax.dynamic_slice_in_dim(vector_part[:, :6], tensor_half * six, six, axis=0).T
    return (
        block_out,
        token_grad,
        grads[:, : 3 * heads_width].reshape(block, 3, heads_width),
        grads[:, 3 * heads_width : 4 * heads_width].T,
        up_out,
        down_out.T,
        vector_part[:, 8].reshape(2, six),
        vector_part[:, 6:8].reshape(2 * block),
        norm_terms[:2],
        norm_terms[2:6],
    )


def solution(mesh):
    fine = Mesh(mesh.devices.reshape((2,) * 7), AXES)
    in_specs = (
        P(AXES, None),
        P(AXES, None),
        P(DP, None),
        P(DP, None, "h"),
        P("h", DP),
        P(DP, "h"),
        P("h", DP),
        P(None, "h"),
        P("h"),
        P(None, DP),
        P(None, DP),
    )
    out_specs = (
        P(AXES, None),
        P(AXES, None),
        P(DP, None, "h"),
        P("h", DP),
        P(DP, "h"),
        P("h", DP),
        P(None, ("h",) + DP),
        P(("h",) + DP),
        P(None, AXES),
        P(None, AXES),
    )
    return jax.shard_map(local, mesh=fine, in_specs=in_specs, out_specs=out_specs, check_vma=False)
```

```python
import functools
import itertools
import math

import jax
import jax.numpy as jnp
from jax import lax
from jax.experimental import pallas as pl
from jax.experimental.pallas import tpu as pltpu
from jax.sharding import Mesh
from jax.sharding import PartitionSpec as P

HEAD_DIM = 64


norm_epsilon = 1e-05
masked_value = -1e30
gelu_factor = 0.7978845608028654


def inner_cols(left_side, right_side):
    return lax.dot_general(
        left_side, right_side, (((1,), (1,)), ((), ())), preferred_element_type=jnp.float32
    )


AXES = ("xh", "xl", "yl", "zh", "zl", "c", "h")
DP = AXES[:6]
NEAR = ("xh", "zh", "h")
RING = {"x": ("xh", "xl"), "y": ("h", "yl"), "z": ("zh", "zl")}
PLACE = {"z": 0, "y": 1, "x": 2}
TURNS = (("x", "y", "z"), ("y", "z", "x"), ("z", "x", "y"))


def swap_roles(values):
    return lax.ppermute(values, ("c", "h"), [(0, 0), (1, 2), (2, 1), (3, 3)])


def pair(values):
    return lax.ppermute(values, "c", [(0, 1), (1, 0)])


def step_along(values, axis):
    high, low = RING[axis]
    order = [name for name in AXES if name in (high, low, "c")]
    moves = []
    for place in itertools.product(range(2), repeat=3):
        target = dict(zip(order, place))
        target[low] ^= 1
        target[high] ^= target["c"]
        moves.append(
            (place[0] * 4 + place[1] * 2 + place[2], sum(target[n] << (2 - i) for i, n in enumerate(order)))
        )
    return lax.ppermute(values, tuple(order), moves)


def gather_near(shard):
    copies = jnp.broadcast_to(shard[None], (8,) + shard.shape)
    return lax.all_to_all(copies, NEAR, split_axis=0, concat_axis=0, tiled=True).reshape(
        8 * shard.shape[0], shard.shape[1]
    )


def gather_far(pieces):
    pieces = [piece.reshape((1, 1, 1) + piece.shape) for piece in pieces]
    for turn in range(3):
        others = [step_along(piece, TURNS[i][turn]) for i, piece in enumerate(pieces)]
        pieces = [
            jnp.concatenate((piece, other), axis=PLACE[TURNS[i][turn]])
            for i, (piece, other) in enumerate(zip(pieces, others))
        ]
    return [piece.reshape(8 * piece.shape[3], piece.shape[4]) for piece in pieces]


def scatter_far(keep, send, turns):
    rows, columns = keep.shape[0] // 4, keep.shape[1]
    axes = list(turns[::-1])
    left = sorted(axes[1:], key=PLACE.get)
    other = step_along(send, axes[0])
    piece = (keep.astype(jnp.float32) + other.astype(jnp.float32)).astype(jnp.bfloat16)
    piece = piece.reshape(2, 2, rows, columns)
    for axis in axes[1:]:
        place = left.index(axis)
        mine = lax.slice_in_dim(piece, 0, 1, axis=place)
        other = step_along(lax.slice_in_dim(piece, 1, 2, axis=place), axis)
        piece = (mine.astype(jnp.float32) + other.astype(jnp.float32)).astype(jnp.bfloat16)
    return piece.reshape(rows, columns)


def scatter_near(block):
    parts = block.reshape(8, block.shape[0] // 8, block.shape[1])
    parts = lax.all_to_all(parts, NEAR, split_axis=0, concat_axis=0, tiled=True)
    return jnp.sum(parts.astype(jnp.float32), axis=0)


def feature_order(width):
    block = width // 64
    place = lax.broadcasted_iota(jnp.int32, (width, width), 1)
    inner = place % block
    near = (place // block) % 8
    far = place // (8 * block)
    xl = lax.axis_index("xl") ^ (far & 1)
    yl = lax.axis_index("yl") ^ ((far >> 1) & 1)
    zl = lax.axis_index("zl") ^ (far >> 2)
    xh, zh, h = near >> 2, (near >> 1) & 1, near & 1
    source = (xh * 32 + xl * 16 + yl * 8 + zh * 4 + zl * 2 + h) * block + inner
    return (lax.broadcasted_iota(jnp.int32, (width, width), 0) == source).astype(jnp.bfloat16)


def column_norm(values):
    mean_val = jnp.mean(values, axis=-1, keepdims=True)
    centered = values - mean_val
    variance = jnp.mean(centered * centered, axis=-1, keepdims=True)
    inverse = lax.rsqrt(variance + norm_epsilon)
    return centered * inverse, inverse


def nn(left, right):
    return jnp.dot(left, right, preferred_element_type=jnp.float32)


def key_mask(segment_row, keys, first, queries):
    column = jnp.transpose(jnp.broadcast_to(segment_row, (8, segment_row.shape[1])))[:keys, :1]
    row = segment_row[:, first : first + queries]
    key_pos = lax.broadcasted_iota(jnp.int32, (keys, queries), 0)
    query_pos = lax.broadcasted_iota(jnp.int32, (keys, queries), 1) + first
    return jnp.where((column == row) & (key_pos <= query_pos), 0.0, masked_value)


def lane_half(values, which):
    lane = lax.broadcasted_iota(jnp.int32, values.shape, 1)
    inside = (lane >= HEAD_DIM) if which else (lane < HEAD_DIM)
    return jnp.where(inside, values, jnp.zeros_like(values))


def attend_kernel(
    score_scale,
    rows_ref,
    vector_ref,
    input_ref,
    output_ref,
    bias_ref,
    segment_ref,
    normed_ref,
    mixed_ref,
    log_ref,
    context_ref,
    attended_ref,
):
    bf16 = jnp.bfloat16
    length = rows_ref.shape[0]
    width = output_ref.shape[1]
    half = length // 2
    unit, _ = column_norm(rows_ref[...].astype(jnp.float32))
    normed_ref[...] = (unit * vector_ref[0:1] + vector_ref[2:3]).astype(bf16)
    mixed = nn(normed_ref[...], input_ref[...])
    mixed_ref[:, :width] = (mixed[:, :width] + bias_ref[0:1]).astype(bf16)
    mixed_ref[:, width : 2 * width] = mixed[:, width : 2 * width].astype(bf16)
    mixed_ref[:, 2 * width :] = (mixed[:, 2 * width :] + bias_ref[1:2]).astype(bf16)
    segment_row = segment_ref[...]
    spans = ((0, half, key_mask(segment_row, half, 0, half)), (half, length, key_mask(segment_row, length, half, half)))
    log_ref[...] = jnp.zeros_like(log_ref)
    for two in range(width // 128):
        at = 128 * two
        query_two = mixed_ref[:, at : at + 128] * jnp.asarray(score_scale, bf16)
        key_two = mixed_ref[:, width + at : width + at + 128]
        value_turned = jnp.transpose(mixed_ref[:, 2 * width + at : 2 * width + at + 128])
        parts = []
        for which in range(2):
            query_rows = lane_half(query_two, which)
            value_rows = value_turned[HEAD_DIM * which : HEAD_DIM * (which + 1)]
            sides = []
            for first, keys, mask in spans:
                scores = inner_cols(key_two[:keys], query_rows[first : first + half]) + mask
                top = jnp.max(scores, axis=0, keepdims=True)
                exponent = jnp.exp(scores - top)
                total = jnp.sum(exponent, axis=0, keepdims=True)
                log_ref[2 * two + which : 2 * two + which + 1, first : first + half] = top + jnp.log(total)
                sides.append(nn(value_rows[:, :keys], exponent.astype(bf16)) / total)
            parts.append(jnp.concatenate(sides, axis=1))
        context_ref[:, at : at + 128] = jnp.transpose(jnp.concatenate(parts, axis=0)).astype(bf16)
    attended_ref[...] = inner_cols(context_ref[...], output_ref[...]).astype(bf16)


def store_blocks(value, place, keep_ref, send_ref, columns):
    rows = value.shape[0] // 8
    counts = [0, 0]
    for block in range(8):
        which = (block >> (2 - place)) & 1
        target = send_ref if which else keep_ref
        at = counts[which] * rows
        counts[which] += 1
        target[at : at + rows, columns] = value[block * rows : (block + 1) * rows].astype(target.dtype)


def feed_kernel(
    rows_ref,
    own_ref,
    other_ref,
    vector_ref,
    up_ref,
    down_ref,
    bias_ref,
    cot_ref,
    middle_ref,
    feed_ref,
    grad_two_ref,
    up_keep_ref,
    up_send_ref,
    down_keep_ref,
    down_send_ref,
    bias_grad_ref,
    normed_ref,
    normed_turned_ref,
    cot_turned_ref,
):
    bf16, f32 = jnp.bfloat16, jnp.float32
    middle = (
        rows_ref[...].astype(f32)
        + (own_ref[...].astype(f32) + other_ref[...].astype(f32))
        + vector_ref[4:5]
    )
    middle_ref[...] = middle
    unit, _ = column_norm(middle)
    normed_ref[...] = (unit * vector_ref[1:2] + vector_ref[3:4]).astype(bf16)
    normed_turned_ref[...] = jnp.transpose(normed_ref[...])
    cot_turned_ref[...] = jnp.transpose(cot_ref[...])
    hidden_width = up_ref.shape[1]
    step = hidden_width // 3
    bias_grad_ref[...] = jnp.zeros_like(bias_grad_ref)
    feed = grad_two = None
    for at in range(0, hidden_width, step):
        columns = slice(at, at + step)
        before = nn(normed_ref[...], up_ref[:, columns]) + bias_ref[:, columns]
        square = before * before
        bend = jnp.tanh(gelu_factor * (before + 0.044715 * before * square))
        opened = 0.5 * (1.0 + bend)
        hidden = (before * opened).astype(bf16)
        slope = opened + 0.5 * before * (1.0 - bend * bend) * (
            gelu_factor * (1.0 + 3.0 * 0.044715 * square)
        )
        grad_before = (nn(cot_ref[...], down_ref[:, columns]) * slope).astype(bf16)
        part = inner_cols(hidden, down_ref[:, columns])
        feed = part if feed is None else feed + part
        part = inner_cols(grad_before, up_ref[:, columns])
        grad_two = part if grad_two is None else grad_two + part
        bias_grad_ref[0:1, columns] = jnp.sum(grad_before.astype(f32), axis=0, keepdims=True)
        store_blocks(nn(cot_turned_ref[...], hidden), PLACE[TURNS[2][2]], down_keep_ref, down_send_ref, columns)
        store_blocks(nn(normed_turned_ref[...], grad_before), PLACE[TURNS[1][2]], up_keep_ref, up_send_ref, columns)
    feed_ref[...] = feed.astype(bf16)
    grad_two_ref[...] = grad_two.astype(bf16)


def attend_back_kernel(
    score_scale,
    middle_ref,
    cot_ref,
    own_ref,
    other_ref,
    vector_ref,
    context_ref,
    mixed_ref,
    log_ref,
    input_ref,
    output_ref,
    segment_ref,
    grad_middle_ref,
    output_grad_ref,
    grad_mixed_ref,
    grad_one_ref,
    sums_ref,
    head_sums_ref,
    grad_context_ref,
):
    bf16, f32 = jnp.bfloat16, jnp.float32
    length = middle_ref.shape[0]
    width = output_ref.shape[1]
    half = length // 2
    unit, inverse = column_norm(middle_ref[...])
    grad_norm = own_ref[...].astype(f32) + other_ref[...].astype(f32)
    scaled = grad_norm * vector_ref[1:2]
    mean_grad = jnp.mean(scaled, axis=-1, keepdims=True)
    mean_cross = jnp.mean(scaled * unit, axis=-1, keepdims=True)
    cot = cot_ref[...].astype(f32)
    grad_middle = cot + inverse * (scaled - mean_grad - unit * mean_cross)
    grad_middle_ref[...] = grad_middle
    sums_ref[...] = jnp.zeros_like(sums_ref)
    sums_ref[0:1] = jnp.sum(grad_norm * unit, axis=0, keepdims=True)
    sums_ref[1:2] = jnp.sum(grad_norm, axis=0, keepdims=True)
    sums_ref[2:3] = jnp.sum(grad_middle, axis=0, keepdims=True)
    sums_ref[3:4] = jnp.sum(cot, axis=0, keepdims=True)
    middle_rows = grad_middle.astype(bf16)
    output_grad_ref[...] = nn(jnp.transpose(middle_rows), context_ref[...]).astype(bf16)
    grad_context_ref[...] = nn(middle_rows, output_ref[...]).astype(bf16)
    segment_row = segment_ref[...]
    spans = ((0, half, key_mask(segment_row, half, 0, half)), (half, length, key_mask(segment_row, length, half, half)))
    head_sums_ref[...] = jnp.zeros_like(head_sums_ref)
    for two in range(width // 128):
        at = 128 * two
        query_two = mixed_ref[:, at : at + 128] * jnp.asarray(score_scale, bf16)
        key_two = mixed_ref[:, width + at : width + at + 128]
        value_two = mixed_ref[:, 2 * width + at : 2 * width + at + 128]
        grad_two = grad_context_ref[:, at : at + 128]
        key_turned = jnp.transpose(key_two)
        grad_queries = []
        grad_keys = [0.0, 0.0]
        grad_values = [0.0, 0.0]
        for which in range(2):
            query_rows = lane_half(query_two, which)
            grad_rows = lane_half(grad_two, which)
            key_rows = key_turned[HEAD_DIM * which : HEAD_DIM * (which + 1)]
            sides = []
            for side, (first, keys, mask) in enumerate(spans):
                query_side = query_rows[first : first + half]
                grad_side = grad_rows[first : first + half]
                log_side = log_ref[2 * two + which : 2 * two + which + 1, first : first + half]
                scores = inner_cols(key_two[:keys], query_side) + mask
                soft = jnp.exp(scores - log_side)
                grad_soft = inner_cols(value_two[:keys], grad_side)
                crossed = soft * grad_soft
                grad_scores = (
                    crossed - soft * jnp.sum(crossed, axis=0, keepdims=True)
                ).astype(bf16)
                grad_keys[side] += nn(grad_scores, query_side)
                grad_values[side] += nn(soft.astype(bf16), grad_side)
                sides.append(nn(key_rows[:, :keys], grad_scores))
            grad_queries.append(jnp.concatenate(sides, axis=1))
        queries_out = jnp.transpose(jnp.concatenate(grad_queries, axis=0)) * score_scale
        for place, value in enumerate((queries_out, grad_keys, grad_values)):
            columns = slice(place * width + at, place * width + at + 128)
            if place == 0:
                grad_mixed_ref[:, columns] = value.astype(bf16)
            else:
                grad_mixed_ref[:half, columns] = (value[0] + value[1][:half]).astype(bf16)
                grad_mixed_ref[half:, columns] = value[1][half:].astype(bf16)
            head_sums_ref[0:1, columns] = jnp.sum(
                grad_mixed_ref[:, columns].astype(f32), axis=0, keepdims=True
            )
    grad_one_ref[...] = inner_cols(grad_mixed_ref[...], input_ref[...]).astype(bf16)


def token_kernel(
    core_ref,
    rows_ref,
    own_ref,
    other_ref,
    grad_middle_ref,
    vector_ref,
    normed_ref,
    grad_mixed_ref,
    output_grad_ref,
    sums_ref,
    bias_terms_ref,
    order_ref,
    token_ref,
    keep_ref,
    send_ref,
    token_full_ref,
    terms_ref,
):
    bf16, f32 = jnp.bfloat16, jnp.float32
    half = token_ref.shape[0]
    width = output_grad_ref.shape[1]
    place = PLACE[TURNS[0][2]]
    unit, inverse = column_norm(rows_ref[...].astype(f32))
    grad_norm = own_ref[...].astype(f32) + other_ref[...].astype(f32)
    scaled = grad_norm * vector_ref[0:1]
    mean_grad = jnp.mean(scaled, axis=-1, keepdims=True)
    mean_cross = jnp.mean(scaled * unit, axis=-1, keepdims=True)
    token_full_ref[...] = (
        grad_middle_ref[...] + inverse * (scaled - mean_grad - unit * mean_cross)
    )
    start = pl.multiple_of(core_ref[0] * half, half)
    token_rows = token_full_ref[pl.ds(start, half), :].astype(bf16)
    token_ref[...] = inner_cols(token_rows, order_ref[...]).astype(bf16)
    terms_ref[...] = jnp.zeros_like(terms_ref)
    terms_ref[0:1] = jnp.sum(grad_norm * unit, axis=0, keepdims=True)
    terms_ref[1:2] = sums_ref[0:1]
    terms_ref[2:3] = jnp.sum(grad_norm, axis=0, keepdims=True)
    terms_ref[3:6] = sums_ref[1:4]
    bias_terms = bias_terms_ref[...]
    high = bias_terms.astype(bf16)
    low = (bias_terms - high.astype(f32)).astype(bf16)
    terms_ref[8:16] = nn(high, order_ref[...]) + nn(low, order_ref[...])
    turned = jnp.transpose(normed_ref[...])
    for at in range(0, 3 * width, width):
        columns = slice(at, at + width)
        store_blocks(nn(turned, grad_mixed_ref[:, columns]), place, keep_ref, send_ref, columns)
    store_blocks(output_grad_ref[...], place, keep_ref, send_ref, slice(3 * width, 4 * width))
    store_blocks(
        jnp.transpose(terms_ref[...]), place, keep_ref, send_ref, slice(4 * width, 4 * width + 128)
    )


def call(kernel, outs, scratch, *operands, smem=0):
    space = [pl.BlockSpec(memory_space=pltpu.SMEM)] * smem
    space += [pl.BlockSpec(memory_space=pltpu.VMEM)] * (len(operands) - smem)
    return pl.pallas_call(
        kernel,
        out_shape=[jax.ShapeDtypeStruct(shape, kind) for shape, kind in outs],
        in_specs=space,
        out_specs=[pl.BlockSpec(memory_space=pltpu.VMEM)] * len(outs),
        scratch_shapes=[pltpu.VMEM(shape, kind) for shape, kind in scratch],
        compiler_params=pltpu.CompilerParams(vmem_limit_bytes=56 * 1024 * 1024),
    )(*operands)


def local(
    tokens,
    cotangent,
    segments,
    input_weight,
    output_weight,
    up_weight,
    down_weight,
    head_bias,
    hidden_bias,
    norm_gains,
    shifts,
):
    bf16, f32 = jnp.bfloat16, jnp.float32
    half, width = tokens.shape
    length = segments.shape[1]
    block = input_weight.shape[0]
    heads_width = input_weight.shape[2]
    hidden_width = up_weight.shape[1]
    local_heads = heads_width // HEAD_DIM
    score_scale = 1.0 / math.sqrt(HEAD_DIM)
    core = lax.axis_index("c")

    spare = jnp.zeros((block, 122), bf16)
    shard = jnp.concatenate(
        (
            input_weight.reshape(block, 3 * heads_width),
            output_weight.T,
            norm_gains.T,
            shifts.T,
            spare,
            up_weight,
            down_weight.T,
        ),
        axis=1,
    )
    near_block = gather_near(swap_roles(shard))
    first_end = 4 * heads_width + 128
    second_end = first_end + hidden_width
    first, up_full, down_full = gather_far(
        (near_block[:, :first_end], near_block[:, first_end:second_end], near_block[:, second_end:])
    )
    input_full = first[:, : 3 * heads_width]
    output_full = first[:, 3 * heads_width : 4 * heads_width]
    vectors = first[:, 4 * heads_width : 4 * heads_width + 8].T.astype(f32)

    small = swap_roles(
        jnp.concatenate(
            (head_bias.reshape(-1), hidden_bias, segments[0].astype(bf16))
        )
    )
    bias_rows = small[: 2 * heads_width].reshape(2, heads_width).astype(f32)
    hidden_row = small[2 * heads_width : 2 * heads_width + hidden_width].astype(f32)
    segment_row = small[2 * heads_width + hidden_width :].astype(f32).reshape(1, length)

    order = feature_order(width)

    def own_half(rows):
        return lax.dynamic_slice_in_dim(rows, core * half, half, axis=0)

    def other_half(rows):
        return lax.dynamic_slice_in_dim(rows, (1 - core) * half, half, axis=0)

    def full_rows(rows):
        return nn(lax.all_gather(swap_roles(rows), "c", axis=0, tiled=True), order).astype(bf16)

    rows = full_rows(tokens)
    cot_rows = full_rows(cotangent)

    normed_one, mixed, log_sums, context, attended = call(
        functools.partial(attend_kernel, score_scale),
        [
            ((length, width), bf16),
            ((length, 3 * heads_width), bf16),
            ((8, length), f32),
            ((length, heads_width), bf16),
            ((length, width), bf16),
        ],
        [],
        rows,
        vectors,
        input_full,
        output_full,
        bias_rows,
        segment_row,
    )
    middle, feed, grad_two, up_keep, up_send, down_keep, down_send, hidden_sums = call(
        feed_kernel,
        [
            ((length, width), f32),
            ((length, width), bf16),
            ((length, width), bf16),
            ((width // 2, hidden_width), bf16),
            ((width // 2, hidden_width), bf16),
            ((width // 2, hidden_width), bf16),
            ((width // 2, hidden_width), bf16),
            ((8, hidden_width), f32),
        ],
        [((length, width), bf16), ((width, length), bf16), ((width, length), bf16)],
        rows,
        attended,
        pair(attended),
        vectors,
        up_full,
        down_full,
        hidden_row.reshape(1, hidden_width),
        cot_rows,
    )
    down_block = scatter_far(down_keep, down_send, TURNS[2])
    up_block = scatter_far(up_keep, up_send, TURNS[1])
    outcome = (
        own_half(middle)
        + own_half(feed).astype(f32)
        + pair(other_half(feed)).astype(f32)
        + vectors[5]
    )
    block_out = swap_roles(inner_cols(outcome.astype(bf16), order).astype(bf16))

    grad_middle, output_grad, grad_mixed, grad_one, sums, head_sums = call(
        functools.partial(attend_back_kernel, score_scale),
        [
            ((length, width), f32),
            ((width, heads_width), bf16),
            ((length, 3 * heads_width), bf16),
            ((length, width), bf16),
            ((8, width), f32),
            ((8, 3 * heads_width), f32),
        ],
        [((length, heads_width), bf16)],
        middle,
        cot_rows,
        grad_two,
        pair(grad_two),
        vectors,
        context,
        mixed,
        log_sums,
        input_full,
        output_full,
        segment_row,
    )
    head_rows = jnp.stack((head_sums[0, :heads_width], head_sums[0, 2 * heads_width :]))
    bias_terms = jnp.concatenate(
        (
            jnp.transpose(hidden_sums[0].reshape(width, 2)),
            jnp.transpose(head_rows.reshape(2, 64, block // 2), (1, 0, 2)).reshape(1, width),
            jnp.zeros((5, width), f32),
        )
    )
    token_grad, first_keep, first_send = call(
        token_kernel,
        [
            ((half, width), bf16),
            ((width // 2, first_end), bf16),
            ((width // 2, first_end), bf16),
        ],
        [((length, width), f32), ((128, width), f32)],
        core.astype(jnp.int32).reshape(1),
        rows,
        grad_one,
        pair(grad_one),
        grad_middle,
        vectors,
        normed_one,
        grad_mixed,
        output_grad,
        sums,
        bias_terms,
        order,
        smem=1,
    )
    token_grad = swap_roles(token_grad)
    first_block = scatter_far(first_keep, first_send, TURNS[0])
    grads = swap_roles(
        scatter_near(jnp.concatenate((first_block, up_block, down_block), axis=1)).astype(bf16)
    ).astype(f32)

    vector_part = grads[:, 4 * heads_width : first_end]
    tensor_half = lax.axis_index("h")
    six = block // 2
    norm_terms = lax.dynamic_slice_in_dim(vector_part[:, :6], tensor_half * six, six, axis=0).T
    return (
        block_out,
        token_grad,
        grads[:, : 3 * heads_width].reshape(block, 3, heads_width),
        grads[:, 3 * heads_width : 4 * heads_width].T,
        grads[:, first_end:second_end],
        grads[:, second_end:].T,
        vector_part[:, 10].reshape(2, six),
        vector_part[:, 8:10].reshape(2 * block),
        norm_terms[:2],
        norm_terms[2:6],
    )


def solution(mesh):
    fine = Mesh(mesh.devices.reshape((2,) * 7), AXES)
    in_specs = (
        P(AXES, None),
        P(AXES, None),
        P(DP, None),
        P(DP, None, "h"),
        P("h", DP),
        P(DP, "h"),
        P("h", DP),
        P(None, "h"),
        P("h"),
        P(None, DP),
        P(None, DP),
    )
    out_specs = (
        P(AXES, None),
        P(AXES, None),
        P(DP, None, "h"),
        P("h", DP),
        P(DP, "h"),
        P("h", DP),
        P(None, ("h",) + DP),
        P(("h",) + DP),
        P(None, AXES),
        P(None, AXES),
    )
    return jax.shard_map(local, mesh=fine, in_specs=in_specs, out_specs=out_specs, check_vma=False)
```

```python
import functools
import itertools
import math

import jax
import jax.numpy as jnp
from jax import lax
from jax.experimental import pallas as pl
from jax.experimental.pallas import tpu as pltpu
from jax.sharding import Mesh
from jax.sharding import PartitionSpec as P

HEAD_DIM = 64


norm_epsilon = 1e-05
masked_value = -1e30
gelu_factor = 0.7978845608028654


def inner_cols(left_side, right_side):
    return lax.dot_general(
        left_side, right_side, (((1,), (1,)), ((), ())), preferred_element_type=jnp.float32
    )


AXES = ("xh", "xl", "yl", "zh", "zl", "c", "h")
DP = AXES[:6]
RING = {"x": ("xh", "xl"), "y": ("h", "yl"), "z": ("zh", "zl")}
PLACE = {"z": 0, "y": 1, "x": 2}
TURNS = (("x", "y", "z"), ("y", "z", "x"), ("z", "x", "y"))


def swap_roles(values):
    return lax.ppermute(values, ("c", "h"), [(0, 0), (1, 2), (2, 1), (3, 3)])


def pair(values):
    return lax.ppermute(values, "c", [(0, 1), (1, 0)])


def step_along(values, axis):
    high, low = RING[axis]
    order = [name for name in AXES if name in (high, low, "c")]
    moves = []
    for place in itertools.product(range(2), repeat=3):
        target = dict(zip(order, place))
        target[low] ^= 1
        target[high] ^= target["c"]
        moves.append(
            (place[0] * 4 + place[1] * 2 + place[2], sum(target[n] << (2 - i) for i, n in enumerate(order)))
        )
    return lax.ppermute(values, tuple(order), moves)


def near_moves(mask, outward):
    moves = []
    for xh, zh, c, h in itertools.product(range(2), repeat=4):
        target = [xh ^ (mask >> 2), zh ^ ((mask >> 1) & 1)]
        target += [h, c ^ (mask & 1)] if outward else [h ^ (mask & 1), c]
        moves.append((xh * 8 + zh * 4 + c * 2 + h, sum(bit << (3 - i) for i, bit in enumerate(target))))
    return moves


def near_permute(values, mask, outward):
    return lax.ppermute(values, ("xh", "zh", "c", "h"), near_moves(mask, outward))


def open_blocks(piece):
    return piece.reshape((1, 1, 1) + piece.shape)


def gather_far(pieces):
    pieces = [open_blocks(piece) for piece in pieces]
    for turn in range(3):
        others = [step_along(piece, TURNS[i][turn]) for i, piece in enumerate(pieces)]
        if turn < 2:
            pieces = [
                jnp.concatenate((piece, other), axis=PLACE[TURNS[i][turn]])
                for i, (piece, other) in enumerate(zip(pieces, others))
            ]
    return [
        [half.reshape(4 * half.shape[3], half.shape[4]) for half in halves]
        for halves in zip(pieces, others)
    ]


def source_block(near, far):
    xl = lax.axis_index("xl") ^ (far & 1)
    yl = lax.axis_index("yl") ^ ((far >> 1) & 1)
    zl = lax.axis_index("zl") ^ (far >> 2)
    xh, zh, h = near >> 2, (near >> 1) & 1, near & 1
    return xh * 32 + xl * 16 + yl * 8 + zh * 4 + zl * 2 + h


def feature_order(width):
    block = width // 64
    place = lax.broadcasted_iota(jnp.int32, (width, width), 1)
    source = source_block((place // block) % 8, place // (8 * block)) * block + place % block
    return (lax.broadcasted_iota(jnp.int32, (width, width), 0) == source).astype(jnp.bfloat16)


def block_order(width):
    block = width // 64
    place = lax.broadcasted_iota(jnp.int32, (width, 64), 0)
    source = source_block((place // block) % 8, place // (8 * block))
    return (lax.broadcasted_iota(jnp.int32, (width, 64), 1) == source).astype(jnp.bfloat16)


def place_rows(rows, columns, row_block, column_block, me):
    block = min(row_block, column_block)
    row = lax.broadcasted_iota(jnp.int32, (rows, columns), 0)
    column = lax.broadcasted_iota(jnp.int32, (rows, columns), 1)
    found = jnp.zeros((rows, columns), jnp.bool_)
    for k in range(8):
        inside = (row >= k * row_block) & (row < k * row_block + block)
        other = (me ^ k) * column_block
        found = found | (inside & (column - other == row - k * row_block))
    return found.astype(jnp.float32).astype(jnp.bfloat16)


def eye(size):
    row = lax.broadcasted_iota(jnp.int32, (size, size), 0)
    column = lax.broadcasted_iota(jnp.int32, (size, size), 1)
    return (row == column).astype(jnp.float32).astype(jnp.bfloat16)


def pack_kernel(input_ref, output_ref, up_ref, down_ref, gains_ref, shifts_ref, shard_ref, small_ref):
    bf16 = jnp.bfloat16
    block, width = input_ref.shape[0], output_ref.shape[0]
    hidden_width = up_ref.shape[1]
    one = eye(block)
    shard_ref[:, : 3 * width] = input_ref[...]
    shard_ref[:, 3 * width : 4 * width] = inner_cols(one, output_ref[...]).astype(bf16)
    small_ref[...] = jnp.zeros_like(small_ref)
    small_ref[0:2] = gains_ref[...].astype(jnp.float32)
    small_ref[2:6] = shifts_ref[...].astype(jnp.float32)
    at = 4 * width + 128
    shard_ref[:, 4 * width : at] = inner_cols(one, small_ref[...].astype(bf16)).astype(bf16)
    shard_ref[:, at : at + hidden_width] = up_ref[...]
    shard_ref[:, at + hidden_width :] = inner_cols(one, down_ref[...]).astype(bf16)


def collect_kernel(me_ref, *refs):
    parts, outs, held_ref = refs[:8], refs[8:11], refs[11]
    block = parts[0].shape[0]
    held_ref[...] = jnp.zeros_like(held_ref)
    for k in range(8):
        held_ref[16 * k : 16 * k + block] = parts[k][...]
    moved = place_rows(8 * block, 128, block, 16, me_ref[0])
    at = 0
    for out in outs:
        columns = out.shape[1]
        out[...] = nn(moved, held_ref[:, at : at + columns]).astype(jnp.bfloat16)
        at += columns


def deal_kernel(me_ref, *refs):
    parts, outs, held_ref = refs[:6], refs[6:14], refs[14]
    rows, block = parts[0].shape[0], outs[0].shape[0]
    moved = place_rows(128, rows, 16, block, me_ref[0])
    at = 0
    for keep, other in zip(parts[::2], parts[1::2]):
        columns = keep.shape[1]
        total = (keep[...].astype(jnp.float32) + other[...].astype(jnp.float32)).astype(jnp.bfloat16)
        held_ref[:, at : at + columns] = nn(moved, total).astype(jnp.bfloat16)
        at += columns
    for k in range(8):
        outs[k][...] = held_ref[16 * k : 16 * k + block]


def unpack_kernel(half_ref, *refs):
    parts = refs[:8]
    input_ref, output_ref, up_ref, down_ref, head_ref, hidden_ref, gain_ref, shift_ref = refs[8:16]
    tall_ref = refs[16]
    f32 = jnp.float32
    block, width = input_ref.shape[0], output_ref.shape[0]
    hidden_width = up_ref.shape[1]
    six = block // 2

    def total(start, size):
        columns = slice(start, start + size)
        value = parts[0][:, columns].astype(f32)
        for part in parts[1:]:
            value = value + part[:, columns].astype(f32)
        return value

    def pick(rows, columns, offset):
        row = lax.broadcasted_iota(jnp.int32, (rows, columns), 0)
        column = lax.broadcasted_iota(jnp.int32, (rows, columns), 1)
        return (row == column + offset).astype(f32)

    def exact(left, right, dims):
        return lax.dot_general(
            left, right, (dims, ((), ())), precision=lax.Precision.HIGHEST, preferred_element_type=f32
        )

    input_ref[...] = total(0, 3 * width)
    at = 4 * width + 128
    up_ref[...] = total(at, hidden_width)
    tall_ref[...] = jnp.zeros_like(tall_ref)
    tall_ref[:block] = total(at + hidden_width, hidden_width)
    down_ref[...] = jnp.transpose(tall_ref[...])[:, :block]
    tall_ref[:block, :width] = total(3 * width, width)
    output_ref[...] = jnp.transpose(tall_ref[:, :width])[:, :block]
    small = total(4 * width, 128)
    norm_terms = exact(small, pick(block, six, half_ref[0] * six), ((0,), (0,)))
    gain_ref[...] = norm_terms[0:2]
    shift_ref[...] = norm_terms[2:6]
    hidden_ref[...] = exact(small[0:1], pick(128, 2 * block, 8), ((1,), (0,)))
    head_ref[0:1] = exact(small[0:1], pick(128, six, 8 + 2 * block), ((1,), (0,)))
    head_ref[1:2] = exact(small[0:1], pick(128, six, 8 + 2 * block + six), ((1,), (0,)))


def fold_kernel(place, keep_ref, other_ref, next_keep_ref, next_send_ref):
    rows = keep_ref.shape[0] // 4
    counts = [0, 0]
    for block in range(4):
        which = (block >> (1 - place)) & 1
        target = next_send_ref if which else next_keep_ref
        at = counts[which] * rows
        counts[which] += 1
        span = slice(block * rows, (block + 1) * rows)
        target[at : at + rows] = (
            keep_ref[span].astype(jnp.float32) + other_ref[span].astype(jnp.float32)
        ).astype(jnp.bfloat16)


def halve_kernel(keep_ref, other_ref, next_keep_ref, next_send_ref):
    rows = keep_ref.shape[0] // 2
    for target, span in ((next_keep_ref, slice(0, rows)), (next_send_ref, slice(rows, 2 * rows))):
        target[...] = (
            keep_ref[span].astype(jnp.float32) + other_ref[span].astype(jnp.float32)
        ).astype(jnp.bfloat16)


def fold(keep, other, kernel):
    shape = ((keep.shape[0] // 2, keep.shape[1]), jnp.bfloat16)
    return call(kernel, [shape, shape], [], keep, other)


def second_fold(turns):
    left = sorted(turns[:2], key=PLACE.get)
    return functools.partial(fold_kernel, left.index(turns[1]))


def column_norm(values):
    mean_val = jnp.mean(values, axis=-1, keepdims=True)
    centered = values - mean_val
    variance = jnp.mean(centered * centered, axis=-1, keepdims=True)
    inverse = lax.rsqrt(variance + norm_epsilon)
    return centered * inverse, inverse


def nn(left, right):
    return jnp.dot(left, right, preferred_element_type=jnp.float32)


def key_mask(segment_row, keys, first, queries):
    column = jnp.transpose(jnp.broadcast_to(segment_row, (8, segment_row.shape[1])))[:keys, :1]
    row = segment_row[:, first : first + queries]
    key_pos = lax.broadcasted_iota(jnp.int32, (keys, queries), 0)
    query_pos = lax.broadcasted_iota(jnp.int32, (keys, queries), 1) + first
    return jnp.where((column == row) & (key_pos <= query_pos), 0.0, masked_value)


def lane_half(values, which):
    lane = lax.broadcasted_iota(jnp.int32, values.shape, 1)
    inside = (lane >= HEAD_DIM) if which else (lane < HEAD_DIM)
    return jnp.where(inside, values, jnp.zeros_like(values))


def attend_kernel(
    score_scale,
    rows_ref,
    low_ref,
    high_ref,
    bias_ref,
    segment_ref,
    vector_ref,
    normed_ref,
    mixed_ref,
    log_ref,
    context_ref,
    attended_ref,
):
    bf16 = jnp.bfloat16
    length = rows_ref.shape[0]
    width = context_ref.shape[1]
    rows = low_ref.shape[0]
    for at, part_ref in ((0, low_ref), (rows, high_ref)):
        turned = jnp.transpose(part_ref[:, 4 * width : 4 * width + 128].astype(jnp.float32))
        vector_ref[:, at : at + rows] = turned[:8]
    half = length // 2
    unit, _ = column_norm(rows_ref[...].astype(jnp.float32))
    normed_ref[...] = (unit * vector_ref[0:1] + vector_ref[2:3]).astype(bf16)
    mixed = nn(normed_ref[:, :rows], low_ref[:, : 3 * width]) + nn(
        normed_ref[:, rows:], high_ref[:, : 3 * width]
    )
    mixed_ref[:, :width] = (mixed[:, :width] + bias_ref[0:1]).astype(bf16)
    mixed_ref[:, width : 2 * width] = mixed[:, width : 2 * width].astype(bf16)
    mixed_ref[:, 2 * width :] = (mixed[:, 2 * width :] + bias_ref[1:2]).astype(bf16)
    segment_row = segment_ref[...]
    spans = ((0, half, key_mask(segment_row, half, 0, half)), (half, length, key_mask(segment_row, length, half, half)))
    log_ref[...] = jnp.zeros_like(log_ref)
    for two in range(width // 128):
        at = 128 * two
        query_two = mixed_ref[:, at : at + 128] * jnp.asarray(score_scale, bf16)
        key_two = mixed_ref[:, width + at : width + at + 128]
        value_turned = jnp.transpose(mixed_ref[:, 2 * width + at : 2 * width + at + 128])
        parts = []
        for which in range(2):
            query_rows = lane_half(query_two, which)
            value_rows = value_turned[HEAD_DIM * which : HEAD_DIM * (which + 1)]
            sides = []
            for first, keys, mask in spans:
                scores = inner_cols(key_two[:keys], query_rows[first : first + half]) + mask
                top = jnp.max(scores, axis=0, keepdims=True)
                exponent = jnp.exp(scores - top)
                total = jnp.sum(exponent, axis=0, keepdims=True)
                log_ref[2 * two + which : 2 * two + which + 1, first : first + half] = top + jnp.log(total)
                sides.append(nn(value_rows[:, :keys], exponent.astype(bf16)) / total)
            parts.append(jnp.concatenate(sides, axis=1))
        context_ref[:, at : at + 128] = jnp.transpose(jnp.concatenate(parts, axis=0)).astype(bf16)
    for at, part_ref in ((0, low_ref), (rows, high_ref)):
        attended_ref[:, at : at + rows] = inner_cols(
            context_ref[...], part_ref[:, 3 * width : 4 * width]
        ).astype(bf16)


def store_blocks(value, place, keep_ref, send_ref, columns):
    rows = value.shape[0] // 8
    counts = [0, 0]
    for block in range(8):
        which = (block >> (2 - place)) & 1
        target = send_ref if which else keep_ref
        at = counts[which] * rows
        counts[which] += 1
        target[at : at + rows, columns] = value[block * rows : (block + 1) * rows].astype(target.dtype)


def join_blocks(place, keep_ref, other_ref, whole_ref):
    rows = whole_ref.shape[0] // 8
    counts = [0, 0]
    for block in range(8):
        which = (block >> (2 - place)) & 1
        at = counts[which] * rows
        counts[which] += 1
        source = other_ref if which else keep_ref
        whole_ref[block * rows : (block + 1) * rows] = source[at : at + rows]


def feed_kernel(
    rows_ref,
    own_ref,
    other_ref,
    vector_ref,
    up_mine_ref,
    up_other_ref,
    down_mine_ref,
    down_other_ref,
    bias_ref,
    cot_ref,
    middle_ref,
    feed_ref,
    grad_two_ref,
    up_keep_ref,
    up_send_ref,
    down_keep_ref,
    down_send_ref,
    bias_grad_ref,
    normed_ref,
    normed_turned_ref,
    cot_turned_ref,
    up_ref,
    down_ref,
):
    bf16, f32 = jnp.bfloat16, jnp.float32
    join_blocks(PLACE[TURNS[1][2]], up_mine_ref, up_other_ref, up_ref)
    join_blocks(PLACE[TURNS[2][2]], down_mine_ref, down_other_ref, down_ref)
    middle = (
        rows_ref[...].astype(f32)
        + (own_ref[...].astype(f32) + other_ref[...].astype(f32))
        + vector_ref[4:5]
    )
    middle_ref[...] = middle
    unit, _ = column_norm(middle)
    normed_ref[...] = (unit * vector_ref[1:2] + vector_ref[3:4]).astype(bf16)
    normed_turned_ref[...] = jnp.transpose(normed_ref[...])
    cot_turned_ref[...] = jnp.transpose(cot_ref[...])
    hidden_width = up_ref.shape[1]
    step = hidden_width // 3
    bias_grad_ref[...] = jnp.zeros_like(bias_grad_ref)
    feed = grad_two = None
    for at in range(0, hidden_width, step):
        columns = slice(at, at + step)
        before = nn(normed_ref[...], up_ref[:, columns]) + bias_ref[:, columns]
        square = before * before
        bend = jnp.tanh(gelu_factor * (before + 0.044715 * before * square))
        opened = 0.5 * (1.0 + bend)
        hidden = (before * opened).astype(bf16)
        slope = opened + 0.5 * before * (1.0 - bend * bend) * (
            gelu_factor * (1.0 + 3.0 * 0.044715 * square)
        )
        grad_before = (nn(cot_ref[...], down_ref[:, columns]) * slope).astype(bf16)
        part = inner_cols(hidden, down_ref[:, columns])
        feed = part if feed is None else feed + part
        part = inner_cols(grad_before, up_ref[:, columns])
        grad_two = part if grad_two is None else grad_two + part
        bias_grad_ref[0:1, columns] = jnp.sum(grad_before.astype(f32), axis=0, keepdims=True)
        store_blocks(nn(cot_turned_ref[...], hidden), PLACE[TURNS[2][2]], down_keep_ref, down_send_ref, columns)
        store_blocks(nn(normed_turned_ref[...], grad_before), PLACE[TURNS[1][2]], up_keep_ref, up_send_ref, columns)
    feed_ref[...] = feed.astype(bf16)
    grad_two_ref[...] = grad_two.astype(bf16)


def attend_back_kernel(
    score_scale,
    middle_ref,
    cot_ref,
    own_ref,
    other_ref,
    vector_ref,
    context_ref,
    mixed_ref,
    log_ref,
    low_ref,
    high_ref,
    segment_ref,
    grad_middle_ref,
    output_grad_ref,
    grad_mixed_ref,
    grad_one_ref,
    sums_ref,
    head_sums_ref,
    grad_context_ref,
):
    bf16, f32 = jnp.bfloat16, jnp.float32
    length = middle_ref.shape[0]
    width = context_ref.shape[1]
    rows = low_ref.shape[0]
    half = length // 2
    unit, inverse = column_norm(middle_ref[...])
    grad_norm = own_ref[...].astype(f32) + other_ref[...].astype(f32)
    scaled = grad_norm * vector_ref[1:2]
    mean_grad = jnp.mean(scaled, axis=-1, keepdims=True)
    mean_cross = jnp.mean(scaled * unit, axis=-1, keepdims=True)
    cot = cot_ref[...].astype(f32)
    grad_middle = cot + inverse * (scaled - mean_grad - unit * mean_cross)
    grad_middle_ref[...] = grad_middle
    sums_ref[...] = jnp.zeros_like(sums_ref)
    sums_ref[0:1] = jnp.sum(grad_norm * unit, axis=0, keepdims=True)
    sums_ref[1:2] = jnp.sum(grad_norm, axis=0, keepdims=True)
    sums_ref[2:3] = jnp.sum(grad_middle, axis=0, keepdims=True)
    sums_ref[3:4] = jnp.sum(cot, axis=0, keepdims=True)
    middle_rows = grad_middle.astype(bf16)
    output_grad_ref[...] = nn(jnp.transpose(middle_rows), context_ref[...]).astype(bf16)
    grad_context_ref[...] = (
        nn(middle_rows[:, :rows], low_ref[:, 3 * width : 4 * width])
        + nn(middle_rows[:, rows:], high_ref[:, 3 * width : 4 * width])
    ).astype(bf16)
    segment_row = segment_ref[...]
    spans = ((0, half, key_mask(segment_row, half, 0, half)), (half, length, key_mask(segment_row, length, half, half)))
    head_sums_ref[...] = jnp.zeros_like(head_sums_ref)
    for two in range(width // 128):
        at = 128 * two
        query_two = mixed_ref[:, at : at + 128] * jnp.asarray(score_scale, bf16)
        key_two = mixed_ref[:, width + at : width + at + 128]
        value_two = mixed_ref[:, 2 * width + at : 2 * width + at + 128]
        grad_two = grad_context_ref[:, at : at + 128]
        key_turned = jnp.transpose(key_two)
        grad_queries = []
        grad_keys = [0.0, 0.0]
        grad_values = [0.0, 0.0]
        for which in range(2):
            query_rows = lane_half(query_two, which)
            grad_rows = lane_half(grad_two, which)
            key_rows = key_turned[HEAD_DIM * which : HEAD_DIM * (which + 1)]
            sides = []
            for side, (first, keys, mask) in enumerate(spans):
                query_side = query_rows[first : first + half]
                grad_side = grad_rows[first : first + half]
                log_side = log_ref[2 * two + which : 2 * two + which + 1, first : first + half]
                scores = inner_cols(key_two[:keys], query_side) + mask
                soft = jnp.exp(scores - log_side)
                grad_soft = inner_cols(value_two[:keys], grad_side)
                crossed = soft * grad_soft
                grad_scores = (
                    crossed - soft * jnp.sum(crossed, axis=0, keepdims=True)
                ).astype(bf16)
                grad_keys[side] += nn(grad_scores, query_side)
                grad_values[side] += nn(soft.astype(bf16), grad_side)
                sides.append(nn(key_rows[:, :keys], grad_scores))
            grad_queries.append(jnp.concatenate(sides, axis=1))
        queries_out = jnp.transpose(jnp.concatenate(grad_queries, axis=0)) * score_scale
        for place, value in enumerate((queries_out, grad_keys, grad_values)):
            columns = slice(place * width + at, place * width + at + 128)
            if place == 0:
                grad_mixed_ref[:, columns] = value.astype(bf16)
            else:
                grad_mixed_ref[:half, columns] = (value[0] + value[1][:half]).astype(bf16)
                grad_mixed_ref[half:, columns] = value[1][half:].astype(bf16)
            head_sums_ref[0:1, columns] = jnp.sum(
                grad_mixed_ref[:, columns].astype(f32), axis=0, keepdims=True
            )
    for at, part_ref in ((0, low_ref), (rows, high_ref)):
        grad_one_ref[:, at : at + rows] = inner_cols(
            grad_mixed_ref[...], part_ref[:, : 3 * width]
        ).astype(bf16)


def token_kernel(
    core_ref,
    rows_ref,
    own_ref,
    other_ref,
    grad_middle_ref,
    vector_ref,
    normed_ref,
    grad_mixed_ref,
    output_grad_ref,
    sums_ref,
    bias_ref,
    block_ref,
    order_ref,
    token_ref,
    keep_ref,
    send_ref,
    token_full_ref,
    terms_ref,
):
    bf16, f32 = jnp.bfloat16, jnp.float32
    half = token_ref.shape[0]
    width = output_grad_ref.shape[1]
    place = PLACE[TURNS[0][2]]
    unit, inverse = column_norm(rows_ref[...].astype(f32))
    grad_norm = own_ref[...].astype(f32) + other_ref[...].astype(f32)
    scaled = grad_norm * vector_ref[0:1]
    mean_grad = jnp.mean(scaled, axis=-1, keepdims=True)
    mean_cross = jnp.mean(scaled * unit, axis=-1, keepdims=True)
    token_full_ref[...] = (
        grad_middle_ref[...] + inverse * (scaled - mean_grad - unit * mean_cross)
    )
    start = pl.multiple_of(core_ref[0] * half, half)
    token_rows = token_full_ref[pl.ds(start, half), :].astype(bf16)
    token_ref[...] = inner_cols(token_rows, order_ref[...]).astype(bf16)
    terms_ref[...] = jnp.zeros_like(terms_ref)
    terms_ref[0:1] = jnp.sum(grad_norm * unit, axis=0, keepdims=True)
    terms_ref[1:2] = sums_ref[0:1]
    terms_ref[2:3] = jnp.sum(grad_norm, axis=0, keepdims=True)
    terms_ref[3:6] = sums_ref[1:4]
    bias = bias_ref[...]
    high = bias.astype(bf16)
    low = (bias - high.astype(f32)).astype(bf16)
    spread = nn(block_ref[...], high) + nn(block_ref[...], low)
    turned = jnp.transpose(normed_ref[...])
    for at in range(0, 3 * width, width):
        columns = slice(at, at + width)
        store_blocks(nn(turned, grad_mixed_ref[:, columns]), place, keep_ref, send_ref, columns)
    store_blocks(output_grad_ref[...], place, keep_ref, send_ref, slice(3 * width, 4 * width))
    store_blocks(
        jnp.transpose(terms_ref[...]) + spread, place, keep_ref, send_ref, slice(4 * width, 4 * width + 128)
    )


def call(kernel, outs, scratch, *operands, smem=0):
    space = [pl.BlockSpec(memory_space=pltpu.SMEM)] * smem
    space += [pl.BlockSpec(memory_space=pltpu.VMEM)] * (len(operands) - smem)
    return pl.pallas_call(
        kernel,
        out_shape=[jax.ShapeDtypeStruct(shape, kind) for shape, kind in outs],
        in_specs=space,
        out_specs=[pl.BlockSpec(memory_space=pltpu.VMEM)] * len(outs),
        scratch_shapes=[pltpu.VMEM(shape, kind) for shape, kind in scratch],
        compiler_params=pltpu.CompilerParams(vmem_limit_bytes=56 * 1024 * 1024),
    )(*operands)


def local(
    tokens,
    cotangent,
    segments,
    input_weight,
    output_weight,
    up_weight,
    down_weight,
    head_bias,
    hidden_bias,
    norm_gains,
    shifts,
):
    bf16, f32 = jnp.bfloat16, jnp.float32
    half, width = tokens.shape
    length = segments.shape[1]
    block = input_weight.shape[0]
    heads_width = input_weight.shape[2]
    hidden_width = up_weight.shape[1]
    local_heads = heads_width // HEAD_DIM
    score_scale = 1.0 / math.sqrt(HEAD_DIM)
    core = lax.axis_index("c")

    first_end = 4 * heads_width + 128
    pack_width = first_end + 2 * hidden_width
    me = (lax.axis_index("xh") * 4 + lax.axis_index("zh") * 2 + lax.axis_index("h")).astype(
        jnp.int32
    ).reshape(1)
    (shard,) = call(
        pack_kernel,
        [((block, pack_width), bf16)],
        [((128, block), f32)],
        input_weight.reshape(block, 3 * heads_width),
        output_weight,
        up_weight,
        down_weight,
        norm_gains,
        shifts,
    )
    parts = [near_permute(shard, k, True) for k in range(8)]
    near = call(
        collect_kernel,
        [
            ((8 * block, first_end), bf16),
            ((8 * block, hidden_width), bf16),
            ((8 * block, hidden_width), bf16),
        ],
        [((128, pack_width), bf16)],
        me,
        *parts,
        smem=1,
    )
    first_halves, up_halves, down_halves = gather_far(near)

    small = swap_roles(
        jnp.concatenate(
            (head_bias.reshape(-1), hidden_bias, segments[0].astype(bf16))
        )
    )
    bias_rows = small[: 2 * heads_width].reshape(2, heads_width).astype(f32)
    hidden_row = small[2 * heads_width : 2 * heads_width + hidden_width].astype(f32)
    segment_row = small[2 * heads_width + hidden_width :].astype(f32).reshape(1, length)

    order = feature_order(width)
    blocks = block_order(width)

    def own_half(rows):
        return lax.dynamic_slice_in_dim(rows, core * half, half, axis=0)

    def other_half(rows):
        return lax.dynamic_slice_in_dim(rows, (1 - core) * half, half, axis=0)

    def full_rows(rows):
        return nn(lax.all_gather(swap_roles(rows), "c", axis=0, tiled=True), order).astype(bf16)

    rows = full_rows(tokens)
    cot_rows = full_rows(cotangent)

    vectors, normed_one, mixed, log_sums, context, attended = call(
        functools.partial(attend_kernel, score_scale),
        [
            ((8, width), f32),
            ((length, width), bf16),
            ((length, 3 * heads_width), bf16),
            ((8, length), f32),
            ((length, heads_width), bf16),
            ((length, width), bf16),
        ],
        [],
        rows,
        *first_halves,
        bias_rows,
        segment_row,
    )
    middle, feed, grad_two, up_keep, up_send, down_keep, down_send, hidden_sums = call(
        feed_kernel,
        [
            ((length, width), f32),
            ((length, width), bf16),
            ((length, width), bf16),
            ((width // 2, hidden_width), bf16),
            ((width // 2, hidden_width), bf16),
            ((width // 2, hidden_width), bf16),
            ((width // 2, hidden_width), bf16),
            ((8, hidden_width), f32),
        ],
        [
            ((length, width), bf16),
            ((width, length), bf16),
            ((width, length), bf16),
            ((width, hidden_width), bf16),
            ((width, hidden_width), bf16),
        ],
        rows,
        attended,
        pair(attended),
        vectors,
        *up_halves,
        *down_halves,
        hidden_row.reshape(1, hidden_width),
        cot_rows,
    )
    down_other = step_along(down_send, TURNS[2][2])
    up_other = step_along(up_send, TURNS[1][2])
    outcome = (
        own_half(middle)
        + own_half(feed).astype(f32)
        + pair(other_half(feed)).astype(f32)
        + vectors[5]
    )
    block_out = swap_roles(inner_cols(outcome.astype(bf16), order).astype(bf16))

    grad_middle, output_grad, grad_mixed, grad_one, sums, head_sums = call(
        functools.partial(attend_back_kernel, score_scale),
        [
            ((length, width), f32),
            ((width, heads_width), bf16),
            ((length, 3 * heads_width), bf16),
            ((length, width), bf16),
            ((8, width), f32),
            ((8, 3 * heads_width), f32),
        ],
        [((length, heads_width), bf16)],
        middle,
        cot_rows,
        grad_two,
        pair(grad_two),
        vectors,
        context,
        mixed,
        log_sums,
        *first_halves,
        segment_row,
    )
    down_keep, down_send = fold(down_keep, down_other, second_fold(TURNS[2]))
    up_keep, up_send = fold(up_keep, up_other, second_fold(TURNS[1]))
    down_other = step_along(down_send, TURNS[2][1])
    up_other = step_along(up_send, TURNS[1][1])
    bias_blocks = jnp.concatenate(
        (
            jnp.zeros((64, 8), f32),
            hidden_sums[0].reshape(64, 2 * block),
            head_sums[0, :heads_width].reshape(64, block // 2),
            head_sums[0, 2 * heads_width :].reshape(64, block // 2),
            jnp.zeros((64, 120 - 3 * block), f32),
        ),
        axis=1,
    )
    grad_one_other = pair(grad_one)
    grad_one_other, down_keep, up_keep = lax.optimization_barrier(
        (grad_one_other, down_keep, up_keep)
    )
    token_grad, first_keep, first_send = call(
        token_kernel,
        [
            ((half, width), bf16),
            ((width // 2, first_end), bf16),
            ((width // 2, first_end), bf16),
        ],
        [((length, width), f32), ((128, width), f32)],
        core.astype(jnp.int32).reshape(1),
        rows,
        grad_one,
        grad_one_other,
        grad_middle,
        vectors,
        normed_one,
        grad_mixed,
        output_grad,
        sums,
        bias_blocks,
        blocks,
        order,
        smem=1,
    )
    token_grad = swap_roles(token_grad)
    first_other = step_along(first_send, TURNS[0][2])
    down_keep, down_send = fold(down_keep, down_other, halve_kernel)
    up_keep, up_send = fold(up_keep, up_other, halve_kernel)
    down_other = step_along(down_send, TURNS[2][0])
    up_other = step_along(up_send, TURNS[1][0])
    first_keep, first_send = fold(first_keep, first_other, second_fold(TURNS[0]))
    first_other = step_along(first_send, TURNS[0][1])
    first_keep, first_send = fold(first_keep, first_other, halve_kernel)
    first_other = step_along(first_send, TURNS[0][0])
    shares = call(
        deal_kernel,
        [((block, pack_width), bf16)] * 8,
        [((128, pack_width), bf16)],
        me,
        first_keep,
        first_other,
        up_keep,
        up_other,
        down_keep,
        down_other,
        smem=1,
    )
    shares = [near_permute(share, k, False) for k, share in enumerate(shares)]
    six = block // 2
    input_grad, output_grad, up_grad, down_grad, head_grad, hidden_grad, gain_grad, shift_grad = call(
        unpack_kernel,
        [
            ((block, 3 * heads_width), f32),
            ((heads_width, block), f32),
            ((block, hidden_width), f32),
            ((hidden_width, block), f32),
            ((2, six), f32),
            ((1, 2 * block), f32),
            ((2, six), f32),
            ((4, six), f32),
        ],
        [((128, hidden_width), f32)],
        lax.axis_index("h").astype(jnp.int32).reshape(1),
        *shares,
        smem=1,
    )
    return (
        block_out,
        token_grad,
        input_grad.reshape(block, 3, heads_width),
        output_grad,
        up_grad,
        down_grad,
        head_grad,
        hidden_grad.reshape(2 * block),
        gain_grad,
        shift_grad,
    )


def solution(mesh):
    fine = Mesh(mesh.devices.reshape((2,) * 7), AXES)
    in_specs = (
        P(AXES, None),
        P(AXES, None),
        P(DP, None),
        P(DP, None, "h"),
        P("h", DP),
        P(DP, "h"),
        P("h", DP),
        P(None, "h"),
        P("h"),
        P(None, DP),
        P(None, DP),
    )
    out_specs = (
        P(AXES, None),
        P(AXES, None),
        P(DP, None, "h"),
        P("h", DP),
        P(DP, "h"),
        P("h", DP),
        P(None, ("h",) + DP),
        P(("h",) + DP),
        P(None, AXES),
        P(None, AXES),
    )
    return jax.shard_map(local, mesh=fine, in_specs=in_specs, out_specs=out_specs, check_vma=False)
```

```python
import functools
import itertools
import math

import jax
import jax.numpy as jnp
from jax import lax
from jax.experimental import pallas as pl
from jax.experimental.pallas import tpu as pltpu
from jax.sharding import Mesh
from jax.sharding import PartitionSpec as P

HEAD_DIM = 64


norm_epsilon = 1e-05
masked_value = -1e30
gelu_factor = 0.7978845608028654


def inner_cols(left_side, right_side):
    return lax.dot_general(
        left_side, right_side, (((1,), (1,)), ((), ())), preferred_element_type=jnp.float32
    )


AXES = ("xh", "xl", "yl", "zh", "zl", "c", "h")
DP = AXES[:6]
RING = {"x": ("xh", "xl"), "y": ("h", "yl"), "z": ("zh", "zl")}
PLACE = {"z": 0, "y": 1, "x": 2}
TURNS = (("x", "y", "z"), ("y", "z", "x"), ("z", "x", "y"))


def swap_roles(values):
    return lax.ppermute(values, ("c", "h"), [(0, 0), (1, 2), (2, 1), (3, 3)])


def pair(values):
    return lax.ppermute(values, "c", [(0, 1), (1, 0)])


def step_along(values, axis):
    high, low = RING[axis]
    order = [name for name in AXES if name in (high, low, "c")]
    moves = []
    for place in itertools.product(range(2), repeat=3):
        target = dict(zip(order, place))
        target[low] ^= 1
        target[high] ^= target["c"]
        moves.append(
            (place[0] * 4 + place[1] * 2 + place[2], sum(target[n] << (2 - i) for i, n in enumerate(order)))
        )
    return lax.ppermute(values, tuple(order), moves)


def cross_roles(values, outward):
    moves = [(0, 1), (1, 3), (2, 0), (3, 2)]
    return lax.ppermute(values, ("c", "h"), moves if outward else [(b, a) for a, b in moves])


def flip(values, axis):
    return lax.ppermute(values, axis, [(0, 1), (1, 0)])


def gather_near(shard):
    parts = jnp.stack((swap_roles(shard), cross_roles(shard, True)))
    parts = jnp.concatenate((parts, flip(parts, "xh")), axis=0)
    return parts, flip(parts, "zh")


def add_low(left, right):
    return (left.astype(jnp.float32) + right.astype(jnp.float32)).astype(jnp.bfloat16)


def scatter_near(keep, send):
    other = flip(send, "zh")
    keep, send = add_low(keep[:2], other[:2]), add_low(keep[2:], other[2:])
    other = flip(send, "xh")
    keep, send = add_low(keep[0], other[0]), add_low(keep[1], other[1])
    return swap_roles(keep), cross_roles(send, False)


def open_blocks(piece):
    return piece.reshape((1, 1, 1) + piece.shape)


def gather_far(pieces):
    pieces = [open_blocks(piece) for piece in pieces]
    for turn in range(3):
        others = [step_along(piece, TURNS[i][turn]) for i, piece in enumerate(pieces)]
        if turn < 2:
            pieces = [
                jnp.concatenate((piece, other), axis=PLACE[TURNS[i][turn]])
                for i, (piece, other) in enumerate(zip(pieces, others))
            ]
    return [
        [half.reshape(4 * half.shape[3], half.shape[4]) for half in halves]
        for halves in zip(pieces, others)
    ]


def source_block(near, far):
    xl = lax.axis_index("xl") ^ (far & 1)
    yl = lax.axis_index("yl") ^ ((far >> 1) & 1)
    zl = lax.axis_index("zl") ^ (far >> 2)
    zh, xh, h = near >> 2, (near >> 1) & 1, near & 1
    return xh * 32 + xl * 16 + yl * 8 + zh * 4 + zl * 2 + h


def feature_order(width):
    block = width // 64
    place = lax.broadcasted_iota(jnp.int32, (width, width), 1)
    source = source_block((place // block) % 8, place // (8 * block)) * block + place % block
    return (lax.broadcasted_iota(jnp.int32, (width, width), 0) == source).astype(jnp.bfloat16)


def block_order(width):
    block = width // 64
    place = lax.broadcasted_iota(jnp.int32, (width, 64), 0)
    source = source_block((place // block) % 8, place // (8 * block))
    return (lax.broadcasted_iota(jnp.int32, (width, 64), 1) == source).astype(jnp.bfloat16)


def place_rows(rows, columns, row_block, column_block, me):
    block = min(row_block, column_block)
    row = lax.broadcasted_iota(jnp.int32, (rows, columns), 0)
    column = lax.broadcasted_iota(jnp.int32, (rows, columns), 1)
    found = jnp.zeros((rows, columns), jnp.bool_)
    for k in range(8):
        inside = (row >= k * row_block) & (row < k * row_block + block)
        other = (me ^ k) * column_block
        found = found | (inside & (column - other == row - k * row_block))
    return found.astype(jnp.float32).astype(jnp.bfloat16)


def eye(size):
    row = lax.broadcasted_iota(jnp.int32, (size, size), 0)
    column = lax.broadcasted_iota(jnp.int32, (size, size), 1)
    return (row == column).astype(jnp.float32).astype(jnp.bfloat16)


def pack_kernel(input_ref, output_ref, up_ref, down_ref, gains_ref, shifts_ref, shard_ref, small_ref):
    bf16 = jnp.bfloat16
    block, width = output_ref.shape
    hidden_width = up_ref.shape[1]
    for i in range(3):
        shard_ref[:, i * width : (i + 1) * width] = input_ref[:, i, :]
    shard_ref[:, 3 * width : 4 * width] = output_ref[...]
    small_ref[...] = jnp.zeros_like(small_ref)
    small_ref[0:2] = gains_ref[...].astype(jnp.float32)
    small_ref[2:6] = shifts_ref[...].astype(jnp.float32)
    at = 4 * width + 128
    shard_ref[:, 4 * width : at] = inner_cols(eye(block), small_ref[...].astype(bf16)).astype(bf16)
    shard_ref[:, at : at + hidden_width] = up_ref[...]
    shard_ref[:, at + hidden_width :] = down_ref[...]


def collect_kernel(me_ref, *refs):
    parts, outs, held_ref = refs[:2], refs[2:5], refs[5]
    block = parts[0].shape[1]
    held_ref[...] = jnp.zeros_like(held_ref)
    for k in range(8):
        held_ref[16 * k : 16 * k + block] = parts[k // 4][k % 4]
    moved = place_rows(8 * block, 128, block, 16, me_ref[0])
    at = 0
    for out in outs:
        columns = out.shape[1]
        out[...] = nn(moved, held_ref[:, at : at + columns]).astype(jnp.bfloat16)
        at += columns


def deal_kernel(me_ref, *refs):
    parts, outs, held_ref = refs[:-3], refs[-3:-1], refs[-1]
    rows, block = parts[0].shape[0], outs[0].shape[1]
    moved = place_rows(128, rows, 16, block, me_ref[0])
    at = 0
    for keep, other in zip(parts[::2], parts[1::2]):
        columns = keep.shape[1]
        total = add_low(keep[...], other[...])
        held_ref[:, at : at + columns] = nn(moved, total).astype(jnp.bfloat16)
        at += columns
    for k in range(8):
        outs[k // 4][k % 4] = held_ref[16 * k : 16 * k + block]


def unpack_kernel(half_ref, *refs):
    parts = refs[:2]
    input_ref, output_ref, up_ref, down_ref, head_ref, hidden_ref, gain_ref, shift_ref = refs[2:]
    f32 = jnp.float32
    block, width = output_ref.shape
    hidden_width = up_ref.shape[1]
    six = block // 2

    def total(start, size):
        columns = slice(start, start + size)
        value = parts[0][:, columns].astype(f32)
        for part in parts[1:]:
            value = value + part[:, columns].astype(f32)
        return value

    def pick(rows, columns, offset):
        row = lax.broadcasted_iota(jnp.int32, (rows, columns), 0)
        column = lax.broadcasted_iota(jnp.int32, (rows, columns), 1)
        return (row == column + offset).astype(f32)

    def exact(left, right, dims):
        return lax.dot_general(
            left, right, (dims, ((), ())), precision=lax.Precision.HIGHEST, preferred_element_type=f32
        )

    for i in range(3):
        input_ref[:, i, :] = total(i * width, width)
    output_ref[...] = total(3 * width, width)
    at = 4 * width + 128
    up_ref[...] = total(at, hidden_width)
    down_ref[...] = total(at + hidden_width, hidden_width)
    small = total(4 * width, 128)
    norm_terms = exact(small, pick(block, six, half_ref[0] * six), ((0,), (0,)))
    gain_ref[...] = norm_terms[0:2]
    shift_ref[...] = norm_terms[2:6]
    hidden_ref[...] = exact(small[0:1], pick(128, 2 * block, 8), ((1,), (0,)))
    head_ref[0:1] = exact(small[0:1], pick(128, six, 8 + 2 * block), ((1,), (0,)))
    head_ref[1:2] = exact(small[0:1], pick(128, six, 8 + 2 * block + six), ((1,), (0,)))


def half_sums(keep, other, place, places):
    rows, columns = keep.shape
    shape = (2,) * places + (rows >> places, columns)
    keep, other = keep.reshape(shape), other.reshape(shape)
    return [
        add_low(
            lax.slice_in_dim(keep, i, i + 1, axis=place), lax.slice_in_dim(other, i, i + 1, axis=place)
        ).reshape(rows // 2, columns)
        for i in range(2)
    ]


def second_turn(keep, send, turns):
    place = sorted(turns[:2], key=PLACE.get).index(turns[1])
    return tuple(half_sums(keep, step_along(send, turns[2]), place, 2))


def third_turn(keep, send, turns):
    return half_sums(keep, step_along(send, turns[1]), 0, 1)


def column_norm(values):
    mean_val = jnp.mean(values, axis=-1, keepdims=True)
    centered = values - mean_val
    variance = jnp.mean(centered * centered, axis=-1, keepdims=True)
    inverse = lax.rsqrt(variance + norm_epsilon)
    return centered * inverse, inverse


def nn(left, right):
    return jnp.dot(left, right, preferred_element_type=jnp.float32)


def key_mask(segment_row, keys, first, queries):
    column = jnp.transpose(jnp.broadcast_to(segment_row, (8, segment_row.shape[1])))[:keys, :1]
    row = segment_row[:, first : first + queries]
    key_pos = lax.broadcasted_iota(jnp.int32, (keys, queries), 0)
    query_pos = lax.broadcasted_iota(jnp.int32, (keys, queries), 1) + first
    return jnp.where((column == row) & (key_pos <= query_pos), 0.0, masked_value)


def lane_half(values, which):
    lane = lax.broadcasted_iota(jnp.int32, values.shape, 1)
    inside = (lane >= HEAD_DIM) if which else (lane < HEAD_DIM)
    return jnp.where(inside, values, jnp.zeros_like(values))


def attend_kernel(
    score_scale,
    rows_ref,
    low_ref,
    high_ref,
    bias_ref,
    segment_ref,
    vector_ref,
    normed_ref,
    mixed_ref,
    log_ref,
    context_ref,
    attended_ref,
):
    bf16 = jnp.bfloat16
    length = rows_ref.shape[0]
    width = context_ref.shape[1]
    rows = low_ref.shape[0]
    for at, part_ref in ((0, low_ref), (rows, high_ref)):
        turned = jnp.transpose(part_ref[:, 4 * width : 4 * width + 128].astype(jnp.float32))
        vector_ref[:, at : at + rows] = turned[:8]
    half = length // 2
    unit, _ = column_norm(rows_ref[...].astype(jnp.float32))
    normed_ref[...] = (unit * vector_ref[0:1] + vector_ref[2:3]).astype(bf16)
    mixed = nn(normed_ref[:, :rows], low_ref[:, : 3 * width]) + nn(
        normed_ref[:, rows:], high_ref[:, : 3 * width]
    )
    mixed_ref[:, :width] = (mixed[:, :width] + bias_ref[0:1]).astype(bf16)
    mixed_ref[:, width : 2 * width] = mixed[:, width : 2 * width].astype(bf16)
    mixed_ref[:, 2 * width :] = (mixed[:, 2 * width :] + bias_ref[1:2]).astype(bf16)
    segment_row = segment_ref[...]
    spans = ((0, half, key_mask(segment_row, half, 0, half)), (half, length, key_mask(segment_row, length, half, half)))
    log_ref[...] = jnp.zeros_like(log_ref)
    for two in range(width // 128):
        at = 128 * two
        query_two = mixed_ref[:, at : at + 128] * jnp.asarray(score_scale, bf16)
        key_two = mixed_ref[:, width + at : width + at + 128]
        value_turned = jnp.transpose(mixed_ref[:, 2 * width + at : 2 * width + at + 128])
        parts = []
        for which in range(2):
            query_rows = lane_half(query_two, which)
            value_rows = value_turned[HEAD_DIM * which : HEAD_DIM * (which + 1)]
            sides = []
            for first, keys, mask in spans:
                scores = inner_cols(key_two[:keys], query_rows[first : first + half]) + mask
                top = jnp.max(scores, axis=0, keepdims=True)
                exponent = jnp.exp(scores - top)
                total = jnp.sum(exponent, axis=0, keepdims=True)
                log_ref[2 * two + which : 2 * two + which + 1, first : first + half] = top + jnp.log(total)
                sides.append(nn(value_rows[:, :keys], exponent.astype(bf16)) / total)
            parts.append(jnp.concatenate(sides, axis=1))
        context_ref[:, at : at + 128] = jnp.transpose(jnp.concatenate(parts, axis=0)).astype(bf16)
    for at, part_ref in ((0, low_ref), (rows, high_ref)):
        attended_ref[:, at : at + rows] = inner_cols(
            context_ref[...], part_ref[:, 3 * width : 4 * width]
        ).astype(bf16)


def store_blocks(value, place, keep_ref, send_ref, columns):
    rows = value.shape[0] // 8
    counts = [0, 0]
    for block in range(8):
        which = (block >> (2 - place)) & 1
        target = send_ref if which else keep_ref
        at = counts[which] * rows
        counts[which] += 1
        target[at : at + rows, columns] = value[block * rows : (block + 1) * rows].astype(target.dtype)


def join_blocks(place, keep_ref, other_ref, whole_ref):
    rows = whole_ref.shape[0] // 8
    counts = [0, 0]
    for block in range(8):
        which = (block >> (2 - place)) & 1
        at = counts[which] * rows
        counts[which] += 1
        source = other_ref if which else keep_ref
        whole_ref[block * rows : (block + 1) * rows] = source[at : at + rows]


def feed_kernel(
    rows_ref,
    own_ref,
    other_ref,
    vector_ref,
    up_mine_ref,
    up_other_ref,
    down_mine_ref,
    down_other_ref,
    bias_ref,
    cot_ref,
    middle_ref,
    feed_ref,
    grad_two_ref,
    up_keep_ref,
    up_send_ref,
    down_keep_ref,
    down_send_ref,
    bias_grad_ref,
    normed_ref,
    normed_turned_ref,
    cot_turned_ref,
    up_ref,
    down_ref,
):
    bf16, f32 = jnp.bfloat16, jnp.float32
    join_blocks(PLACE[TURNS[1][2]], up_mine_ref, up_other_ref, up_ref)
    join_blocks(PLACE[TURNS[2][2]], down_mine_ref, down_other_ref, down_ref)
    middle = (
        rows_ref[...].astype(f32)
        + (own_ref[...].astype(f32) + other_ref[...].astype(f32))
        + vector_ref[4:5]
    )
    middle_ref[...] = middle
    unit, _ = column_norm(middle)
    normed_ref[...] = (unit * vector_ref[1:2] + vector_ref[3:4]).astype(bf16)
    normed_turned_ref[...] = jnp.transpose(normed_ref[...])
    cot_turned_ref[...] = jnp.transpose(cot_ref[...])
    hidden_width = up_ref.shape[1]
    step = hidden_width // 3
    bias_grad_ref[...] = jnp.zeros_like(bias_grad_ref)
    feed = grad_two = None
    for at in range(0, hidden_width, step):
        columns = slice(at, at + step)
        before = nn(normed_ref[...], up_ref[:, columns]) + bias_ref[:, columns]
        square = before * before
        bend = jnp.tanh(gelu_factor * (before + 0.044715 * before * square))
        opened = 0.5 * (1.0 + bend)
        hidden = (before * opened).astype(bf16)
        slope = opened + 0.5 * before * (1.0 - bend * bend) * (
            gelu_factor * (1.0 + 3.0 * 0.044715 * square)
        )
        grad_before = (nn(cot_ref[...], down_ref[:, columns]) * slope).astype(bf16)
        part = inner_cols(hidden, down_ref[:, columns])
        feed = part if feed is None else feed + part
        part = inner_cols(grad_before, up_ref[:, columns])
        grad_two = part if grad_two is None else grad_two + part
        bias_grad_ref[0:1, columns] = jnp.sum(grad_before.astype(f32), axis=0, keepdims=True)
        store_blocks(nn(cot_turned_ref[...], hidden), PLACE[TURNS[2][2]], down_keep_ref, down_send_ref, columns)
        store_blocks(nn(normed_turned_ref[...], grad_before), PLACE[TURNS[1][2]], up_keep_ref, up_send_ref, columns)
    feed_ref[...] = feed.astype(bf16)
    grad_two_ref[...] = grad_two.astype(bf16)


def attend_back_kernel(
    score_scale,
    middle_ref,
    cot_ref,
    own_ref,
    other_ref,
    vector_ref,
    context_ref,
    mixed_ref,
    log_ref,
    low_ref,
    high_ref,
    segment_ref,
    normed_ref,
    grad_middle_ref,
    grad_one_ref,
    sums_ref,
    head_sums_ref,
    keep_a_ref,
    send_a_ref,
    keep_b_ref,
    send_b_ref,
    keep_c_ref,
    send_c_ref,
    grad_context_ref,
    grad_mixed_ref,
):
    bf16, f32 = jnp.bfloat16, jnp.float32
    length = middle_ref.shape[0]
    width = context_ref.shape[1]
    rows = low_ref.shape[0]
    half = length // 2
    unit, inverse = column_norm(middle_ref[...])
    grad_norm = own_ref[...].astype(f32) + other_ref[...].astype(f32)
    scaled = grad_norm * vector_ref[1:2]
    mean_grad = jnp.mean(scaled, axis=-1, keepdims=True)
    mean_cross = jnp.mean(scaled * unit, axis=-1, keepdims=True)
    cot = cot_ref[...].astype(f32)
    grad_middle = cot + inverse * (scaled - mean_grad - unit * mean_cross)
    grad_middle_ref[...] = grad_middle
    sums_ref[...] = jnp.zeros_like(sums_ref)
    sums_ref[0:1] = jnp.sum(grad_norm * unit, axis=0, keepdims=True)
    sums_ref[1:2] = jnp.sum(grad_norm, axis=0, keepdims=True)
    sums_ref[2:3] = jnp.sum(grad_middle, axis=0, keepdims=True)
    sums_ref[3:4] = jnp.sum(cot, axis=0, keepdims=True)
    middle_rows = grad_middle.astype(bf16)
    third = keep_a_ref.shape[1]
    store_blocks(
        nn(jnp.transpose(middle_rows), context_ref[...]),
        PLACE[TURNS[2][2]],
        keep_c_ref,
        send_c_ref,
        slice(third - width, third),
    )
    grad_context_ref[...] = (
        nn(middle_rows[:, :rows], low_ref[:, 3 * width : 4 * width])
        + nn(middle_rows[:, rows:], high_ref[:, 3 * width : 4 * width])
    ).astype(bf16)
    segment_row = segment_ref[...]
    spans = ((0, half, key_mask(segment_row, half, 0, half)), (half, length, key_mask(segment_row, length, half, half)))
    head_sums_ref[...] = jnp.zeros_like(head_sums_ref)
    for two in range(width // 128):
        at = 128 * two
        query_two = mixed_ref[:, at : at + 128] * jnp.asarray(score_scale, bf16)
        key_two = mixed_ref[:, width + at : width + at + 128]
        value_two = mixed_ref[:, 2 * width + at : 2 * width + at + 128]
        grad_two = grad_context_ref[:, at : at + 128]
        key_turned = jnp.transpose(key_two)
        grad_queries = []
        grad_keys = [0.0, 0.0]
        grad_values = [0.0, 0.0]
        for which in range(2):
            query_rows = lane_half(query_two, which)
            grad_rows = lane_half(grad_two, which)
            key_rows = key_turned[HEAD_DIM * which : HEAD_DIM * (which + 1)]
            sides = []
            for side, (first, keys, mask) in enumerate(spans):
                query_side = query_rows[first : first + half]
                grad_side = grad_rows[first : first + half]
                log_side = log_ref[2 * two + which : 2 * two + which + 1, first : first + half]
                scores = inner_cols(key_two[:keys], query_side) + mask
                soft = jnp.exp(scores - log_side)
                grad_soft = inner_cols(value_two[:keys], grad_side)
                crossed = soft * grad_soft
                grad_scores = (
                    crossed - soft * jnp.sum(crossed, axis=0, keepdims=True)
                ).astype(bf16)
                grad_keys[side] += nn(grad_scores, query_side)
                grad_values[side] += nn(soft.astype(bf16), grad_side)
                sides.append(nn(key_rows[:, :keys], grad_scores))
            grad_queries.append(jnp.concatenate(sides, axis=1))
        queries_out = jnp.transpose(jnp.concatenate(grad_queries, axis=0)) * score_scale
        for place, value in enumerate((queries_out, grad_keys, grad_values)):
            columns = slice(place * width + at, place * width + at + 128)
            if place == 0:
                grad_mixed_ref[:, columns] = value.astype(bf16)
            else:
                grad_mixed_ref[:half, columns] = (value[0] + value[1][:half]).astype(bf16)
                grad_mixed_ref[half:, columns] = value[1][half:].astype(bf16)
            head_sums_ref[0:1, columns] = jnp.sum(
                grad_mixed_ref[:, columns].astype(f32), axis=0, keepdims=True
            )
    for at, part_ref in ((0, low_ref), (rows, high_ref)):
        grad_one_ref[:, at : at + rows] = inner_cols(
            grad_mixed_ref[...], part_ref[:, : 3 * width]
        ).astype(bf16)
    turned = jnp.transpose(normed_ref[...])
    targets = ((keep_a_ref, send_a_ref), (keep_b_ref, send_b_ref), (keep_c_ref, send_c_ref))
    for i, (keep_ref, send_ref) in enumerate(targets):
        size = min(third, 3 * width - i * third)
        store_blocks(
            nn(turned, grad_mixed_ref[:, i * third : i * third + size]),
            PLACE[TURNS[i][2]],
            keep_ref,
            send_ref,
            slice(0, size),
        )


def token_kernel(
    core_ref,
    rows_ref,
    own_ref,
    other_ref,
    grad_middle_ref,
    vector_ref,
    sums_ref,
    bias_ref,
    block_ref,
    order_ref,
    token_ref,
    keep_ref,
    send_ref,
    token_full_ref,
    terms_ref,
):
    bf16, f32 = jnp.bfloat16, jnp.float32
    half = token_ref.shape[0]
    place = PLACE[TURNS[0][2]]
    unit, inverse = column_norm(rows_ref[...].astype(f32))
    grad_norm = own_ref[...].astype(f32) + other_ref[...].astype(f32)
    scaled = grad_norm * vector_ref[0:1]
    mean_grad = jnp.mean(scaled, axis=-1, keepdims=True)
    mean_cross = jnp.mean(scaled * unit, axis=-1, keepdims=True)
    token_full_ref[...] = (
        grad_middle_ref[...] + inverse * (scaled - mean_grad - unit * mean_cross)
    )
    start = pl.multiple_of(core_ref[0] * half, half)
    token_rows = token_full_ref[pl.ds(start, half), :].astype(bf16)
    token_ref[...] = inner_cols(token_rows, order_ref[...]).astype(bf16)
    terms_ref[...] = jnp.zeros_like(terms_ref)
    terms_ref[0:1] = jnp.sum(grad_norm * unit, axis=0, keepdims=True)
    terms_ref[1:2] = sums_ref[0:1]
    terms_ref[2:3] = jnp.sum(grad_norm, axis=0, keepdims=True)
    terms_ref[3:6] = sums_ref[1:4]
    bias = bias_ref[...]
    high = bias.astype(bf16)
    low = (bias - high.astype(f32)).astype(bf16)
    spread = nn(block_ref[...], high) + nn(block_ref[...], low)
    store_blocks(
        jnp.transpose(terms_ref[...]) + spread, place, keep_ref, send_ref, slice(0, 128)
    )


def call(kernel, outs, scratch, *operands, smem=0):
    space = [pl.BlockSpec(memory_space=pltpu.SMEM)] * smem
    space += [pl.BlockSpec(memory_space=pltpu.VMEM)] * (len(operands) - smem)
    return pl.pallas_call(
        kernel,
        out_shape=[jax.ShapeDtypeStruct(shape, kind) for shape, kind in outs],
        in_specs=space,
        out_specs=[pl.BlockSpec(memory_space=pltpu.VMEM)] * len(outs),
        scratch_shapes=[pltpu.VMEM(shape, kind) for shape, kind in scratch],
        compiler_params=pltpu.CompilerParams(vmem_limit_bytes=56 * 1024 * 1024),
    )(*operands)


def local(
    tokens,
    cotangent,
    segments,
    input_weight,
    output_weight,
    up_weight,
    down_weight,
    head_bias,
    hidden_bias,
    norm_gains,
    shifts,
):
    bf16, f32 = jnp.bfloat16, jnp.float32
    half, width = tokens.shape
    length = segments.shape[1]
    block = input_weight.shape[0]
    heads_width = input_weight.shape[2]
    hidden_width = up_weight.shape[1]
    local_heads = heads_width // HEAD_DIM
    score_scale = 1.0 / math.sqrt(HEAD_DIM)
    core = lax.axis_index("c")

    first_end = 4 * heads_width + 128
    pack_width = first_end + 2 * hidden_width
    me = (
        (lax.axis_index("zh") * 4 + lax.axis_index("xh") * 2 + lax.axis_index("h"))
        .astype(jnp.int32)
        .reshape(1)
    )
    (shard,) = call(
        pack_kernel,
        [((block, pack_width), bf16)],
        [((128, block), f32)],
        input_weight,
        output_weight.T,
        up_weight,
        down_weight.T,
        norm_gains,
        shifts,
    )
    order = feature_order(width)
    blocks = block_order(width)
    parts, order, blocks = lax.optimization_barrier((gather_near(shard), order, blocks))
    near = call(
        collect_kernel,
        [
            ((8 * block, first_end), bf16),
            ((8 * block, hidden_width), bf16),
            ((8 * block, hidden_width), bf16),
        ],
        [((128, pack_width), bf16)],
        me,
        *parts,
        smem=1,
    )
    first_halves, up_halves, down_halves = gather_far(near)

    small = swap_roles(
        jnp.concatenate(
            (head_bias.reshape(-1), hidden_bias, segments[0].astype(bf16))
        )
    )
    bias_rows = small[: 2 * heads_width].reshape(2, heads_width).astype(f32)
    hidden_row = small[2 * heads_width : 2 * heads_width + hidden_width].astype(f32)
    segment_row = small[2 * heads_width + hidden_width :].astype(f32).reshape(1, length)

    def own_half(rows):
        return lax.dynamic_slice_in_dim(rows, core * half, half, axis=0)

    def other_half(rows):
        return lax.dynamic_slice_in_dim(rows, (1 - core) * half, half, axis=0)

    def full_rows(rows):
        return nn(lax.all_gather(swap_roles(rows), "c", axis=0, tiled=True), order).astype(bf16)

    rows = full_rows(tokens)
    cot_rows = full_rows(cotangent)

    vectors, normed_one, mixed, log_sums, context, attended = call(
        functools.partial(attend_kernel, score_scale),
        [
            ((8, width), f32),
            ((length, width), bf16),
            ((length, 3 * heads_width), bf16),
            ((8, length), f32),
            ((length, heads_width), bf16),
            ((length, width), bf16),
        ],
        [],
        rows,
        *first_halves,
        bias_rows,
        segment_row,
    )
    middle, feed, grad_two, up_keep, up_send, down_keep, down_send, hidden_sums = call(
        feed_kernel,
        [
            ((length, width), f32),
            ((length, width), bf16),
            ((length, width), bf16),
            ((width // 2, hidden_width), bf16),
            ((width // 2, hidden_width), bf16),
            ((width // 2, hidden_width), bf16),
            ((width // 2, hidden_width), bf16),
            ((8, hidden_width), f32),
        ],
        [
            ((length, width), bf16),
            ((width, length), bf16),
            ((width, length), bf16),
            ((width, hidden_width), bf16),
            ((width, hidden_width), bf16),
        ],
        rows,
        attended,
        pair(attended),
        vectors,
        *up_halves,
        *down_halves,
        hidden_row.reshape(1, hidden_width),
        cot_rows,
    )
    down_other = step_along(down_send, TURNS[2][2])
    up_other = step_along(up_send, TURNS[1][2])
    outcome = (
        own_half(middle)
        + own_half(feed).astype(f32)
        + pair(other_half(feed)).astype(f32)
        + vectors[5]
    )
    block_out = swap_roles(inner_cols(outcome.astype(bf16), order).astype(bf16))

    grad_middle, grad_one, sums, head_sums, *first_grads = call(
        functools.partial(attend_back_kernel, score_scale),
        [
            ((length, width), f32),
            ((length, width), bf16),
            ((8, width), f32),
            ((8, 3 * heads_width), f32),
        ]
        + [((width // 2, 4 * heads_width // 3), bf16)] * 6,
        [((length, heads_width), bf16), ((length, 3 * heads_width), bf16)],
        middle,
        cot_rows,
        grad_two,
        pair(grad_two),
        vectors,
        context,
        mixed,
        log_sums,
        *first_halves,
        segment_row,
        normed_one,
    )
    down_keep, down_send = half_sums(down_keep, down_other, 1, 2)
    up_keep, up_send = half_sums(up_keep, up_other, 0, 2)
    down_other = step_along(down_send, TURNS[2][1])
    up_other = step_along(up_send, TURNS[1][1])
    bias_blocks = jnp.concatenate(
        (
            jnp.zeros((64, 8), f32),
            hidden_sums[0].reshape(64, 2 * block),
            head_sums[0, :heads_width].reshape(64, block // 2),
            head_sums[0, 2 * heads_width :].reshape(64, block // 2),
            jnp.zeros((64, 120 - 3 * block), f32),
        ),
        axis=1,
    )
    grad_one_other = pair(grad_one)
    grad_one_other, down_keep, up_keep = lax.optimization_barrier(
        (grad_one_other, down_keep, up_keep)
    )
    token_grad, small_keep, small_send = call(
        token_kernel,
        [
            ((half, width), bf16),
            ((width // 2, 128), bf16),
            ((width // 2, 128), bf16),
        ],
        [((length, width), f32), ((128, width), f32)],
        core.astype(jnp.int32).reshape(1),
        rows,
        grad_one,
        grad_one_other,
        grad_middle,
        vectors,
        sums,
        bias_blocks,
        blocks,
        order,
        smem=1,
    )
    token_grad = swap_roles(token_grad)
    down_keep, down_send = half_sums(down_keep, down_other, 0, 1)
    up_keep, up_send = half_sums(up_keep, up_other, 0, 1)
    last = [(up_keep, up_send, TURNS[1]), (down_keep, down_send, TURNS[2])]
    pieces = [(first_grads[2 * i], first_grads[2 * i + 1], TURNS[i]) for i in range(3)]
    pieces.append((small_keep, small_send, TURNS[0]))
    pieces = [second_turn(*piece) + (piece[2],) for piece in pieces]
    pieces = [(*third_turn(*piece), piece[2]) for piece in pieces]
    operands = []
    for keep, send, turns in pieces + last:
        operands += [keep, step_along(send, turns[0])]
    shares = call(
        deal_kernel,
        [((4, block, pack_width), bf16)] * 2,
        [((128, pack_width), bf16)],
        me,
        *operands,
        smem=1,
    )
    shares = scatter_near(*shares)
    six = block // 2
    input_grad, output_grad, up_grad, down_grad, head_grad, hidden_grad, gain_grad, shift_grad = call(
        unpack_kernel,
        [
            ((block, 3, heads_width), f32),
            ((block, heads_width), f32),
            ((block, hidden_width), f32),
            ((block, hidden_width), f32),
            ((2, six), f32),
            ((1, 2 * block), f32),
            ((2, six), f32),
            ((4, six), f32),
        ],
        [],
        lax.axis_index("h").astype(jnp.int32).reshape(1),
        *shares,
        smem=1,
    )
    return (
        block_out,
        token_grad,
        input_grad,
        output_grad.T,
        up_grad,
        down_grad.T,
        head_grad,
        hidden_grad.reshape(2 * block),
        gain_grad,
        shift_grad,
    )


def solution(mesh):
    fine = Mesh(mesh.devices.reshape((2,) * 7), AXES)
    in_specs = (
        P(AXES, None),
        P(AXES, None),
        P(DP, None),
        P(DP, None, "h"),
        P("h", DP),
        P(DP, "h"),
        P("h", DP),
        P(None, "h"),
        P("h"),
        P(None, DP),
        P(None, DP),
    )
    out_specs = (
        P(AXES, None),
        P(AXES, None),
        P(DP, None, "h"),
        P("h", DP),
        P(DP, "h"),
        P("h", DP),
        P(None, ("h",) + DP),
        P(("h",) + DP),
        P(None, AXES),
        P(None, AXES),
    )
    return jax.shard_map(local, mesh=fine, in_specs=in_specs, out_specs=out_specs, check_vma=False)
```

```python
import functools
import itertools
import math

import jax
import jax.numpy as jnp
from jax import lax
from jax.experimental import pallas as pl
from jax.experimental.pallas import tpu as pltpu
from jax.sharding import Mesh
from jax.sharding import PartitionSpec as P

HEAD_DIM = 64


norm_epsilon = 1e-05
masked_value = -1e30
gelu_factor = 0.7978845608028654


def inner_cols(left_side, right_side):
    return lax.dot_general(
        left_side, right_side, (((1,), (1,)), ((), ())), preferred_element_type=jnp.float32
    )


AXES = ("xh", "xl", "yl", "zh", "zl", "c", "h")
DP = AXES[:6]
RING = {"x": ("xh", "xl"), "y": ("h", "yl"), "z": ("zh", "zl")}
PLACE = {"z": 0, "y": 1, "x": 2}
TURNS = (("x", "y", "z"), ("y", "z", "x"), ("z", "x", "y"))


def swap_roles(values):
    return lax.ppermute(values, ("c", "h"), [(0, 0), (1, 2), (2, 1), (3, 3)])


def pair(values):
    return lax.ppermute(values, "c", [(0, 1), (1, 0)])


def step_along(values, axis):
    high, low = RING[axis]
    order = [name for name in AXES if name in (high, low, "c")]
    moves = []
    for place in itertools.product(range(2), repeat=3):
        target = dict(zip(order, place))
        target[low] ^= 1
        target[high] ^= target["c"]
        moves.append(
            (place[0] * 4 + place[1] * 2 + place[2], sum(target[n] << (2 - i) for i, n in enumerate(order)))
        )
    return lax.ppermute(values, tuple(order), moves)


def cross_roles(values, outward):
    moves = [(0, 1), (1, 3), (2, 0), (3, 2)]
    return lax.ppermute(values, ("c", "h"), moves if outward else [(b, a) for a, b in moves])


def flip(values, axis):
    return lax.ppermute(values, axis, [(0, 1), (1, 0)])


def gather_near(shard):
    parts = jnp.concatenate((swap_roles(shard), cross_roles(shard, True)), axis=0)
    parts = jnp.concatenate((parts, flip(parts, "xh")), axis=0)
    return parts, flip(parts, "zh")


def add_low(left, right):
    return (left.astype(jnp.float32) + right.astype(jnp.float32)).astype(jnp.bfloat16)


def scatter_near(keep, send):
    for axis in ("zh", "xh"):
        other = flip(send, axis)
        rows = keep.shape[0] // 2
        keep, send = add_low(keep[:rows], other[:rows]), add_low(keep[rows:], other[rows:])
    return swap_roles(keep), cross_roles(send, False)


def open_blocks(piece):
    return piece.reshape((1, 1, 1) + piece.shape)


def gather_far(pieces):
    pieces = [open_blocks(piece) for piece in pieces]
    for turn in range(3):
        others = [step_along(piece, TURNS[i][turn]) for i, piece in enumerate(pieces)]
        if turn < 2:
            pieces = [
                jnp.concatenate((piece, other), axis=PLACE[TURNS[i][turn]])
                for i, (piece, other) in enumerate(zip(pieces, others))
            ]
    return [
        [half.reshape(4 * half.shape[3], half.shape[4]) for half in halves]
        for halves in zip(pieces, others)
    ]


def source_block(near, far):
    xl = lax.axis_index("xl") ^ (far & 1)
    yl = lax.axis_index("yl") ^ ((far >> 1) & 1)
    zl = lax.axis_index("zl") ^ (far >> 2)
    zh, xh, h = near >> 2, (near >> 1) & 1, near & 1
    return xh * 32 + xl * 16 + yl * 8 + zh * 4 + zl * 2 + h


def feature_order(width):
    block = width // 64
    place = lax.broadcasted_iota(jnp.int32, (width, width), 1)
    source = source_block((place // block) % 8, place // (8 * block)) * block + place % block
    return (lax.broadcasted_iota(jnp.int32, (width, width), 0) == source).astype(jnp.bfloat16)


def block_order(width):
    block = width // 64
    place = lax.broadcasted_iota(jnp.int32, (width, 64), 0)
    source = source_block((place // block) % 8, place // (8 * block))
    return (lax.broadcasted_iota(jnp.int32, (width, 64), 1) == source).astype(jnp.bfloat16)


def bias_fold(hidden_width, width):
    rows = hidden_width + 2 * width
    row = lax.broadcasted_iota(jnp.int32, (rows, 128), 0)
    column = lax.broadcasted_iota(jnp.int32, (rows, 128), 1)
    many, few = hidden_width // 64, width // 64
    target = jnp.where(
        row < hidden_width,
        row % many,
        many + (row - hidden_width) % few + few * (row >= hidden_width + width).astype(jnp.int32),
    )
    return (column == target + 8).astype(jnp.bfloat16)


def place_rows(rows, me):
    block = rows // 8
    row = lax.broadcasted_iota(jnp.int32, (rows, rows), 0)
    column = lax.broadcasted_iota(jnp.int32, (rows, rows), 1)
    found = jnp.zeros((rows, rows), jnp.float32)
    for k in range(8):
        inside = (row >= k * block) & (row < (k + 1) * block)
        same = column - (me ^ k) * block == row - k * block
        found = jnp.where(inside & same, 1.0, found)
    return found.astype(jnp.bfloat16)


def eye(size):
    row = lax.broadcasted_iota(jnp.int32, (size, size), 0)
    column = lax.broadcasted_iota(jnp.int32, (size, size), 1)
    return (row == column).astype(jnp.float32).astype(jnp.bfloat16)


def pack_kernel(input_ref, output_ref, up_ref, down_ref, gains_ref, shifts_ref, shard_ref, small_ref):
    bf16 = jnp.bfloat16
    block, width = output_ref.shape
    hidden_width = up_ref.shape[1]
    for i in range(3):
        shard_ref[:, i * width : (i + 1) * width] = input_ref[:, i, :]
    shard_ref[:, 3 * width : 4 * width] = output_ref[...]
    small_ref[...] = jnp.zeros_like(small_ref)
    small_ref[0:2] = gains_ref[...].astype(jnp.float32)
    small_ref[2:6] = shifts_ref[...].astype(jnp.float32)
    at = 4 * width + 128
    shard_ref[:, 4 * width : at] = inner_cols(eye(block), small_ref[...].astype(bf16)).astype(bf16)
    shard_ref[:, at : at + hidden_width] = up_ref[...]
    shard_ref[:, at + hidden_width :] = down_ref[...]


def collect_kernel(me_ref, *refs):
    parts, outs, held_ref = refs[:2], refs[2:5], refs[5]
    rows = held_ref.shape[0]
    held_ref[: rows // 2] = parts[0][...]
    held_ref[rows // 2 :] = parts[1][...]
    moved = place_rows(rows, me_ref[0])
    at = 0
    for out in outs:
        columns = out.shape[1]
        out[...] = nn(moved, held_ref[:, at : at + columns]).astype(jnp.bfloat16)
        at += columns


def deal_kernel(me_ref, cross_ref, *refs):
    parts, outs = refs[:-2], refs[-2:]
    rows = parts[0].shape[0]
    moved = place_rows(rows, me_ref[0])
    at = 0
    for i, (keep, other) in enumerate(zip(parts[::2], parts[1::2])):
        columns = keep.shape[1]
        total = add_low(keep[...], other[...])
        if i == 2:
            lane = lax.broadcasted_iota(jnp.int32, cross_ref.shape, 1)
            cross = jnp.where(lane < 8, cross_ref[...].astype(jnp.float32), 0.0)
            total = jnp.concatenate((total[:, : columns - 128], add_low(total[:, columns - 128 :], cross)), axis=1)
        total = nn(moved, total).astype(jnp.bfloat16)
        outs[0][:, at : at + columns] = total[: rows // 2]
        outs[1][:, at : at + columns] = total[rows // 2 :]
        at += columns


def unpack_kernel(half_ref, *refs):
    parts = refs[:2]
    input_ref, output_ref, up_ref, down_ref, head_ref, hidden_ref, gain_ref, shift_ref = refs[2:]
    f32 = jnp.float32
    block, width = output_ref.shape
    hidden_width = up_ref.shape[1]
    six = block // 2

    def total(start, size):
        columns = slice(start, start + size)
        value = parts[0][:, columns].astype(f32)
        for part in parts[1:]:
            value = value + part[:, columns].astype(f32)
        return value

    def pick(rows, columns, offset):
        row = lax.broadcasted_iota(jnp.int32, (rows, columns), 0)
        column = lax.broadcasted_iota(jnp.int32, (rows, columns), 1)
        return (row == column + offset).astype(f32)

    def exact(left, right, dims):
        return lax.dot_general(
            left, right, (dims, ((), ())), precision=lax.Precision.HIGHEST, preferred_element_type=f32
        )

    for i in range(3):
        input_ref[:, i, :] = total(i * width, width)
    output_ref[...] = total(3 * width, width)
    at = 4 * width + 128
    up_ref[...] = total(at, hidden_width)
    down_ref[...] = total(at + hidden_width, hidden_width)
    small = total(4 * width, 128)
    norm_terms = exact(small, pick(block, six, half_ref[0] * six), ((0,), (0,)))
    gain_ref[...] = norm_terms[0:2]
    shift_ref[...] = norm_terms[2:6]
    hidden_ref[...] = exact(small[0:1], pick(128, 2 * block, 8), ((1,), (0,)))
    head_ref[0:1] = exact(small[0:1], pick(128, six, 8 + 2 * block), ((1,), (0,)))
    head_ref[1:2] = exact(small[0:1], pick(128, six, 8 + 2 * block + six), ((1,), (0,)))


def half_sums(keep, other, place, places):
    rows, columns = keep.shape
    shape = (2,) * places + (rows >> places, columns)
    keep, other = keep.reshape(shape), other.reshape(shape)
    return [
        add_low(
            lax.slice_in_dim(keep, i, i + 1, axis=place), lax.slice_in_dim(other, i, i + 1, axis=place)
        ).reshape(rows // 2, columns)
        for i in range(2)
    ]


def second_turn(keep, send, turns):
    place = sorted(turns[:2], key=PLACE.get).index(turns[1])
    return tuple(half_sums(keep, step_along(send, turns[2]), place, 2))


def third_turn(keep, send, turns):
    return half_sums(keep, step_along(send, turns[1]), 0, 1)


def column_norm(values):
    mean_val = jnp.mean(values, axis=-1, keepdims=True)
    centered = values - mean_val
    variance = jnp.mean(centered * centered, axis=-1, keepdims=True)
    inverse = lax.rsqrt(variance + norm_epsilon)
    return centered * inverse, inverse


def nn(left, right):
    return jnp.dot(left, right, preferred_element_type=jnp.float32)


def key_mask(segment_row, keys, first, queries):
    column = jnp.transpose(jnp.broadcast_to(segment_row, (8, segment_row.shape[1])))[:keys, :1]
    row = segment_row[:, first : first + queries]
    key_pos = lax.broadcasted_iota(jnp.int32, (keys, queries), 0)
    query_pos = lax.broadcasted_iota(jnp.int32, (keys, queries), 1) + first
    return jnp.where((column == row) & (key_pos <= query_pos), 0.0, masked_value)


def lane_half(values, which):
    lane = lax.broadcasted_iota(jnp.int32, values.shape, 1)
    inside = (lane >= HEAD_DIM) if which else (lane < HEAD_DIM)
    return jnp.where(inside, values, jnp.zeros_like(values))


def attend_kernel(
    score_scale,
    rows_ref,
    low_ref,
    high_ref,
    bias_ref,
    segment_ref,
    vector_ref,
    normed_ref,
    mixed_ref,
    log_ref,
    context_ref,
    attended_ref,
):
    bf16 = jnp.bfloat16
    length = rows_ref.shape[0]
    width = context_ref.shape[1]
    rows = low_ref.shape[0]
    for at, part_ref in ((0, low_ref), (rows, high_ref)):
        turned = jnp.transpose(part_ref[:, 4 * width : 4 * width + 128].astype(jnp.float32))
        vector_ref[:, at : at + rows] = turned[:8]
    half = length // 2
    unit, _ = column_norm(rows_ref[...].astype(jnp.float32))
    normed_ref[...] = (unit * vector_ref[0:1] + vector_ref[2:3]).astype(bf16)
    mixed = nn(normed_ref[:, :rows], low_ref[:, : 3 * width]) + nn(
        normed_ref[:, rows:], high_ref[:, : 3 * width]
    )
    mixed_ref[:, :width] = (mixed[:, :width] + bias_ref[0:1]).astype(bf16)
    mixed_ref[:, width : 2 * width] = mixed[:, width : 2 * width].astype(bf16)
    mixed_ref[:, 2 * width :] = (mixed[:, 2 * width :] + bias_ref[1:2]).astype(bf16)
    segment_row = segment_ref[...]
    spans = ((0, half, key_mask(segment_row, half, 0, half)), (half, length, key_mask(segment_row, length, half, half)))
    log_ref[...] = jnp.zeros_like(log_ref)
    for two in range(width // 128):
        at = 128 * two
        query_two = mixed_ref[:, at : at + 128] * jnp.asarray(score_scale, bf16)
        key_two = mixed_ref[:, width + at : width + at + 128]
        value_turned = jnp.transpose(mixed_ref[:, 2 * width + at : 2 * width + at + 128])
        parts = []
        for which in range(2):
            query_rows = lane_half(query_two, which)
            value_rows = value_turned[HEAD_DIM * which : HEAD_DIM * (which + 1)]
            sides = []
            for first, keys, mask in spans:
                scores = inner_cols(key_two[:keys], query_rows[first : first + half]) + mask
                top = jnp.max(scores, axis=0, keepdims=True)
                exponent = jnp.exp(scores - top)
                total = jnp.sum(exponent, axis=0, keepdims=True)
                log_ref[2 * two + which : 2 * two + which + 1, first : first + half] = top + jnp.log(total)
                sides.append(nn(value_rows[:, :keys], exponent.astype(bf16)) / total)
            parts.append(jnp.concatenate(sides, axis=1))
        context_ref[:, at : at + 128] = jnp.transpose(jnp.concatenate(parts, axis=0)).astype(bf16)
    for at, part_ref in ((0, low_ref), (rows, high_ref)):
        attended_ref[:, at : at + rows] = inner_cols(
            context_ref[...], part_ref[:, 3 * width : 4 * width]
        ).astype(bf16)


def store_blocks(value, place, keep_ref, send_ref, columns):
    rows = value.shape[0] // 8
    counts = [0, 0]
    for block in range(8):
        which = (block >> (2 - place)) & 1
        target = send_ref if which else keep_ref
        at = counts[which] * rows
        counts[which] += 1
        target[at : at + rows, columns] = value[block * rows : (block + 1) * rows].astype(target.dtype)


def join_blocks(place, keep_ref, other_ref, whole_ref):
    rows = whole_ref.shape[0] // 8
    counts = [0, 0]
    for block in range(8):
        which = (block >> (2 - place)) & 1
        at = counts[which] * rows
        counts[which] += 1
        source = other_ref if which else keep_ref
        whole_ref[block * rows : (block + 1) * rows] = source[at : at + rows]


def feed_kernel(
    rows_ref,
    own_ref,
    other_ref,
    vector_ref,
    up_mine_ref,
    up_other_ref,
    down_mine_ref,
    down_other_ref,
    bias_ref,
    cot_ref,
    middle_ref,
    feed_ref,
    grad_two_ref,
    up_keep_ref,
    up_send_ref,
    down_keep_ref,
    down_send_ref,
    bias_grad_ref,
    normed_ref,
    normed_turned_ref,
    cot_turned_ref,
    up_ref,
    down_ref,
):
    bf16, f32 = jnp.bfloat16, jnp.float32
    join_blocks(PLACE[TURNS[1][2]], up_mine_ref, up_other_ref, up_ref)
    join_blocks(PLACE[TURNS[2][2]], down_mine_ref, down_other_ref, down_ref)
    middle = (
        rows_ref[...].astype(f32)
        + (own_ref[...].astype(f32) + other_ref[...].astype(f32))
        + vector_ref[4:5]
    )
    middle_ref[...] = middle
    unit, _ = column_norm(middle)
    normed_ref[...] = (unit * vector_ref[1:2] + vector_ref[3:4]).astype(bf16)
    normed_turned_ref[...] = jnp.transpose(normed_ref[...])
    cot_turned_ref[...] = jnp.transpose(cot_ref[...])
    hidden_width = up_ref.shape[1]
    step = hidden_width // 3
    bias_grad_ref[...] = jnp.zeros_like(bias_grad_ref)
    feed = grad_two = None
    for at in range(0, hidden_width, step):
        columns = slice(at, at + step)
        before = nn(normed_ref[...], up_ref[:, columns]) + bias_ref[:, columns]
        square = before * before
        bend = jnp.tanh(gelu_factor * (before + 0.044715 * before * square))
        opened = 0.5 * (1.0 + bend)
        hidden = (before * opened).astype(bf16)
        slope = opened + 0.5 * before * (1.0 - bend * bend) * (
            gelu_factor * (1.0 + 3.0 * 0.044715 * square)
        )
        grad_before = (nn(cot_ref[...], down_ref[:, columns]) * slope).astype(bf16)
        part = inner_cols(hidden, down_ref[:, columns])
        feed = part if feed is None else feed + part
        part = inner_cols(grad_before, up_ref[:, columns])
        grad_two = part if grad_two is None else grad_two + part
        bias_grad_ref[0:1, columns] = jnp.sum(grad_before.astype(f32), axis=0, keepdims=True)
        store_blocks(nn(cot_turned_ref[...], hidden), PLACE[TURNS[2][2]], down_keep_ref, down_send_ref, columns)
        store_blocks(nn(normed_turned_ref[...], grad_before), PLACE[TURNS[1][2]], up_keep_ref, up_send_ref, columns)
    feed_ref[...] = feed.astype(bf16)
    grad_two_ref[...] = grad_two.astype(bf16)


def attend_back_kernel(
    score_scale,
    middle_ref,
    cot_ref,
    own_ref,
    other_ref,
    vector_ref,
    context_ref,
    mixed_ref,
    log_ref,
    low_ref,
    high_ref,
    segment_ref,
    normed_ref,
    rows_ref,
    hidden_sums_ref,
    fold_ref,
    block_ref,
    grad_middle_ref,
    grad_one_ref,
    keep_a_ref,
    send_a_ref,
    keep_b_ref,
    send_b_ref,
    keep_c_ref,
    send_c_ref,
    grad_context_ref,
    grad_mixed_ref,
    terms_ref,
    bias_ref,
):
    bf16, f32 = jnp.bfloat16, jnp.float32
    length = middle_ref.shape[0]
    width = context_ref.shape[1]
    rows = low_ref.shape[0]
    half = length // 2
    unit, inverse = column_norm(middle_ref[...])
    grad_norm = own_ref[...].astype(f32) + other_ref[...].astype(f32)
    scaled = grad_norm * vector_ref[1:2]
    mean_grad = jnp.mean(scaled, axis=-1, keepdims=True)
    mean_cross = jnp.mean(scaled * unit, axis=-1, keepdims=True)
    cot = cot_ref[...].astype(f32)
    grad_middle = cot + inverse * (scaled - mean_grad - unit * mean_cross)
    grad_middle_ref[...] = grad_middle
    terms_ref[...] = jnp.zeros_like(terms_ref)
    terms_ref[1:2] = 0.5 * jnp.sum(grad_norm * unit, axis=0, keepdims=True)
    terms_ref[3:4] = 0.5 * jnp.sum(grad_norm, axis=0, keepdims=True)
    terms_ref[4:5] = 0.5 * jnp.sum(grad_middle, axis=0, keepdims=True)
    terms_ref[5:6] = 0.5 * jnp.sum(cot, axis=0, keepdims=True)
    hidden_width = hidden_sums_ref.shape[1]
    bias_ref[:, :hidden_width] = hidden_sums_ref[0:1]
    middle_rows = grad_middle.astype(bf16)
    third = keep_a_ref.shape[1]
    last = keep_c_ref.shape[1]
    store_blocks(
        nn(jnp.transpose(middle_rows), context_ref[...]),
        PLACE[TURNS[2][2]],
        keep_c_ref,
        send_c_ref,
        slice(third - width, third),
    )
    grad_context_ref[...] = (
        nn(middle_rows[:, :rows], low_ref[:, 3 * width : 4 * width])
        + nn(middle_rows[:, rows:], high_ref[:, 3 * width : 4 * width])
    ).astype(bf16)
    segment_row = segment_ref[...]
    spans = ((0, half, key_mask(segment_row, half, 0, half)), (half, length, key_mask(segment_row, length, half, half)))
    for two in range(width // 128):
        at = 128 * two
        query_two = mixed_ref[:, at : at + 128] * jnp.asarray(score_scale, bf16)
        key_two = mixed_ref[:, width + at : width + at + 128]
        value_two = mixed_ref[:, 2 * width + at : 2 * width + at + 128]
        grad_two = grad_context_ref[:, at : at + 128]
        key_turned = jnp.transpose(key_two)
        grad_queries = []
        grad_keys = [0.0, 0.0]
        grad_values = [0.0, 0.0]
        for which in range(2):
            query_rows = lane_half(query_two, which)
            grad_rows = lane_half(grad_two, which)
            key_rows = key_turned[HEAD_DIM * which : HEAD_DIM * (which + 1)]
            sides = []
            for side, (first, keys, mask) in enumerate(spans):
                query_side = query_rows[first : first + half]
                grad_side = grad_rows[first : first + half]
                log_side = log_ref[2 * two + which : 2 * two + which + 1, first : first + half]
                scores = inner_cols(key_two[:keys], query_side) + mask
                soft = jnp.exp(scores - log_side)
                grad_soft = inner_cols(value_two[:keys], grad_side)
                crossed = soft * grad_soft
                grad_scores = (
                    crossed - soft * jnp.sum(crossed, axis=0, keepdims=True)
                ).astype(bf16)
                grad_keys[side] += nn(grad_scores, query_side)
                grad_values[side] += nn(soft.astype(bf16), grad_side)
                sides.append(nn(key_rows[:, :keys], grad_scores))
            grad_queries.append(jnp.concatenate(sides, axis=1))
        queries_out = jnp.transpose(jnp.concatenate(grad_queries, axis=0)) * score_scale
        for place, value in enumerate((queries_out, grad_keys, grad_values)):
            columns = slice(place * width + at, place * width + at + 128)
            if place == 0:
                grad_mixed_ref[:, columns] = value.astype(bf16)
            else:
                grad_mixed_ref[:half, columns] = (value[0] + value[1][:half]).astype(bf16)
                grad_mixed_ref[half:, columns] = value[1][half:].astype(bf16)
            if place != 1:
                start = hidden_width + (place // 2) * width + at
                bias_ref[:, start : start + 128] = jnp.sum(
                    grad_mixed_ref[:, columns].astype(f32), axis=0, keepdims=True
                )
    unit, _ = column_norm(rows_ref[...].astype(f32))
    for at, part_ref in ((0, low_ref), (rows, high_ref)):
        columns = slice(at, at + rows)
        grad_one = inner_cols(grad_mixed_ref[...], part_ref[:, : 3 * width])
        grad_one_ref[:, columns] = grad_one.astype(bf16)
        terms_ref[0:1, columns] = jnp.sum(grad_one * unit[:, columns], axis=0, keepdims=True)
        terms_ref[2:3, columns] = jnp.sum(grad_one, axis=0, keepdims=True)
    row = lax.broadcasted_iota(jnp.int32, (64, bias_ref.shape[1]), 0)
    lane = lax.broadcasted_iota(jnp.int32, (64, bias_ref.shape[1]), 1)
    inside = jnp.zeros(row.shape, jnp.bool_)
    for start, size in ((0, hidden_width), (hidden_width, width), (hidden_width + width, width)):
        first = row * (size // 64) + start
        inside = inside | ((lane >= first) & (lane < first + size // 64))
    spread = jnp.where(inside, bias_ref[...], 0.0)
    for matrix_ref in (fold_ref, block_ref):
        high = spread.astype(bf16)
        rest = (spread - high.astype(f32)).astype(bf16)
        if matrix_ref is fold_ref:
            spread = nn(high, matrix_ref[...]) + nn(rest, matrix_ref[...])
        else:
            spread = nn(matrix_ref[...], high) + nn(matrix_ref[...], rest)
    store_blocks(
        jnp.transpose(terms_ref[...]) + spread,
        PLACE[TURNS[2][2]],
        keep_c_ref,
        send_c_ref,
        slice(third, last),
    )
    turned = jnp.transpose(normed_ref[...])
    targets = ((keep_a_ref, send_a_ref), (keep_b_ref, send_b_ref), (keep_c_ref, send_c_ref))
    for i, (keep_ref, send_ref) in enumerate(targets):
        size = min(third, 3 * width - i * third)
        store_blocks(
            nn(turned, grad_mixed_ref[:, i * third : i * third + size]),
            PLACE[TURNS[i][2]],
            keep_ref,
            send_ref,
            slice(0, size),
        )


def token_kernel(
    core_ref,
    rows_ref,
    own_ref,
    other_ref,
    grad_middle_ref,
    vector_ref,
    order_ref,
    token_ref,
    token_full_ref,
):
    bf16, f32 = jnp.bfloat16, jnp.float32
    half = token_ref.shape[0]
    unit, inverse = column_norm(rows_ref[...].astype(f32))
    grad_norm = own_ref[...].astype(f32) + other_ref[...].astype(f32)
    scaled = grad_norm * vector_ref[0:1]
    mean_grad = jnp.mean(scaled, axis=-1, keepdims=True)
    mean_cross = jnp.mean(scaled * unit, axis=-1, keepdims=True)
    token_full_ref[...] = (
        grad_middle_ref[...] + inverse * (scaled - mean_grad - unit * mean_cross)
    )
    start = pl.multiple_of(core_ref[0] * half, half)
    token_rows = token_full_ref[pl.ds(start, half), :].astype(bf16)
    token_ref[...] = inner_cols(token_rows, order_ref[...]).astype(bf16)


def call(kernel, outs, scratch, *operands, smem=0):
    space = [pl.BlockSpec(memory_space=pltpu.SMEM)] * smem
    space += [pl.BlockSpec(memory_space=pltpu.VMEM)] * (len(operands) - smem)
    return pl.pallas_call(
        kernel,
        out_shape=[jax.ShapeDtypeStruct(shape, kind) for shape, kind in outs],
        in_specs=space,
        out_specs=[pl.BlockSpec(memory_space=pltpu.VMEM)] * len(outs),
        scratch_shapes=[pltpu.VMEM(shape, kind) for shape, kind in scratch],
        compiler_params=pltpu.CompilerParams(vmem_limit_bytes=56 * 1024 * 1024),
    )(*operands)


def local(
    tokens,
    cotangent,
    segments,
    input_weight,
    output_weight,
    up_weight,
    down_weight,
    head_bias,
    hidden_bias,
    norm_gains,
    shifts,
):
    bf16, f32 = jnp.bfloat16, jnp.float32
    half, width = tokens.shape
    length = segments.shape[1]
    block = input_weight.shape[0]
    heads_width = input_weight.shape[2]
    hidden_width = up_weight.shape[1]
    local_heads = heads_width // HEAD_DIM
    score_scale = 1.0 / math.sqrt(HEAD_DIM)
    core = lax.axis_index("c")

    first_end = 4 * heads_width + 128
    pack_width = first_end + 2 * hidden_width
    me = (
        (lax.axis_index("zh") * 4 + lax.axis_index("xh") * 2 + lax.axis_index("h"))
        .astype(jnp.int32)
        .reshape(1)
    )
    (shard,) = call(
        pack_kernel,
        [((block, pack_width), bf16)],
        [((128, block), f32)],
        input_weight,
        output_weight.T,
        up_weight,
        down_weight.T,
        norm_gains,
        shifts,
    )
    order = feature_order(width)
    blocks = block_order(width)
    folds = bias_fold(hidden_width, heads_width)

    def full_rows(rows):
        return nn(lax.all_gather(swap_roles(rows), "c", axis=0, tiled=True), order).astype(bf16)

    rows = full_rows(tokens)
    cot_rows = full_rows(cotangent)

    parts, order, blocks, folds, rows, cot_rows = lax.optimization_barrier(
        (gather_near(shard), order, blocks, folds, rows, cot_rows)
    )
    near = call(
        collect_kernel,
        [
            ((8 * block, first_end), bf16),
            ((8 * block, hidden_width), bf16),
            ((8 * block, hidden_width), bf16),
        ],
        [((8 * block, pack_width), bf16)],
        me,
        *parts,
        smem=1,
    )
    small = swap_roles(
        jnp.concatenate(
            (head_bias.reshape(-1), hidden_bias, segments[0].astype(bf16))
        )
    )
    bias_rows = small[: 2 * heads_width].reshape(2, heads_width).astype(f32)
    hidden_row = small[2 * heads_width : 2 * heads_width + hidden_width].astype(f32)
    segment_row = small[2 * heads_width + hidden_width :].astype(f32).reshape(1, length)
    first_halves, up_halves, down_halves = gather_far(near)

    def own_half(rows):
        return lax.dynamic_slice_in_dim(rows, core * half, half, axis=0)

    def other_half(rows):
        return lax.dynamic_slice_in_dim(rows, (1 - core) * half, half, axis=0)

    vectors, normed_one, mixed, log_sums, context, attended = call(
        functools.partial(attend_kernel, score_scale),
        [
            ((8, width), f32),
            ((length, width), bf16),
            ((length, 3 * heads_width), bf16),
            ((8, length), f32),
            ((length, heads_width), bf16),
            ((length, width), bf16),
        ],
        [],
        rows,
        *first_halves,
        bias_rows,
        segment_row,
    )
    middle, feed, grad_two, up_keep, up_send, down_keep, down_send, hidden_sums = call(
        feed_kernel,
        [
            ((length, width), f32),
            ((length, width), bf16),
            ((length, width), bf16),
            ((width // 2, hidden_width), bf16),
            ((width // 2, hidden_width), bf16),
            ((width // 2, hidden_width), bf16),
            ((width // 2, hidden_width), bf16),
            ((8, hidden_width), f32),
        ],
        [
            ((length, width), bf16),
            ((width, length), bf16),
            ((width, length), bf16),
            ((width, hidden_width), bf16),
            ((width, hidden_width), bf16),
        ],
        rows,
        attended,
        pair(attended),
        vectors,
        *up_halves,
        *down_halves,
        hidden_row.reshape(1, hidden_width),
        cot_rows,
    )
    down_other = step_along(down_send, TURNS[2][2])
    up_other = step_along(up_send, TURNS[1][2])
    outcome = (
        own_half(middle)
        + own_half(feed).astype(f32)
        + pair(other_half(feed)).astype(f32)
        + vectors[5]
    )
    block_out = swap_roles(inner_cols(outcome.astype(bf16), order).astype(bf16))

    grad_middle, grad_one, *first_grads = call(
        functools.partial(attend_back_kernel, score_scale),
        [
            ((length, width), f32),
            ((length, width), bf16),
        ]
        + [((width // 2, 4 * heads_width // 3), bf16)] * 4
        + [((width // 2, 4 * heads_width // 3 + 128), bf16)] * 2,
        [
            ((length, heads_width), bf16),
            ((length, 3 * heads_width), bf16),
            ((128, width), f32),
            ((1, hidden_width + 2 * heads_width), f32),
        ],
        middle,
        cot_rows,
        grad_two,
        pair(grad_two),
        vectors,
        context,
        mixed,
        log_sums,
        *first_halves,
        segment_row,
        normed_one,
        rows,
        hidden_sums,
        folds,
        blocks,
    )
    down_keep, down_send = half_sums(down_keep, down_other, 1, 2)
    up_keep, up_send = half_sums(up_keep, up_other, 0, 2)
    down_other = step_along(down_send, TURNS[2][1])
    up_other = step_along(up_send, TURNS[1][1])
    grad_one_other = pair(grad_one)
    (token_grad,) = call(
        token_kernel,
        [((half, width), bf16)],
        [((length, width), f32)],
        core.astype(jnp.int32).reshape(1),
        rows,
        grad_one,
        grad_one_other,
        grad_middle,
        vectors,
        order,
        smem=1,
    )
    token_grad = swap_roles(token_grad)
    down_keep, down_send = half_sums(down_keep, down_other, 0, 1)
    up_keep, up_send = half_sums(up_keep, up_other, 0, 1)
    last = [(up_keep, up_send, TURNS[1]), (down_keep, down_send, TURNS[2])]
    pieces = [(first_grads[2 * i], first_grads[2 * i + 1], TURNS[i]) for i in range(3)]
    pieces = [second_turn(*piece) + (piece[2],) for piece in pieces]
    pieces = [(*third_turn(*piece), piece[2]) for piece in pieces]
    operands = []
    for keep, send, turns in pieces + last:
        operands += [keep, step_along(send, turns[0])]
    cross = pair(add_low(operands[4][:, -128:], operands[5][:, -128:]))
    shares = call(
        deal_kernel,
        [((4 * block, pack_width), bf16)] * 2,
        [],
        me,
        cross,
        *operands,
        smem=1,
    )
    shares = scatter_near(*shares)
    six = block // 2
    input_grad, output_grad, up_grad, down_grad, head_grad, hidden_grad, gain_grad, shift_grad = call(
        unpack_kernel,
        [
            ((block, 3, heads_width), f32),
            ((block, heads_width), f32),
            ((block, hidden_width), f32),
            ((block, hidden_width), f32),
            ((2, six), f32),
            ((1, 2 * block), f32),
            ((2, six), f32),
            ((4, six), f32),
        ],
        [],
        lax.axis_index("h").astype(jnp.int32).reshape(1),
        *shares,
        smem=1,
    )
    return (
        block_out,
        token_grad,
        input_grad,
        output_grad.T,
        up_grad,
        down_grad.T,
        head_grad,
        hidden_grad.reshape(2 * block),
        gain_grad,
        shift_grad,
    )


def solution(mesh):
    fine = Mesh(mesh.devices.reshape((2,) * 7), AXES)
    in_specs = (
        P(AXES, None),
        P(AXES, None),
        P(DP, None),
        P(DP, None, "h"),
        P("h", DP),
        P(DP, "h"),
        P("h", DP),
        P(None, "h"),
        P("h"),
        P(None, DP),
        P(None, DP),
    )
    out_specs = (
        P(AXES, None),
        P(AXES, None),
        P(DP, None, "h"),
        P("h", DP),
        P(DP, "h"),
        P("h", DP),
        P(None, ("h",) + DP),
        P(("h",) + DP),
        P(None, AXES),
        P(None, AXES),
    )
    return jax.shard_map(local, mesh=fine, in_specs=in_specs, out_specs=out_specs, check_vma=False)
```

```python
import functools
import itertools
import math

import jax
import jax.numpy as jnp
import numpy as np
from jax import lax
from jax.experimental import pallas as pl
from jax.experimental.pallas import tpu as pltpu
from jax.sharding import Mesh
from jax.sharding import PartitionSpec as P

HEAD_DIM = 64


norm_epsilon = 1e-05
masked_value = -1e30
gelu_factor = 0.7978845608028654


def inner_cols(left_side, right_side):
    return lax.dot_general(
        left_side, right_side, (((1,), (1,)), ((), ())), preferred_element_type=jnp.float32
    )


AXES = ("xh", "xl", "yl", "zh", "zl", "c", "h")
DP = AXES[:6]
RING = {"x": ("xh", "xl"), "y": ("h", "yl"), "z": ("zh", "zl")}
PLACE = {"z": 0, "y": 1, "x": 2}
TURNS = (("x", "y", "z"), ("y", "z", "x"), ("z", "x", "y"))


def swap_roles(values):
    return lax.ppermute(values, ("c", "h"), [(0, 0), (1, 2), (2, 1), (3, 3)])


def pair(values):
    return lax.ppermute(values, "c", [(0, 1), (1, 0)])


def step_along(values, axis):
    high, low = RING[axis]
    order = [name for name in AXES if name in (high, low, "c")]
    moves = []
    for place in itertools.product(range(2), repeat=3):
        target = dict(zip(order, place))
        target[low] ^= 1
        target[high] ^= target["c"]
        moves.append(
            (place[0] * 4 + place[1] * 2 + place[2], sum(target[n] << (2 - i) for i, n in enumerate(order)))
        )
    return lax.ppermute(values, tuple(order), moves)


def cross_roles(values, outward):
    moves = [(0, 1), (1, 3), (2, 0), (3, 2)]
    return lax.ppermute(values, ("c", "h"), moves if outward else [(b, a) for a, b in moves])


def flip(values, axis):
    return lax.ppermute(values, axis, [(0, 1), (1, 0)])


def gather_near(shard):
    parts = jnp.concatenate((swap_roles(shard), cross_roles(shard, True)), axis=0)
    parts = jnp.concatenate((parts, flip(parts, "xh")), axis=0)
    return parts, flip(parts, "zh")


def add_low(left, right):
    return (left.astype(jnp.float32) + right.astype(jnp.float32)).astype(jnp.bfloat16)


def scatter_near(keep, send, tied):
    for axis in ("zh", "xh"):
        other = flip(send, axis)
        rows = keep.shape[0] // 2
        keep, send = add_low(keep[:rows], other[:rows]), add_low(keep[rows:], other[rows:])
        if axis == "zh":
            keep, send, tied = lax.optimization_barrier((keep, send, tied))
    return swap_roles(keep), cross_roles(send, False), tied


def open_blocks(piece):
    return piece.reshape((1, 1, 1) + piece.shape)


def gather_far(pieces, turn_lists, tied=()):
    pieces = [open_blocks(piece) for piece in pieces]
    for turn in range(3):
        if turn == 2 and tied:
            pieces, tied = lax.optimization_barrier((pieces, tied))
        others = [step_along(piece, turns[turn]) for piece, turns in zip(pieces, turn_lists)]
        if turn < 2:
            pieces = [
                jnp.concatenate((piece, other), axis=PLACE[turns[turn]])
                for piece, other, turns in zip(pieces, others, turn_lists)
            ]
    halves = [
        [half.reshape(4 * half.shape[3], half.shape[4]) for half in both]
        for both in zip(pieces, others)
    ]
    return halves, tied


def source_blocks(width):
    place = np.arange(width, dtype=np.int32) // (width // 64)
    near, far = place % 8, place // 8
    fixed = ((near >> 1) & 1) * 32 + (near >> 2) * 4 + (near & 1)
    xl = lax.axis_index("xl") ^ (far & 1)
    yl = lax.axis_index("yl") ^ ((far >> 1) & 1)
    zl = lax.axis_index("zl") ^ (far >> 2)
    return lax.optimization_barrier(fixed + xl * 16 + yl * 8 + zl * 2)


def feature_order(sources, width):
    block = width // 64
    inner = np.arange(width, dtype=np.int32) % block
    source = lax.optimization_barrier(sources * block + inner)
    return (lax.broadcasted_iota(jnp.int32, (width, width), 0) == source[None]).astype(jnp.bfloat16)


def block_order(sources, width):
    return (lax.broadcasted_iota(jnp.int32, (width, 64), 1) == sources[:, None]).astype(jnp.bfloat16)


def bias_fold(hidden_width, width):
    many, few = hidden_width // 64, width // 64
    target = np.concatenate(
        (
            np.arange(hidden_width) % many,
            np.arange(width) % few + many,
            np.arange(width) % few + many + few,
        )
    )
    return jnp.asarray(np.arange(128)[None] == target[:, None] + 8, jnp.bfloat16)


def place_rows(rows, me):
    block = rows // 8
    row = lax.broadcasted_iota(jnp.int32, (rows, rows), 0)
    column = lax.broadcasted_iota(jnp.int32, (rows, rows), 1)
    found = jnp.zeros((rows, rows), jnp.float32)
    for k in range(8):
        inside = (row >= k * block) & (row < (k + 1) * block)
        same = column - (me ^ k) * block == row - k * block
        found = jnp.where(inside & same, 1.0, found)
    return found.astype(jnp.bfloat16)


def eye(size):
    row = lax.broadcasted_iota(jnp.int32, (size, size), 0)
    column = lax.broadcasted_iota(jnp.int32, (size, size), 1)
    return (row == column).astype(jnp.float32).astype(jnp.bfloat16)


def pack_kernel(input_ref, output_ref, up_ref, down_ref, gains_ref, shifts_ref, shard_ref, feed_ref, small_ref):
    bf16 = jnp.bfloat16
    block, width = output_ref.shape
    hidden_width = up_ref.shape[1]
    for i in range(3):
        shard_ref[:, i * width : (i + 1) * width] = input_ref[:, i, :]
    shard_ref[:, 3 * width : 4 * width] = output_ref[...]
    small_ref[...] = jnp.zeros_like(small_ref)
    small_ref[0:2] = gains_ref[...].astype(jnp.float32)
    small_ref[2:6] = shifts_ref[...].astype(jnp.float32)
    shard_ref[:, 4 * width :] = inner_cols(eye(block), small_ref[...].astype(bf16)).astype(bf16)
    feed_ref[:, :hidden_width] = up_ref[...]
    feed_ref[:, hidden_width:] = down_ref[...]


def collect_kernel(me_ref, *refs):
    parts, outs, held_ref = refs[:2], refs[2:-1], refs[-1]
    rows = held_ref.shape[0]
    held_ref[: rows // 2] = parts[0][...]
    held_ref[rows // 2 :] = parts[1][...]
    moved = place_rows(rows, me_ref[0])
    at = 0
    for out in outs:
        columns = out.shape[1]
        out[...] = nn(moved, held_ref[:, at : at + columns]).astype(jnp.bfloat16)
        at += columns


def deal_kernel(me_ref, cross_ref, *refs):
    parts, outs = refs[:-2], refs[-2:]
    rows = parts[0].shape[0]
    moved = place_rows(rows, me_ref[0])
    at = 0
    for i, (keep, other) in enumerate(zip(parts[::2], parts[1::2])):
        columns = keep.shape[1]
        total = add_low(keep[...], other[...])
        if i == 2:
            lane = lax.broadcasted_iota(jnp.int32, cross_ref.shape, 1)
            cross = jnp.where(lane < 8, cross_ref[...].astype(jnp.float32), 0.0)
            total = jnp.concatenate((total[:, : columns - 128], add_low(total[:, columns - 128 :], cross)), axis=1)
        total = nn(moved, total).astype(jnp.bfloat16)
        outs[0][:, at : at + columns] = total[: rows // 2]
        outs[1][:, at : at + columns] = total[rows // 2 :]
        at += columns


def unpack_kernel(half_ref, *refs):
    parts = refs[:2]
    input_ref, output_ref, up_ref, down_ref, head_ref, hidden_ref, gain_ref, shift_ref = refs[2:]
    f32 = jnp.float32
    block, width = output_ref.shape
    hidden_width = up_ref.shape[1]
    six = block // 2

    def total(start, size):
        columns = slice(start, start + size)
        value = parts[0][:, columns].astype(f32)
        for part in parts[1:]:
            value = value + part[:, columns].astype(f32)
        return value

    def pick(rows, columns, offset):
        row = lax.broadcasted_iota(jnp.int32, (rows, columns), 0)
        column = lax.broadcasted_iota(jnp.int32, (rows, columns), 1)
        return (row == column + offset).astype(f32)

    def exact(left, right, dims):
        return lax.dot_general(
            left, right, (dims, ((), ())), precision=lax.Precision.HIGHEST, preferred_element_type=f32
        )

    for i in range(3):
        input_ref[:, i, :] = total(i * width, width)
    output_ref[...] = total(3 * width, width)
    at = 4 * width + 128
    up_ref[...] = total(at, hidden_width)
    down_ref[...] = total(at + hidden_width, hidden_width)
    small = total(4 * width, 128)
    norm_terms = exact(small, pick(block, six, half_ref[0] * six), ((0,), (0,)))
    gain_ref[...] = norm_terms[0:2]
    shift_ref[...] = norm_terms[2:6]
    hidden_ref[...] = exact(small[0:1], pick(128, 2 * block, 8), ((1,), (0,)))
    head_ref[0:1] = exact(small[0:1], pick(128, six, 8 + 2 * block), ((1,), (0,)))
    head_ref[1:2] = exact(small[0:1], pick(128, six, 8 + 2 * block + six), ((1,), (0,)))


def half_sums(keep, other, place, places):
    rows, columns = keep.shape
    shape = (2,) * places + (rows >> places, columns)
    keep, other = keep.reshape(shape), other.reshape(shape)
    return [
        add_low(
            lax.slice_in_dim(keep, i, i + 1, axis=place), lax.slice_in_dim(other, i, i + 1, axis=place)
        ).reshape(rows // 2, columns)
        for i in range(2)
    ]


def second_turn(keep, send, turns):
    place = sorted(turns[:2], key=PLACE.get).index(turns[1])
    return tuple(half_sums(keep, step_along(send, turns[2]), place, 2))


def third_turn(keep, send, turns):
    return half_sums(keep, step_along(send, turns[1]), 0, 1)


def column_norm(values):
    mean_val = jnp.mean(values, axis=-1, keepdims=True)
    centered = values - mean_val
    variance = jnp.mean(centered * centered, axis=-1, keepdims=True)
    inverse = lax.rsqrt(variance + norm_epsilon)
    return centered * inverse, inverse


def nn(left, right):
    return jnp.dot(left, right, preferred_element_type=jnp.float32)


def key_mask(segment_row, keys, first, queries):
    column = jnp.transpose(jnp.broadcast_to(segment_row, (8, segment_row.shape[1])))[:keys, :1]
    row = segment_row[:, first : first + queries]
    key_pos = lax.broadcasted_iota(jnp.int32, (keys, queries), 0)
    query_pos = lax.broadcasted_iota(jnp.int32, (keys, queries), 1) + first
    return jnp.where((column == row) & (key_pos <= query_pos), 0.0, masked_value)


def lane_half(values, which):
    lane = lax.broadcasted_iota(jnp.int32, values.shape, 1)
    inside = (lane >= HEAD_DIM) if which else (lane < HEAD_DIM)
    return jnp.where(inside, values, jnp.zeros_like(values))


def attend_kernel(
    score_scale,
    rows_ref,
    low_ref,
    high_ref,
    bias_ref,
    segment_ref,
    vector_ref,
    normed_ref,
    mixed_ref,
    log_ref,
    context_ref,
    attended_ref,
):
    bf16 = jnp.bfloat16
    length = rows_ref.shape[0]
    width = context_ref.shape[1]
    rows = low_ref.shape[0]
    for at, part_ref in ((0, low_ref), (rows, high_ref)):
        turned = jnp.transpose(part_ref[:, 4 * width : 4 * width + 128].astype(jnp.float32))
        vector_ref[:, at : at + rows] = turned[:8]
    half = length // 2
    unit, _ = column_norm(rows_ref[...].astype(jnp.float32))
    normed_ref[...] = (unit * vector_ref[0:1] + vector_ref[2:3]).astype(bf16)
    mixed = nn(normed_ref[:, :rows], low_ref[:, : 3 * width]) + nn(
        normed_ref[:, rows:], high_ref[:, : 3 * width]
    )
    mixed_ref[:, :width] = (mixed[:, :width] + bias_ref[0:1]).astype(bf16)
    mixed_ref[:, width : 2 * width] = mixed[:, width : 2 * width].astype(bf16)
    mixed_ref[:, 2 * width :] = (mixed[:, 2 * width :] + bias_ref[1:2]).astype(bf16)
    segment_row = segment_ref[...]
    spans = ((0, half, key_mask(segment_row, half, 0, half)), (half, length, key_mask(segment_row, length, half, half)))
    log_ref[...] = jnp.zeros_like(log_ref)
    for two in range(width // 128):
        at = 128 * two
        query_two = mixed_ref[:, at : at + 128] * jnp.asarray(score_scale, bf16)
        key_two = mixed_ref[:, width + at : width + at + 128]
        value_turned = jnp.transpose(mixed_ref[:, 2 * width + at : 2 * width + at + 128])
        parts = []
        for which in range(2):
            query_rows = lane_half(query_two, which)
            value_rows = value_turned[HEAD_DIM * which : HEAD_DIM * (which + 1)]
            sides = []
            for first, keys, mask in spans:
                scores = inner_cols(key_two[:keys], query_rows[first : first + half]) + mask
                top = jnp.max(scores, axis=0, keepdims=True)
                exponent = jnp.exp(scores - top)
                total = jnp.sum(exponent, axis=0, keepdims=True)
                log_ref[2 * two + which : 2 * two + which + 1, first : first + half] = top + jnp.log(total)
                sides.append(nn(value_rows[:, :keys], exponent.astype(bf16)) / total)
            parts.append(jnp.concatenate(sides, axis=1))
        context_ref[:, at : at + 128] = jnp.transpose(jnp.concatenate(parts, axis=0)).astype(bf16)
    for at, part_ref in ((0, low_ref), (rows, high_ref)):
        attended_ref[:, at : at + rows] = inner_cols(
            context_ref[...], part_ref[:, 3 * width : 4 * width]
        ).astype(bf16)


def store_blocks(value, place, keep_ref, send_ref, columns):
    rows = value.shape[0] // 8
    counts = [0, 0]
    for block in range(8):
        which = (block >> (2 - place)) & 1
        target = send_ref if which else keep_ref
        at = counts[which] * rows
        counts[which] += 1
        target[at : at + rows, columns] = value[block * rows : (block + 1) * rows].astype(target.dtype)


def join_blocks(place, keep_ref, other_ref, whole_ref):
    rows = whole_ref.shape[0] // 8
    counts = [0, 0]
    for block in range(8):
        which = (block >> (2 - place)) & 1
        at = counts[which] * rows
        counts[which] += 1
        source = other_ref if which else keep_ref
        whole_ref[block * rows : (block + 1) * rows] = source[at : at + rows]


def feed_kernel(
    rows_ref,
    own_ref,
    other_ref,
    vector_ref,
    up_mine_ref,
    up_other_ref,
    down_mine_ref,
    down_other_ref,
    bias_ref,
    cot_ref,
    middle_ref,
    feed_ref,
    grad_two_ref,
    up_keep_ref,
    up_send_ref,
    down_keep_ref,
    down_send_ref,
    bias_grad_ref,
    normed_ref,
    normed_turned_ref,
    cot_turned_ref,
    up_ref,
    down_ref,
):
    bf16, f32 = jnp.bfloat16, jnp.float32
    join_blocks(PLACE[TURNS[1][2]], up_mine_ref, up_other_ref, up_ref)
    join_blocks(PLACE[TURNS[2][2]], down_mine_ref, down_other_ref, down_ref)
    middle = (
        rows_ref[...].astype(f32)
        + (own_ref[...].astype(f32) + other_ref[...].astype(f32))
        + vector_ref[4:5]
    )
    middle_ref[...] = middle
    unit, _ = column_norm(middle)
    normed_ref[...] = (unit * vector_ref[1:2] + vector_ref[3:4]).astype(bf16)
    normed_turned_ref[...] = jnp.transpose(normed_ref[...])
    cot_turned_ref[...] = jnp.transpose(cot_ref[...])
    hidden_width = up_ref.shape[1]
    step = hidden_width // 3
    bias_grad_ref[...] = jnp.zeros_like(bias_grad_ref)
    feed = grad_two = None
    for at in range(0, hidden_width, step):
        columns = slice(at, at + step)
        before = nn(normed_ref[...], up_ref[:, columns]) + bias_ref[:, columns]
        square = before * before
        bend = jnp.tanh(gelu_factor * (before + 0.044715 * before * square))
        opened = 0.5 * (1.0 + bend)
        hidden = (before * opened).astype(bf16)
        slope = opened + 0.5 * before * (1.0 - bend * bend) * (
            gelu_factor * (1.0 + 3.0 * 0.044715 * square)
        )
        grad_before = (nn(cot_ref[...], down_ref[:, columns]) * slope).astype(bf16)
        part = inner_cols(hidden, down_ref[:, columns])
        feed = part if feed is None else feed + part
        part = inner_cols(grad_before, up_ref[:, columns])
        grad_two = part if grad_two is None else grad_two + part
        bias_grad_ref[0:1, columns] = jnp.sum(grad_before.astype(f32), axis=0, keepdims=True)
        store_blocks(nn(cot_turned_ref[...], hidden), PLACE[TURNS[2][2]], down_keep_ref, down_send_ref, columns)
        store_blocks(nn(normed_turned_ref[...], grad_before), PLACE[TURNS[1][2]], up_keep_ref, up_send_ref, columns)
    feed_ref[...] = feed.astype(bf16)
    grad_two_ref[...] = grad_two.astype(bf16)


def attend_back_kernel(
    score_scale,
    middle_ref,
    cot_ref,
    own_ref,
    other_ref,
    vector_ref,
    context_ref,
    mixed_ref,
    log_ref,
    low_ref,
    high_ref,
    segment_ref,
    normed_ref,
    rows_ref,
    hidden_sums_ref,
    fold_ref,
    block_ref,
    grad_middle_ref,
    grad_one_ref,
    keep_a_ref,
    send_a_ref,
    keep_b_ref,
    send_b_ref,
    keep_c_ref,
    send_c_ref,
    grad_context_ref,
    grad_mixed_ref,
    terms_ref,
    bias_ref,
):
    bf16, f32 = jnp.bfloat16, jnp.float32
    length = middle_ref.shape[0]
    width = context_ref.shape[1]
    rows = low_ref.shape[0]
    half = length // 2
    unit, inverse = column_norm(middle_ref[...])
    grad_norm = own_ref[...].astype(f32) + other_ref[...].astype(f32)
    scaled = grad_norm * vector_ref[1:2]
    mean_grad = jnp.mean(scaled, axis=-1, keepdims=True)
    mean_cross = jnp.mean(scaled * unit, axis=-1, keepdims=True)
    cot = cot_ref[...].astype(f32)
    grad_middle = cot + inverse * (scaled - mean_grad - unit * mean_cross)
    grad_middle_ref[...] = grad_middle
    terms_ref[...] = jnp.zeros_like(terms_ref)
    terms_ref[1:2] = 0.5 * jnp.sum(grad_norm * unit, axis=0, keepdims=True)
    terms_ref[3:4] = 0.5 * jnp.sum(grad_norm, axis=0, keepdims=True)
    terms_ref[4:5] = 0.5 * jnp.sum(grad_middle, axis=0, keepdims=True)
    terms_ref[5:6] = 0.5 * jnp.sum(cot, axis=0, keepdims=True)
    hidden_width = hidden_sums_ref.shape[1]
    bias_ref[:, :hidden_width] = hidden_sums_ref[0:1]
    middle_rows = grad_middle.astype(bf16)
    third = keep_a_ref.shape[1]
    last = keep_c_ref.shape[1]
    store_blocks(
        nn(jnp.transpose(middle_rows), context_ref[...]),
        PLACE[TURNS[2][2]],
        keep_c_ref,
        send_c_ref,
        slice(third - width, third),
    )
    grad_context_ref[...] = (
        nn(middle_rows[:, :rows], low_ref[:, 3 * width : 4 * width])
        + nn(middle_rows[:, rows:], high_ref[:, 3 * width : 4 * width])
    ).astype(bf16)
    segment_row = segment_ref[...]
    spans = ((0, half, key_mask(segment_row, half, 0, half)), (half, length, key_mask(segment_row, length, half, half)))
    for two in range(width // 128):
        at = 128 * two
        query_two = mixed_ref[:, at : at + 128] * jnp.asarray(score_scale, bf16)
        key_two = mixed_ref[:, width + at : width + at + 128]
        value_two = mixed_ref[:, 2 * width + at : 2 * width + at + 128]
        grad_two = grad_context_ref[:, at : at + 128]
        key_turned = jnp.transpose(key_two)
        grad_queries = []
        grad_keys = [0.0, 0.0]
        grad_values = [0.0, 0.0]
        for which in range(2):
            query_rows = lane_half(query_two, which)
            grad_rows = lane_half(grad_two, which)
            key_rows = key_turned[HEAD_DIM * which : HEAD_DIM * (which + 1)]
            sides = []
            for side, (first, keys, mask) in enumerate(spans):
                query_side = query_rows[first : first + half]
                grad_side = grad_rows[first : first + half]
                log_side = log_ref[2 * two + which : 2 * two + which + 1, first : first + half]
                scores = inner_cols(key_two[:keys], query_side) + mask
                soft = jnp.exp(scores - log_side)
                grad_soft = inner_cols(value_two[:keys], grad_side)
                crossed = soft * grad_soft
                grad_scores = (
                    crossed - soft * jnp.sum(crossed, axis=0, keepdims=True)
                ).astype(bf16)
                grad_keys[side] += nn(grad_scores, query_side)
                grad_values[side] += nn(soft.astype(bf16), grad_side)
                sides.append(nn(key_rows[:, :keys], grad_scores))
            grad_queries.append(jnp.concatenate(sides, axis=1))
        queries_out = jnp.transpose(jnp.concatenate(grad_queries, axis=0)) * score_scale
        for place, value in enumerate((queries_out, grad_keys, grad_values)):
            columns = slice(place * width + at, place * width + at + 128)
            if place == 0:
                grad_mixed_ref[:, columns] = value.astype(bf16)
            else:
                grad_mixed_ref[:half, columns] = (value[0] + value[1][:half]).astype(bf16)
                grad_mixed_ref[half:, columns] = value[1][half:].astype(bf16)
            if place != 1:
                start = hidden_width + (place // 2) * width + at
                bias_ref[:, start : start + 128] = jnp.sum(
                    grad_mixed_ref[:, columns].astype(f32), axis=0, keepdims=True
                )
    unit, _ = column_norm(rows_ref[...].astype(f32))
    for at, part_ref in ((0, low_ref), (rows, high_ref)):
        columns = slice(at, at + rows)
        grad_one = inner_cols(grad_mixed_ref[...], part_ref[:, : 3 * width])
        grad_one_ref[:, columns] = grad_one.astype(bf16)
        terms_ref[0:1, columns] = jnp.sum(grad_one * unit[:, columns], axis=0, keepdims=True)
        terms_ref[2:3, columns] = jnp.sum(grad_one, axis=0, keepdims=True)
    row = lax.broadcasted_iota(jnp.int32, (64, bias_ref.shape[1]), 0)
    lane = lax.broadcasted_iota(jnp.int32, (64, bias_ref.shape[1]), 1)
    inside = jnp.zeros(row.shape, jnp.bool_)
    for start, size in ((0, hidden_width), (hidden_width, width), (hidden_width + width, width)):
        first = row * (size // 64) + start
        inside = inside | ((lane >= first) & (lane < first + size // 64))
    spread = jnp.where(inside, bias_ref[...], 0.0)
    for matrix_ref in (fold_ref, block_ref):
        high = spread.astype(bf16)
        rest = (spread - high.astype(f32)).astype(bf16)
        if matrix_ref is fold_ref:
            spread = nn(high, matrix_ref[...]) + nn(rest, matrix_ref[...])
        else:
            spread = nn(matrix_ref[...], high) + nn(matrix_ref[...], rest)
    store_blocks(
        jnp.transpose(terms_ref[...]) + spread,
        PLACE[TURNS[2][2]],
        keep_c_ref,
        send_c_ref,
        slice(third, last),
    )
    turned = jnp.transpose(normed_ref[...])
    targets = ((keep_a_ref, send_a_ref), (keep_b_ref, send_b_ref), (keep_c_ref, send_c_ref))
    for i, (keep_ref, send_ref) in enumerate(targets):
        size = min(third, 3 * width - i * third)
        store_blocks(
            nn(turned, grad_mixed_ref[:, i * third : i * third + size]),
            PLACE[TURNS[i][2]],
            keep_ref,
            send_ref,
            slice(0, size),
        )


def token_kernel(
    core_ref,
    rows_ref,
    own_ref,
    other_ref,
    grad_middle_ref,
    vector_ref,
    order_ref,
    token_ref,
    token_full_ref,
):
    bf16, f32 = jnp.bfloat16, jnp.float32
    half = token_ref.shape[0]
    unit, inverse = column_norm(rows_ref[...].astype(f32))
    grad_norm = own_ref[...].astype(f32) + other_ref[...].astype(f32)
    scaled = grad_norm * vector_ref[0:1]
    mean_grad = jnp.mean(scaled, axis=-1, keepdims=True)
    mean_cross = jnp.mean(scaled * unit, axis=-1, keepdims=True)
    token_full_ref[...] = (
        grad_middle_ref[...] + inverse * (scaled - mean_grad - unit * mean_cross)
    )
    start = pl.multiple_of(core_ref[0] * half, half)
    token_rows = token_full_ref[pl.ds(start, half), :].astype(bf16)
    token_ref[...] = inner_cols(token_rows, order_ref[...]).astype(bf16)


def call(kernel, outs, scratch, *operands, smem=0):
    space = [pl.BlockSpec(memory_space=pltpu.SMEM)] * smem
    space += [pl.BlockSpec(memory_space=pltpu.VMEM)] * (len(operands) - smem)
    return pl.pallas_call(
        kernel,
        out_shape=[jax.ShapeDtypeStruct(shape, kind) for shape, kind in outs],
        in_specs=space,
        out_specs=[pl.BlockSpec(memory_space=pltpu.VMEM)] * len(outs),
        scratch_shapes=[pltpu.VMEM(shape, kind) for shape, kind in scratch],
        compiler_params=pltpu.CompilerParams(vmem_limit_bytes=56 * 1024 * 1024),
    )(*operands)


def local(
    tokens,
    cotangent,
    segments,
    input_weight,
    output_weight,
    up_weight,
    down_weight,
    head_bias,
    hidden_bias,
    norm_gains,
    shifts,
):
    bf16, f32 = jnp.bfloat16, jnp.float32
    half, width = tokens.shape
    length = segments.shape[1]
    block = input_weight.shape[0]
    heads_width = input_weight.shape[2]
    hidden_width = up_weight.shape[1]
    local_heads = heads_width // HEAD_DIM
    score_scale = 1.0 / math.sqrt(HEAD_DIM)
    core = lax.axis_index("c")

    first_end = 4 * heads_width + 128
    pack_width = first_end + 2 * hidden_width
    me = (
        (lax.axis_index("zh") * 4 + lax.axis_index("xh") * 2 + lax.axis_index("h"))
        .astype(jnp.int32)
        .reshape(1)
    )
    shard, feed_shard = call(
        pack_kernel,
        [((block, first_end), bf16), ((block, 2 * hidden_width), bf16)],
        [((128, block), f32)],
        input_weight,
        output_weight.T,
        up_weight,
        down_weight.T,
        norm_gains,
        shifts,
    )
    sources = source_blocks(width)
    order = lax.optimization_barrier(feature_order(sources, width))
    blocks = block_order(sources, width)
    folds = bias_fold(hidden_width, heads_width)

    def full_rows(rows):
        return nn(lax.all_gather(swap_roles(rows), "c", axis=0, tiled=True), order).astype(bf16)

    rows = full_rows(tokens)
    cot_rows = full_rows(cotangent)

    first_parts, feed_shard, order = lax.optimization_barrier((gather_near(shard), feed_shard, order))

    def collect(parts, *sizes):
        columns = sum(sizes)
        return call(
            collect_kernel,
            [((8 * block, size), bf16) for size in sizes],
            [((8 * block, columns), bf16)],
            me,
            *parts,
            smem=1,
        )

    small = swap_roles(
        jnp.concatenate(
            (head_bias.reshape(-1), hidden_bias, segments[0].astype(bf16))
        )
    )
    bias_rows = small[: 2 * heads_width].reshape(2, heads_width).astype(f32)
    hidden_row = small[2 * heads_width : 2 * heads_width + hidden_width].astype(f32)
    segment_row = small[2 * heads_width + hidden_width :].astype(f32).reshape(1, length)
    ((first_halves,), (rows, segment_row, bias_rows)) = gather_far(
        collect(first_parts, first_end), TURNS[:1], (rows, segment_row, bias_rows)
    )
    feed_parts, cot_rows, blocks = lax.optimization_barrier(
        (gather_near(feed_shard), cot_rows, blocks)
    )
    (up_halves, down_halves), _ = gather_far(
        collect(feed_parts, hidden_width, hidden_width), TURNS[1:]
    )

    def own_half(rows):
        return lax.dynamic_slice_in_dim(rows, core * half, half, axis=0)

    def other_half(rows):
        return lax.dynamic_slice_in_dim(rows, (1 - core) * half, half, axis=0)

    vectors, normed_one, mixed, log_sums, context, attended = call(
        functools.partial(attend_kernel, score_scale),
        [
            ((8, width), f32),
            ((length, width), bf16),
            ((length, 3 * heads_width), bf16),
            ((8, length), f32),
            ((length, heads_width), bf16),
            ((length, width), bf16),
        ],
        [],
        rows,
        *first_halves,
        bias_rows,
        segment_row,
    )
    middle, feed, grad_two, up_keep, up_send, down_keep, down_send, hidden_sums = call(
        feed_kernel,
        [
            ((length, width), f32),
            ((length, width), bf16),
            ((length, width), bf16),
            ((width // 2, hidden_width), bf16),
            ((width // 2, hidden_width), bf16),
            ((width // 2, hidden_width), bf16),
            ((width // 2, hidden_width), bf16),
            ((8, hidden_width), f32),
        ],
        [
            ((length, width), bf16),
            ((width, length), bf16),
            ((width, length), bf16),
            ((width, hidden_width), bf16),
            ((width, hidden_width), bf16),
        ],
        rows,
        attended,
        pair(attended),
        vectors,
        *up_halves,
        *down_halves,
        hidden_row.reshape(1, hidden_width),
        cot_rows,
    )
    down_other = step_along(down_send, TURNS[2][2])
    up_other = step_along(up_send, TURNS[1][2])
    outcome = (
        own_half(middle)
        + own_half(feed).astype(f32)
        + pair(other_half(feed)).astype(f32)
        + vectors[5]
    )
    block_out = inner_cols(outcome.astype(bf16), order).astype(bf16)

    grad_middle, grad_one, *first_grads = call(
        functools.partial(attend_back_kernel, score_scale),
        [
            ((length, width), f32),
            ((length, width), bf16),
        ]
        + [((width // 2, 4 * heads_width // 3), bf16)] * 4
        + [((width // 2, 4 * heads_width // 3 + 128), bf16)] * 2,
        [
            ((length, heads_width), bf16),
            ((length, 3 * heads_width), bf16),
            ((128, width), f32),
            ((1, hidden_width + 2 * heads_width), f32),
        ],
        middle,
        cot_rows,
        grad_two,
        pair(grad_two),
        vectors,
        context,
        mixed,
        log_sums,
        *first_halves,
        segment_row,
        normed_one,
        rows,
        hidden_sums,
        folds,
        blocks,
    )
    down_keep, down_send = half_sums(down_keep, down_other, 1, 2)
    up_keep, up_send = half_sums(up_keep, up_other, 0, 2)
    down_other = step_along(down_send, TURNS[2][1])
    up_other = step_along(up_send, TURNS[1][1])
    grad_one_other = pair(grad_one)
    (token_grad,) = call(
        token_kernel,
        [((half, width), bf16)],
        [((length, width), f32)],
        core.astype(jnp.int32).reshape(1),
        rows,
        grad_one,
        grad_one_other,
        grad_middle,
        vectors,
        order,
        smem=1,
    )
    down_keep, down_send = half_sums(down_keep, down_other, 0, 1)
    up_keep, up_send = half_sums(up_keep, up_other, 0, 1)
    last = [(up_keep, up_send, TURNS[1]), (down_keep, down_send, TURNS[2])]
    pieces = [(first_grads[2 * i], first_grads[2 * i + 1], TURNS[i]) for i in range(3)]
    pieces = [second_turn(*piece) + (piece[2],) for piece in pieces]
    pieces = [(*third_turn(*piece), piece[2]) for piece in pieces]
    operands = []
    for keep, send, turns in pieces + last:
        operands += [keep, step_along(send, turns[0])]
    cross = pair(add_low(operands[4][:, -128:], operands[5][:, -128:]))
    shares = call(
        deal_kernel,
        [((4 * block, pack_width), bf16)] * 2,
        [],
        me,
        cross,
        *operands,
        smem=1,
    )
    *shares, (block_out, token_grad) = scatter_near(*shares, (block_out, token_grad))
    block_out, token_grad = swap_roles(block_out), swap_roles(token_grad)
    six = block // 2
    input_grad, output_grad, up_grad, down_grad, head_grad, hidden_grad, gain_grad, shift_grad = call(
        unpack_kernel,
        [
            ((block, 3, heads_width), f32),
            ((block, heads_width), f32),
            ((block, hidden_width), f32),
            ((block, hidden_width), f32),
            ((2, six), f32),
            ((1, 2 * block), f32),
            ((2, six), f32),
            ((4, six), f32),
        ],
        [],
        lax.axis_index("h").astype(jnp.int32).reshape(1),
        *shares,
        smem=1,
    )
    return (
        block_out,
        token_grad,
        input_grad,
        output_grad.T,
        up_grad,
        down_grad.T,
        head_grad,
        hidden_grad.reshape(2 * block),
        gain_grad,
        shift_grad,
    )


def solution(mesh):
    fine = Mesh(mesh.devices.reshape((2,) * 7), AXES)
    in_specs = (
        P(AXES, None),
        P(AXES, None),
        P(DP, None),
        P(DP, None, "h"),
        P("h", DP),
        P(DP, "h"),
        P("h", DP),
        P(None, "h"),
        P("h"),
        P(None, DP),
        P(None, DP),
    )
    out_specs = (
        P(AXES, None),
        P(AXES, None),
        P(DP, None, "h"),
        P("h", DP),
        P(DP, "h"),
        P("h", DP),
        P(None, ("h",) + DP),
        P(("h",) + DP),
        P(None, AXES),
        P(None, AXES),
    )
    return jax.shard_map(local, mesh=fine, in_specs=in_specs, out_specs=out_specs, check_vma=False)
```

```python
import functools
import itertools
import math

import jax
import jax.numpy as jnp
import numpy as np
from jax import lax
from jax.experimental import pallas as pl
from jax.experimental.pallas import tpu as pltpu
from jax.sharding import Mesh
from jax.sharding import PartitionSpec as P

HEAD_DIM = 64


norm_epsilon = 1e-05
masked_value = -1e30
gelu_factor = 0.7978845608028654


def inner_cols(left_side, right_side):
    return lax.dot_general(
        left_side, right_side, (((1,), (1,)), ((), ())), preferred_element_type=jnp.float32
    )


AXES = ("xh", "xl", "yl", "zh", "zl", "c", "h")
DP = AXES[:6]
RING = {"x": ("xh", "xl"), "y": ("h", "yl"), "z": ("zh", "zl")}
PLACE = {"z": 0, "y": 1, "x": 2}
TURNS = (("x", "y", "z"), ("y", "z", "x"), ("z", "x", "y"))


def swap_roles(values):
    return lax.ppermute(values, ("c", "h"), [(0, 0), (1, 2), (2, 1), (3, 3)])


def pair(values):
    return lax.ppermute(values, "c", [(0, 1), (1, 0)])


def step_along(values, axis):
    high, low = RING[axis]
    order = [name for name in AXES if name in (high, low, "c")]
    moves = []
    for place in itertools.product(range(2), repeat=3):
        target = dict(zip(order, place))
        target[low] ^= 1
        target[high] ^= target["c"]
        moves.append(
            (place[0] * 4 + place[1] * 2 + place[2], sum(target[n] << (2 - i) for i, n in enumerate(order)))
        )
    return lax.ppermute(values, tuple(order), moves)


def cross_roles(values, outward):
    moves = [(0, 1), (1, 3), (2, 0), (3, 2)]
    return lax.ppermute(values, ("c", "h"), moves if outward else [(b, a) for a, b in moves])


def flip(values, place):
    moves = []
    for xh, zh in itertools.product(range(2), repeat=2):
        moves.append((xh * 2 + zh, (xh ^ (place & 1)) * 2 + (zh ^ (place >> 1))))
    return lax.ppermute(values, ("xh", "zh"), moves)


def gather_near(shard):
    own = jnp.concatenate((swap_roles(shard), cross_roles(shard, True)), axis=0)
    return [own] + [flip(own, place) for place in range(1, 4)]


def add_low(left, right):
    return (left.astype(jnp.float32) + right.astype(jnp.float32)).astype(jnp.bfloat16)


def scatter_near(parts, tied):
    others = [flip(part, place) for place, part in enumerate(parts) if place]
    total = parts[0].astype(jnp.float32)
    for other in others:
        total = total + other.astype(jnp.float32)
    total, tied = lax.optimization_barrier((total.astype(jnp.bfloat16), tied))
    rows = total.shape[0] // 2
    return swap_roles(total[:rows]), cross_roles(total[rows:], False), tied


def open_blocks(piece):
    return piece.reshape((1, 1, 1) + piece.shape)


def gather_far(pieces):
    pieces = [open_blocks(piece) for piece in pieces]
    for turn in range(3):
        others = [step_along(piece, TURNS[i][turn]) for i, piece in enumerate(pieces)]
        if turn < 2:
            pieces = [
                jnp.concatenate((piece, other), axis=PLACE[TURNS[i][turn]])
                for i, (piece, other) in enumerate(zip(pieces, others))
            ]
    return [
        [half.reshape(4 * half.shape[3], half.shape[4]) for half in halves]
        for halves in zip(pieces, others)
    ]


def source_blocks(width):
    place = np.arange(width, dtype=np.int32) // (width // 64)
    near, far = place % 8, place // 8
    fixed = ((near >> 1) & 1) * 32 + (near >> 2) * 4 + (near & 1)
    xl = lax.axis_index("xl") ^ (far & 1)
    yl = lax.axis_index("yl") ^ ((far >> 1) & 1)
    zl = lax.axis_index("zl") ^ (far >> 2)
    return lax.optimization_barrier(fixed + xl * 16 + yl * 8 + zl * 2)


def feature_order(sources, width):
    block = width // 64
    inner = np.arange(width, dtype=np.int32) % block
    source = lax.optimization_barrier(sources * block + inner)
    return (lax.broadcasted_iota(jnp.int32, (width, width), 0) == source[None]).astype(jnp.bfloat16)


def block_order(sources, width):
    return (lax.broadcasted_iota(jnp.int32, (width, 64), 1) == sources[:, None]).astype(jnp.bfloat16)


def bias_fold(hidden_width, width):
    many, few = hidden_width // 64, width // 64
    target = np.concatenate(
        (
            np.arange(hidden_width) % many,
            np.arange(width) % few + many,
            np.arange(width) % few + many + few,
        )
    )
    return jnp.asarray(np.arange(128)[None] == target[:, None] + 8, jnp.bfloat16)


def place_rows(rows, me):
    block = rows // 8
    row = lax.broadcasted_iota(jnp.int32, (rows, rows), 0)
    column = lax.broadcasted_iota(jnp.int32, (rows, rows), 1)
    found = jnp.zeros((rows, rows), jnp.float32)
    for k in range(8):
        inside = (row >= k * block) & (row < (k + 1) * block)
        same = column - (me ^ k) * block == row - k * block
        found = jnp.where(inside & same, 1.0, found)
    return found.astype(jnp.bfloat16)


def eye(size):
    row = lax.broadcasted_iota(jnp.int32, (size, size), 0)
    column = lax.broadcasted_iota(jnp.int32, (size, size), 1)
    return (row == column).astype(jnp.float32).astype(jnp.bfloat16)


def pack_kernel(input_ref, output_ref, up_ref, down_ref, gains_ref, shifts_ref, shard_ref, small_ref):
    bf16 = jnp.bfloat16
    block, width = output_ref.shape
    hidden_width = up_ref.shape[1]
    for i in range(3):
        shard_ref[:, i * width : (i + 1) * width] = input_ref[:, i, :]
    shard_ref[:, 3 * width : 4 * width] = output_ref[...]
    small_ref[...] = jnp.zeros_like(small_ref)
    small_ref[0:2] = gains_ref[...].astype(jnp.float32)
    small_ref[2:6] = shifts_ref[...].astype(jnp.float32)
    at = 4 * width + 128
    shard_ref[:, 4 * width : at] = inner_cols(eye(block), small_ref[...].astype(bf16)).astype(bf16)
    shard_ref[:, at : at + hidden_width] = up_ref[...]
    shard_ref[:, at + hidden_width :] = down_ref[...]


def collect_kernel(me_ref, *refs):
    parts, outs, held_ref = refs[:4], refs[4:-1], refs[-1]
    rows = held_ref.shape[0]
    for i, part in enumerate(parts):
        held_ref[i * rows // 4 : (i + 1) * rows // 4] = part[...].astype(jnp.float32)
    moved = place_rows(rows, me_ref[0])
    at = 0
    for out in outs:
        columns = out.shape[1]
        held = held_ref[:, at : at + columns].astype(jnp.bfloat16)
        out[...] = nn(moved, held).astype(jnp.bfloat16)
        at += columns


def deal_kernel(me_ref, cross_ref, *refs):
    parts, outs = refs[:-4], refs[-4:]
    rows = parts[0].shape[0]
    moved = place_rows(rows, me_ref[0])
    at = 0
    for i, (keep, other) in enumerate(zip(parts[::2], parts[1::2])):
        columns = keep.shape[1]
        total = add_low(keep[...], other[...])
        if i == 2:
            lane = lax.broadcasted_iota(jnp.int32, cross_ref.shape, 1)
            cross = jnp.where(lane < 8, cross_ref[...].astype(jnp.float32), 0.0)
            total = jnp.concatenate((total[:, : columns - 128], add_low(total[:, columns - 128 :], cross)), axis=1)
        total = nn(moved, total)
        for i, out in enumerate(outs):
            part = total[i * rows // 4 : (i + 1) * rows // 4]
            out[:, at : at + columns] = part.astype(jnp.bfloat16)
        at += columns


def unpack_kernel(half_ref, *refs):
    parts = refs[:2]
    input_ref, output_ref, up_ref, down_ref, head_ref, hidden_ref, gain_ref, shift_ref = refs[2:]
    f32 = jnp.float32
    block, width = output_ref.shape
    hidden_width = up_ref.shape[1]
    six = block // 2

    def total(start, size):
        columns = slice(start, start + size)
        value = parts[0][:, columns].astype(f32)
        for part in parts[1:]:
            value = value + part[:, columns].astype(f32)
        return value

    def pick(rows, columns, offset):
        row = lax.broadcasted_iota(jnp.int32, (rows, columns), 0)
        column = lax.broadcasted_iota(jnp.int32, (rows, columns), 1)
        return (row == column + offset).astype(f32)

    def exact(left, right, dims):
        return lax.dot_general(
            left, right, (dims, ((), ())), precision=lax.Precision.HIGHEST, preferred_element_type=f32
        )

    for i in range(3):
        input_ref[:, i, :] = total(i * width, width)
    output_ref[...] = total(3 * width, width)
    at = 4 * width + 128
    up_ref[...] = total(at, hidden_width)
    down_ref[...] = total(at + hidden_width, hidden_width)
    small = total(4 * width, 128)
    norm_terms = exact(small, pick(block, six, half_ref[0] * six), ((0,), (0,)))
    gain_ref[...] = norm_terms[0:2]
    shift_ref[...] = norm_terms[2:6]
    hidden_ref[...] = exact(small[0:1], pick(128, 2 * block, 8), ((1,), (0,)))
    head_ref[0:1] = exact(small[0:1], pick(128, six, 8 + 2 * block), ((1,), (0,)))
    head_ref[1:2] = exact(small[0:1], pick(128, six, 8 + 2 * block + six), ((1,), (0,)))


def half_sums(keep, other, place, places):
    rows, columns = keep.shape
    shape = (2,) * places + (rows >> places, columns)
    keep, other = keep.reshape(shape), other.reshape(shape)
    return [
        add_low(
            lax.slice_in_dim(keep, i, i + 1, axis=place), lax.slice_in_dim(other, i, i + 1, axis=place)
        ).reshape(rows // 2, columns)
        for i in range(2)
    ]


def second_turn(keep, send, turns):
    place = sorted(turns[:2], key=PLACE.get).index(turns[1])
    return tuple(half_sums(keep, step_along(send, turns[2]), place, 2))


def third_turn(keep, send, turns):
    return half_sums(keep, step_along(send, turns[1]), 0, 1)


def column_norm(values):
    mean_val = jnp.mean(values, axis=-1, keepdims=True)
    centered = values - mean_val
    variance = jnp.mean(centered * centered, axis=-1, keepdims=True)
    inverse = lax.rsqrt(variance + norm_epsilon)
    return centered * inverse, inverse


def nn(left, right):
    return jnp.dot(left, right, preferred_element_type=jnp.float32)


def key_mask(segment_row, keys, first, queries):
    column = jnp.transpose(jnp.broadcast_to(segment_row, (8, segment_row.shape[1])))[:keys, :1]
    row = segment_row[:, first : first + queries]
    key_pos = lax.broadcasted_iota(jnp.int32, (keys, queries), 0)
    query_pos = lax.broadcasted_iota(jnp.int32, (keys, queries), 1) + first
    return jnp.where((column == row) & (key_pos <= query_pos), 0.0, masked_value)


def lane_half(values, which):
    lane = lax.broadcasted_iota(jnp.int32, values.shape, 1)
    inside = (lane >= HEAD_DIM) if which else (lane < HEAD_DIM)
    return jnp.where(inside, values, jnp.zeros_like(values))


def attend_kernel(
    score_scale,
    rows_ref,
    low_ref,
    high_ref,
    bias_ref,
    segment_ref,
    vector_ref,
    normed_ref,
    mixed_ref,
    log_ref,
    context_ref,
    attended_ref,
):
    bf16 = jnp.bfloat16
    length = rows_ref.shape[0]
    width = context_ref.shape[1]
    rows = low_ref.shape[0]
    for at, part_ref in ((0, low_ref), (rows, high_ref)):
        turned = jnp.transpose(part_ref[:, 4 * width : 4 * width + 128].astype(jnp.float32))
        vector_ref[:, at : at + rows] = turned[:8]
    half = length // 2
    unit, _ = column_norm(rows_ref[...].astype(jnp.float32))
    normed_ref[...] = (unit * vector_ref[0:1] + vector_ref[2:3]).astype(bf16)
    mixed = nn(normed_ref[:, :rows], low_ref[:, : 3 * width]) + nn(
        normed_ref[:, rows:], high_ref[:, : 3 * width]
    )
    mixed_ref[:, :width] = (mixed[:, :width] + bias_ref[0:1]).astype(bf16)
    mixed_ref[:, width : 2 * width] = mixed[:, width : 2 * width].astype(bf16)
    mixed_ref[:, 2 * width :] = (mixed[:, 2 * width :] + bias_ref[1:2]).astype(bf16)
    segment_row = segment_ref[...]
    spans = ((0, half, key_mask(segment_row, half, 0, half)), (half, length, key_mask(segment_row, length, half, half)))
    log_ref[...] = jnp.zeros_like(log_ref)
    for two in range(width // 128):
        at = 128 * two
        query_two = mixed_ref[:, at : at + 128] * jnp.asarray(score_scale, bf16)
        key_two = mixed_ref[:, width + at : width + at + 128]
        value_turned = jnp.transpose(mixed_ref[:, 2 * width + at : 2 * width + at + 128])
        parts = []
        for which in range(2):
            query_rows = lane_half(query_two, which)
            value_rows = value_turned[HEAD_DIM * which : HEAD_DIM * (which + 1)]
            sides = []
            for first, keys, mask in spans:
                scores = inner_cols(key_two[:keys], query_rows[first : first + half]) + mask
                top = jnp.max(scores, axis=0, keepdims=True)
                exponent = jnp.exp(scores - top)
                total = jnp.sum(exponent, axis=0, keepdims=True)
                log_ref[2 * two + which : 2 * two + which + 1, first : first + half] = top + jnp.log(total)
                sides.append(nn(value_rows[:, :keys], exponent.astype(bf16)) / total)
            parts.append(jnp.concatenate(sides, axis=1))
        context_ref[:, at : at + 128] = jnp.transpose(jnp.concatenate(parts, axis=0)).astype(bf16)
    for at, part_ref in ((0, low_ref), (rows, high_ref)):
        attended_ref[:, at : at + rows] = inner_cols(
            context_ref[...], part_ref[:, 3 * width : 4 * width]
        ).astype(bf16)


def store_blocks(value, place, keep_ref, send_ref, columns):
    rows = value.shape[0] // 8
    counts = [0, 0]
    for block in range(8):
        which = (block >> (2 - place)) & 1
        target = send_ref if which else keep_ref
        at = counts[which] * rows
        counts[which] += 1
        target[at : at + rows, columns] = value[block * rows : (block + 1) * rows].astype(target.dtype)


def join_blocks(place, keep_ref, other_ref, whole_ref):
    rows = whole_ref.shape[0] // 8
    counts = [0, 0]
    for block in range(8):
        which = (block >> (2 - place)) & 1
        at = counts[which] * rows
        counts[which] += 1
        source = other_ref if which else keep_ref
        whole_ref[block * rows : (block + 1) * rows] = source[at : at + rows]


def feed_kernel(
    rows_ref,
    own_ref,
    other_ref,
    vector_ref,
    up_mine_ref,
    up_other_ref,
    down_mine_ref,
    down_other_ref,
    bias_ref,
    cot_ref,
    middle_ref,
    feed_ref,
    grad_two_ref,
    up_keep_ref,
    up_send_ref,
    down_keep_ref,
    down_send_ref,
    bias_grad_ref,
    normed_ref,
    normed_turned_ref,
    cot_turned_ref,
    up_ref,
    down_ref,
    feed_sum_ref,
    grad_two_sum_ref,
):
    bf16, f32 = jnp.bfloat16, jnp.float32

    @pl.when(pl.program_id(0) == 0)
    def _():
        middle = (
            rows_ref[...].astype(f32)
            + (own_ref[...].astype(f32) + other_ref[...].astype(f32))
            + vector_ref[4:5]
        )
        middle_ref[...] = middle
        unit, _ = column_norm(middle)
        normed_ref[...] = (unit * vector_ref[1:2] + vector_ref[3:4]).astype(bf16)
        normed_turned_ref[...] = jnp.transpose(normed_ref[...])
        cot_turned_ref[...] = jnp.transpose(cot_ref[...])
        feed_sum_ref[...] = jnp.zeros_like(feed_sum_ref)
        grad_two_sum_ref[...] = jnp.zeros_like(grad_two_sum_ref)

    join_blocks(PLACE[TURNS[1][2]], up_mine_ref, up_other_ref, up_ref)
    join_blocks(PLACE[TURNS[2][2]], down_mine_ref, down_other_ref, down_ref)
    before = nn(normed_ref[...], up_ref[...]) + bias_ref[...]
    square = before * before
    bend = jnp.tanh(gelu_factor * (before + 0.044715 * before * square))
    opened = 0.5 * (1.0 + bend)
    hidden = (before * opened).astype(bf16)
    slope = opened + 0.5 * before * (1.0 - bend * bend) * (
        gelu_factor * (1.0 + 3.0 * 0.044715 * square)
    )
    grad_before = (nn(cot_ref[...], down_ref[...]) * slope).astype(bf16)
    feed_sum_ref[...] += inner_cols(hidden, down_ref[...])
    grad_two_sum_ref[...] += inner_cols(grad_before, up_ref[...])
    bias_grad_ref[...] = jnp.broadcast_to(
        jnp.sum(grad_before.astype(f32), axis=0, keepdims=True), bias_grad_ref.shape
    )
    columns = slice(0, up_ref.shape[1])
    store_blocks(nn(cot_turned_ref[...], hidden), PLACE[TURNS[2][2]], down_keep_ref, down_send_ref, columns)
    store_blocks(nn(normed_turned_ref[...], grad_before), PLACE[TURNS[1][2]], up_keep_ref, up_send_ref, columns)

    @pl.when(pl.program_id(0) == pl.num_programs(0) - 1)
    def _():
        feed_ref[...] = feed_sum_ref[...].astype(bf16)
        grad_two_ref[...] = grad_two_sum_ref[...].astype(bf16)


def attend_back_kernel(
    score_scale,
    middle_ref,
    cot_ref,
    own_ref,
    other_ref,
    vector_ref,
    context_ref,
    mixed_ref,
    log_ref,
    low_ref,
    high_ref,
    segment_ref,
    normed_ref,
    rows_ref,
    hidden_sums_ref,
    fold_ref,
    block_ref,
    grad_middle_ref,
    grad_one_ref,
    keep_a_ref,
    send_a_ref,
    keep_b_ref,
    send_b_ref,
    keep_c_ref,
    send_c_ref,
    grad_context_ref,
    grad_mixed_ref,
    terms_ref,
    bias_ref,
):
    bf16, f32 = jnp.bfloat16, jnp.float32
    length = middle_ref.shape[0]
    width = context_ref.shape[1]
    rows = low_ref.shape[0]
    half = length // 2
    unit, inverse = column_norm(middle_ref[...])
    grad_norm = own_ref[...].astype(f32) + other_ref[...].astype(f32)
    scaled = grad_norm * vector_ref[1:2]
    mean_grad = jnp.mean(scaled, axis=-1, keepdims=True)
    mean_cross = jnp.mean(scaled * unit, axis=-1, keepdims=True)
    cot = cot_ref[...].astype(f32)
    grad_middle = cot + inverse * (scaled - mean_grad - unit * mean_cross)
    grad_middle_ref[...] = grad_middle
    terms_ref[...] = jnp.zeros_like(terms_ref)
    terms_ref[1:2] = 0.5 * jnp.sum(grad_norm * unit, axis=0, keepdims=True)
    terms_ref[3:4] = 0.5 * jnp.sum(grad_norm, axis=0, keepdims=True)
    terms_ref[4:5] = 0.5 * jnp.sum(grad_middle, axis=0, keepdims=True)
    terms_ref[5:6] = 0.5 * jnp.sum(cot, axis=0, keepdims=True)
    hidden_width = hidden_sums_ref.shape[1]
    bias_ref[:, :hidden_width] = hidden_sums_ref[0:1]
    middle_rows = grad_middle.astype(bf16)
    third = keep_a_ref.shape[1]
    last = keep_c_ref.shape[1]
    store_blocks(
        nn(jnp.transpose(middle_rows), context_ref[...]),
        PLACE[TURNS[2][2]],
        keep_c_ref,
        send_c_ref,
        slice(third - width, third),
    )
    grad_context_ref[...] = (
        nn(middle_rows[:, :rows], low_ref[:, 3 * width : 4 * width])
        + nn(middle_rows[:, rows:], high_ref[:, 3 * width : 4 * width])
    ).astype(bf16)
    segment_row = segment_ref[...]
    spans = ((0, half, key_mask(segment_row, half, 0, half)), (half, length, key_mask(segment_row, length, half, half)))
    for two in range(width // 128):
        at = 128 * two
        query_two = mixed_ref[:, at : at + 128] * jnp.asarray(score_scale, bf16)
        key_two = mixed_ref[:, width + at : width + at + 128]
        value_two = mixed_ref[:, 2 * width + at : 2 * width + at + 128]
        grad_two = grad_context_ref[:, at : at + 128]
        key_turned = jnp.transpose(key_two)
        grad_queries = []
        grad_keys = [0.0, 0.0]
        grad_values = [0.0, 0.0]
        for which in range(2):
            query_rows = lane_half(query_two, which)
            grad_rows = lane_half(grad_two, which)
            key_rows = key_turned[HEAD_DIM * which : HEAD_DIM * (which + 1)]
            sides = []
            for side, (first, keys, mask) in enumerate(spans):
                query_side = query_rows[first : first + half]
                grad_side = grad_rows[first : first + half]
                log_side = log_ref[2 * two + which : 2 * two + which + 1, first : first + half]
                scores = inner_cols(key_two[:keys], query_side) + mask
                soft = jnp.exp(scores - log_side)
                grad_soft = inner_cols(value_two[:keys], grad_side)
                crossed = soft * grad_soft
                grad_scores = (
                    crossed - soft * jnp.sum(crossed, axis=0, keepdims=True)
                ).astype(bf16)
                grad_keys[side] += nn(grad_scores, query_side)
                grad_values[side] += nn(soft.astype(bf16), grad_side)
                sides.append(nn(key_rows[:, :keys], grad_scores))
            grad_queries.append(jnp.concatenate(sides, axis=1))
        queries_out = jnp.transpose(jnp.concatenate(grad_queries, axis=0)) * score_scale
        for place, value in enumerate((queries_out, grad_keys, grad_values)):
            columns = slice(place * width + at, place * width + at + 128)
            if place == 0:
                grad_mixed_ref[:, columns] = value.astype(bf16)
            else:
                grad_mixed_ref[:half, columns] = (value[0] + value[1][:half]).astype(bf16)
                grad_mixed_ref[half:, columns] = value[1][half:].astype(bf16)
            if place != 1:
                start = hidden_width + (place // 2) * width + at
                bias_ref[:, start : start + 128] = jnp.sum(
                    grad_mixed_ref[:, columns].astype(f32), axis=0, keepdims=True
                )
    unit, _ = column_norm(rows_ref[...].astype(f32))
    for at, part_ref in ((0, low_ref), (rows, high_ref)):
        columns = slice(at, at + rows)
        grad_one = inner_cols(grad_mixed_ref[...], part_ref[:, : 3 * width])
        grad_one_ref[:, columns] = grad_one.astype(bf16)
        terms_ref[0:1, columns] = jnp.sum(grad_one * unit[:, columns], axis=0, keepdims=True)
        terms_ref[2:3, columns] = jnp.sum(grad_one, axis=0, keepdims=True)
    row = lax.broadcasted_iota(jnp.int32, (64, bias_ref.shape[1]), 0)
    lane = lax.broadcasted_iota(jnp.int32, (64, bias_ref.shape[1]), 1)
    inside = jnp.zeros(row.shape, jnp.bool_)
    for start, size in ((0, hidden_width), (hidden_width, width), (hidden_width + width, width)):
        first = row * (size // 64) + start
        inside = inside | ((lane >= first) & (lane < first + size // 64))
    spread = jnp.where(inside, bias_ref[...], 0.0)
    for matrix_ref in (fold_ref, block_ref):
        high = spread.astype(bf16)
        rest = (spread - high.astype(f32)).astype(bf16)
        if matrix_ref is fold_ref:
            spread = nn(high, matrix_ref[...]) + nn(rest, matrix_ref[...])
        else:
            spread = nn(matrix_ref[...], high) + nn(matrix_ref[...], rest)
    store_blocks(
        jnp.transpose(terms_ref[...]) + spread,
        PLACE[TURNS[2][2]],
        keep_c_ref,
        send_c_ref,
        slice(third, last),
    )
    turned = jnp.transpose(normed_ref[...])
    targets = ((keep_a_ref, send_a_ref), (keep_b_ref, send_b_ref), (keep_c_ref, send_c_ref))
    for i, (keep_ref, send_ref) in enumerate(targets):
        size = min(third, 3 * width - i * third)
        store_blocks(
            nn(turned, grad_mixed_ref[:, i * third : i * third + size]),
            PLACE[TURNS[i][2]],
            keep_ref,
            send_ref,
            slice(0, size),
        )


def token_kernel(
    core_ref,
    rows_ref,
    own_ref,
    other_ref,
    grad_middle_ref,
    vector_ref,
    order_ref,
    token_ref,
    token_full_ref,
):
    bf16, f32 = jnp.bfloat16, jnp.float32
    half = token_ref.shape[0]
    unit, inverse = column_norm(rows_ref[...].astype(f32))
    grad_norm = own_ref[...].astype(f32) + other_ref[...].astype(f32)
    scaled = grad_norm * vector_ref[0:1]
    mean_grad = jnp.mean(scaled, axis=-1, keepdims=True)
    mean_cross = jnp.mean(scaled * unit, axis=-1, keepdims=True)
    token_full_ref[...] = (
        grad_middle_ref[...] + inverse * (scaled - mean_grad - unit * mean_cross)
    )
    start = pl.multiple_of(core_ref[0] * half, half)
    token_rows = token_full_ref[pl.ds(start, half), :].astype(bf16)
    token_ref[...] = inner_cols(token_rows, order_ref[...]).astype(bf16)


def call(kernel, outs, scratch, *operands, smem=0):
    space = [pl.BlockSpec(memory_space=pltpu.SMEM)] * smem
    space += [pl.BlockSpec(memory_space=pltpu.VMEM)] * (len(operands) - smem)
    return pl.pallas_call(
        kernel,
        out_shape=[jax.ShapeDtypeStruct(shape, kind) for shape, kind in outs],
        in_specs=space,
        out_specs=[pl.BlockSpec(memory_space=pltpu.VMEM)] * len(outs),
        scratch_shapes=[pltpu.VMEM(shape, kind) for shape, kind in scratch],
        compiler_params=pltpu.CompilerParams(vmem_limit_bytes=56 * 1024 * 1024),
    )(*operands)


def local(
    tokens,
    cotangent,
    segments,
    input_weight,
    output_weight,
    up_weight,
    down_weight,
    head_bias,
    hidden_bias,
    norm_gains,
    shifts,
):
    bf16, f32 = jnp.bfloat16, jnp.float32
    half, width = tokens.shape
    length = segments.shape[1]
    block = input_weight.shape[0]
    heads_width = input_weight.shape[2]
    hidden_width = up_weight.shape[1]
    local_heads = heads_width // HEAD_DIM
    score_scale = 1.0 / math.sqrt(HEAD_DIM)
    core = lax.axis_index("c")

    first_end = 4 * heads_width + 128
    pack_width = first_end + 2 * hidden_width
    me = (
        (lax.axis_index("zh") * 4 + lax.axis_index("xh") * 2 + lax.axis_index("h"))
        .astype(jnp.int32)
        .reshape(1)
    )
    (shard,) = call(
        pack_kernel,
        [((block, pack_width), bf16)],
        [((128, block), f32)],
        input_weight,
        output_weight.T,
        up_weight,
        down_weight.T,
        norm_gains,
        shifts,
    )
    sources = source_blocks(width)
    order = lax.optimization_barrier(feature_order(sources, width))
    blocks = block_order(sources, width)
    folds = bias_fold(hidden_width, heads_width)

    def full_rows(rows):
        return nn(lax.all_gather(swap_roles(rows), "c", axis=0, tiled=True), order).astype(bf16)

    rows = full_rows(tokens)
    cot_rows = full_rows(cotangent)

    parts, order, blocks, folds, rows, cot_rows = lax.optimization_barrier(
        (gather_near(shard), order, blocks, folds, rows, cot_rows)
    )
    near = call(
        collect_kernel,
        [((8 * block, size), bf16) for size in (first_end, hidden_width, hidden_width)],
        [((8 * block, pack_width), f32)],
        me,
        *parts,
        smem=1,
    )
    small = swap_roles(
        jnp.concatenate(
            (head_bias.reshape(-1), hidden_bias, segments[0].astype(bf16))
        )
    )
    bias_rows = small[: 2 * heads_width].reshape(2, heads_width).astype(f32)
    hidden_row = small[2 * heads_width : 2 * heads_width + hidden_width].astype(f32)
    segment_row = small[2 * heads_width + hidden_width :].astype(f32).reshape(1, length)
    first_halves, up_halves, down_halves = gather_far(near)

    def own_half(rows):
        return lax.dynamic_slice_in_dim(rows, core * half, half, axis=0)

    def other_half(rows):
        return lax.dynamic_slice_in_dim(rows, (1 - core) * half, half, axis=0)

    vectors, normed_one, mixed, log_sums, context, attended = call(
        functools.partial(attend_kernel, score_scale),
        [
            ((8, width), f32),
            ((length, width), bf16),
            ((length, 3 * heads_width), bf16),
            ((8, length), f32),
            ((length, heads_width), bf16),
            ((length, width), bf16),
        ],
        [],
        rows,
        *first_halves,
        bias_rows,
        segment_row,
    )
    third = hidden_width // 3

    def whole(*shape):
        return pl.BlockSpec(shape, lambda j: (0, 0))

    def cut(rows_of):
        return pl.BlockSpec((rows_of, third), lambda j: (0, j))

    def kept(shape, kind):
        return jax.ShapeDtypeStruct(shape, kind)

    middle, feed, grad_two, up_keep, up_send, down_keep, down_send, hidden_sums = pl.pallas_call(
        feed_kernel,
        grid=(3,),
        out_shape=[
            kept((length, width), f32),
            kept((length, width), bf16),
            kept((length, width), bf16),
        ]
        + [kept((width // 2, hidden_width), bf16)] * 4
        + [kept((8, hidden_width), f32)],
        in_specs=[whole(length, width)] * 3
        + [whole(8, width)]
        + [cut(width // 2)] * 4
        + [cut(1), whole(length, width)],
        out_specs=[whole(length, width)] * 3 + [cut(width // 2)] * 4 + [cut(8)],
        scratch_shapes=[
            pltpu.VMEM((length, width), bf16),
            pltpu.VMEM((width, length), bf16),
            pltpu.VMEM((width, length), bf16),
            pltpu.VMEM((width, third), bf16),
            pltpu.VMEM((width, third), bf16),
            pltpu.VMEM((length, width), f32),
            pltpu.VMEM((length, width), f32),
        ],
        compiler_params=pltpu.CompilerParams(vmem_limit_bytes=56 * 1024 * 1024),
    )(
        rows,
        attended,
        pair(attended),
        vectors,
        *up_halves,
        *down_halves,
        hidden_row.reshape(1, hidden_width),
        cot_rows,
    )
    down_other = step_along(down_send, TURNS[2][2])
    up_other = step_along(up_send, TURNS[1][2])
    outcome = (
        own_half(middle)
        + own_half(feed).astype(f32)
        + pair(other_half(feed)).astype(f32)
        + vectors[5]
    )
    block_out = inner_cols(outcome.astype(bf16), order).astype(bf16)

    grad_middle, grad_one, *first_grads = call(
        functools.partial(attend_back_kernel, score_scale),
        [
            ((length, width), f32),
            ((length, width), bf16),
        ]
        + [((width // 2, 4 * heads_width // 3), bf16)] * 4
        + [((width // 2, 4 * heads_width // 3 + 128), bf16)] * 2,
        [
            ((length, heads_width), bf16),
            ((length, 3 * heads_width), bf16),
            ((128, width), f32),
            ((1, hidden_width + 2 * heads_width), f32),
        ],
        middle,
        cot_rows,
        grad_two,
        pair(grad_two),
        vectors,
        context,
        mixed,
        log_sums,
        *first_halves,
        segment_row,
        normed_one,
        rows,
        hidden_sums,
        folds,
        blocks,
    )
    down_keep, down_send = half_sums(down_keep, down_other, 1, 2)
    up_keep, up_send = half_sums(up_keep, up_other, 0, 2)
    down_other = step_along(down_send, TURNS[2][1])
    up_other = step_along(up_send, TURNS[1][1])
    grad_one_other = pair(grad_one)
    (token_grad,) = call(
        token_kernel,
        [((half, width), bf16)],
        [((length, width), f32)],
        core.astype(jnp.int32).reshape(1),
        rows,
        grad_one,
        grad_one_other,
        grad_middle,
        vectors,
        order,
        smem=1,
    )
    down_keep, down_send = half_sums(down_keep, down_other, 0, 1)
    up_keep, up_send = half_sums(up_keep, up_other, 0, 1)
    last = [(up_keep, up_send, TURNS[1]), (down_keep, down_send, TURNS[2])]
    pieces = [(first_grads[2 * i], first_grads[2 * i + 1], TURNS[i]) for i in range(3)]
    pieces = [second_turn(*piece) + (piece[2],) for piece in pieces]
    pieces = [(*third_turn(*piece), piece[2]) for piece in pieces]
    operands = []
    for keep, send, turns in pieces + last:
        operands += [keep, step_along(send, turns[0])]
    cross = pair(add_low(operands[4][:, -128:], operands[5][:, -128:]))
    shares = call(
        deal_kernel,
        [((2 * block, pack_width), bf16)] * 4,
        [],
        me,
        cross,
        *operands,
        smem=1,
    )
    *shares, (block_out, token_grad) = scatter_near(shares, (block_out, token_grad))
    block_out, token_grad = swap_roles(block_out), swap_roles(token_grad)
    six = block // 2
    input_grad, output_grad, up_grad, down_grad, head_grad, hidden_grad, gain_grad, shift_grad = call(
        unpack_kernel,
        [
            ((block, 3, heads_width), f32),
            ((block, heads_width), f32),
            ((block, hidden_width), f32),
            ((block, hidden_width), f32),
            ((2, six), f32),
            ((1, 2 * block), f32),
            ((2, six), f32),
            ((4, six), f32),
        ],
        [],
        lax.axis_index("h").astype(jnp.int32).reshape(1),
        *shares,
        smem=1,
    )
    return (
        block_out,
        token_grad,
        input_grad,
        output_grad.T,
        up_grad,
        down_grad.T,
        head_grad,
        hidden_grad.reshape(2 * block),
        gain_grad,
        shift_grad,
    )


def solution(mesh):
    fine = Mesh(mesh.devices.reshape((2,) * 7), AXES)
    in_specs = (
        P(AXES, None),
        P(AXES, None),
        P(DP, None),
        P(DP, None, "h"),
        P("h", DP),
        P(DP, "h"),
        P("h", DP),
        P(None, "h"),
        P("h"),
        P(None, DP),
        P(None, DP),
    )
    out_specs = (
        P(AXES, None),
        P(AXES, None),
        P(DP, None, "h"),
        P("h", DP),
        P(DP, "h"),
        P("h", DP),
        P(None, ("h",) + DP),
        P(("h",) + DP),
        P(None, AXES),
        P(None, AXES),
    )
    return jax.shard_map(local, mesh=fine, in_specs=in_specs, out_specs=out_specs, check_vma=False)
```

```python
import functools
import itertools
import math

import jax
import jax.numpy as jnp
import numpy as np
from jax import lax
from jax.experimental import pallas as pl
from jax.experimental.pallas import tpu as pltpu
from jax.sharding import Mesh
from jax.sharding import PartitionSpec as P

HEAD_DIM = 64


norm_epsilon = 1e-05
masked_value = -1e30
gelu_factor = 0.7978845608028654


def inner_cols(left_side, right_side):
    return lax.dot_general(
        left_side, right_side, (((1,), (1,)), ((), ())), preferred_element_type=jnp.float32
    )


AXES = ("xh", "xl", "yl", "zh", "zl", "c", "h")
DP = AXES[:6]
RING = {"x": ("xh", "xl"), "y": ("h", "yl"), "z": ("zh", "zl")}
PLACE = {"z": 0, "y": 1, "x": 2}
TURNS = (("x", "y", "z"), ("y", "z", "x"), ("z", "x", "y"))


def swap_roles(values):
    return lax.ppermute(values, ("c", "h"), [(0, 0), (1, 2), (2, 1), (3, 3)])


def pair(values):
    return lax.ppermute(values, "c", [(0, 1), (1, 0)])


def step_along(values, axis):
    high, low = RING[axis]
    order = [name for name in AXES if name in (high, low, "c")]
    moves = []
    for place in itertools.product(range(2), repeat=3):
        target = dict(zip(order, place))
        target[low] ^= 1
        target[high] ^= target["c"]
        moves.append(
            (place[0] * 4 + place[1] * 2 + place[2], sum(target[n] << (2 - i) for i, n in enumerate(order)))
        )
    return lax.ppermute(values, tuple(order), moves)


def cross_roles(values, outward):
    moves = [(0, 1), (1, 3), (2, 0), (3, 2)]
    return lax.ppermute(values, ("c", "h"), moves if outward else [(b, a) for a, b in moves])


def flip(values, place):
    moves = []
    for xh, zh in itertools.product(range(2), repeat=2):
        moves.append((xh * 2 + zh, (xh ^ (place & 1)) * 2 + (zh ^ (place >> 1))))
    return lax.ppermute(values, ("xh", "zh"), moves)


def gather_near(shard):
    own = jnp.concatenate((swap_roles(shard), cross_roles(shard, True)), axis=0)
    return [own] + [flip(own, place) for place in range(1, 4)]


def add_low(left, right):
    return (left.astype(jnp.float32) + right.astype(jnp.float32)).astype(jnp.bfloat16)


def scatter_near(parts):
    others = [flip(part, place) for place, part in enumerate(parts) if place]
    total = parts[0].astype(jnp.float32)
    for other in others:
        total = total + other.astype(jnp.float32)
    total = total.astype(jnp.bfloat16)
    rows = total.shape[0] // 2
    return swap_roles(total[:rows]), cross_roles(total[rows:], False)


def open_blocks(piece):
    return piece.reshape((1, 1, 1) + piece.shape)


def gather_far(pieces):
    pieces = [open_blocks(piece) for piece in pieces]
    for turn in range(3):
        others = [step_along(piece, TURNS[i][turn]) for i, piece in enumerate(pieces)]
        if turn < 2:
            pieces = [
                jnp.concatenate((piece, other), axis=PLACE[TURNS[i][turn]])
                for i, (piece, other) in enumerate(zip(pieces, others))
            ]
    return [
        [half.reshape(4 * half.shape[3], half.shape[4]) for half in halves]
        for halves in zip(pieces, others)
    ]


def source_blocks(width):
    place = np.arange(width, dtype=np.int32) // (width // 64)
    near, far = place % 8, place // 8
    fixed = ((near >> 1) & 1) * 32 + (near >> 2) * 4 + (near & 1)
    xl = lax.axis_index("xl") ^ (far & 1)
    yl = lax.axis_index("yl") ^ ((far >> 1) & 1)
    zl = lax.axis_index("zl") ^ (far >> 2)
    return lax.optimization_barrier(fixed + xl * 16 + yl * 8 + zl * 2)


def feature_order(sources, width):
    block = width // 64
    inner = np.arange(width, dtype=np.int32) % block
    source = lax.optimization_barrier(sources * block + inner)
    return (lax.broadcasted_iota(jnp.int32, (width, width), 0) == source[None]).astype(jnp.bfloat16)


def block_order(sources, width):
    return (lax.broadcasted_iota(jnp.int32, (width, 64), 1) == sources[:, None]).astype(jnp.bfloat16)


def bias_fold(hidden_width, width):
    many, few = hidden_width // 64, width // 64
    target = np.concatenate(
        (
            np.arange(hidden_width) % many,
            np.arange(width) % few + many,
            np.arange(width) % few + many + few,
        )
    )
    return jnp.asarray(np.arange(128)[None] == target[:, None] + 8, jnp.bfloat16)


def place_rows(rows, me):
    block = rows // 8
    row = lax.broadcasted_iota(jnp.int32, (rows, rows), 0)
    column = lax.broadcasted_iota(jnp.int32, (rows, rows), 1)
    found = jnp.zeros((rows, rows), jnp.float32)
    for k in range(8):
        inside = (row >= k * block) & (row < (k + 1) * block)
        same = column - (me ^ k) * block == row - k * block
        found = jnp.where(inside & same, 1.0, found)
    return found.astype(jnp.bfloat16)


def eye(size):
    row = lax.broadcasted_iota(jnp.int32, (size, size), 0)
    column = lax.broadcasted_iota(jnp.int32, (size, size), 1)
    return (row == column).astype(jnp.float32).astype(jnp.bfloat16)


def pack_kernel(input_ref, output_ref, up_ref, down_ref, gains_ref, shifts_ref, shard_ref, small_ref):
    bf16 = jnp.bfloat16
    block, width = output_ref.shape
    hidden_width = up_ref.shape[1]
    for i in range(3):
        shard_ref[:, i * width : (i + 1) * width] = input_ref[:, i, :]
    shard_ref[:, 3 * width : 4 * width] = output_ref[...]
    small_ref[...] = jnp.zeros_like(small_ref)
    small_ref[0:2] = gains_ref[...].astype(jnp.float32)
    small_ref[2:6] = shifts_ref[...].astype(jnp.float32)
    at = 4 * width + 128
    shard_ref[:, 4 * width : at] = inner_cols(eye(block), small_ref[...].astype(bf16)).astype(bf16)
    shard_ref[:, at : at + hidden_width] = up_ref[...]
    shard_ref[:, at + hidden_width :] = down_ref[...]


def collect_kernel(me_ref, *refs):
    parts, outs, held_ref = refs[:4], refs[4:-1], refs[-1]
    rows = held_ref.shape[0]
    for i, part in enumerate(parts):
        held_ref[i * rows // 4 : (i + 1) * rows // 4] = part[...].astype(jnp.float32)
    moved = place_rows(rows, me_ref[0])
    at = 0
    for out in outs:
        columns = out.shape[1]
        held = held_ref[:, at : at + columns].astype(jnp.bfloat16)
        out[...] = nn(moved, held).astype(jnp.bfloat16)
        at += columns


def deal_kernel(me_ref, cross_ref, *refs):
    parts, outs = refs[:-4], refs[-4:]
    rows = parts[0].shape[0]
    moved = place_rows(rows, me_ref[0])
    at = 0
    for i, (keep, other) in enumerate(zip(parts[::2], parts[1::2])):
        columns = keep.shape[1]
        total = add_low(keep[...], other[...])
        if i == 2:
            lane = lax.broadcasted_iota(jnp.int32, cross_ref.shape, 1)
            cross = jnp.where(lane < 8, cross_ref[...].astype(jnp.float32), 0.0)
            total = jnp.concatenate((total[:, : columns - 128], add_low(total[:, columns - 128 :], cross)), axis=1)
        total = nn(moved, total)
        for i, out in enumerate(outs):
            part = total[i * rows // 4 : (i + 1) * rows // 4]
            out[:, at : at + columns] = part.astype(jnp.bfloat16)
        at += columns


def unpack_kernel(half_ref, *refs):
    parts = refs[:2]
    input_ref, output_ref, up_ref, down_ref, head_ref, hidden_ref, gain_ref, shift_ref = refs[2:]
    f32 = jnp.float32
    block, width = output_ref.shape
    hidden_width = up_ref.shape[1]
    six = block // 2

    def total(start, size):
        columns = slice(start, start + size)
        value = parts[0][:, columns].astype(f32)
        for part in parts[1:]:
            value = value + part[:, columns].astype(f32)
        return value

    def pick(rows, columns, offset):
        row = lax.broadcasted_iota(jnp.int32, (rows, columns), 0)
        column = lax.broadcasted_iota(jnp.int32, (rows, columns), 1)
        return (row == column + offset).astype(f32)

    def exact(left, right, dims):
        return lax.dot_general(
            left, right, (dims, ((), ())), precision=lax.Precision.HIGHEST, preferred_element_type=f32
        )

    for i in range(3):
        input_ref[:, i, :] = total(i * width, width)
    output_ref[...] = total(3 * width, width)
    at = 4 * width + 128
    up_ref[...] = total(at, hidden_width)
    down_ref[...] = total(at + hidden_width, hidden_width)
    small = total(4 * width, 128)
    norm_terms = exact(small, pick(block, six, half_ref[0] * six), ((0,), (0,)))
    gain_ref[...] = norm_terms[0:2]
    shift_ref[...] = norm_terms[2:6]
    hidden_ref[...] = exact(small[0:1], pick(128, 2 * block, 8), ((1,), (0,)))
    head_ref[0:1] = exact(small[0:1], pick(128, six, 8 + 2 * block), ((1,), (0,)))
    head_ref[1:2] = exact(small[0:1], pick(128, six, 8 + 2 * block + six), ((1,), (0,)))


def half_sums(keep, other, place, places):
    rows, columns = keep.shape
    shape = (2,) * places + (rows >> places, columns)
    keep, other = keep.reshape(shape), other.reshape(shape)
    return [
        add_low(
            lax.slice_in_dim(keep, i, i + 1, axis=place), lax.slice_in_dim(other, i, i + 1, axis=place)
        ).reshape(rows // 2, columns)
        for i in range(2)
    ]


def column_norm(values):
    mean_val = jnp.mean(values, axis=-1, keepdims=True)
    centered = values - mean_val
    variance = jnp.mean(centered * centered, axis=-1, keepdims=True)
    inverse = lax.rsqrt(variance + norm_epsilon)
    return centered * inverse, inverse


def nn(left, right):
    return jnp.dot(left, right, preferred_element_type=jnp.float32)


def key_mask(segment_row, keys, first, queries):
    column = jnp.transpose(jnp.broadcast_to(segment_row, (8, segment_row.shape[1])))[:keys, :1]
    row = segment_row[:, first : first + queries]
    key_pos = lax.broadcasted_iota(jnp.int32, (keys, queries), 0)
    query_pos = lax.broadcasted_iota(jnp.int32, (keys, queries), 1) + first
    return jnp.where((column == row) & (key_pos <= query_pos), 0.0, masked_value)


def lane_half(values, which):
    lane = lax.broadcasted_iota(jnp.int32, values.shape, 1)
    inside = (lane >= HEAD_DIM) if which else (lane < HEAD_DIM)
    return jnp.where(inside, values, jnp.zeros_like(values))


def attend_kernel(
    score_scale,
    rows_ref,
    low_ref,
    high_ref,
    bias_ref,
    segment_ref,
    vector_ref,
    normed_ref,
    mixed_ref,
    log_ref,
    context_ref,
    attended_ref,
):
    bf16 = jnp.bfloat16
    length = rows_ref.shape[0]
    width = context_ref.shape[1]
    rows = low_ref.shape[0]
    for at, part_ref in ((0, low_ref), (rows, high_ref)):
        turned = jnp.transpose(part_ref[:, 4 * width : 4 * width + 128].astype(jnp.float32))
        vector_ref[:, at : at + rows] = turned[:8]
    half = length // 2
    unit, _ = column_norm(rows_ref[...].astype(jnp.float32))
    normed_ref[...] = (unit * vector_ref[0:1] + vector_ref[2:3]).astype(bf16)
    mixed = nn(normed_ref[:, :rows], low_ref[:, : 3 * width]) + nn(
        normed_ref[:, rows:], high_ref[:, : 3 * width]
    )
    mixed_ref[:, :width] = (mixed[:, :width] + bias_ref[0:1]).astype(bf16)
    mixed_ref[:, width : 2 * width] = mixed[:, width : 2 * width].astype(bf16)
    mixed_ref[:, 2 * width :] = (mixed[:, 2 * width :] + bias_ref[1:2]).astype(bf16)
    segment_row = segment_ref[...]
    spans = ((0, half, key_mask(segment_row, half, 0, half)), (half, length, key_mask(segment_row, length, half, half)))
    log_ref[...] = jnp.zeros_like(log_ref)
    for two in range(width // 128):
        at = 128 * two
        query_two = mixed_ref[:, at : at + 128] * jnp.asarray(score_scale, bf16)
        key_two = mixed_ref[:, width + at : width + at + 128]
        value_turned = jnp.transpose(mixed_ref[:, 2 * width + at : 2 * width + at + 128])
        parts = []
        for which in range(2):
            query_rows = lane_half(query_two, which)
            value_rows = value_turned[HEAD_DIM * which : HEAD_DIM * (which + 1)]
            sides = []
            for first, keys, mask in spans:
                scores = inner_cols(key_two[:keys], query_rows[first : first + half]) + mask
                top = jnp.max(scores, axis=0, keepdims=True)
                exponent = jnp.exp(scores - top)
                total = jnp.sum(exponent, axis=0, keepdims=True)
                log_ref[2 * two + which : 2 * two + which + 1, first : first + half] = top + jnp.log(total)
                sides.append(nn(value_rows[:, :keys], exponent.astype(bf16)) / total)
            parts.append(jnp.concatenate(sides, axis=1))
        context_ref[:, at : at + 128] = jnp.transpose(jnp.concatenate(parts, axis=0)).astype(bf16)
    for at, part_ref in ((0, low_ref), (rows, high_ref)):
        attended_ref[:, at : at + rows] = inner_cols(
            context_ref[...], part_ref[:, 3 * width : 4 * width]
        ).astype(bf16)


def store_blocks(value, place, keep_ref, send_ref, columns):
    rows = value.shape[0] // 8
    counts = [0, 0]
    for block in range(8):
        which = (block >> (2 - place)) & 1
        target = send_ref if which else keep_ref
        at = counts[which] * rows
        counts[which] += 1
        target[at : at + rows, columns] = value[block * rows : (block + 1) * rows].astype(target.dtype)


def join_blocks(place, keep_ref, other_ref, whole_ref):
    rows = whole_ref.shape[0] // 8
    counts = [0, 0]
    for block in range(8):
        which = (block >> (2 - place)) & 1
        at = counts[which] * rows
        counts[which] += 1
        source = other_ref if which else keep_ref
        whole_ref[block * rows : (block + 1) * rows] = source[at : at + rows]


def feed_kernel(
    rows_ref,
    own_ref,
    other_ref,
    vector_ref,
    up_mine_ref,
    up_other_ref,
    down_mine_ref,
    down_other_ref,
    bias_ref,
    cot_ref,
    middle_ref,
    feed_ref,
    grad_two_ref,
    up_keep_ref,
    up_send_ref,
    down_keep_ref,
    down_send_ref,
    bias_grad_ref,
    normed_ref,
    normed_turned_ref,
    cot_turned_ref,
    up_ref,
    down_ref,
    feed_sum_ref,
    grad_two_sum_ref,
):
    bf16, f32 = jnp.bfloat16, jnp.float32

    @pl.when(pl.program_id(0) == 0)
    def _():
        middle = (
            rows_ref[...].astype(f32)
            + (own_ref[...].astype(f32) + other_ref[...].astype(f32))
            + vector_ref[4:5]
        )
        middle_ref[...] = middle
        unit, _ = column_norm(middle)
        normed_ref[...] = (unit * vector_ref[1:2] + vector_ref[3:4]).astype(bf16)
        normed_turned_ref[...] = jnp.transpose(normed_ref[...])
        cot_turned_ref[...] = jnp.transpose(cot_ref[...])
        feed_sum_ref[...] = jnp.zeros_like(feed_sum_ref)
        grad_two_sum_ref[...] = jnp.zeros_like(grad_two_sum_ref)

    join_blocks(PLACE[TURNS[1][2]], up_mine_ref, up_other_ref, up_ref)
    join_blocks(PLACE[TURNS[2][2]], down_mine_ref, down_other_ref, down_ref)
    before = nn(normed_ref[...], up_ref[...]) + bias_ref[...]
    square = before * before
    bend = jnp.tanh(gelu_factor * (before + 0.044715 * before * square))
    opened = 0.5 * (1.0 + bend)
    hidden = (before * opened).astype(bf16)
    slope = opened + 0.5 * before * (1.0 - bend * bend) * (
        gelu_factor * (1.0 + 3.0 * 0.044715 * square)
    )
    grad_before = (nn(cot_ref[...], down_ref[...]) * slope).astype(bf16)
    feed_sum_ref[...] += inner_cols(hidden, down_ref[...])
    grad_two_sum_ref[...] += inner_cols(grad_before, up_ref[...])
    bias_grad_ref[...] = jnp.broadcast_to(
        jnp.sum(grad_before.astype(f32), axis=0, keepdims=True), bias_grad_ref.shape
    )
    columns = slice(0, up_ref.shape[1])
    store_blocks(nn(cot_turned_ref[...], hidden), PLACE[TURNS[2][2]], down_keep_ref, down_send_ref, columns)
    store_blocks(nn(normed_turned_ref[...], grad_before), PLACE[TURNS[1][2]], up_keep_ref, up_send_ref, columns)

    @pl.when(pl.program_id(0) == pl.num_programs(0) - 1)
    def _():
        feed_ref[...] = feed_sum_ref[...].astype(bf16)
        grad_two_ref[...] = grad_two_sum_ref[...].astype(bf16)


def attend_back_kernel(
    score_scale,
    middle_ref,
    cot_ref,
    own_ref,
    other_ref,
    vector_ref,
    context_ref,
    mixed_ref,
    log_ref,
    low_ref,
    high_ref,
    segment_ref,
    normed_ref,
    rows_ref,
    hidden_sums_ref,
    fold_ref,
    block_ref,
    grad_middle_ref,
    grad_one_ref,
    keep_a_ref,
    send_a_ref,
    keep_b_ref,
    send_b_ref,
    keep_c_ref,
    send_c_ref,
    grad_context_ref,
    grad_mixed_ref,
    terms_ref,
    bias_ref,
):
    bf16, f32 = jnp.bfloat16, jnp.float32
    length = middle_ref.shape[0]
    width = context_ref.shape[1]
    rows = low_ref.shape[0]
    half = length // 2
    unit, inverse = column_norm(middle_ref[...])
    grad_norm = own_ref[...].astype(f32) + other_ref[...].astype(f32)
    scaled = grad_norm * vector_ref[1:2]
    mean_grad = jnp.mean(scaled, axis=-1, keepdims=True)
    mean_cross = jnp.mean(scaled * unit, axis=-1, keepdims=True)
    cot = cot_ref[...].astype(f32)
    grad_middle = cot + inverse * (scaled - mean_grad - unit * mean_cross)
    grad_middle_ref[...] = grad_middle
    terms_ref[...] = jnp.zeros_like(terms_ref)
    terms_ref[1:2] = 0.5 * jnp.sum(grad_norm * unit, axis=0, keepdims=True)
    terms_ref[3:4] = 0.5 * jnp.sum(grad_norm, axis=0, keepdims=True)
    terms_ref[4:5] = 0.5 * jnp.sum(grad_middle, axis=0, keepdims=True)
    terms_ref[5:6] = 0.5 * jnp.sum(cot, axis=0, keepdims=True)
    hidden_width = hidden_sums_ref.shape[1]
    bias_ref[:, :hidden_width] = hidden_sums_ref[0:1]
    middle_rows = grad_middle.astype(bf16)
    third = keep_a_ref.shape[1]
    last = keep_c_ref.shape[1]
    store_blocks(
        nn(jnp.transpose(middle_rows), context_ref[...]),
        PLACE[TURNS[2][2]],
        keep_c_ref,
        send_c_ref,
        slice(third - width, third),
    )
    grad_context_ref[...] = (
        nn(middle_rows[:, :rows], low_ref[:, 3 * width : 4 * width])
        + nn(middle_rows[:, rows:], high_ref[:, 3 * width : 4 * width])
    ).astype(bf16)
    segment_row = segment_ref[...]
    spans = ((0, half, key_mask(segment_row, half, 0, half)), (half, length, key_mask(segment_row, length, half, half)))
    for two in range(width // 128):
        at = 128 * two
        query_two = mixed_ref[:, at : at + 128] * jnp.asarray(score_scale, bf16)
        key_two = mixed_ref[:, width + at : width + at + 128]
        value_two = mixed_ref[:, 2 * width + at : 2 * width + at + 128]
        grad_two = grad_context_ref[:, at : at + 128]
        key_turned = jnp.transpose(key_two)
        grad_queries = []
        grad_keys = [0.0, 0.0]
        grad_values = [0.0, 0.0]
        for which in range(2):
            query_rows = lane_half(query_two, which)
            grad_rows = lane_half(grad_two, which)
            key_rows = key_turned[HEAD_DIM * which : HEAD_DIM * (which + 1)]
            sides = []
            for side, (first, keys, mask) in enumerate(spans):
                query_side = query_rows[first : first + half]
                grad_side = grad_rows[first : first + half]
                log_side = log_ref[2 * two + which : 2 * two + which + 1, first : first + half]
                scores = inner_cols(key_two[:keys], query_side) + mask
                soft = jnp.exp(scores - log_side)
                grad_soft = inner_cols(value_two[:keys], grad_side)
                crossed = soft * grad_soft
                grad_scores = (
                    crossed - soft * jnp.sum(crossed, axis=0, keepdims=True)
                ).astype(bf16)
                grad_keys[side] += nn(grad_scores, query_side)
                grad_values[side] += nn(soft.astype(bf16), grad_side)
                sides.append(nn(key_rows[:, :keys], grad_scores))
            grad_queries.append(jnp.concatenate(sides, axis=1))
        queries_out = jnp.transpose(jnp.concatenate(grad_queries, axis=0)) * score_scale
        for place, value in enumerate((queries_out, grad_keys, grad_values)):
            columns = slice(place * width + at, place * width + at + 128)
            if place == 0:
                grad_mixed_ref[:, columns] = value.astype(bf16)
            else:
                grad_mixed_ref[:half, columns] = (value[0] + value[1][:half]).astype(bf16)
                grad_mixed_ref[half:, columns] = value[1][half:].astype(bf16)
            if place != 1:
                start = hidden_width + (place // 2) * width + at
                bias_ref[:, start : start + 128] = jnp.sum(
                    grad_mixed_ref[:, columns].astype(f32), axis=0, keepdims=True
                )
    unit, _ = column_norm(rows_ref[...].astype(f32))
    for at, part_ref in ((0, low_ref), (rows, high_ref)):
        columns = slice(at, at + rows)
        grad_one = inner_cols(grad_mixed_ref[...], part_ref[:, : 3 * width])
        grad_one_ref[:, columns] = grad_one.astype(bf16)
        terms_ref[0:1, columns] = jnp.sum(grad_one * unit[:, columns], axis=0, keepdims=True)
        terms_ref[2:3, columns] = jnp.sum(grad_one, axis=0, keepdims=True)
    row = lax.broadcasted_iota(jnp.int32, (64, bias_ref.shape[1]), 0)
    lane = lax.broadcasted_iota(jnp.int32, (64, bias_ref.shape[1]), 1)
    inside = jnp.zeros(row.shape, jnp.bool_)
    for start, size in ((0, hidden_width), (hidden_width, width), (hidden_width + width, width)):
        first = row * (size // 64) + start
        inside = inside | ((lane >= first) & (lane < first + size // 64))
    spread = jnp.where(inside, bias_ref[...], 0.0)
    for matrix_ref in (fold_ref, block_ref):
        high = spread.astype(bf16)
        rest = (spread - high.astype(f32)).astype(bf16)
        if matrix_ref is fold_ref:
            spread = nn(high, matrix_ref[...]) + nn(rest, matrix_ref[...])
        else:
            spread = nn(matrix_ref[...], high) + nn(matrix_ref[...], rest)
    store_blocks(
        jnp.transpose(terms_ref[...]) + spread,
        PLACE[TURNS[2][2]],
        keep_c_ref,
        send_c_ref,
        slice(third, last),
    )
    turned = jnp.transpose(normed_ref[...])
    targets = ((keep_a_ref, send_a_ref), (keep_b_ref, send_b_ref), (keep_c_ref, send_c_ref))
    for i, (keep_ref, send_ref) in enumerate(targets):
        size = min(third, 3 * width - i * third)
        store_blocks(
            nn(turned, grad_mixed_ref[:, i * third : i * third + size]),
            PLACE[TURNS[i][2]],
            keep_ref,
            send_ref,
            slice(0, size),
        )


def token_kernel(
    core_ref,
    rows_ref,
    own_ref,
    other_ref,
    grad_middle_ref,
    vector_ref,
    order_ref,
    token_ref,
    token_full_ref,
):
    bf16, f32 = jnp.bfloat16, jnp.float32
    half = token_ref.shape[0]
    unit, inverse = column_norm(rows_ref[...].astype(f32))
    grad_norm = own_ref[...].astype(f32) + other_ref[...].astype(f32)
    scaled = grad_norm * vector_ref[0:1]
    mean_grad = jnp.mean(scaled, axis=-1, keepdims=True)
    mean_cross = jnp.mean(scaled * unit, axis=-1, keepdims=True)
    token_full_ref[...] = (
        grad_middle_ref[...] + inverse * (scaled - mean_grad - unit * mean_cross)
    )
    start = pl.multiple_of(core_ref[0] * half, half)
    token_rows = token_full_ref[pl.ds(start, half), :].astype(bf16)
    token_ref[...] = inner_cols(token_rows, order_ref[...]).astype(bf16)


def call(kernel, outs, scratch, *operands, smem=0):
    space = [pl.BlockSpec(memory_space=pltpu.SMEM)] * smem
    space += [pl.BlockSpec(memory_space=pltpu.VMEM)] * (len(operands) - smem)
    return pl.pallas_call(
        kernel,
        out_shape=[jax.ShapeDtypeStruct(shape, kind) for shape, kind in outs],
        in_specs=space,
        out_specs=[pl.BlockSpec(memory_space=pltpu.VMEM)] * len(outs),
        scratch_shapes=[pltpu.VMEM(shape, kind) for shape, kind in scratch],
        compiler_params=pltpu.CompilerParams(vmem_limit_bytes=56 * 1024 * 1024),
    )(*operands)


def local(
    tokens,
    cotangent,
    segments,
    input_weight,
    output_weight,
    up_weight,
    down_weight,
    head_bias,
    hidden_bias,
    norm_gains,
    shifts,
):
    bf16, f32 = jnp.bfloat16, jnp.float32
    half, width = tokens.shape
    length = segments.shape[1]
    block = input_weight.shape[0]
    heads_width = input_weight.shape[2]
    hidden_width = up_weight.shape[1]
    local_heads = heads_width // HEAD_DIM
    score_scale = 1.0 / math.sqrt(HEAD_DIM)
    core = lax.axis_index("c")

    first_end = 4 * heads_width + 128
    pack_width = first_end + 2 * hidden_width
    me = (
        (lax.axis_index("zh") * 4 + lax.axis_index("xh") * 2 + lax.axis_index("h"))
        .astype(jnp.int32)
        .reshape(1)
    )
    (shard,) = call(
        pack_kernel,
        [((block, pack_width), bf16)],
        [((128, block), f32)],
        input_weight,
        output_weight.T,
        up_weight,
        down_weight.T,
        norm_gains,
        shifts,
    )
    sources = source_blocks(width)
    order = lax.optimization_barrier(feature_order(sources, width))
    blocks = block_order(sources, width)
    folds = bias_fold(hidden_width, heads_width)

    def full_rows(rows):
        return nn(lax.all_gather(swap_roles(rows), "c", axis=0, tiled=True), order).astype(bf16)

    rows = full_rows(tokens)
    cot_rows = full_rows(cotangent)

    parts, order, blocks, folds, rows, cot_rows = lax.optimization_barrier(
        (gather_near(shard), order, blocks, folds, rows, cot_rows)
    )
    near = call(
        collect_kernel,
        [((8 * block, size), bf16) for size in (first_end, hidden_width, hidden_width)],
        [((8 * block, pack_width), f32)],
        me,
        *parts,
        smem=1,
    )
    small = swap_roles(
        jnp.concatenate(
            (head_bias.reshape(-1), hidden_bias, segments[0].astype(bf16))
        )
    )
    bias_rows = small[: 2 * heads_width].reshape(2, heads_width).astype(f32)
    hidden_row = small[2 * heads_width : 2 * heads_width + hidden_width].astype(f32)
    segment_row = small[2 * heads_width + hidden_width :].astype(f32).reshape(1, length)
    first_halves, up_halves, down_halves = gather_far(near)

    def own_half(rows):
        return lax.dynamic_slice_in_dim(rows, core * half, half, axis=0)

    def other_half(rows):
        return lax.dynamic_slice_in_dim(rows, (1 - core) * half, half, axis=0)

    vectors, normed_one, mixed, log_sums, context, attended = call(
        functools.partial(attend_kernel, score_scale),
        [
            ((8, width), f32),
            ((length, width), bf16),
            ((length, 3 * heads_width), bf16),
            ((8, length), f32),
            ((length, heads_width), bf16),
            ((length, width), bf16),
        ],
        [],
        rows,
        *first_halves,
        bias_rows,
        segment_row,
    )
    third = hidden_width // 3

    def whole(*shape):
        return pl.BlockSpec(shape, lambda j: (0, 0))

    def cut(rows_of):
        return pl.BlockSpec((rows_of, third), lambda j: (0, j))

    def shaped(shape, kind):
        return jax.ShapeDtypeStruct(shape, kind)

    middle, feed, grad_two, up_keep, up_send, down_keep, down_send, hidden_sums = pl.pallas_call(
        feed_kernel,
        grid=(3,),
        out_shape=[
            shaped((length, width), f32),
            shaped((length, width), bf16),
            shaped((length, width), bf16),
        ]
        + [shaped((width // 2, hidden_width), bf16)] * 4
        + [shaped((8, hidden_width), f32)],
        in_specs=[whole(length, width)] * 3
        + [whole(8, width)]
        + [cut(width // 2)] * 4
        + [cut(1), whole(length, width)],
        out_specs=[whole(length, width)] * 3 + [cut(width // 2)] * 4 + [cut(8)],
        scratch_shapes=[
            pltpu.VMEM((length, width), bf16),
            pltpu.VMEM((width, length), bf16),
            pltpu.VMEM((width, length), bf16),
            pltpu.VMEM((width, third), bf16),
            pltpu.VMEM((width, third), bf16),
            pltpu.VMEM((length, width), f32),
            pltpu.VMEM((length, width), f32),
        ],
        compiler_params=pltpu.CompilerParams(vmem_limit_bytes=56 * 1024 * 1024),
    )(
        rows,
        attended,
        pair(attended),
        vectors,
        *up_halves,
        *down_halves,
        hidden_row.reshape(1, hidden_width),
        cot_rows,
    )
    down_other = step_along(down_send, TURNS[2][2])
    up_other = step_along(up_send, TURNS[1][2])
    grad_two_other, feed_other = lax.optimization_barrier((pair(grad_two), pair(other_half(feed))))
    grad_middle, grad_one, *first_grads = call(
        functools.partial(attend_back_kernel, score_scale),
        [
            ((length, width), f32),
            ((length, width), bf16),
        ]
        + [((width // 2, 4 * heads_width // 3), bf16)] * 4
        + [((width // 2, 4 * heads_width // 3 + 128), bf16)] * 2,
        [
            ((length, heads_width), bf16),
            ((length, 3 * heads_width), bf16),
            ((128, width), f32),
            ((1, hidden_width + 2 * heads_width), f32),
        ],
        middle,
        cot_rows,
        grad_two,
        grad_two_other,
        vectors,
        context,
        mixed,
        log_sums,
        *first_halves,
        segment_row,
        normed_one,
        rows,
        hidden_sums,
        folds,
        blocks,
    )
    first_grads, grad_one, up_other, down_other = lax.optimization_barrier(
        (first_grads, grad_one, up_other, down_other)
    )
    turn_lists = TURNS + TURNS[1:]
    kept = list(first_grads[0::2])
    others = [step_along(send, TURNS[i][2]) for i, send in enumerate(first_grads[1::2])]

    def folded(keep, other, i, turn):
        turns = turn_lists[i]
        if turn == 1:
            place = sorted(turns[:2], key=PLACE.get).index(turns[1])
            keep, send = half_sums(keep, other, place, 2)
        else:
            keep, send = half_sums(keep, other, 0, 1)
        return keep, step_along(send, turns[turn])

    feeds = [folded(up_keep, up_other, 3, 1), folded(down_keep, down_other, 4, 1)]
    grad_one_other = pair(grad_one)
    outcome = (
        own_half(middle)
        + own_half(feed).astype(f32)
        + feed_other.astype(f32)
        + vectors[5]
    )
    block_out = inner_cols(outcome.astype(bf16), order).astype(bf16)

    others, feeds, grad_one_other, block_out = lax.optimization_barrier(
        (others, feeds, grad_one_other, block_out)
    )
    pieces = [folded(keep, other, i, 1) for i, (keep, other) in enumerate(zip(kept, others))]
    feeds = [folded(*feeds[0], 3, 0), folded(*feeds[1], 4, 0)]
    (token_grad,) = call(
        token_kernel,
        [((half, width), bf16)],
        [((length, width), f32)],
        core.astype(jnp.int32).reshape(1),
        rows,
        grad_one,
        grad_one_other,
        grad_middle,
        vectors,
        order,
        smem=1,
    )
    pieces, feeds, token_grad = lax.optimization_barrier((pieces, feeds, token_grad))
    pieces = [folded(*piece, i, 0) for i, piece in enumerate(pieces)]
    operands = []
    for piece in pieces + feeds:
        operands += piece
    cross = pair(add_low(operands[4][:, -128:], operands[5][:, -128:]))
    shares = call(
        deal_kernel,
        [((2 * block, pack_width), bf16)] * 4,
        [],
        me,
        cross,
        *operands,
        smem=1,
    )
    shares, block_out, token_grad = lax.optimization_barrier((shares, block_out, token_grad))
    block_out, token_grad = swap_roles(block_out), swap_roles(token_grad)
    shares = scatter_near(shares)
    six = block // 2
    input_grad, output_grad, up_grad, down_grad, head_grad, hidden_grad, gain_grad, shift_grad = call(
        unpack_kernel,
        [
            ((block, 3, heads_width), f32),
            ((block, heads_width), f32),
            ((block, hidden_width), f32),
            ((block, hidden_width), f32),
            ((2, six), f32),
            ((1, 2 * block), f32),
            ((2, six), f32),
            ((4, six), f32),
        ],
        [],
        lax.axis_index("h").astype(jnp.int32).reshape(1),
        *shares,
        smem=1,
    )
    return (
        block_out,
        token_grad,
        input_grad,
        output_grad.T,
        up_grad,
        down_grad.T,
        head_grad,
        hidden_grad.reshape(2 * block),
        gain_grad,
        shift_grad,
    )


def solution(mesh):
    fine = Mesh(mesh.devices.reshape((2,) * 7), AXES)
    in_specs = (
        P(AXES, None),
        P(AXES, None),
        P(DP, None),
        P(DP, None, "h"),
        P("h", DP),
        P(DP, "h"),
        P("h", DP),
        P(None, "h"),
        P("h"),
        P(None, DP),
        P(None, DP),
    )
    out_specs = (
        P(AXES, None),
        P(AXES, None),
        P(DP, None, "h"),
        P("h", DP),
        P(DP, "h"),
        P("h", DP),
        P(None, ("h",) + DP),
        P(("h",) + DP),
        P(None, AXES),
        P(None, AXES),
    )
    return jax.shard_map(local, mesh=fine, in_specs=in_specs, out_specs=out_specs, check_vma=False)
```

```python
import functools
import itertools
import math

import jax
import jax.numpy as jnp
import numpy as np
from jax import lax
from jax.experimental import pallas as pl
from jax.experimental.pallas import tpu as pltpu
from jax.sharding import Mesh
from jax.sharding import PartitionSpec as P

HEAD_DIM = 64


norm_epsilon = 1e-05
masked_value = -1e30
gelu_factor = 0.7978845608028654


def inner_cols(left_side, right_side):
    return lax.dot_general(
        left_side, right_side, (((1,), (1,)), ((), ())), preferred_element_type=jnp.float32
    )


AXES = ("xh", "xl", "yl", "zh", "zl", "c", "h")
DP = AXES[:6]
RING = {"x": ("xh", "xl"), "y": ("h", "yl"), "z": ("zh", "zl")}
PLACE = {"z": 0, "y": 1, "x": 2}
TURNS = (("x", "y", "z"), ("y", "z", "x"), ("z", "x", "y"))


def swap_roles(values):
    return lax.ppermute(values, ("c", "h"), [(0, 0), (1, 2), (2, 1), (3, 3)])


def pair(values):
    return lax.ppermute(values, "c", [(0, 1), (1, 0)])


def step_along(values, axis):
    high, low = RING[axis]
    order = [name for name in AXES if name in (high, low, "c")]
    moves = []
    for place in itertools.product(range(2), repeat=3):
        target = dict(zip(order, place))
        target[low] ^= 1
        target[high] ^= target["c"]
        moves.append(
            (place[0] * 4 + place[1] * 2 + place[2], sum(target[n] << (2 - i) for i, n in enumerate(order)))
        )
    return lax.ppermute(values, tuple(order), moves)


def cross_roles(values, outward):
    moves = [(0, 1), (1, 3), (2, 0), (3, 2)]
    return lax.ppermute(values, ("c", "h"), moves if outward else [(b, a) for a, b in moves])


def flip(values, place):
    moves = []
    for xh, zh in itertools.product(range(2), repeat=2):
        moves.append((xh * 2 + zh, (xh ^ (place & 1)) * 2 + (zh ^ (place >> 1))))
    return lax.ppermute(values, ("xh", "zh"), moves)


def gather_near(shard):
    own = jnp.concatenate((swap_roles(shard), cross_roles(shard, True)), axis=0)
    return [own] + [flip(own, place) for place in range(1, 4)]


def add_low(left, right):
    return (left.astype(jnp.float32) + right.astype(jnp.float32)).astype(jnp.bfloat16)


def scatter_near(parts):
    others = [flip(part, place) for place, part in enumerate(parts) if place]
    total = parts[0].astype(jnp.float32)
    for other in others:
        total = total + other.astype(jnp.float32)
    total = total.astype(jnp.bfloat16)
    rows = total.shape[0] // 2
    return swap_roles(total[:rows]), cross_roles(total[rows:], False)


def open_blocks(piece):
    return piece.reshape((1, 1, 1) + piece.shape)


def gather_far(pieces):
    pieces = [open_blocks(piece) for piece in pieces]
    others = [step_along(piece, TURNS[i][0]) for i, piece in enumerate(pieces)]
    quarters = []
    for turns, piece, other in zip(TURNS, pieces, others):
        both = jnp.concatenate((piece, other), axis=PLACE[turns[0]])
        quarters.append(both.reshape(2 * piece.shape[3], piece.shape[4]))
    seconds = [step_along(quarter, TURNS[i][1]) for i, quarter in enumerate(quarters)]
    thirds = [step_along(quarter, TURNS[i][2]) for i, quarter in enumerate(quarters)]
    fourths = [step_along(second, TURNS[i][2]) for i, second in enumerate(seconds)]
    return list(zip(quarters, seconds, thirds, fourths))


def source_blocks(width):
    place = np.arange(width, dtype=np.int32) // (width // 64)
    near, far = place % 8, place // 8
    fixed = ((near >> 1) & 1) * 32 + (near >> 2) * 4 + (near & 1)
    xl = lax.axis_index("xl") ^ (far & 1)
    yl = lax.axis_index("yl") ^ ((far >> 1) & 1)
    zl = lax.axis_index("zl") ^ (far >> 2)
    return lax.optimization_barrier(fixed + xl * 16 + yl * 8 + zl * 2)


def feature_order(sources, width):
    block = width // 64
    inner = np.arange(width, dtype=np.int32) % block
    source = lax.optimization_barrier(sources * block + inner)
    return (lax.broadcasted_iota(jnp.int32, (width, width), 0) == source[None]).astype(jnp.bfloat16)


def block_order(sources, width):
    return (lax.broadcasted_iota(jnp.int32, (width, 64), 1) == sources[:, None]).astype(jnp.bfloat16)


def bias_fold(hidden_width, width):
    many, few = hidden_width // 64, width // 64
    target = np.concatenate(
        (
            np.arange(hidden_width) % many,
            np.arange(width) % few + many,
            np.arange(width) % few + many + few,
        )
    )
    return jnp.asarray(np.arange(128)[None] == target[:, None] + 8, jnp.bfloat16)


def place_rows(rows, me):
    block = rows // 8
    row = lax.broadcasted_iota(jnp.int32, (rows, rows), 0)
    column = lax.broadcasted_iota(jnp.int32, (rows, rows), 1)
    found = jnp.zeros((rows, rows), jnp.float32)
    for k in range(8):
        inside = (row >= k * block) & (row < (k + 1) * block)
        same = column - (me ^ k) * block == row - k * block
        found = jnp.where(inside & same, 1.0, found)
    return found.astype(jnp.bfloat16)


def eye(size):
    row = lax.broadcasted_iota(jnp.int32, (size, size), 0)
    column = lax.broadcasted_iota(jnp.int32, (size, size), 1)
    return (row == column).astype(jnp.float32).astype(jnp.bfloat16)


def pack_kernel(input_ref, output_ref, up_ref, down_ref, gains_ref, shifts_ref, shard_ref, small_ref):
    bf16 = jnp.bfloat16
    block, width = output_ref.shape
    hidden_width = up_ref.shape[1]
    for i in range(3):
        shard_ref[:, i * width : (i + 1) * width] = input_ref[:, i, :]
    shard_ref[:, 3 * width : 4 * width] = output_ref[...]
    small_ref[...] = jnp.zeros_like(small_ref)
    small_ref[0:2] = gains_ref[...].astype(jnp.float32)
    small_ref[2:6] = shifts_ref[...].astype(jnp.float32)
    at = 4 * width + 128
    shard_ref[:, 4 * width : at] = inner_cols(eye(block), small_ref[...].astype(bf16)).astype(bf16)
    shard_ref[:, at : at + hidden_width] = up_ref[...]
    shard_ref[:, at + hidden_width :] = down_ref[...]


def collect_kernel(me_ref, *refs):
    parts, outs, held_ref = refs[:4], refs[4:-1], refs[-1]
    rows = held_ref.shape[0]
    for i, part in enumerate(parts):
        held_ref[i * rows // 4 : (i + 1) * rows // 4] = part[...].astype(jnp.float32)
    moved = place_rows(rows, me_ref[0])
    at = 0
    for out in outs:
        columns = out.shape[1]
        held = held_ref[:, at : at + columns].astype(jnp.bfloat16)
        out[...] = nn(moved, held).astype(jnp.bfloat16)
        at += columns


def deal_kernel(me_ref, cross_ref, *refs):
    parts, outs = refs[:-4], refs[-4:]
    rows = parts[0].shape[0]
    moved = place_rows(rows, me_ref[0])
    at = 0
    for i, (keep, other) in enumerate(zip(parts[::2], parts[1::2])):
        columns = keep.shape[1]
        total = add_low(keep[...], other[...])
        if i == 2:
            lane = lax.broadcasted_iota(jnp.int32, cross_ref.shape, 1)
            cross = jnp.where(lane < 8, cross_ref[...].astype(jnp.float32), 0.0)
            total = jnp.concatenate((total[:, : columns - 128], add_low(total[:, columns - 128 :], cross)), axis=1)
        total = nn(moved, total)
        for i, out in enumerate(outs):
            part = total[i * rows // 4 : (i + 1) * rows // 4]
            out[:, at : at + columns] = part.astype(jnp.bfloat16)
        at += columns


def unpack_kernel(half_ref, *refs):
    parts = refs[:2]
    input_ref, output_ref, up_ref, down_ref, head_ref, hidden_ref, gain_ref, shift_ref = refs[2:]
    f32 = jnp.float32
    block, width = output_ref.shape
    hidden_width = up_ref.shape[1]
    six = block // 2

    def total(start, size):
        columns = slice(start, start + size)
        value = parts[0][:, columns].astype(f32)
        for part in parts[1:]:
            value = value + part[:, columns].astype(f32)
        return value

    def pick(rows, columns, offset):
        row = lax.broadcasted_iota(jnp.int32, (rows, columns), 0)
        column = lax.broadcasted_iota(jnp.int32, (rows, columns), 1)
        return (row == column + offset).astype(f32)

    def exact(left, right, dims):
        return lax.dot_general(
            left, right, (dims, ((), ())), precision=lax.Precision.HIGHEST, preferred_element_type=f32
        )

    for i in range(3):
        input_ref[:, i, :] = total(i * width, width)
    output_ref[...] = total(3 * width, width)
    at = 4 * width + 128
    up_ref[...] = total(at, hidden_width)
    down_ref[...] = total(at + hidden_width, hidden_width)
    small = total(4 * width, 128)
    norm_terms = exact(small, pick(block, six, half_ref[0] * six), ((0,), (0,)))
    gain_ref[...] = norm_terms[0:2]
    shift_ref[...] = norm_terms[2:6]
    hidden_ref[...] = exact(small[0:1], pick(128, 2 * block, 8), ((1,), (0,)))
    head_ref[0:1] = exact(small[0:1], pick(128, six, 8 + 2 * block), ((1,), (0,)))
    head_ref[1:2] = exact(small[0:1], pick(128, six, 8 + 2 * block + six), ((1,), (0,)))


def fold_kernel(layouts, *refs):
    ins, outs = refs[: 2 * len(layouts)], refs[2 * len(layouts) :]
    for i, (bits, place) in enumerate(layouts):
        keep_ref, other_ref = ins[2 * i : 2 * i + 2]
        rows = keep_ref.shape[0] >> bits
        counts = [0, 0]
        for block in range(1 << bits):
            which = (block >> (bits - 1 - place)) & 1
            at = counts[which] * rows
            counts[which] += 1
            span = slice(block * rows, (block + 1) * rows)
            outs[2 * i + which][at : at + rows] = add_low(keep_ref[span], other_ref[span])


def fold(pairs, turn_lists, turns_left):
    layouts = []
    for turns, left in zip(turn_lists, turns_left):
        place = sorted(turns[:left], key=PLACE.get).index(turns[left - 1])
        layouts.append((left, place))
    outs = []
    for keep, _ in pairs:
        outs += [((keep.shape[0] // 2, keep.shape[1]), jnp.bfloat16)] * 2
    parts = call(functools.partial(fold_kernel, layouts), outs, [], *[x for pair_of in pairs for x in pair_of])
    return [
        (keep, step_along(send, turns[left - 1]))
        for keep, send, turns, left in zip(parts[0::2], parts[1::2], turn_lists, turns_left)
    ]


def column_norm(values):
    mean_val = jnp.mean(values, axis=-1, keepdims=True)
    centered = values - mean_val
    variance = jnp.mean(centered * centered, axis=-1, keepdims=True)
    inverse = lax.rsqrt(variance + norm_epsilon)
    return centered * inverse, inverse


def nn(left, right):
    return jnp.dot(left, right, preferred_element_type=jnp.float32)


def key_mask(segment_row, keys, first, queries):
    column = jnp.transpose(jnp.broadcast_to(segment_row, (8, segment_row.shape[1])))[:keys, :1]
    row = segment_row[:, first : first + queries]
    key_pos = lax.broadcasted_iota(jnp.int32, (keys, queries), 0)
    query_pos = lax.broadcasted_iota(jnp.int32, (keys, queries), 1) + first
    return jnp.where((column == row) & (key_pos <= query_pos), 0.0, masked_value)


def lane_half(values, which):
    lane = lax.broadcasted_iota(jnp.int32, values.shape, 1)
    inside = (lane >= HEAD_DIM) if which else (lane < HEAD_DIM)
    return jnp.where(inside, values, jnp.zeros_like(values))


def attend_kernel(
    score_scale,
    rows_ref,
    quarter_0_ref,
    quarter_1_ref,
    quarter_2_ref,
    quarter_3_ref,
    bias_ref,
    segment_ref,
    vector_ref,
    normed_ref,
    mixed_ref,
    log_ref,
    context_ref,
    attended_ref,
    weight_ref,
):
    bf16 = jnp.bfloat16
    length = rows_ref.shape[0]
    width = context_ref.shape[1]
    join_blocks(TURNS[0], (quarter_0_ref, quarter_1_ref, quarter_2_ref, quarter_3_ref), weight_ref)
    vector_ref[...] = jnp.transpose(weight_ref[:, 4 * width : 4 * width + 128].astype(jnp.float32))[:8]
    half = length // 2
    unit, _ = column_norm(rows_ref[...].astype(jnp.float32))
    normed_ref[...] = (unit * vector_ref[0:1] + vector_ref[2:3]).astype(bf16)
    mixed = nn(normed_ref[...], weight_ref[:, : 3 * width])
    mixed_ref[:, :width] = (mixed[:, :width] + bias_ref[0:1]).astype(bf16)
    mixed_ref[:, width : 2 * width] = mixed[:, width : 2 * width].astype(bf16)
    mixed_ref[:, 2 * width :] = (mixed[:, 2 * width :] + bias_ref[1:2]).astype(bf16)
    segment_row = segment_ref[...]
    spans = ((0, half, key_mask(segment_row, half, 0, half)), (half, length, key_mask(segment_row, length, half, half)))
    log_ref[...] = jnp.zeros_like(log_ref)
    for two in range(width // 128):
        at = 128 * two
        query_two = mixed_ref[:, at : at + 128] * jnp.asarray(score_scale, bf16)
        key_two = mixed_ref[:, width + at : width + at + 128]
        value_turned = jnp.transpose(mixed_ref[:, 2 * width + at : 2 * width + at + 128])
        parts = []
        for which in range(2):
            query_rows = lane_half(query_two, which)
            value_rows = value_turned[HEAD_DIM * which : HEAD_DIM * (which + 1)]
            sides = []
            for first, keys, mask in spans:
                scores = inner_cols(key_two[:keys], query_rows[first : first + half]) + mask
                top = jnp.max(scores, axis=0, keepdims=True)
                exponent = jnp.exp(scores - top)
                total = jnp.sum(exponent, axis=0, keepdims=True)
                log_ref[2 * two + which : 2 * two + which + 1, first : first + half] = top + jnp.log(total)
                sides.append(nn(value_rows[:, :keys], exponent.astype(bf16)) / total)
            parts.append(jnp.concatenate(sides, axis=1))
        context_ref[:, at : at + 128] = jnp.transpose(jnp.concatenate(parts, axis=0)).astype(bf16)
    attended_ref[...] = inner_cols(
        context_ref[...], weight_ref[:, 3 * width : 4 * width]
    ).astype(bf16)


def store_blocks(value, place, keep_ref, send_ref, columns):
    rows = value.shape[0] // 8
    counts = [0, 0]
    for block in range(8):
        which = (block >> (2 - place)) & 1
        target = send_ref if which else keep_ref
        at = counts[which] * rows
        counts[which] += 1
        target[at : at + rows, columns] = value[block * rows : (block + 1) * rows].astype(target.dtype)


def join_blocks(turns, quarter_refs, whole_ref):
    rows = whole_ref.shape[0] // 8
    bit = [2 - PLACE[axis] for axis in turns]
    for block in range(8):
        which = ((block >> bit[1]) & 1) + 2 * ((block >> bit[2]) & 1)
        at = ((block >> bit[0]) & 1) * rows
        whole_ref[block * rows : (block + 1) * rows] = quarter_refs[which][at : at + rows]


def feed_kernel(
    rows_ref,
    own_ref,
    other_ref,
    vector_ref,
    up_0_ref,
    up_1_ref,
    up_2_ref,
    up_3_ref,
    down_0_ref,
    down_1_ref,
    down_2_ref,
    down_3_ref,
    bias_ref,
    cot_ref,
    middle_ref,
    feed_ref,
    grad_two_ref,
    up_keep_ref,
    up_send_ref,
    down_keep_ref,
    down_send_ref,
    bias_grad_ref,
    normed_ref,
    normed_turned_ref,
    cot_turned_ref,
    up_ref,
    down_ref,
    feed_sum_ref,
    grad_two_sum_ref,
):
    bf16, f32 = jnp.bfloat16, jnp.float32

    @pl.when(pl.program_id(0) == 0)
    def _():
        middle = (
            rows_ref[...].astype(f32)
            + (own_ref[...].astype(f32) + other_ref[...].astype(f32))
            + vector_ref[4:5]
        )
        middle_ref[...] = middle
        unit, _ = column_norm(middle)
        normed_ref[...] = (unit * vector_ref[1:2] + vector_ref[3:4]).astype(bf16)
        normed_turned_ref[...] = jnp.transpose(normed_ref[...])
        cot_turned_ref[...] = jnp.transpose(cot_ref[...])
        feed_sum_ref[...] = jnp.zeros_like(feed_sum_ref)
        grad_two_sum_ref[...] = jnp.zeros_like(grad_two_sum_ref)

    join_blocks(TURNS[1], (up_0_ref, up_1_ref, up_2_ref, up_3_ref), up_ref)
    join_blocks(TURNS[2], (down_0_ref, down_1_ref, down_2_ref, down_3_ref), down_ref)
    before = nn(normed_ref[...], up_ref[...]) + bias_ref[...]
    square = before * before
    bend = jnp.tanh(gelu_factor * (before + 0.044715 * before * square))
    opened = 0.5 * (1.0 + bend)
    hidden = (before * opened).astype(bf16)
    slope = opened + 0.5 * before * (1.0 - bend * bend) * (
        gelu_factor * (1.0 + 3.0 * 0.044715 * square)
    )
    grad_before = (nn(cot_ref[...], down_ref[...]) * slope).astype(bf16)
    feed_sum_ref[...] += inner_cols(hidden, down_ref[...])
    grad_two_sum_ref[...] += inner_cols(grad_before, up_ref[...])
    bias_grad_ref[...] = jnp.broadcast_to(
        jnp.sum(grad_before.astype(f32), axis=0, keepdims=True), bias_grad_ref.shape
    )
    columns = slice(0, up_ref.shape[1])
    store_blocks(nn(cot_turned_ref[...], hidden), PLACE[TURNS[2][2]], down_keep_ref, down_send_ref, columns)
    store_blocks(nn(normed_turned_ref[...], grad_before), PLACE[TURNS[1][2]], up_keep_ref, up_send_ref, columns)

    @pl.when(pl.program_id(0) == pl.num_programs(0) - 1)
    def _():
        feed_ref[...] = feed_sum_ref[...].astype(bf16)
        grad_two_ref[...] = grad_two_sum_ref[...].astype(bf16)


def attend_back_kernel(
    score_scale,
    middle_ref,
    cot_ref,
    own_ref,
    other_ref,
    vector_ref,
    context_ref,
    mixed_ref,
    log_ref,
    weight_ref,
    segment_ref,
    normed_ref,
    rows_ref,
    hidden_sums_ref,
    fold_ref,
    block_ref,
    grad_middle_ref,
    grad_one_ref,
    keep_a_ref,
    send_a_ref,
    keep_b_ref,
    send_b_ref,
    keep_c_ref,
    send_c_ref,
    grad_context_ref,
    grad_mixed_ref,
    terms_ref,
    bias_ref,
):
    bf16, f32 = jnp.bfloat16, jnp.float32
    length = middle_ref.shape[0]
    width = context_ref.shape[1]
    half = length // 2
    unit, inverse = column_norm(middle_ref[...])
    grad_norm = own_ref[...].astype(f32) + other_ref[...].astype(f32)
    scaled = grad_norm * vector_ref[1:2]
    mean_grad = jnp.mean(scaled, axis=-1, keepdims=True)
    mean_cross = jnp.mean(scaled * unit, axis=-1, keepdims=True)
    cot = cot_ref[...].astype(f32)
    grad_middle = cot + inverse * (scaled - mean_grad - unit * mean_cross)
    grad_middle_ref[...] = grad_middle
    terms_ref[...] = jnp.zeros_like(terms_ref)
    terms_ref[1:2] = 0.5 * jnp.sum(grad_norm * unit, axis=0, keepdims=True)
    terms_ref[3:4] = 0.5 * jnp.sum(grad_norm, axis=0, keepdims=True)
    terms_ref[4:5] = 0.5 * jnp.sum(grad_middle, axis=0, keepdims=True)
    terms_ref[5:6] = 0.5 * jnp.sum(cot, axis=0, keepdims=True)
    hidden_width = hidden_sums_ref.shape[1]
    bias_ref[:, :hidden_width] = hidden_sums_ref[0:1]
    middle_rows = grad_middle.astype(bf16)
    third = keep_a_ref.shape[1]
    last = keep_c_ref.shape[1]
    store_blocks(
        nn(jnp.transpose(middle_rows), context_ref[...]),
        PLACE[TURNS[2][2]],
        keep_c_ref,
        send_c_ref,
        slice(third - width, third),
    )
    grad_context_ref[...] = nn(middle_rows, weight_ref[:, 3 * width : 4 * width]).astype(bf16)
    segment_row = segment_ref[...]
    spans = ((0, half, key_mask(segment_row, half, 0, half)), (half, length, key_mask(segment_row, length, half, half)))
    for two in range(width // 128):
        at = 128 * two
        query_two = mixed_ref[:, at : at + 128] * jnp.asarray(score_scale, bf16)
        key_two = mixed_ref[:, width + at : width + at + 128]
        value_two = mixed_ref[:, 2 * width + at : 2 * width + at + 128]
        grad_two = grad_context_ref[:, at : at + 128]
        key_turned = jnp.transpose(key_two)
        grad_queries = []
        grad_keys = [0.0, 0.0]
        grad_values = [0.0, 0.0]
        for which in range(2):
            query_rows = lane_half(query_two, which)
            grad_rows = lane_half(grad_two, which)
            key_rows = key_turned[HEAD_DIM * which : HEAD_DIM * (which + 1)]
            sides = []
            for side, (first, keys, mask) in enumerate(spans):
                query_side = query_rows[first : first + half]
                grad_side = grad_rows[first : first + half]
                log_side = log_ref[2 * two + which : 2 * two + which + 1, first : first + half]
                scores = inner_cols(key_two[:keys], query_side) + mask
                soft = jnp.exp(scores - log_side)
                grad_soft = inner_cols(value_two[:keys], grad_side)
                crossed = soft * grad_soft
                grad_scores = (
                    crossed - soft * jnp.sum(crossed, axis=0, keepdims=True)
                ).astype(bf16)
                grad_keys[side] += nn(grad_scores, query_side)
                grad_values[side] += nn(soft.astype(bf16), grad_side)
                sides.append(nn(key_rows[:, :keys], grad_scores))
            grad_queries.append(jnp.concatenate(sides, axis=1))
        queries_out = jnp.transpose(jnp.concatenate(grad_queries, axis=0)) * score_scale
        for place, value in enumerate((queries_out, grad_keys, grad_values)):
            columns = slice(place * width + at, place * width + at + 128)
            if place == 0:
                grad_mixed_ref[:, columns] = value.astype(bf16)
            else:
                grad_mixed_ref[:half, columns] = (value[0] + value[1][:half]).astype(bf16)
                grad_mixed_ref[half:, columns] = value[1][half:].astype(bf16)
            if place != 1:
                start = hidden_width + (place // 2) * width + at
                bias_ref[:, start : start + 128] = jnp.sum(
                    grad_mixed_ref[:, columns].astype(f32), axis=0, keepdims=True
                )
    unit, _ = column_norm(rows_ref[...].astype(f32))
    grad_one = inner_cols(grad_mixed_ref[...], weight_ref[:, : 3 * width])
    grad_one_ref[...] = grad_one.astype(bf16)
    terms_ref[0:1] = jnp.sum(grad_one * unit, axis=0, keepdims=True)
    terms_ref[2:3] = jnp.sum(grad_one, axis=0, keepdims=True)
    row = lax.broadcasted_iota(jnp.int32, (64, bias_ref.shape[1]), 0)
    lane = lax.broadcasted_iota(jnp.int32, (64, bias_ref.shape[1]), 1)
    inside = jnp.zeros(row.shape, jnp.bool_)
    for start, size in ((0, hidden_width), (hidden_width, width), (hidden_width + width, width)):
        first = row * (size // 64) + start
        inside = inside | ((lane >= first) & (lane < first + size // 64))
    spread = jnp.where(inside, bias_ref[...], 0.0)
    for matrix_ref in (fold_ref, block_ref):
        high = spread.astype(bf16)
        rest = (spread - high.astype(f32)).astype(bf16)
        if matrix_ref is fold_ref:
            spread = nn(high, matrix_ref[...]) + nn(rest, matrix_ref[...])
        else:
            spread = nn(matrix_ref[...], high) + nn(matrix_ref[...], rest)
    store_blocks(
        jnp.transpose(terms_ref[...]) + spread,
        PLACE[TURNS[2][2]],
        keep_c_ref,
        send_c_ref,
        slice(third, last),
    )
    turned = jnp.transpose(normed_ref[...])
    targets = ((keep_a_ref, send_a_ref), (keep_b_ref, send_b_ref), (keep_c_ref, send_c_ref))
    for i, (keep_ref, send_ref) in enumerate(targets):
        size = min(third, 3 * width - i * third)
        store_blocks(
            nn(turned, grad_mixed_ref[:, i * third : i * third + size]),
            PLACE[TURNS[i][2]],
            keep_ref,
            send_ref,
            slice(0, size),
        )


def token_kernel(
    core_ref,
    rows_ref,
    own_ref,
    other_ref,
    grad_middle_ref,
    vector_ref,
    order_ref,
    token_ref,
    token_full_ref,
):
    bf16, f32 = jnp.bfloat16, jnp.float32
    half = token_ref.shape[0]
    unit, inverse = column_norm(rows_ref[...].astype(f32))
    grad_norm = own_ref[...].astype(f32) + other_ref[...].astype(f32)
    scaled = grad_norm * vector_ref[0:1]
    mean_grad = jnp.mean(scaled, axis=-1, keepdims=True)
    mean_cross = jnp.mean(scaled * unit, axis=-1, keepdims=True)
    token_full_ref[...] = (
        grad_middle_ref[...] + inverse * (scaled - mean_grad - unit * mean_cross)
    )
    start = pl.multiple_of(core_ref[0] * half, half)
    token_rows = token_full_ref[pl.ds(start, half), :].astype(bf16)
    token_ref[...] = inner_cols(token_rows, order_ref[...]).astype(bf16)


def call(kernel, outs, scratch, *operands, smem=0):
    space = [pl.BlockSpec(memory_space=pltpu.SMEM)] * smem
    space += [pl.BlockSpec(memory_space=pltpu.VMEM)] * (len(operands) - smem)
    return pl.pallas_call(
        kernel,
        out_shape=[jax.ShapeDtypeStruct(shape, kind) for shape, kind in outs],
        in_specs=space,
        out_specs=[pl.BlockSpec(memory_space=pltpu.VMEM)] * len(outs),
        scratch_shapes=[pltpu.VMEM(shape, kind) for shape, kind in scratch],
        compiler_params=pltpu.CompilerParams(vmem_limit_bytes=56 * 1024 * 1024),
    )(*operands)


def local(
    tokens,
    cotangent,
    segments,
    input_weight,
    output_weight,
    up_weight,
    down_weight,
    head_bias,
    hidden_bias,
    norm_gains,
    shifts,
):
    bf16, f32 = jnp.bfloat16, jnp.float32
    half, width = tokens.shape
    length = segments.shape[1]
    block = input_weight.shape[0]
    heads_width = input_weight.shape[2]
    hidden_width = up_weight.shape[1]
    local_heads = heads_width // HEAD_DIM
    score_scale = 1.0 / math.sqrt(HEAD_DIM)
    core = lax.axis_index("c")

    first_end = 4 * heads_width + 128
    pack_width = first_end + 2 * hidden_width
    me = (
        (lax.axis_index("zh") * 4 + lax.axis_index("xh") * 2 + lax.axis_index("h"))
        .astype(jnp.int32)
        .reshape(1)
    )
    (shard,) = call(
        pack_kernel,
        [((block, pack_width), bf16)],
        [((128, block), f32)],
        input_weight,
        output_weight.T,
        up_weight,
        down_weight.T,
        norm_gains,
        shifts,
    )
    sources = source_blocks(width)
    order = lax.optimization_barrier(feature_order(sources, width))
    blocks = block_order(sources, width)
    folds = bias_fold(hidden_width, heads_width)

    def full_rows(rows):
        return nn(lax.all_gather(swap_roles(rows), "c", axis=0, tiled=True), order).astype(bf16)

    rows = full_rows(tokens)
    cot_rows = full_rows(cotangent)

    small = swap_roles(
        jnp.concatenate(
            (head_bias.reshape(-1), hidden_bias, segments[0].astype(bf16))
        )
    )
    bias_rows = small[: 2 * heads_width].reshape(2, heads_width).astype(f32)
    hidden_row = small[2 * heads_width : 2 * heads_width + hidden_width].astype(f32)
    segment_row = small[2 * heads_width + hidden_width :].astype(f32).reshape(1, length)
    tied = (order, blocks, folds, rows, cot_rows, bias_rows, hidden_row, segment_row)
    parts, tied = lax.optimization_barrier((gather_near(shard), tied))
    order, blocks, folds, rows, cot_rows, bias_rows, hidden_row, segment_row = tied
    near = call(
        collect_kernel,
        [((8 * block, size), bf16) for size in (first_end, hidden_width, hidden_width)],
        [((8 * block, pack_width), f32)],
        me,
        *parts,
        smem=1,
    )
    first_quarters, up_quarters, down_quarters = gather_far(near)

    def own_half(rows):
        return lax.dynamic_slice_in_dim(rows, core * half, half, axis=0)

    def other_half(rows):
        return lax.dynamic_slice_in_dim(rows, (1 - core) * half, half, axis=0)

    vectors, normed_one, mixed, log_sums, context, attended, first_weight = call(
        functools.partial(attend_kernel, score_scale),
        [
            ((8, width), f32),
            ((length, width), bf16),
            ((length, 3 * heads_width), bf16),
            ((8, length), f32),
            ((length, heads_width), bf16),
            ((length, width), bf16),
            ((width, first_end), bf16),
        ],
        [],
        rows,
        *first_quarters,
        bias_rows,
        segment_row,
    )
    third = hidden_width // 3

    def whole(*shape):
        return pl.BlockSpec(shape, lambda j: (0, 0))

    def cut(rows_of):
        return pl.BlockSpec((rows_of, third), lambda j: (0, j))

    def shaped(shape, kind):
        return jax.ShapeDtypeStruct(shape, kind)

    middle, feed, grad_two, up_keep, up_send, down_keep, down_send, hidden_sums = pl.pallas_call(
        feed_kernel,
        grid=(3,),
        out_shape=[
            shaped((length, width), f32),
            shaped((length, width), bf16),
            shaped((length, width), bf16),
        ]
        + [shaped((width // 2, hidden_width), bf16)] * 4
        + [shaped((8, hidden_width), f32)],
        in_specs=[whole(length, width)] * 3
        + [whole(8, width)]
        + [cut(width // 4)] * 8
        + [cut(1), whole(length, width)],
        out_specs=[whole(length, width)] * 3 + [cut(width // 2)] * 4 + [cut(8)],
        scratch_shapes=[
            pltpu.VMEM((length, width), bf16),
            pltpu.VMEM((width, length), bf16),
            pltpu.VMEM((width, length), bf16),
            pltpu.VMEM((width, third), bf16),
            pltpu.VMEM((width, third), bf16),
            pltpu.VMEM((length, width), f32),
            pltpu.VMEM((length, width), f32),
        ],
        compiler_params=pltpu.CompilerParams(vmem_limit_bytes=56 * 1024 * 1024),
    )(
        rows,
        attended,
        pair(attended),
        vectors,
        *up_quarters,
        *down_quarters,
        hidden_row.reshape(1, hidden_width),
        cot_rows,
    )
    down_other = step_along(down_send, TURNS[2][2])
    up_other = step_along(up_send, TURNS[1][2])
    grad_two_other, feed_other = lax.optimization_barrier((pair(grad_two), pair(other_half(feed))))
    grad_middle, grad_one, *first_grads = call(
        functools.partial(attend_back_kernel, score_scale),
        [
            ((length, width), f32),
            ((length, width), bf16),
        ]
        + [((width // 2, 4 * heads_width // 3), bf16)] * 4
        + [((width // 2, 4 * heads_width // 3 + 128), bf16)] * 2,
        [
            ((length, heads_width), bf16),
            ((length, 3 * heads_width), bf16),
            ((128, width), f32),
            ((1, hidden_width + 2 * heads_width), f32),
        ],
        middle,
        cot_rows,
        grad_two,
        grad_two_other,
        vectors,
        context,
        mixed,
        log_sums,
        first_weight,
        segment_row,
        normed_one,
        rows,
        hidden_sums,
        folds,
        blocks,
    )
    first_grads, grad_one, up_other, down_other = lax.optimization_barrier(
        (first_grads, grad_one, up_other, down_other)
    )
    turn_lists = TURNS + TURNS[1:]
    pieces = [
        (keep, step_along(send, turns[2]))
        for keep, send, turns in zip(first_grads[0::2], first_grads[1::2], TURNS)
    ]
    feeds = fold(((up_keep, up_other), (down_keep, down_other)), TURNS[1:], (2, 2))
    grad_one_other = pair(grad_one)
    outcome = (
        own_half(middle)
        + own_half(feed).astype(f32)
        + feed_other.astype(f32)
        + vectors[5]
    )
    block_out = inner_cols(outcome.astype(bf16), order).astype(bf16)

    pieces, feeds, grad_one_other, block_out = lax.optimization_barrier(
        (pieces, feeds, grad_one_other, block_out)
    )
    pieces = fold(pieces + feeds, turn_lists, (2, 2, 2, 1, 1))
    (token_grad,) = call(
        token_kernel,
        [((half, width), bf16)],
        [((length, width), f32)],
        core.astype(jnp.int32).reshape(1),
        rows,
        grad_one,
        grad_one_other,
        grad_middle,
        vectors,
        order,
        smem=1,
    )
    pieces, token_grad = lax.optimization_barrier((pieces, token_grad))
    pieces = fold(pieces[:3], TURNS, (1, 1, 1)) + pieces[3:]
    operands = []
    for piece in pieces:
        operands += piece
    cross = pair(add_low(operands[4][:, -128:], operands[5][:, -128:]))
    shares = call(
        deal_kernel,
        [((2 * block, pack_width), bf16)] * 4,
        [],
        me,
        cross,
        *operands,
        smem=1,
    )
    shares, block_out, token_grad = lax.optimization_barrier((shares, block_out, token_grad))
    block_out, token_grad = swap_roles(block_out), swap_roles(token_grad)
    shares = scatter_near(shares)
    six = block // 2
    input_grad, output_grad, up_grad, down_grad, head_grad, hidden_grad, gain_grad, shift_grad = call(
        unpack_kernel,
        [
            ((block, 3, heads_width), f32),
            ((block, heads_width), f32),
            ((block, hidden_width), f32),
            ((block, hidden_width), f32),
            ((2, six), f32),
            ((1, 2 * block), f32),
            ((2, six), f32),
            ((4, six), f32),
        ],
        [],
        lax.axis_index("h").astype(jnp.int32).reshape(1),
        *shares,
        smem=1,
    )
    return (
        block_out,
        token_grad,
        input_grad,
        output_grad.T,
        up_grad,
        down_grad.T,
        head_grad,
        hidden_grad.reshape(2 * block),
        gain_grad,
        shift_grad,
    )


def solution(mesh):
    fine = Mesh(mesh.devices.reshape((2,) * 7), AXES)
    in_specs = (
        P(AXES, None),
        P(AXES, None),
        P(DP, None),
        P(DP, None, "h"),
        P("h", DP),
        P(DP, "h"),
        P("h", DP),
        P(None, "h"),
        P("h"),
        P(None, DP),
        P(None, DP),
    )
    out_specs = (
        P(AXES, None),
        P(AXES, None),
        P(DP, None, "h"),
        P("h", DP),
        P(DP, "h"),
        P("h", DP),
        P(None, ("h",) + DP),
        P(("h",) + DP),
        P(None, AXES),
        P(None, AXES),
    )
    return jax.shard_map(local, mesh=fine, in_specs=in_specs, out_specs=out_specs, check_vma=False)
```

```python
import functools
import itertools
import math

import jax
import jax.numpy as jnp
import numpy as np
from jax import lax
from jax.experimental import pallas as pl
from jax.experimental.pallas import tpu as pltpu
from jax.sharding import Mesh
from jax.sharding import PartitionSpec as P

HEAD_DIM = 64


norm_epsilon = 1e-05
masked_value = -1e30
gelu_factor = 0.7978845608028654


def inner_cols(left_side, right_side):
    return lax.dot_general(
        left_side, right_side, (((1,), (1,)), ((), ())), preferred_element_type=jnp.float32
    )


AXES = ("xh", "xl", "yl", "zh", "zl", "c", "h")
DP = AXES[:6]
RING = {"x": ("xh", "xl"), "y": ("h", "yl"), "z": ("zh", "zl")}
PLACE = {"z": 0, "y": 1, "x": 2}
TURNS = (("x", "y", "z"), ("y", "z", "x"), ("z", "x", "y"))


def swap_roles(values):
    return lax.ppermute(values, ("c", "h"), [(0, 0), (1, 2), (2, 1), (3, 3)])


def pair(values):
    return lax.ppermute(values, "c", [(0, 1), (1, 0)])


def step_along(values, axis):
    high, low = RING[axis]
    order = [name for name in AXES if name in (high, low, "c")]
    moves = []
    for place in itertools.product(range(2), repeat=3):
        target = dict(zip(order, place))
        target[low] ^= 1
        target[high] ^= target["c"]
        moves.append(
            (place[0] * 4 + place[1] * 2 + place[2], sum(target[n] << (2 - i) for i, n in enumerate(order)))
        )
    return lax.ppermute(values, tuple(order), moves)


def cross_roles(values, outward):
    moves = [(0, 1), (1, 3), (2, 0), (3, 2)]
    return lax.ppermute(values, ("c", "h"), moves if outward else [(b, a) for a, b in moves])


def flip(values, place):
    moves = []
    for xh, zh in itertools.product(range(2), repeat=2):
        moves.append((xh * 2 + zh, (xh ^ (place & 1)) * 2 + (zh ^ (place >> 1))))
    return lax.ppermute(values, ("xh", "zh"), moves)


def gather_near(shard):
    own = jnp.concatenate((swap_roles(shard), cross_roles(shard, True)), axis=0)
    return [own] + [flip(own, place) for place in range(1, 4)]


def add_low(left, right):
    return (left.astype(jnp.float32) + right.astype(jnp.float32)).astype(jnp.bfloat16)


def scatter_near(parts):
    others = [flip(part, place) for place, part in enumerate(parts) if place]
    total = parts[0].astype(jnp.float32)
    for other in others:
        total = total + other.astype(jnp.float32)
    total = total.astype(jnp.bfloat16)
    rows = total.shape[0] // 2
    return swap_roles(total[:rows]), cross_roles(total[rows:], False)


def open_blocks(piece):
    return piece.reshape((1, 1, 1) + piece.shape)


def gather_far(pieces):
    pieces = [open_blocks(piece) for piece in pieces]
    others = [step_along(piece, TURNS[i][0]) for i, piece in enumerate(pieces)]
    quarters = []
    for turns, piece, other in zip(TURNS, pieces, others):
        both = jnp.concatenate((piece, other), axis=PLACE[turns[0]])
        quarters.append(both.reshape(2 * piece.shape[3], piece.shape[4]))
    seconds = [step_along(quarter, TURNS[i][1]) for i, quarter in enumerate(quarters)]
    thirds = [step_along(quarter, TURNS[i][2]) for i, quarter in enumerate(quarters)]
    fourths = [step_along(seconds[0], TURNS[0][2])]
    seconds, thirds, fourths = lax.optimization_barrier((seconds, thirds, fourths))
    fourths += [step_along(seconds[i], TURNS[i][2]) for i in range(1, 3)]
    return list(zip(quarters, seconds, thirds, fourths))


def source_blocks(width):
    place = np.arange(width, dtype=np.int32) // (width // 64)
    near, far = place % 8, place // 8
    fixed = ((near >> 1) & 1) * 32 + (near >> 2) * 4 + (near & 1)
    xl = lax.axis_index("xl") ^ (far & 1)
    yl = lax.axis_index("yl") ^ ((far >> 1) & 1)
    zl = lax.axis_index("zl") ^ (far >> 2)
    return lax.optimization_barrier(fixed + xl * 16 + yl * 8 + zl * 2)


def feature_order(sources, width):
    block = width // 64
    inner = np.arange(width, dtype=np.int32) % block
    source = lax.optimization_barrier(sources * block + inner)
    return (lax.broadcasted_iota(jnp.int32, (width, width), 0) == source[None]).astype(jnp.bfloat16)


def block_order(sources, width):
    return (lax.broadcasted_iota(jnp.int32, (width, 64), 1) == sources[:, None]).astype(jnp.bfloat16)


def bias_fold(hidden_width, width):
    many, few = hidden_width // 64, width // 64
    target = np.concatenate(
        (
            np.arange(hidden_width) % many,
            np.arange(width) % few + many,
            np.arange(width) % few + many + few,
        )
    )
    return jnp.asarray(np.arange(128)[None] == target[:, None] + 8, jnp.bfloat16)


def place_rows(rows, me):
    block = rows // 8
    row = lax.broadcasted_iota(jnp.int32, (rows, rows), 0)
    column = lax.broadcasted_iota(jnp.int32, (rows, rows), 1)
    found = jnp.zeros((rows, rows), jnp.float32)
    for k in range(8):
        inside = (row >= k * block) & (row < (k + 1) * block)
        same = column - (me ^ k) * block == row - k * block
        found = jnp.where(inside & same, 1.0, found)
    return found.astype(jnp.bfloat16)


def eye(size):
    row = lax.broadcasted_iota(jnp.int32, (size, size), 0)
    column = lax.broadcasted_iota(jnp.int32, (size, size), 1)
    return (row == column).astype(jnp.float32).astype(jnp.bfloat16)


def pack_kernel(input_ref, output_ref, up_ref, down_ref, gains_ref, shifts_ref, shard_ref, small_ref):
    bf16 = jnp.bfloat16
    block, width = output_ref.shape
    hidden_width = up_ref.shape[1]
    for i in range(3):
        shard_ref[:, i * width : (i + 1) * width] = input_ref[:, i, :]
    shard_ref[:, 3 * width : 4 * width] = output_ref[...]
    small_ref[...] = jnp.zeros_like(small_ref)
    small_ref[0:2] = gains_ref[...].astype(jnp.float32)
    small_ref[2:6] = shifts_ref[...].astype(jnp.float32)
    at = 4 * width + 128
    shard_ref[:, 4 * width : at] = inner_cols(eye(block), small_ref[...].astype(bf16)).astype(bf16)
    shard_ref[:, at : at + hidden_width] = up_ref[...]
    shard_ref[:, at + hidden_width :] = down_ref[...]


def collect_kernel(me_ref, *refs):
    parts, outs, held_ref = refs[:4], refs[4:-1], refs[-1]
    rows = held_ref.shape[0]
    for i, part in enumerate(parts):
        held_ref[i * rows // 4 : (i + 1) * rows // 4] = part[...].astype(jnp.float32)
    moved = place_rows(rows, me_ref[0])
    at = 0
    for out in outs:
        columns = out.shape[1]
        held = held_ref[:, at : at + columns].astype(jnp.bfloat16)
        out[...] = nn(moved, held).astype(jnp.bfloat16)
        at += columns


def deal_kernel(me_ref, cross_ref, *refs):
    parts, outs = refs[:-4], refs[-4:]
    rows = parts[0].shape[0]
    moved = place_rows(rows, me_ref[0])
    at = 0
    for i, (keep, other) in enumerate(zip(parts[::2], parts[1::2])):
        columns = keep.shape[1]
        total = add_low(keep[...], other[...])
        if i == 2:
            lane = lax.broadcasted_iota(jnp.int32, cross_ref.shape, 1)
            cross = jnp.where(lane < 8, cross_ref[...].astype(jnp.float32), 0.0)
            total = jnp.concatenate((total[:, : columns - 128], add_low(total[:, columns - 128 :], cross)), axis=1)
        total = nn(moved, total)
        for i, out in enumerate(outs):
            part = total[i * rows // 4 : (i + 1) * rows // 4]
            out[:, at : at + columns] = part.astype(jnp.bfloat16)
        at += columns


def unpack_kernel(half_ref, *refs):
    parts = refs[:2]
    input_ref, output_ref, up_ref, down_ref, head_ref, hidden_ref, gain_ref, shift_ref = refs[2:]
    f32 = jnp.float32
    block, width = output_ref.shape
    hidden_width = up_ref.shape[1]
    six = block // 2

    def total(start, size):
        columns = slice(start, start + size)
        value = parts[0][:, columns].astype(f32)
        for part in parts[1:]:
            value = value + part[:, columns].astype(f32)
        return value

    def pick(rows, columns, offset):
        row = lax.broadcasted_iota(jnp.int32, (rows, columns), 0)
        column = lax.broadcasted_iota(jnp.int32, (rows, columns), 1)
        return (row == column + offset).astype(f32)

    def exact(left, right, dims):
        return lax.dot_general(
            left, right, (dims, ((), ())), precision=lax.Precision.HIGHEST, preferred_element_type=f32
        )

    for i in range(3):
        input_ref[:, i, :] = total(i * width, width)
    output_ref[...] = total(3 * width, width)
    at = 4 * width + 128
    up_ref[...] = total(at, hidden_width)
    down_ref[...] = total(at + hidden_width, hidden_width)
    small = total(4 * width, 128)
    norm_terms = exact(small, pick(block, six, half_ref[0] * six), ((0,), (0,)))
    gain_ref[...] = norm_terms[0:2]
    shift_ref[...] = norm_terms[2:6]
    hidden_ref[...] = exact(small[0:1], pick(128, 2 * block, 8), ((1,), (0,)))
    head_ref[0:1] = exact(small[0:1], pick(128, six, 8 + 2 * block), ((1,), (0,)))
    head_ref[1:2] = exact(small[0:1], pick(128, six, 8 + 2 * block + six), ((1,), (0,)))


def fold_kernel(layouts, *refs):
    ins, outs = refs[: 2 * len(layouts)], refs[2 * len(layouts) :]
    for i, (bits, place) in enumerate(layouts):
        keep_ref, other_ref = ins[2 * i : 2 * i + 2]
        rows = keep_ref.shape[0] >> bits
        counts = [0, 0]
        for block in range(1 << bits):
            which = (block >> (bits - 1 - place)) & 1
            at = counts[which] * rows
            counts[which] += 1
            span = slice(block * rows, (block + 1) * rows)
            outs[2 * i + which][at : at + rows] = add_low(keep_ref[span], other_ref[span])


def fold_apart(keep, other, turns, left):
    place = sorted(turns[:left], key=PLACE.get).index(turns[left - 1])
    rows, columns = keep.shape
    shape = (2,) * left + (rows >> left, columns)
    keep, other = keep.reshape(shape), other.reshape(shape)
    sums = []
    for i in range(2):
        part = add_low(
            lax.slice_in_dim(keep, i, i + 1, axis=place), lax.slice_in_dim(other, i, i + 1, axis=place)
        )
        sums.append(part.reshape(rows // 2, columns))
    return sums[0], step_along(sums[1], turns[left - 1])


def fold(pairs, turn_lists, turns_left):
    layouts = []
    for turns, left in zip(turn_lists, turns_left):
        place = sorted(turns[:left], key=PLACE.get).index(turns[left - 1])
        layouts.append((left, place))
    outs = []
    for keep, _ in pairs:
        outs += [((keep.shape[0] // 2, keep.shape[1]), jnp.bfloat16)] * 2
    parts = call(functools.partial(fold_kernel, layouts), outs, [], *[x for pair_of in pairs for x in pair_of])
    return [
        (keep, step_along(send, turns[left - 1]))
        for keep, send, turns, left in zip(parts[0::2], parts[1::2], turn_lists, turns_left)
    ]


def column_norm(values):
    mean_val = jnp.mean(values, axis=-1, keepdims=True)
    centered = values - mean_val
    variance = jnp.mean(centered * centered, axis=-1, keepdims=True)
    inverse = lax.rsqrt(variance + norm_epsilon)
    return centered * inverse, inverse


def nn(left, right):
    return jnp.dot(left, right, preferred_element_type=jnp.float32)


def key_mask(segment_row, keys, first, queries):
    column = jnp.transpose(jnp.broadcast_to(segment_row, (8, segment_row.shape[1])))[:keys, :1]
    row = segment_row[:, first : first + queries]
    key_pos = lax.broadcasted_iota(jnp.int32, (keys, queries), 0)
    query_pos = lax.broadcasted_iota(jnp.int32, (keys, queries), 1) + first
    return jnp.where((column == row) & (key_pos <= query_pos), 0.0, masked_value)


def lane_half(values, which):
    lane = lax.broadcasted_iota(jnp.int32, values.shape, 1)
    inside = (lane >= HEAD_DIM) if which else (lane < HEAD_DIM)
    return jnp.where(inside, values, jnp.zeros_like(values))


def attend_kernel(
    score_scale,
    rows_ref,
    quarter_0_ref,
    quarter_1_ref,
    quarter_2_ref,
    quarter_3_ref,
    bias_ref,
    segment_ref,
    vector_ref,
    normed_ref,
    mixed_ref,
    log_ref,
    context_ref,
    attended_ref,
    weight_ref,
):
    bf16 = jnp.bfloat16
    length = rows_ref.shape[0]
    width = context_ref.shape[1]
    join_blocks(TURNS[0], (quarter_0_ref, quarter_1_ref, quarter_2_ref, quarter_3_ref), weight_ref)
    vector_ref[...] = jnp.transpose(weight_ref[:, 4 * width : 4 * width + 128].astype(jnp.float32))[:8]
    half = length // 2
    unit, _ = column_norm(rows_ref[...].astype(jnp.float32))
    normed_ref[...] = (unit * vector_ref[0:1] + vector_ref[2:3]).astype(bf16)
    mixed = nn(normed_ref[...], weight_ref[:, : 3 * width])
    mixed_ref[:, :width] = (mixed[:, :width] + bias_ref[0:1]).astype(bf16)
    mixed_ref[:, width : 2 * width] = mixed[:, width : 2 * width].astype(bf16)
    mixed_ref[:, 2 * width :] = (mixed[:, 2 * width :] + bias_ref[1:2]).astype(bf16)
    segment_row = segment_ref[...]
    spans = ((0, half, key_mask(segment_row, half, 0, half)), (half, length, key_mask(segment_row, length, half, half)))
    log_ref[...] = jnp.zeros_like(log_ref)
    for two in range(width // 128):
        at = 128 * two
        query_two = mixed_ref[:, at : at + 128] * jnp.asarray(score_scale, bf16)
        key_two = mixed_ref[:, width + at : width + at + 128]
        value_turned = jnp.transpose(mixed_ref[:, 2 * width + at : 2 * width + at + 128])
        parts = []
        for which in range(2):
            query_rows = lane_half(query_two, which)
            value_rows = value_turned[HEAD_DIM * which : HEAD_DIM * (which + 1)]
            sides = []
            for first, keys, mask in spans:
                scores = inner_cols(key_two[:keys], query_rows[first : first + half]) + mask
                top = jnp.max(scores, axis=0, keepdims=True)
                exponent = jnp.exp(scores - top)
                total = jnp.sum(exponent, axis=0, keepdims=True)
                log_ref[2 * two + which : 2 * two + which + 1, first : first + half] = top + jnp.log(total)
                sides.append(nn(value_rows[:, :keys], exponent.astype(bf16)) / total)
            parts.append(jnp.concatenate(sides, axis=1))
        context_ref[:, at : at + 128] = jnp.transpose(jnp.concatenate(parts, axis=0)).astype(bf16)
    attended_ref[...] = inner_cols(
        context_ref[...], weight_ref[:, 3 * width : 4 * width]
    ).astype(bf16)


def store_blocks(value, place, keep_ref, send_ref, columns):
    rows = value.shape[0] // 8
    counts = [0, 0]
    for block in range(8):
        which = (block >> (2 - place)) & 1
        target = send_ref if which else keep_ref
        at = counts[which] * rows
        counts[which] += 1
        target[at : at + rows, columns] = value[block * rows : (block + 1) * rows].astype(target.dtype)


def join_blocks(turns, quarter_refs, whole_ref):
    rows = whole_ref.shape[0] // 8
    bit = [2 - PLACE[axis] for axis in turns]
    for block in range(8):
        which = ((block >> bit[1]) & 1) + 2 * ((block >> bit[2]) & 1)
        at = ((block >> bit[0]) & 1) * rows
        whole_ref[block * rows : (block + 1) * rows] = quarter_refs[which][at : at + rows]


def feed_kernel(
    rows_ref,
    own_ref,
    other_ref,
    vector_ref,
    up_0_ref,
    up_1_ref,
    up_2_ref,
    up_3_ref,
    down_0_ref,
    down_1_ref,
    down_2_ref,
    down_3_ref,
    bias_ref,
    cot_ref,
    middle_ref,
    feed_ref,
    grad_two_ref,
    up_keep_ref,
    up_send_ref,
    down_keep_ref,
    down_send_ref,
    bias_grad_ref,
    normed_ref,
    normed_turned_ref,
    cot_turned_ref,
    up_ref,
    down_ref,
    feed_sum_ref,
    grad_two_sum_ref,
):
    bf16, f32 = jnp.bfloat16, jnp.float32

    @pl.when(pl.program_id(0) == 0)
    def _():
        middle = (
            rows_ref[...].astype(f32)
            + (own_ref[...].astype(f32) + other_ref[...].astype(f32))
            + vector_ref[4:5]
        )
        middle_ref[...] = middle
        unit, _ = column_norm(middle)
        normed_ref[...] = (unit * vector_ref[1:2] + vector_ref[3:4]).astype(bf16)
        normed_turned_ref[...] = jnp.transpose(normed_ref[...])
        cot_turned_ref[...] = jnp.transpose(cot_ref[...])
        feed_sum_ref[...] = jnp.zeros_like(feed_sum_ref)
        grad_two_sum_ref[...] = jnp.zeros_like(grad_two_sum_ref)

    join_blocks(TURNS[1], (up_0_ref, up_1_ref, up_2_ref, up_3_ref), up_ref)
    join_blocks(TURNS[2], (down_0_ref, down_1_ref, down_2_ref, down_3_ref), down_ref)
    before = nn(normed_ref[...], up_ref[...]) + bias_ref[...]
    square = before * before
    bend = jnp.tanh(gelu_factor * (before + 0.044715 * before * square))
    opened = 0.5 * (1.0 + bend)
    hidden = (before * opened).astype(bf16)
    slope = opened + 0.5 * before * (1.0 - bend * bend) * (
        gelu_factor * (1.0 + 3.0 * 0.044715 * square)
    )
    grad_before = (nn(cot_ref[...], down_ref[...]) * slope).astype(bf16)
    feed_sum_ref[...] += inner_cols(hidden, down_ref[...])
    grad_two_sum_ref[...] += inner_cols(grad_before, up_ref[...])
    bias_grad_ref[...] = jnp.broadcast_to(
        jnp.sum(grad_before.astype(f32), axis=0, keepdims=True), bias_grad_ref.shape
    )
    columns = slice(0, up_ref.shape[1])
    store_blocks(nn(cot_turned_ref[...], hidden), PLACE[TURNS[2][2]], down_keep_ref, down_send_ref, columns)
    store_blocks(nn(normed_turned_ref[...], grad_before), PLACE[TURNS[1][2]], up_keep_ref, up_send_ref, columns)

    @pl.when(pl.program_id(0) == pl.num_programs(0) - 1)
    def _():
        feed_ref[...] = feed_sum_ref[...].astype(bf16)
        grad_two_ref[...] = grad_two_sum_ref[...].astype(bf16)


def attend_back_kernel(
    score_scale,
    middle_ref,
    cot_ref,
    own_ref,
    other_ref,
    vector_ref,
    context_ref,
    mixed_ref,
    log_ref,
    weight_ref,
    segment_ref,
    normed_ref,
    rows_ref,
    hidden_sums_ref,
    fold_ref,
    block_ref,
    grad_middle_ref,
    grad_one_ref,
    keep_a_ref,
    send_a_ref,
    keep_b_ref,
    send_b_ref,
    keep_c_ref,
    send_c_ref,
    grad_context_ref,
    grad_mixed_ref,
    terms_ref,
    bias_ref,
):
    bf16, f32 = jnp.bfloat16, jnp.float32
    length = middle_ref.shape[0]
    width = context_ref.shape[1]
    half = length // 2
    unit, inverse = column_norm(middle_ref[...])
    grad_norm = own_ref[...].astype(f32) + other_ref[...].astype(f32)
    scaled = grad_norm * vector_ref[1:2]
    mean_grad = jnp.mean(scaled, axis=-1, keepdims=True)
    mean_cross = jnp.mean(scaled * unit, axis=-1, keepdims=True)
    cot = cot_ref[...].astype(f32)
    grad_middle = cot + inverse * (scaled - mean_grad - unit * mean_cross)
    grad_middle_ref[...] = grad_middle
    terms_ref[...] = jnp.zeros_like(terms_ref)
    terms_ref[1:2] = 0.5 * jnp.sum(grad_norm * unit, axis=0, keepdims=True)
    terms_ref[3:4] = 0.5 * jnp.sum(grad_norm, axis=0, keepdims=True)
    terms_ref[4:5] = 0.5 * jnp.sum(grad_middle, axis=0, keepdims=True)
    terms_ref[5:6] = 0.5 * jnp.sum(cot, axis=0, keepdims=True)
    hidden_width = hidden_sums_ref.shape[1]
    bias_ref[:, :hidden_width] = hidden_sums_ref[0:1]
    middle_rows = grad_middle.astype(bf16)
    third = keep_a_ref.shape[1]
    last = keep_c_ref.shape[1]
    store_blocks(
        nn(jnp.transpose(middle_rows), context_ref[...]),
        PLACE[TURNS[2][2]],
        keep_c_ref,
        send_c_ref,
        slice(third - width, third),
    )
    grad_context_ref[...] = nn(middle_rows, weight_ref[:, 3 * width : 4 * width]).astype(bf16)
    segment_row = segment_ref[...]
    spans = ((0, half, key_mask(segment_row, half, 0, half)), (half, length, key_mask(segment_row, length, half, half)))
    for two in range(width // 128):
        at = 128 * two
        query_two = mixed_ref[:, at : at + 128] * jnp.asarray(score_scale, bf16)
        key_two = mixed_ref[:, width + at : width + at + 128]
        value_two = mixed_ref[:, 2 * width + at : 2 * width + at + 128]
        grad_two = grad_context_ref[:, at : at + 128]
        key_turned = jnp.transpose(key_two)
        grad_queries = []
        grad_keys = [0.0, 0.0]
        grad_values = [0.0, 0.0]
        for which in range(2):
            query_rows = lane_half(query_two, which)
            grad_rows = lane_half(grad_two, which)
            key_rows = key_turned[HEAD_DIM * which : HEAD_DIM * (which + 1)]
            sides = []
            for side, (first, keys, mask) in enumerate(spans):
                query_side = query_rows[first : first + half]
                grad_side = grad_rows[first : first + half]
                log_side = log_ref[2 * two + which : 2 * two + which + 1, first : first + half]
                scores = inner_cols(key_two[:keys], query_side) + mask
                soft = jnp.exp(scores - log_side)
                grad_soft = inner_cols(value_two[:keys], grad_side)
                crossed = soft * grad_soft
                grad_scores = (
                    crossed - soft * jnp.sum(crossed, axis=0, keepdims=True)
                ).astype(bf16)
                grad_keys[side] += nn(grad_scores, query_side)
                grad_values[side] += nn(soft.astype(bf16), grad_side)
                sides.append(nn(key_rows[:, :keys], grad_scores))
            grad_queries.append(jnp.concatenate(sides, axis=1))
        queries_out = jnp.transpose(jnp.concatenate(grad_queries, axis=0)) * score_scale
        for place, value in enumerate((queries_out, grad_keys, grad_values)):
            columns = slice(place * width + at, place * width + at + 128)
            if place == 0:
                grad_mixed_ref[:, columns] = value.astype(bf16)
            else:
                grad_mixed_ref[:half, columns] = (value[0] + value[1][:half]).astype(bf16)
                grad_mixed_ref[half:, columns] = value[1][half:].astype(bf16)
            if place != 1:
                start = hidden_width + (place // 2) * width + at
                bias_ref[:, start : start + 128] = jnp.sum(
                    grad_mixed_ref[:, columns].astype(f32), axis=0, keepdims=True
                )
    unit, _ = column_norm(rows_ref[...].astype(f32))
    grad_one = inner_cols(grad_mixed_ref[...], weight_ref[:, : 3 * width])
    grad_one_ref[...] = grad_one.astype(bf16)
    terms_ref[0:1] = jnp.sum(grad_one * unit, axis=0, keepdims=True)
    terms_ref[2:3] = jnp.sum(grad_one, axis=0, keepdims=True)
    row = lax.broadcasted_iota(jnp.int32, (64, bias_ref.shape[1]), 0)
    lane = lax.broadcasted_iota(jnp.int32, (64, bias_ref.shape[1]), 1)
    inside = jnp.zeros(row.shape, jnp.bool_)
    for start, size in ((0, hidden_width), (hidden_width, width), (hidden_width + width, width)):
        first = row * (size // 64) + start
        inside = inside | ((lane >= first) & (lane < first + size // 64))
    spread = jnp.where(inside, bias_ref[...], 0.0)
    for matrix_ref in (fold_ref, block_ref):
        high = spread.astype(bf16)
        rest = (spread - high.astype(f32)).astype(bf16)
        if matrix_ref is fold_ref:
            spread = nn(high, matrix_ref[...]) + nn(rest, matrix_ref[...])
        else:
            spread = nn(matrix_ref[...], high) + nn(matrix_ref[...], rest)
    store_blocks(
        jnp.transpose(terms_ref[...]) + spread,
        PLACE[TURNS[2][2]],
        keep_c_ref,
        send_c_ref,
        slice(third, last),
    )
    turned = jnp.transpose(normed_ref[...])
    targets = ((keep_a_ref, send_a_ref), (keep_b_ref, send_b_ref), (keep_c_ref, send_c_ref))
    for i, (keep_ref, send_ref) in enumerate(targets):
        size = min(third, 3 * width - i * third)
        store_blocks(
            nn(turned, grad_mixed_ref[:, i * third : i * third + size]),
            PLACE[TURNS[i][2]],
            keep_ref,
            send_ref,
            slice(0, size),
        )


def token_kernel(
    core_ref,
    rows_ref,
    own_ref,
    other_ref,
    grad_middle_ref,
    vector_ref,
    order_ref,
    token_ref,
    token_full_ref,
):
    bf16, f32 = jnp.bfloat16, jnp.float32
    half = token_ref.shape[0]
    unit, inverse = column_norm(rows_ref[...].astype(f32))
    grad_norm = own_ref[...].astype(f32) + other_ref[...].astype(f32)
    scaled = grad_norm * vector_ref[0:1]
    mean_grad = jnp.mean(scaled, axis=-1, keepdims=True)
    mean_cross = jnp.mean(scaled * unit, axis=-1, keepdims=True)
    token_full_ref[...] = (
        grad_middle_ref[...] + inverse * (scaled - mean_grad - unit * mean_cross)
    )
    start = pl.multiple_of(core_ref[0] * half, half)
    token_rows = token_full_ref[pl.ds(start, half), :].astype(bf16)
    token_ref[...] = inner_cols(token_rows, order_ref[...]).astype(bf16)


def work(microseconds):
    return pl.CostEstimate(flops=microseconds * 10**9, bytes_accessed=microseconds * 10**6, transcendentals=0)


def call(kernel, outs, scratch, *operands, smem=0, cost=None):
    space = [pl.BlockSpec(memory_space=pltpu.SMEM)] * smem
    space += [pl.BlockSpec(memory_space=pltpu.VMEM)] * (len(operands) - smem)
    return pl.pallas_call(
        kernel,
        out_shape=[jax.ShapeDtypeStruct(shape, kind) for shape, kind in outs],
        in_specs=space,
        out_specs=[pl.BlockSpec(memory_space=pltpu.VMEM)] * len(outs),
        scratch_shapes=[pltpu.VMEM(shape, kind) for shape, kind in scratch],
        compiler_params=pltpu.CompilerParams(vmem_limit_bytes=56 * 1024 * 1024),
        cost_estimate=None if cost is None else work(cost),
    )(*operands)


def local(
    tokens,
    cotangent,
    segments,
    input_weight,
    output_weight,
    up_weight,
    down_weight,
    head_bias,
    hidden_bias,
    norm_gains,
    shifts,
):
    bf16, f32 = jnp.bfloat16, jnp.float32
    half, width = tokens.shape
    length = segments.shape[1]
    block = input_weight.shape[0]
    heads_width = input_weight.shape[2]
    hidden_width = up_weight.shape[1]
    local_heads = heads_width // HEAD_DIM
    score_scale = 1.0 / math.sqrt(HEAD_DIM)
    core = lax.axis_index("c")

    first_end = 4 * heads_width + 128
    pack_width = first_end + 2 * hidden_width
    me = (
        (lax.axis_index("zh") * 4 + lax.axis_index("xh") * 2 + lax.axis_index("h"))
        .astype(jnp.int32)
        .reshape(1)
    )
    (shard,) = call(
        pack_kernel,
        [((block, pack_width), bf16)],
        [((128, block), f32)],
        input_weight,
        output_weight.T,
        up_weight,
        down_weight.T,
        norm_gains,
        shifts,
    )
    sources = source_blocks(width)
    order = lax.optimization_barrier(feature_order(sources, width))
    blocks = block_order(sources, width)
    folds = bias_fold(hidden_width, heads_width)

    def full_rows(rows):
        return nn(lax.all_gather(swap_roles(rows), "c", axis=0, tiled=True), order).astype(bf16)

    rows = full_rows(tokens)
    cot_rows = full_rows(cotangent)

    parts, order, blocks, folds, rows, cot_rows = lax.optimization_barrier(
        (gather_near(shard), order, blocks, folds, rows, cot_rows)
    )
    near = call(
        collect_kernel,
        [((8 * block, size), bf16) for size in (first_end, hidden_width, hidden_width)],
        [((8 * block, pack_width), f32)],
        me,
        *parts,
        smem=1,
    )
    small = swap_roles(
        jnp.concatenate(
            (head_bias.reshape(-1), hidden_bias, segments[0].astype(bf16))
        )
    )
    bias_rows = small[: 2 * heads_width].reshape(2, heads_width).astype(f32)
    hidden_row = small[2 * heads_width : 2 * heads_width + hidden_width].astype(f32)
    segment_row = small[2 * heads_width + hidden_width :].astype(f32).reshape(1, length)
    first_quarters, up_quarters, down_quarters = gather_far(near)

    def own_half(rows):
        return lax.dynamic_slice_in_dim(rows, core * half, half, axis=0)

    def other_half(rows):
        return lax.dynamic_slice_in_dim(rows, (1 - core) * half, half, axis=0)

    vectors, normed_one, mixed, log_sums, context, attended, first_weight = call(
        functools.partial(attend_kernel, score_scale),
        [
            ((8, width), f32),
            ((length, width), bf16),
            ((length, 3 * heads_width), bf16),
            ((8, length), f32),
            ((length, heads_width), bf16),
            ((length, width), bf16),
            ((width, first_end), bf16),
        ],
        [],
        rows,
        *first_quarters,
        bias_rows,
        segment_row,
        cost=9,
    )
    third = hidden_width // 3

    def whole(*shape):
        return pl.BlockSpec(shape, lambda j: (0, 0))

    def cut(rows_of):
        return pl.BlockSpec((rows_of, third), lambda j: (0, j))

    def shaped(shape, kind):
        return jax.ShapeDtypeStruct(shape, kind)

    middle, feed, grad_two, up_keep, up_send, down_keep, down_send, hidden_sums = pl.pallas_call(
        feed_kernel,
        grid=(3,),
        out_shape=[
            shaped((length, width), f32),
            shaped((length, width), bf16),
            shaped((length, width), bf16),
        ]
        + [shaped((width // 2, hidden_width), bf16)] * 4
        + [shaped((8, hidden_width), f32)],
        in_specs=[whole(length, width)] * 3
        + [whole(8, width)]
        + [cut(width // 4)] * 8
        + [cut(1), whole(length, width)],
        out_specs=[whole(length, width)] * 3 + [cut(width // 2)] * 4 + [cut(8)],
        scratch_shapes=[
            pltpu.VMEM((length, width), bf16),
            pltpu.VMEM((width, length), bf16),
            pltpu.VMEM((width, length), bf16),
            pltpu.VMEM((width, third), bf16),
            pltpu.VMEM((width, third), bf16),
            pltpu.VMEM((length, width), f32),
            pltpu.VMEM((length, width), f32),
        ],
        compiler_params=pltpu.CompilerParams(vmem_limit_bytes=56 * 1024 * 1024),
        cost_estimate=work(15),
    )(
        rows,
        attended,
        pair(attended),
        vectors,
        *up_quarters,
        *down_quarters,
        hidden_row.reshape(1, hidden_width),
        cot_rows,
    )
    down_other = step_along(down_send, TURNS[2][2])
    up_other = step_along(up_send, TURNS[1][2])
    feed_other = pair(other_half(feed))
    outcome = (
        own_half(middle)
        + own_half(feed).astype(f32)
        + feed_other.astype(f32)
        + vectors[5]
    )
    block_out = inner_cols(outcome.astype(bf16), order).astype(bf16)
    grad_two_other, block_out = lax.optimization_barrier((pair(grad_two), block_out))
    block_out = swap_roles(block_out)
    grad_middle, grad_one, *first_grads = call(
        functools.partial(attend_back_kernel, score_scale),
        [
            ((length, width), f32),
            ((length, width), bf16),
        ]
        + [((width // 2, 4 * heads_width // 3), bf16)] * 4
        + [((width // 2, 4 * heads_width // 3 + 128), bf16)] * 2,
        [
            ((length, heads_width), bf16),
            ((length, 3 * heads_width), bf16),
            ((128, width), f32),
            ((1, hidden_width + 2 * heads_width), f32),
        ],
        middle,
        cot_rows,
        grad_two,
        grad_two_other,
        vectors,
        context,
        mixed,
        log_sums,
        first_weight,
        segment_row,
        normed_one,
        rows,
        hidden_sums,
        folds,
        blocks,
        cost=16,
    )
    first_grads, grad_one, up_other, down_other = lax.optimization_barrier(
        (first_grads, grad_one, up_other, down_other)
    )
    turn_lists = TURNS + TURNS[1:]
    pieces = [
        (keep, step_along(send, turns[2]))
        for keep, send, turns in zip(first_grads[0::2], first_grads[1::2], TURNS)
    ]
    feeds = [
        fold_apart(up_keep, up_other, TURNS[1], 2),
        fold_apart(down_keep, down_other, TURNS[2], 2),
    ]
    grad_one_other = pair(grad_one)
    pieces, feeds, grad_one_other = lax.optimization_barrier((pieces, feeds, grad_one_other))
    pieces = fold(pieces + feeds, turn_lists, (2, 2, 2, 1, 1))
    (token_grad,) = call(
        token_kernel,
        [((half, width), bf16)],
        [((length, width), f32)],
        core.astype(jnp.int32).reshape(1),
        rows,
        grad_one,
        grad_one_other,
        grad_middle,
        vectors,
        order,
        smem=1,
        cost=5,
    )
    pieces, token_grad = lax.optimization_barrier((pieces, token_grad))
    pieces = [fold_apart(*piece, turns, 1) for piece, turns in zip(pieces, TURNS)] + pieces[3:]
    operands = []
    for piece in pieces:
        operands += piece
    cross = pair(add_low(operands[4][:, -128:], operands[5][:, -128:]))
    shares = call(
        deal_kernel,
        [((2 * block, pack_width), bf16)] * 4,
        [],
        me,
        cross,
        *operands,
        smem=1,
    )
    shares, token_grad = lax.optimization_barrier((shares, token_grad))
    token_grad = swap_roles(token_grad)
    shares = scatter_near(shares)
    six = block // 2
    input_grad, output_grad, up_grad, down_grad, head_grad, hidden_grad, gain_grad, shift_grad = call(
        unpack_kernel,
        [
            ((block, 3, heads_width), f32),
            ((block, heads_width), f32),
            ((block, hidden_width), f32),
            ((block, hidden_width), f32),
            ((2, six), f32),
            ((1, 2 * block), f32),
            ((2, six), f32),
            ((4, six), f32),
        ],
        [],
        lax.axis_index("h").astype(jnp.int32).reshape(1),
        *shares,
        smem=1,
    )
    return (
        block_out,
        token_grad,
        input_grad,
        output_grad.T,
        up_grad,
        down_grad.T,
        head_grad,
        hidden_grad.reshape(2 * block),
        gain_grad,
        shift_grad,
    )


def solution(mesh):
    fine = Mesh(mesh.devices.reshape((2,) * 7), AXES)
    in_specs = (
        P(AXES, None),
        P(AXES, None),
        P(DP, None),
        P(DP, None, "h"),
        P("h", DP),
        P(DP, "h"),
        P("h", DP),
        P(None, "h"),
        P("h"),
        P(None, DP),
        P(None, DP),
    )
    out_specs = (
        P(AXES, None),
        P(AXES, None),
        P(DP, None, "h"),
        P("h", DP),
        P(DP, "h"),
        P("h", DP),
        P(None, ("h",) + DP),
        P(("h",) + DP),
        P(None, AXES),
        P(None, AXES),
    )
    return jax.shard_map(local, mesh=fine, in_specs=in_specs, out_specs=out_specs, check_vma=False)
```

```python
import functools
import itertools
import math

import jax
import jax.numpy as jnp
import numpy as np
from jax import lax
from jax.experimental import pallas as pl
from jax.experimental.pallas import tpu as pltpu
from jax.sharding import Mesh
from jax.sharding import PartitionSpec as P

HEAD_DIM = 64


norm_epsilon = 1e-05
masked_value = -1e30
gelu_factor = 0.7978845608028654


def inner_cols(left_side, right_side):
    return lax.dot_general(
        left_side, right_side, (((1,), (1,)), ((), ())), preferred_element_type=jnp.float32
    )


AXES = ("xh", "xl", "yl", "zh", "zl", "c", "h")
DP = AXES[:6]
RING = {"x": ("xh", "xl"), "y": ("h", "yl"), "z": ("zh", "zl")}
PLACE = {"z": 0, "y": 1, "x": 2}
TURNS = (("x", "y", "z"), ("y", "z", "x"), ("z", "x", "y"))


def swap_roles(values):
    return lax.ppermute(values, ("c", "h"), [(0, 0), (1, 2), (2, 1), (3, 3)])


def pair(values):
    return lax.ppermute(values, "c", [(0, 1), (1, 0)])


def step_along(values, axis):
    high, low = RING[axis]
    order = [name for name in AXES if name in (high, low, "c")]
    moves = []
    for place in itertools.product(range(2), repeat=3):
        target = dict(zip(order, place))
        target[low] ^= 1
        target[high] ^= target["c"]
        moves.append(
            (place[0] * 4 + place[1] * 2 + place[2], sum(target[n] << (2 - i) for i, n in enumerate(order)))
        )
    return lax.ppermute(values, tuple(order), moves)


def cross_roles(values, outward):
    moves = [(0, 1), (1, 3), (2, 0), (3, 2)]
    return lax.ppermute(values, ("c", "h"), moves if outward else [(b, a) for a, b in moves])


def flip(values, place):
    moves = []
    for xh, zh in itertools.product(range(2), repeat=2):
        moves.append((xh * 2 + zh, (xh ^ (place & 1)) * 2 + (zh ^ (place >> 1))))
    return lax.ppermute(values, ("xh", "zh"), moves)


def gather_near(shard):
    own = jnp.concatenate((swap_roles(shard), cross_roles(shard, True)), axis=0)
    return [own] + [flip(own, place) for place in range(1, 4)]


def add_low(left, right):
    return (left.astype(jnp.float32) + right.astype(jnp.float32)).astype(jnp.bfloat16)


def scatter_near(parts):
    others = [flip(part, place) for place, part in enumerate(parts) if place]
    total = parts[0].astype(jnp.float32)
    for other in others:
        total = total + other.astype(jnp.float32)
    total = total.astype(jnp.bfloat16)
    rows = total.shape[0] // 2
    return swap_roles(total[:rows]), cross_roles(total[rows:], False)


def open_blocks(piece):
    return piece.reshape((1, 1, 1) + piece.shape)


def gather_far(pieces):
    pieces = [open_blocks(piece) for piece in pieces]
    others = [step_along(piece, TURNS[i][0]) for i, piece in enumerate(pieces)]
    others = lax.optimization_barrier(others)
    quarters = []
    for turns, piece, other in zip(TURNS, pieces, others):
        both = jnp.concatenate((piece, other), axis=PLACE[turns[0]])
        quarters.append(both.reshape(2 * piece.shape[3], piece.shape[4]))
    seconds = [step_along(quarter, TURNS[i][1]) for i, quarter in enumerate(quarters)]
    thirds = [step_along(quarter, TURNS[i][2]) for i, quarter in enumerate(quarters)]
    fourths = [step_along(second, TURNS[i][2]) for i, second in enumerate(seconds)]
    return list(zip(quarters, seconds, thirds, fourths))


def source_blocks(width):
    place = np.arange(width, dtype=np.int32) // (width // 64)
    near, far = place % 8, place // 8
    fixed = ((near >> 1) & 1) * 32 + (near >> 2) * 4 + (near & 1)
    xl = lax.axis_index("xl") ^ (far & 1)
    yl = lax.axis_index("yl") ^ ((far >> 1) & 1)
    zl = lax.axis_index("zl") ^ (far >> 2)
    return lax.optimization_barrier(fixed + xl * 16 + yl * 8 + zl * 2)


def feature_order(sources, width):
    block = width // 64
    inner = np.arange(width, dtype=np.int32) % block
    source = lax.optimization_barrier(sources * block + inner)
    return (lax.broadcasted_iota(jnp.int32, (width, width), 0) == source[None]).astype(jnp.bfloat16)


def block_order(sources, width):
    return (lax.broadcasted_iota(jnp.int32, (width, 64), 1) == sources[:, None]).astype(jnp.bfloat16)


def bias_fold(hidden_width, width):
    many, few = hidden_width // 64, width // 64
    target = np.concatenate(
        (
            np.arange(hidden_width) % many,
            np.arange(width) % few + many,
            np.arange(width) % few + many + few,
        )
    )
    return jnp.asarray(np.arange(128)[None] == target[:, None] + 8, jnp.bfloat16)


def place_rows(rows, me):
    block = rows // 8
    row = lax.broadcasted_iota(jnp.int32, (rows, rows), 0)
    column = lax.broadcasted_iota(jnp.int32, (rows, rows), 1)
    found = jnp.zeros((rows, rows), jnp.float32)
    for k in range(8):
        inside = (row >= k * block) & (row < (k + 1) * block)
        same = column - (me ^ k) * block == row - k * block
        found = jnp.where(inside & same, 1.0, found)
    return found.astype(jnp.bfloat16)


def eye(size):
    row = lax.broadcasted_iota(jnp.int32, (size, size), 0)
    column = lax.broadcasted_iota(jnp.int32, (size, size), 1)
    return (row == column).astype(jnp.float32).astype(jnp.bfloat16)


def pack_kernel(input_ref, output_ref, up_ref, down_ref, gains_ref, shifts_ref, shard_ref, small_ref):
    bf16 = jnp.bfloat16
    block, width = output_ref.shape
    hidden_width = up_ref.shape[1]
    for i in range(3):
        shard_ref[:, i * width : (i + 1) * width] = input_ref[:, i, :]
    shard_ref[:, 3 * width : 4 * width] = output_ref[...]
    small_ref[...] = jnp.zeros_like(small_ref)
    small_ref[0:2] = gains_ref[...].astype(jnp.float32)
    small_ref[2:6] = shifts_ref[...].astype(jnp.float32)
    at = 4 * width + 128
    shard_ref[:, 4 * width : at] = inner_cols(eye(block), small_ref[...].astype(bf16)).astype(bf16)
    shard_ref[:, at : at + hidden_width] = up_ref[...]
    shard_ref[:, at + hidden_width :] = down_ref[...]


def collect_kernel(me_ref, *refs):
    parts, outs, held_ref = refs[:4], refs[4:-1], refs[-1]
    rows = held_ref.shape[0]
    for i, part in enumerate(parts):
        held_ref[i * rows // 4 : (i + 1) * rows // 4] = part[...].astype(jnp.float32)
    moved = place_rows(rows, me_ref[0])
    at = 0
    for out in outs:
        columns = out.shape[1]
        held = held_ref[:, at : at + columns].astype(jnp.bfloat16)
        out[...] = nn(moved, held).astype(jnp.bfloat16)
        at += columns


def deal_kernel(me_ref, cross_ref, *refs):
    parts, outs = refs[:-4], refs[-4:]
    rows = parts[0].shape[0]
    moved = place_rows(rows, me_ref[0])
    at = 0
    for i, (keep, other) in enumerate(zip(parts[::2], parts[1::2])):
        columns = keep.shape[1]
        total = add_low(keep[...], other[...])
        if i == 2:
            lane = lax.broadcasted_iota(jnp.int32, cross_ref.shape, 1)
            cross = jnp.where(lane < 8, cross_ref[...].astype(jnp.float32), 0.0)
            total = jnp.concatenate((total[:, : columns - 128], add_low(total[:, columns - 128 :], cross)), axis=1)
        total = nn(moved, total)
        for i, out in enumerate(outs):
            part = total[i * rows // 4 : (i + 1) * rows // 4]
            out[:, at : at + columns] = part.astype(jnp.bfloat16)
        at += columns


def unpack_kernel(half_ref, *refs):
    parts = refs[:2]
    input_ref, output_ref, up_ref, down_ref, head_ref, hidden_ref, gain_ref, shift_ref = refs[2:]
    f32 = jnp.float32
    block, width = output_ref.shape
    hidden_width = up_ref.shape[1]
    six = block // 2

    def total(start, size):
        columns = slice(start, start + size)
        value = parts[0][:, columns].astype(f32)
        for part in parts[1:]:
            value = value + part[:, columns].astype(f32)
        return value

    def pick(rows, columns, offset):
        row = lax.broadcasted_iota(jnp.int32, (rows, columns), 0)
        column = lax.broadcasted_iota(jnp.int32, (rows, columns), 1)
        return (row == column + offset).astype(f32)

    def exact(left, right, dims):
        return lax.dot_general(
            left, right, (dims, ((), ())), precision=lax.Precision.HIGHEST, preferred_element_type=f32
        )

    for i in range(3):
        input_ref[:, i, :] = total(i * width, width)
    output_ref[...] = total(3 * width, width)
    at = 4 * width + 128
    up_ref[...] = total(at, hidden_width)
    down_ref[...] = total(at + hidden_width, hidden_width)
    small = total(4 * width, 128)
    norm_terms = exact(small, pick(block, six, half_ref[0] * six), ((0,), (0,)))
    gain_ref[...] = norm_terms[0:2]
    shift_ref[...] = norm_terms[2:6]
    hidden_ref[...] = exact(small[0:1], pick(128, 2 * block, 8), ((1,), (0,)))
    head_ref[0:1] = exact(small[0:1], pick(128, six, 8 + 2 * block), ((1,), (0,)))
    head_ref[1:2] = exact(small[0:1], pick(128, six, 8 + 2 * block + six), ((1,), (0,)))


def fold_kernel(layouts, *refs):
    ins, outs = refs[: 2 * len(layouts)], refs[2 * len(layouts) :]
    for i, (bits, place) in enumerate(layouts):
        keep_ref, other_ref = ins[2 * i : 2 * i + 2]
        rows = keep_ref.shape[0] >> bits
        counts = [0, 0]
        for block in range(1 << bits):
            which = (block >> (bits - 1 - place)) & 1
            at = counts[which] * rows
            counts[which] += 1
            span = slice(block * rows, (block + 1) * rows)
            outs[2 * i + which][at : at + rows] = add_low(keep_ref[span], other_ref[span])


def fold_apart(keep, other, turns, left):
    place = sorted(turns[:left], key=PLACE.get).index(turns[left - 1])
    rows, columns = keep.shape
    shape = (2,) * left + (rows >> left, columns)
    keep, other = keep.reshape(shape), other.reshape(shape)
    sums = []
    for i in range(2):
        part = add_low(
            lax.slice_in_dim(keep, i, i + 1, axis=place), lax.slice_in_dim(other, i, i + 1, axis=place)
        )
        sums.append(part.reshape(rows // 2, columns))
    return sums


def fold(pairs, turn_lists, turns_left):
    layouts = []
    for turns, left in zip(turn_lists, turns_left):
        place = sorted(turns[:left], key=PLACE.get).index(turns[left - 1])
        layouts.append((left, place))
    outs = []
    for keep, _ in pairs:
        outs += [((keep.shape[0] // 2, keep.shape[1]), jnp.bfloat16)] * 2
    parts = call(functools.partial(fold_kernel, layouts), outs, [], *[x for pair_of in pairs for x in pair_of])
    return [
        (keep, step_along(send, turns[left - 1]))
        for keep, send, turns, left in zip(parts[0::2], parts[1::2], turn_lists, turns_left)
    ]


def column_norm(values):
    mean_val = jnp.mean(values, axis=-1, keepdims=True)
    centered = values - mean_val
    variance = jnp.mean(centered * centered, axis=-1, keepdims=True)
    inverse = lax.rsqrt(variance + norm_epsilon)
    return centered * inverse, inverse


def nn(left, right):
    return jnp.dot(left, right, preferred_element_type=jnp.float32)


def key_mask(segment_row, keys, first, queries):
    column = jnp.transpose(jnp.broadcast_to(segment_row, (8, segment_row.shape[1])))[:keys, :1]
    row = segment_row[:, first : first + queries]
    key_pos = lax.broadcasted_iota(jnp.int32, (keys, queries), 0)
    query_pos = lax.broadcasted_iota(jnp.int32, (keys, queries), 1) + first
    return jnp.where((column == row) & (key_pos <= query_pos), 0.0, masked_value)


def lane_half(values, which):
    lane = lax.broadcasted_iota(jnp.int32, values.shape, 1)
    inside = (lane >= HEAD_DIM) if which else (lane < HEAD_DIM)
    return jnp.where(inside, values, jnp.zeros_like(values))


def attend_kernel(
    score_scale,
    rows_ref,
    quarter_0_ref,
    quarter_1_ref,
    quarter_2_ref,
    quarter_3_ref,
    bias_ref,
    segment_ref,
    vector_ref,
    normed_ref,
    mixed_ref,
    log_ref,
    context_ref,
    attended_ref,
    weight_ref,
):
    bf16 = jnp.bfloat16
    length = rows_ref.shape[0]
    width = context_ref.shape[1]
    join_blocks(TURNS[0], (quarter_0_ref, quarter_1_ref, quarter_2_ref, quarter_3_ref), weight_ref)
    vector_ref[...] = jnp.transpose(weight_ref[:, 4 * width : 4 * width + 128].astype(jnp.float32))[:8]
    half = length // 2
    unit, _ = column_norm(rows_ref[...].astype(jnp.float32))
    normed_ref[...] = (unit * vector_ref[0:1] + vector_ref[2:3]).astype(bf16)
    mixed = nn(normed_ref[...], weight_ref[:, : 3 * width])
    mixed_ref[:, :width] = (mixed[:, :width] + bias_ref[0:1]).astype(bf16)
    mixed_ref[:, width : 2 * width] = mixed[:, width : 2 * width].astype(bf16)
    mixed_ref[:, 2 * width :] = (mixed[:, 2 * width :] + bias_ref[1:2]).astype(bf16)
    segment_row = segment_ref[...]
    spans = ((0, half, key_mask(segment_row, half, 0, half)), (half, length, key_mask(segment_row, length, half, half)))
    log_ref[...] = jnp.zeros_like(log_ref)
    for two in range(width // 128):
        at = 128 * two
        query_two = mixed_ref[:, at : at + 128] * jnp.asarray(score_scale, bf16)
        key_two = mixed_ref[:, width + at : width + at + 128]
        value_turned = jnp.transpose(mixed_ref[:, 2 * width + at : 2 * width + at + 128])
        parts = []
        for which in range(2):
            query_rows = lane_half(query_two, which)
            value_rows = value_turned[HEAD_DIM * which : HEAD_DIM * (which + 1)]
            sides = []
            for first, keys, mask in spans:
                scores = inner_cols(key_two[:keys], query_rows[first : first + half]) + mask
                top = jnp.max(scores, axis=0, keepdims=True)
                exponent = jnp.exp(scores - top)
                total = jnp.sum(exponent, axis=0, keepdims=True)
                log_ref[2 * two + which : 2 * two + which + 1, first : first + half] = top + jnp.log(total)
                sides.append(nn(value_rows[:, :keys], exponent.astype(bf16)) / total)
            parts.append(jnp.concatenate(sides, axis=1))
        context_ref[:, at : at + 128] = jnp.transpose(jnp.concatenate(parts, axis=0)).astype(bf16)
    attended_ref[...] = inner_cols(
        context_ref[...], weight_ref[:, 3 * width : 4 * width]
    ).astype(bf16)


def store_blocks(value, place, keep_ref, send_ref, columns):
    rows = value.shape[0] // 8
    counts = [0, 0]
    for block in range(8):
        which = (block >> (2 - place)) & 1
        target = send_ref if which else keep_ref
        at = counts[which] * rows
        counts[which] += 1
        target[at : at + rows, columns] = value[block * rows : (block + 1) * rows].astype(target.dtype)


def join_blocks(turns, quarter_refs, whole_ref):
    rows = whole_ref.shape[0] // 8
    bit = [2 - PLACE[axis] for axis in turns]
    for block in range(8):
        which = ((block >> bit[1]) & 1) + 2 * ((block >> bit[2]) & 1)
        at = ((block >> bit[0]) & 1) * rows
        whole_ref[block * rows : (block + 1) * rows] = quarter_refs[which][at : at + rows]


def feed_kernel(
    rows_ref,
    own_ref,
    other_ref,
    vector_ref,
    up_0_ref,
    up_1_ref,
    up_2_ref,
    up_3_ref,
    down_0_ref,
    down_1_ref,
    down_2_ref,
    down_3_ref,
    bias_ref,
    cot_ref,
    middle_ref,
    feed_ref,
    grad_two_ref,
    up_keep_ref,
    up_send_ref,
    down_keep_ref,
    down_send_ref,
    bias_grad_ref,
    normed_ref,
    normed_turned_ref,
    cot_turned_ref,
    up_ref,
    down_ref,
    feed_sum_ref,
    grad_two_sum_ref,
):
    bf16, f32 = jnp.bfloat16, jnp.float32

    @pl.when(pl.program_id(0) == 0)
    def _():
        middle = (
            rows_ref[...].astype(f32)
            + (own_ref[...].astype(f32) + other_ref[...].astype(f32))
            + vector_ref[4:5]
        )
        middle_ref[...] = middle
        unit, _ = column_norm(middle)
        normed_ref[...] = (unit * vector_ref[1:2] + vector_ref[3:4]).astype(bf16)
        normed_turned_ref[...] = jnp.transpose(normed_ref[...])
        cot_turned_ref[...] = jnp.transpose(cot_ref[...])
        feed_sum_ref[...] = jnp.zeros_like(feed_sum_ref)
        grad_two_sum_ref[...] = jnp.zeros_like(grad_two_sum_ref)

    join_blocks(TURNS[1], (up_0_ref, up_1_ref, up_2_ref, up_3_ref), up_ref)
    join_blocks(TURNS[2], (down_0_ref, down_1_ref, down_2_ref, down_3_ref), down_ref)
    before = nn(normed_ref[...], up_ref[...]) + bias_ref[...]
    square = before * before
    bend = jnp.tanh(gelu_factor * (before + 0.044715 * before * square))
    opened = 0.5 * (1.0 + bend)
    hidden = (before * opened).astype(bf16)
    slope = opened + 0.5 * before * (1.0 - bend * bend) * (
        gelu_factor * (1.0 + 3.0 * 0.044715 * square)
    )
    grad_before = (nn(cot_ref[...], down_ref[...]) * slope).astype(bf16)
    feed_sum_ref[...] += inner_cols(hidden, down_ref[...])
    grad_two_sum_ref[...] += inner_cols(grad_before, up_ref[...])
    bias_grad_ref[...] = jnp.broadcast_to(
        jnp.sum(grad_before.astype(f32), axis=0, keepdims=True), bias_grad_ref.shape
    )
    columns = slice(0, up_ref.shape[1])
    store_blocks(nn(cot_turned_ref[...], hidden), PLACE[TURNS[2][2]], down_keep_ref, down_send_ref, columns)
    store_blocks(nn(normed_turned_ref[...], grad_before), PLACE[TURNS[1][2]], up_keep_ref, up_send_ref, columns)

    @pl.when(pl.program_id(0) == pl.num_programs(0) - 1)
    def _():
        feed_ref[...] = feed_sum_ref[...].astype(bf16)
        grad_two_ref[...] = grad_two_sum_ref[...].astype(bf16)


def attend_back_kernel(
    score_scale,
    middle_ref,
    cot_ref,
    own_ref,
    other_ref,
    vector_ref,
    context_ref,
    mixed_ref,
    log_ref,
    weight_ref,
    segment_ref,
    normed_ref,
    rows_ref,
    hidden_sums_ref,
    fold_ref,
    block_ref,
    grad_middle_ref,
    grad_one_ref,
    keep_a_ref,
    send_a_ref,
    keep_b_ref,
    send_b_ref,
    keep_c_ref,
    send_c_ref,
    grad_context_ref,
    grad_mixed_ref,
    terms_ref,
    bias_ref,
):
    bf16, f32 = jnp.bfloat16, jnp.float32
    length = middle_ref.shape[0]
    width = context_ref.shape[1]
    half = length // 2
    unit, inverse = column_norm(middle_ref[...])
    grad_norm = own_ref[...].astype(f32) + other_ref[...].astype(f32)
    scaled = grad_norm * vector_ref[1:2]
    mean_grad = jnp.mean(scaled, axis=-1, keepdims=True)
    mean_cross = jnp.mean(scaled * unit, axis=-1, keepdims=True)
    cot = cot_ref[...].astype(f32)
    grad_middle = cot + inverse * (scaled - mean_grad - unit * mean_cross)
    grad_middle_ref[...] = grad_middle
    terms_ref[...] = jnp.zeros_like(terms_ref)
    terms_ref[1:2] = 0.5 * jnp.sum(grad_norm * unit, axis=0, keepdims=True)
    terms_ref[3:4] = 0.5 * jnp.sum(grad_norm, axis=0, keepdims=True)
    terms_ref[4:5] = 0.5 * jnp.sum(grad_middle, axis=0, keepdims=True)
    terms_ref[5:6] = 0.5 * jnp.sum(cot, axis=0, keepdims=True)
    hidden_width = hidden_sums_ref.shape[1]
    bias_ref[:, :hidden_width] = hidden_sums_ref[0:1]
    middle_rows = grad_middle.astype(bf16)
    third = keep_a_ref.shape[1]
    last = keep_c_ref.shape[1]
    store_blocks(
        nn(jnp.transpose(middle_rows), context_ref[...]),
        PLACE[TURNS[2][2]],
        keep_c_ref,
        send_c_ref,
        slice(third - width, third),
    )
    grad_context_ref[...] = nn(middle_rows, weight_ref[:, 3 * width : 4 * width]).astype(bf16)
    segment_row = segment_ref[...]
    spans = ((0, half, key_mask(segment_row, half, 0, half)), (half, length, key_mask(segment_row, length, half, half)))
    for two in range(width // 128):
        at = 128 * two
        query_two = mixed_ref[:, at : at + 128] * jnp.asarray(score_scale, bf16)
        key_two = mixed_ref[:, width + at : width + at + 128]
        value_two = mixed_ref[:, 2 * width + at : 2 * width + at + 128]
        grad_two = grad_context_ref[:, at : at + 128]
        key_turned = jnp.transpose(key_two)
        grad_queries = []
        grad_keys = [0.0, 0.0]
        grad_values = [0.0, 0.0]
        for which in range(2):
            query_rows = lane_half(query_two, which)
            grad_rows = lane_half(grad_two, which)
            key_rows = key_turned[HEAD_DIM * which : HEAD_DIM * (which + 1)]
            sides = []
            for side, (first, keys, mask) in enumerate(spans):
                query_side = query_rows[first : first + half]
                grad_side = grad_rows[first : first + half]
                log_side = log_ref[2 * two + which : 2 * two + which + 1, first : first + half]
                scores = inner_cols(key_two[:keys], query_side) + mask
                soft = jnp.exp(scores - log_side)
                grad_soft = inner_cols(value_two[:keys], grad_side)
                crossed = soft * grad_soft
                grad_scores = (
                    crossed - soft * jnp.sum(crossed, axis=0, keepdims=True)
                ).astype(bf16)
                grad_keys[side] += nn(grad_scores, query_side)
                grad_values[side] += nn(soft.astype(bf16), grad_side)
                sides.append(nn(key_rows[:, :keys], grad_scores))
            grad_queries.append(jnp.concatenate(sides, axis=1))
        queries_out = jnp.transpose(jnp.concatenate(grad_queries, axis=0)) * score_scale
        for place, value in enumerate((queries_out, grad_keys, grad_values)):
            columns = slice(place * width + at, place * width + at + 128)
            if place == 0:
                grad_mixed_ref[:, columns] = value.astype(bf16)
            else:
                grad_mixed_ref[:half, columns] = (value[0] + value[1][:half]).astype(bf16)
                grad_mixed_ref[half:, columns] = value[1][half:].astype(bf16)
            if place != 1:
                start = hidden_width + (place // 2) * width + at
                bias_ref[:, start : start + 128] = jnp.sum(
                    grad_mixed_ref[:, columns].astype(f32), axis=0, keepdims=True
                )
    unit, _ = column_norm(rows_ref[...].astype(f32))
    grad_one = inner_cols(grad_mixed_ref[...], weight_ref[:, : 3 * width])
    grad_one_ref[...] = grad_one.astype(bf16)
    terms_ref[0:1] = jnp.sum(grad_one * unit, axis=0, keepdims=True)
    terms_ref[2:3] = jnp.sum(grad_one, axis=0, keepdims=True)
    row = lax.broadcasted_iota(jnp.int32, (64, bias_ref.shape[1]), 0)
    lane = lax.broadcasted_iota(jnp.int32, (64, bias_ref.shape[1]), 1)
    inside = jnp.zeros(row.shape, jnp.bool_)
    for start, size in ((0, hidden_width), (hidden_width, width), (hidden_width + width, width)):
        first = row * (size // 64) + start
        inside = inside | ((lane >= first) & (lane < first + size // 64))
    spread = jnp.where(inside, bias_ref[...], 0.0)
    for matrix_ref in (fold_ref, block_ref):
        high = spread.astype(bf16)
        rest = (spread - high.astype(f32)).astype(bf16)
        if matrix_ref is fold_ref:
            spread = nn(high, matrix_ref[...]) + nn(rest, matrix_ref[...])
        else:
            spread = nn(matrix_ref[...], high) + nn(matrix_ref[...], rest)
    store_blocks(
        jnp.transpose(terms_ref[...]) + spread,
        PLACE[TURNS[2][2]],
        keep_c_ref,
        send_c_ref,
        slice(third, last),
    )
    turned = jnp.transpose(normed_ref[...])
    targets = ((keep_a_ref, send_a_ref), (keep_b_ref, send_b_ref), (keep_c_ref, send_c_ref))
    for i, (keep_ref, send_ref) in enumerate(targets):
        size = min(third, 3 * width - i * third)
        store_blocks(
            nn(turned, grad_mixed_ref[:, i * third : i * third + size]),
            PLACE[TURNS[i][2]],
            keep_ref,
            send_ref,
            slice(0, size),
        )


def token_kernel(
    core_ref,
    rows_ref,
    own_ref,
    other_ref,
    grad_middle_ref,
    vector_ref,
    order_ref,
    token_ref,
    token_full_ref,
):
    bf16, f32 = jnp.bfloat16, jnp.float32
    half = token_ref.shape[0]
    unit, inverse = column_norm(rows_ref[...].astype(f32))
    grad_norm = own_ref[...].astype(f32) + other_ref[...].astype(f32)
    scaled = grad_norm * vector_ref[0:1]
    mean_grad = jnp.mean(scaled, axis=-1, keepdims=True)
    mean_cross = jnp.mean(scaled * unit, axis=-1, keepdims=True)
    token_full_ref[...] = (
        grad_middle_ref[...] + inverse * (scaled - mean_grad - unit * mean_cross)
    )
    start = pl.multiple_of(core_ref[0] * half, half)
    token_rows = token_full_ref[pl.ds(start, half), :].astype(bf16)
    token_ref[...] = inner_cols(token_rows, order_ref[...]).astype(bf16)


def call(kernel, outs, scratch, *operands, smem=0):
    space = [pl.BlockSpec(memory_space=pltpu.SMEM)] * smem
    space += [pl.BlockSpec(memory_space=pltpu.VMEM)] * (len(operands) - smem)
    return pl.pallas_call(
        kernel,
        out_shape=[jax.ShapeDtypeStruct(shape, kind) for shape, kind in outs],
        in_specs=space,
        out_specs=[pl.BlockSpec(memory_space=pltpu.VMEM)] * len(outs),
        scratch_shapes=[pltpu.VMEM(shape, kind) for shape, kind in scratch],
        compiler_params=pltpu.CompilerParams(vmem_limit_bytes=56 * 1024 * 1024),
    )(*operands)


def local(
    tokens,
    cotangent,
    segments,
    input_weight,
    output_weight,
    up_weight,
    down_weight,
    head_bias,
    hidden_bias,
    norm_gains,
    shifts,
):
    bf16, f32 = jnp.bfloat16, jnp.float32
    half, width = tokens.shape
    length = segments.shape[1]
    block = input_weight.shape[0]
    heads_width = input_weight.shape[2]
    hidden_width = up_weight.shape[1]
    local_heads = heads_width // HEAD_DIM
    score_scale = 1.0 / math.sqrt(HEAD_DIM)
    core = lax.axis_index("c")

    first_end = 4 * heads_width + 128
    pack_width = first_end + 2 * hidden_width
    me = (
        (lax.axis_index("zh") * 4 + lax.axis_index("xh") * 2 + lax.axis_index("h"))
        .astype(jnp.int32)
        .reshape(1)
    )
    (shard,) = call(
        pack_kernel,
        [((block, pack_width), bf16)],
        [((128, block), f32)],
        input_weight,
        output_weight.T,
        up_weight,
        down_weight.T,
        norm_gains,
        shifts,
    )
    sources = source_blocks(width)
    order = lax.optimization_barrier(feature_order(sources, width))
    blocks = block_order(sources, width)
    folds = bias_fold(hidden_width, heads_width)

    def full_rows(rows):
        return nn(lax.all_gather(swap_roles(rows), "c", axis=0, tiled=True), order).astype(bf16)

    rows = full_rows(tokens)
    cot_rows = full_rows(cotangent)

    parts, order, blocks, folds, rows, cot_rows = lax.optimization_barrier(
        (gather_near(shard), order, blocks, folds, rows, cot_rows)
    )
    near = call(
        collect_kernel,
        [((8 * block, size), bf16) for size in (first_end, hidden_width, hidden_width)],
        [((8 * block, pack_width), f32)],
        me,
        *parts,
        smem=1,
    )
    small = swap_roles(
        jnp.concatenate(
            (head_bias.reshape(-1), hidden_bias, segments[0].astype(bf16))
        )
    )
    bias_rows = small[: 2 * heads_width].reshape(2, heads_width).astype(f32)
    hidden_row = small[2 * heads_width : 2 * heads_width + hidden_width].astype(f32)
    segment_row = small[2 * heads_width + hidden_width :].astype(f32).reshape(1, length)
    first_quarters, up_quarters, down_quarters = gather_far(near)

    def own_half(rows):
        return lax.dynamic_slice_in_dim(rows, core * half, half, axis=0)

    def other_half(rows):
        return lax.dynamic_slice_in_dim(rows, (1 - core) * half, half, axis=0)

    vectors, normed_one, mixed, log_sums, context, attended, first_weight = call(
        functools.partial(attend_kernel, score_scale),
        [
            ((8, width), f32),
            ((length, width), bf16),
            ((length, 3 * heads_width), bf16),
            ((8, length), f32),
            ((length, heads_width), bf16),
            ((length, width), bf16),
            ((width, first_end), bf16),
        ],
        [],
        rows,
        *first_quarters,
        bias_rows,
        segment_row,
    )
    third = hidden_width // 3

    def whole(*shape):
        return pl.BlockSpec(shape, lambda j: (0, 0))

    def cut(rows_of):
        return pl.BlockSpec((rows_of, third), lambda j: (0, j))

    def shaped(shape, kind):
        return jax.ShapeDtypeStruct(shape, kind)

    middle, feed, grad_two, up_keep, up_send, down_keep, down_send, hidden_sums = pl.pallas_call(
        feed_kernel,
        grid=(3,),
        out_shape=[
            shaped((length, width), f32),
            shaped((length, width), bf16),
            shaped((length, width), bf16),
        ]
        + [shaped((width // 2, hidden_width), bf16)] * 4
        + [shaped((8, hidden_width), f32)],
        in_specs=[whole(length, width)] * 3
        + [whole(8, width)]
        + [cut(width // 4)] * 8
        + [cut(1), whole(length, width)],
        out_specs=[whole(length, width)] * 3 + [cut(width // 2)] * 4 + [cut(8)],
        scratch_shapes=[
            pltpu.VMEM((length, width), bf16),
            pltpu.VMEM((width, length), bf16),
            pltpu.VMEM((width, length), bf16),
            pltpu.VMEM((width, third), bf16),
            pltpu.VMEM((width, third), bf16),
            pltpu.VMEM((length, width), f32),
            pltpu.VMEM((length, width), f32),
        ],
        compiler_params=pltpu.CompilerParams(vmem_limit_bytes=56 * 1024 * 1024),
    )(
        rows,
        attended,
        pair(attended),
        vectors,
        *up_quarters,
        *down_quarters,
        hidden_row.reshape(1, hidden_width),
        cot_rows,
    )
    down_other = step_along(down_send, TURNS[2][2])
    up_other = step_along(up_send, TURNS[1][2])
    feed_other = pair(other_half(feed))
    outcome = (
        own_half(middle)
        + own_half(feed).astype(f32)
        + feed_other.astype(f32)
        + vectors[5]
    )
    block_out = inner_cols(outcome.astype(bf16), order).astype(bf16)
    grad_two_other, block_out = lax.optimization_barrier((pair(grad_two), block_out))
    grad_middle, grad_one, *first_grads = call(
        functools.partial(attend_back_kernel, score_scale),
        [
            ((length, width), f32),
            ((length, width), bf16),
        ]
        + [((width // 2, 4 * heads_width // 3), bf16)] * 4
        + [((width // 2, 4 * heads_width // 3 + 128), bf16)] * 2,
        [
            ((length, heads_width), bf16),
            ((length, 3 * heads_width), bf16),
            ((128, width), f32),
            ((1, hidden_width + 2 * heads_width), f32),
        ],
        middle,
        cot_rows,
        grad_two,
        grad_two_other,
        vectors,
        context,
        mixed,
        log_sums,
        first_weight,
        segment_row,
        normed_one,
        rows,
        hidden_sums,
        folds,
        blocks,
    )
    first_grads, grad_one, up_other, down_other = lax.optimization_barrier(
        (first_grads, grad_one, up_other, down_other)
    )
    turn_lists = TURNS + TURNS[1:]
    pieces = [
        (keep, step_along(send, turns[2]))
        for keep, send, turns in zip(first_grads[0::2], first_grads[1::2], TURNS)
    ]
    feeds = [
        fold_apart(up_keep, up_other, TURNS[1], 2),
        fold_apart(down_keep, down_other, TURNS[2], 2),
    ]
    grad_one_other = pair(grad_one)
    block_out = swap_roles(block_out)
    pieces, feeds, grad_one_other, block_out = lax.optimization_barrier(
        (pieces, feeds, grad_one_other, block_out)
    )
    pieces = fold(pieces, TURNS, (2, 2, 2))
    feeds = [(keep, step_along(send, turns[1])) for (keep, send), turns in zip(feeds, TURNS[1:])]
    (token_grad,) = call(
        token_kernel,
        [((half, width), bf16)],
        [((length, width), f32)],
        core.astype(jnp.int32).reshape(1),
        rows,
        grad_one,
        grad_one_other,
        grad_middle,
        vectors,
        order,
        smem=1,
    )
    pieces, feeds, token_grad = lax.optimization_barrier((pieces, feeds, token_grad))
    pieces = [
        (keep, step_along(send, turns[0]))
        for turns, (keep, send) in (
            (turns, fold_apart(*piece, turns, 1)) for piece, turns in zip(pieces + feeds, turn_lists)
        )
    ]
    operands = []
    for piece in pieces:
        operands += piece
    cross = pair(add_low(operands[4][:, -128:], operands[5][:, -128:]))
    shares = call(
        deal_kernel,
        [((2 * block, pack_width), bf16)] * 4,
        [],
        me,
        cross,
        *operands,
        smem=1,
    )
    shares, token_grad = lax.optimization_barrier((shares, token_grad))
    token_grad = swap_roles(token_grad)
    shares = scatter_near(shares)
    six = block // 2
    input_grad, output_grad, up_grad, down_grad, head_grad, hidden_grad, gain_grad, shift_grad = call(
        unpack_kernel,
        [
            ((block, 3, heads_width), f32),
            ((block, heads_width), f32),
            ((block, hidden_width), f32),
            ((block, hidden_width), f32),
            ((2, six), f32),
            ((1, 2 * block), f32),
            ((2, six), f32),
            ((4, six), f32),
        ],
        [],
        lax.axis_index("h").astype(jnp.int32).reshape(1),
        *shares,
        smem=1,
    )
    return (
        block_out,
        token_grad,
        input_grad,
        output_grad.T,
        up_grad,
        down_grad.T,
        head_grad,
        hidden_grad.reshape(2 * block),
        gain_grad,
        shift_grad,
    )


def solution(mesh):
    fine = Mesh(mesh.devices.reshape((2,) * 7), AXES)
    in_specs = (
        P(AXES, None),
        P(AXES, None),
        P(DP, None),
        P(DP, None, "h"),
        P("h", DP),
        P(DP, "h"),
        P("h", DP),
        P(None, "h"),
        P("h"),
        P(None, DP),
        P(None, DP),
    )
    out_specs = (
        P(AXES, None),
        P(AXES, None),
        P(DP, None, "h"),
        P("h", DP),
        P(DP, "h"),
        P("h", DP),
        P(None, ("h",) + DP),
        P(("h",) + DP),
        P(None, AXES),
        P(None, AXES),
    )
    return jax.shard_map(local, mesh=fine, in_specs=in_specs, out_specs=out_specs, check_vma=False)
```

```python
import functools
import itertools
import math

import jax
import jax.numpy as jnp
import numpy as np
from jax import lax
from jax.experimental import pallas as pl
from jax.experimental.pallas import tpu as pltpu
from jax.sharding import Mesh
from jax.sharding import PartitionSpec as P

HEAD_DIM = 64


norm_epsilon = 1e-05
masked_value = -1e30
gelu_factor = 0.7978845608028654


def inner_cols(left_side, right_side):
    return lax.dot_general(
        left_side, right_side, (((1,), (1,)), ((), ())), preferred_element_type=jnp.float32
    )


AXES = ("xh", "xl", "yl", "zh", "zl", "c", "h")
DP = AXES[:6]
RING = {"x": ("xh", "xl"), "y": ("h", "yl"), "z": ("zh", "zl")}
PLACE = {"z": 0, "y": 1, "x": 2}
TURNS = (("x", "y", "z"), ("y", "z", "x"), ("z", "x", "y"))


def swap_roles(values):
    return lax.ppermute(values, ("c", "h"), [(0, 0), (1, 2), (2, 1), (3, 3)])


def pair(values):
    return lax.ppermute(values, "c", [(0, 1), (1, 0)])


def step_along(values, axis):
    high, low = RING[axis]
    order = [name for name in AXES if name in (high, low, "c")]
    moves = []
    for place in itertools.product(range(2), repeat=3):
        target = dict(zip(order, place))
        target[low] ^= 1
        target[high] ^= target["c"]
        moves.append(
            (place[0] * 4 + place[1] * 2 + place[2], sum(target[n] << (2 - i) for i, n in enumerate(order)))
        )
    return lax.ppermute(values, tuple(order), moves)


def cross_roles(values, outward):
    moves = [(0, 1), (1, 3), (2, 0), (3, 2)]
    return lax.ppermute(values, ("c", "h"), moves if outward else [(b, a) for a, b in moves])


def flip(values, place):
    moves = []
    for xh, zh in itertools.product(range(2), repeat=2):
        moves.append((xh * 2 + zh, (xh ^ (place & 1)) * 2 + (zh ^ (place >> 1))))
    return lax.ppermute(values, ("xh", "zh"), moves)


def gather_near(shard):
    own = jnp.concatenate((swap_roles(shard), cross_roles(shard, True)), axis=0)
    return [own] + [flip(own, place) for place in range(1, 4)]


def add_low(left, right):
    return (left.astype(jnp.float32) + right.astype(jnp.float32)).astype(jnp.bfloat16)


def scatter_near(parts):
    others = [flip(part, place) for place, part in enumerate(parts) if place]
    total = parts[0].astype(jnp.float32)
    for other in others:
        total = total + other.astype(jnp.float32)
    total = total.astype(jnp.bfloat16)
    rows = total.shape[0] // 2
    return swap_roles(total[:rows]), cross_roles(total[rows:], False)


def open_blocks(piece):
    return piece.reshape((1, 1, 1) + piece.shape)


def gather_far(pieces):
    pieces = [open_blocks(piece) for piece in pieces]

    def joined(piece, other, axis):
        return jnp.concatenate((piece, other), axis=PLACE[axis])

    def flat(piece):
        return piece.reshape(-1, piece.shape[4])

    others = [step_along(piece, TURNS[i][0]) for i, piece in enumerate(pieces)]
    others = lax.optimization_barrier(others)
    pieces = [joined(piece, other, TURNS[i][0]) for i, (piece, other) in enumerate(zip(pieces, others))]
    others = [step_along(piece, TURNS[i][1]) for i, piece in enumerate(pieces)]
    first = [flat(pieces[0]), flat(others[0])]
    first += [step_along(part, TURNS[0][2]) for part in first]
    wholes = [joined(pieces[i], others[i], TURNS[i][1]) for i in (1, 2)]
    others = [flat(step_along(whole, TURNS[i][2])) for i, whole in zip((1, 2), wholes)]
    first, wholes = lax.optimization_barrier((first, wholes))
    return first, (flat(wholes[0]), others[0]), (flat(wholes[1]), others[1])


def source_blocks(width):
    place = np.arange(width, dtype=np.int32) // (width // 64)
    near, far = place % 8, place // 8
    fixed = ((near >> 1) & 1) * 32 + (near >> 2) * 4 + (near & 1)
    xl = lax.axis_index("xl") ^ (far & 1)
    yl = lax.axis_index("yl") ^ ((far >> 1) & 1)
    zl = lax.axis_index("zl") ^ (far >> 2)
    return lax.optimization_barrier(fixed + xl * 16 + yl * 8 + zl * 2)


def feature_order(sources, width):
    block = width // 64
    inner = np.arange(width, dtype=np.int32) % block
    source = lax.optimization_barrier(sources * block + inner)
    return (lax.broadcasted_iota(jnp.int32, (width, width), 0) == source[None]).astype(jnp.bfloat16)


def block_order(sources, width):
    return (lax.broadcasted_iota(jnp.int32, (width, 64), 1) == sources[:, None]).astype(jnp.bfloat16)


def bias_fold(hidden_width, width):
    many, few = hidden_width // 64, width // 64
    target = np.concatenate(
        (
            np.arange(hidden_width) % many,
            np.arange(width) % few + many,
            np.arange(width) % few + many + few,
        )
    )
    return jnp.asarray(np.arange(128)[None] == target[:, None] + 8, jnp.bfloat16)


def place_rows(rows, me):
    block = rows // 8
    row = lax.broadcasted_iota(jnp.int32, (rows, rows), 0)
    column = lax.broadcasted_iota(jnp.int32, (rows, rows), 1)
    found = jnp.zeros((rows, rows), jnp.float32)
    for k in range(8):
        inside = (row >= k * block) & (row < (k + 1) * block)
        same = column - (me ^ k) * block == row - k * block
        found = jnp.where(inside & same, 1.0, found)
    return found.astype(jnp.bfloat16)


def eye(size):
    row = lax.broadcasted_iota(jnp.int32, (size, size), 0)
    column = lax.broadcasted_iota(jnp.int32, (size, size), 1)
    return (row == column).astype(jnp.float32).astype(jnp.bfloat16)


def pack_kernel(input_ref, output_ref, up_ref, down_ref, gains_ref, shifts_ref, shard_ref, small_ref):
    bf16 = jnp.bfloat16
    block, width = output_ref.shape
    hidden_width = up_ref.shape[1]
    for i in range(3):
        shard_ref[:, i * width : (i + 1) * width] = input_ref[:, i, :]
    shard_ref[:, 3 * width : 4 * width] = output_ref[...]
    small_ref[...] = jnp.zeros_like(small_ref)
    small_ref[0:2] = gains_ref[...].astype(jnp.float32)
    small_ref[2:6] = shifts_ref[...].astype(jnp.float32)
    at = 4 * width + 128
    shard_ref[:, 4 * width : at] = inner_cols(eye(block), small_ref[...].astype(bf16)).astype(bf16)
    shard_ref[:, at : at + hidden_width] = up_ref[...]
    shard_ref[:, at + hidden_width :] = down_ref[...]


def collect_kernel(me_ref, *refs):
    parts, outs, held_ref = refs[:4], refs[4:-1], refs[-1]
    rows = held_ref.shape[0]
    for i, part in enumerate(parts):
        held_ref[i * rows // 4 : (i + 1) * rows // 4] = part[...].astype(jnp.float32)
    moved = place_rows(rows, me_ref[0])
    at = 0
    for out in outs:
        columns = out.shape[1]
        held = held_ref[:, at : at + columns].astype(jnp.bfloat16)
        out[...] = nn(moved, held).astype(jnp.bfloat16)
        at += columns


def deal_kernel(me_ref, cross_ref, *refs):
    parts, outs = refs[:-4], refs[-4:]
    rows = parts[0].shape[0]
    moved = place_rows(rows, me_ref[0])
    at = 0
    for i, (keep, other) in enumerate(zip(parts[::2], parts[1::2])):
        columns = keep.shape[1]
        total = add_low(keep[...], other[...])
        if i == 2:
            lane = lax.broadcasted_iota(jnp.int32, cross_ref.shape, 1)
            cross = jnp.where(lane < 8, cross_ref[...].astype(jnp.float32), 0.0)
            total = jnp.concatenate((total[:, : columns - 128], add_low(total[:, columns - 128 :], cross)), axis=1)
        total = nn(moved, total)
        for i, out in enumerate(outs):
            part = total[i * rows // 4 : (i + 1) * rows // 4]
            out[:, at : at + columns] = part.astype(jnp.bfloat16)
        at += columns


def unpack_kernel(half_ref, *refs):
    parts = refs[:2]
    input_ref, output_ref, up_ref, down_ref, head_ref, hidden_ref, gain_ref, shift_ref = refs[2:]
    f32 = jnp.float32
    block, width = output_ref.shape
    hidden_width = up_ref.shape[1]
    six = block // 2

    def total(start, size):
        columns = slice(start, start + size)
        value = parts[0][:, columns].astype(f32)
        for part in parts[1:]:
            value = value + part[:, columns].astype(f32)
        return value

    def pick(rows, columns, offset):
        row = lax.broadcasted_iota(jnp.int32, (rows, columns), 0)
        column = lax.broadcasted_iota(jnp.int32, (rows, columns), 1)
        return (row == column + offset).astype(f32)

    def exact(left, right, dims):
        return lax.dot_general(
            left, right, (dims, ((), ())), precision=lax.Precision.HIGHEST, preferred_element_type=f32
        )

    for i in range(3):
        input_ref[:, i, :] = total(i * width, width)
    output_ref[...] = total(3 * width, width)
    at = 4 * width + 128
    up_ref[...] = total(at, hidden_width)
    down_ref[...] = total(at + hidden_width, hidden_width)
    small = total(4 * width, 128)
    norm_terms = exact(small, pick(block, six, half_ref[0] * six), ((0,), (0,)))
    gain_ref[...] = norm_terms[0:2]
    shift_ref[...] = norm_terms[2:6]
    hidden_ref[...] = exact(small[0:1], pick(128, 2 * block, 8), ((1,), (0,)))
    head_ref[0:1] = exact(small[0:1], pick(128, six, 8 + 2 * block), ((1,), (0,)))
    head_ref[1:2] = exact(small[0:1], pick(128, six, 8 + 2 * block + six), ((1,), (0,)))


def fold_kernel(layouts, *refs):
    ins, outs = refs[: 2 * len(layouts)], refs[2 * len(layouts) :]
    for i, (bits, place) in enumerate(layouts):
        keep_ref, other_ref = ins[2 * i : 2 * i + 2]
        rows = keep_ref.shape[0] >> bits
        counts = [0, 0]
        for block in range(1 << bits):
            which = (block >> (bits - 1 - place)) & 1
            at = counts[which] * rows
            counts[which] += 1
            span = slice(block * rows, (block + 1) * rows)
            outs[2 * i + which][at : at + rows] = add_low(keep_ref[span], other_ref[span])


def fold_apart(keep, other, turns, left):
    place = sorted(turns[:left], key=PLACE.get).index(turns[left - 1])
    rows, columns = keep.shape
    shape = (2,) * left + (rows >> left, columns)
    keep, other = keep.reshape(shape), other.reshape(shape)
    sums = []
    for i in range(2):
        part = add_low(
            lax.slice_in_dim(keep, i, i + 1, axis=place), lax.slice_in_dim(other, i, i + 1, axis=place)
        )
        sums.append(part.reshape(rows // 2, columns))
    return sums


def fold(pairs, turn_lists, turns_left):
    layouts = []
    for turns, left in zip(turn_lists, turns_left):
        place = sorted(turns[:left], key=PLACE.get).index(turns[left - 1])
        layouts.append((left, place))
    outs = []
    for keep, _ in pairs:
        outs += [((keep.shape[0] // 2, keep.shape[1]), jnp.bfloat16)] * 2
    parts = call(functools.partial(fold_kernel, layouts), outs, [], *[x for pair_of in pairs for x in pair_of])
    return [
        (keep, step_along(send, turns[left - 1]))
        for keep, send, turns, left in zip(parts[0::2], parts[1::2], turn_lists, turns_left)
    ]


def column_norm(values):
    mean_val = jnp.mean(values, axis=-1, keepdims=True)
    centered = values - mean_val
    variance = jnp.mean(centered * centered, axis=-1, keepdims=True)
    inverse = lax.rsqrt(variance + norm_epsilon)
    return centered * inverse, inverse


def nn(left, right):
    return jnp.dot(left, right, preferred_element_type=jnp.float32)


def key_mask(segment_row, keys, first, queries):
    column = jnp.transpose(jnp.broadcast_to(segment_row, (8, segment_row.shape[1])))[:keys, :1]
    row = segment_row[:, first : first + queries]
    key_pos = lax.broadcasted_iota(jnp.int32, (keys, queries), 0)
    query_pos = lax.broadcasted_iota(jnp.int32, (keys, queries), 1) + first
    return jnp.where((column == row) & (key_pos <= query_pos), 0.0, masked_value)


def lane_half(values, which):
    lane = lax.broadcasted_iota(jnp.int32, values.shape, 1)
    inside = (lane >= HEAD_DIM) if which else (lane < HEAD_DIM)
    return jnp.where(inside, values, jnp.zeros_like(values))


def attend_kernel(
    score_scale,
    rows_ref,
    quarter_0_ref,
    quarter_1_ref,
    quarter_2_ref,
    quarter_3_ref,
    bias_ref,
    segment_ref,
    vector_ref,
    normed_ref,
    mixed_ref,
    log_ref,
    context_ref,
    attended_ref,
    weight_ref,
):
    bf16 = jnp.bfloat16
    length = rows_ref.shape[0]
    width = context_ref.shape[1]
    join_blocks(TURNS[0], (quarter_0_ref, quarter_1_ref, quarter_2_ref, quarter_3_ref), weight_ref)
    vector_ref[...] = jnp.transpose(weight_ref[:, 4 * width : 4 * width + 128].astype(jnp.float32))[:8]
    half = length // 2
    unit, _ = column_norm(rows_ref[...].astype(jnp.float32))
    normed_ref[...] = (unit * vector_ref[0:1] + vector_ref[2:3]).astype(bf16)
    mixed = nn(normed_ref[...], weight_ref[:, : 3 * width])
    mixed_ref[:, :width] = (mixed[:, :width] + bias_ref[0:1]).astype(bf16)
    mixed_ref[:, width : 2 * width] = mixed[:, width : 2 * width].astype(bf16)
    mixed_ref[:, 2 * width :] = (mixed[:, 2 * width :] + bias_ref[1:2]).astype(bf16)
    segment_row = segment_ref[...]
    spans = ((0, half, key_mask(segment_row, half, 0, half)), (half, length, key_mask(segment_row, length, half, half)))
    log_ref[...] = jnp.zeros_like(log_ref)
    for two in range(width // 128):
        at = 128 * two
        query_two = mixed_ref[:, at : at + 128] * jnp.asarray(score_scale, bf16)
        key_two = mixed_ref[:, width + at : width + at + 128]
        value_turned = jnp.transpose(mixed_ref[:, 2 * width + at : 2 * width + at + 128])
        parts = []
        for which in range(2):
            query_rows = lane_half(query_two, which)
            value_rows = value_turned[HEAD_DIM * which : HEAD_DIM * (which + 1)]
            sides = []
            for first, keys, mask in spans:
                scores = inner_cols(key_two[:keys], query_rows[first : first + half]) + mask
                top = jnp.max(scores, axis=0, keepdims=True)
                exponent = jnp.exp(scores - top)
                total = jnp.sum(exponent, axis=0, keepdims=True)
                log_ref[2 * two + which : 2 * two + which + 1, first : first + half] = top + jnp.log(total)
                sides.append(nn(value_rows[:, :keys], exponent.astype(bf16)) / total)
            parts.append(jnp.concatenate(sides, axis=1))
        context_ref[:, at : at + 128] = jnp.transpose(jnp.concatenate(parts, axis=0)).astype(bf16)
    attended_ref[...] = inner_cols(
        context_ref[...], weight_ref[:, 3 * width : 4 * width]
    ).astype(bf16)


def store_blocks(value, place, keep_ref, send_ref, columns):
    rows = value.shape[0] // 8
    counts = [0, 0]
    for block in range(8):
        which = (block >> (2 - place)) & 1
        target = send_ref if which else keep_ref
        at = counts[which] * rows
        counts[which] += 1
        target[at : at + rows, columns] = value[block * rows : (block + 1) * rows].astype(target.dtype)


def join_blocks(turns, quarter_refs, whole_ref):
    rows = whole_ref.shape[0] // 8
    bit = [2 - PLACE[axis] for axis in turns]
    for block in range(8):
        which = ((block >> bit[1]) & 1) + 2 * ((block >> bit[2]) & 1)
        at = ((block >> bit[0]) & 1) * rows
        whole_ref[block * rows : (block + 1) * rows] = quarter_refs[which][at : at + rows]


def join_halves(place, half_refs, whole_ref):
    rows = whole_ref.shape[0] // 8
    counts = [0, 0]
    for block in range(8):
        which = (block >> (2 - place)) & 1
        at = counts[which] * rows
        counts[which] += 1
        whole_ref[block * rows : (block + 1) * rows] = half_refs[which][at : at + rows]


def feed_kernel(
    rows_ref,
    own_ref,
    other_ref,
    vector_ref,
    up_mine_ref,
    up_other_ref,
    down_mine_ref,
    down_other_ref,
    bias_ref,
    cot_ref,
    middle_ref,
    feed_ref,
    grad_two_ref,
    up_keep_ref,
    up_send_ref,
    down_keep_ref,
    down_send_ref,
    bias_grad_ref,
    normed_ref,
    normed_turned_ref,
    cot_turned_ref,
    up_ref,
    down_ref,
    feed_sum_ref,
    grad_two_sum_ref,
):
    bf16, f32 = jnp.bfloat16, jnp.float32

    @pl.when(pl.program_id(0) == 0)
    def _():
        middle = (
            rows_ref[...].astype(f32)
            + (own_ref[...].astype(f32) + other_ref[...].astype(f32))
            + vector_ref[4:5]
        )
        middle_ref[...] = middle
        unit, _ = column_norm(middle)
        normed_ref[...] = (unit * vector_ref[1:2] + vector_ref[3:4]).astype(bf16)
        normed_turned_ref[...] = jnp.transpose(normed_ref[...])
        cot_turned_ref[...] = jnp.transpose(cot_ref[...])
        feed_sum_ref[...] = jnp.zeros_like(feed_sum_ref)
        grad_two_sum_ref[...] = jnp.zeros_like(grad_two_sum_ref)

    join_halves(PLACE[TURNS[1][2]], (up_mine_ref, up_other_ref), up_ref)
    join_halves(PLACE[TURNS[2][2]], (down_mine_ref, down_other_ref), down_ref)
    before = nn(normed_ref[...], up_ref[...]) + bias_ref[...]
    square = before * before
    bend = jnp.tanh(gelu_factor * (before + 0.044715 * before * square))
    opened = 0.5 * (1.0 + bend)
    hidden = (before * opened).astype(bf16)
    slope = opened + 0.5 * before * (1.0 - bend * bend) * (
        gelu_factor * (1.0 + 3.0 * 0.044715 * square)
    )
    grad_before = (nn(cot_ref[...], down_ref[...]) * slope).astype(bf16)
    feed_sum_ref[...] += inner_cols(hidden, down_ref[...])
    grad_two_sum_ref[...] += inner_cols(grad_before, up_ref[...])
    bias_grad_ref[...] = jnp.broadcast_to(
        jnp.sum(grad_before.astype(f32), axis=0, keepdims=True), bias_grad_ref.shape
    )
    columns = slice(0, up_ref.shape[1])
    store_blocks(nn(cot_turned_ref[...], hidden), PLACE[TURNS[2][2]], down_keep_ref, down_send_ref, columns)
    store_blocks(nn(normed_turned_ref[...], grad_before), PLACE[TURNS[1][2]], up_keep_ref, up_send_ref, columns)

    @pl.when(pl.program_id(0) == pl.num_programs(0) - 1)
    def _():
        feed_ref[...] = feed_sum_ref[...].astype(bf16)
        grad_two_ref[...] = grad_two_sum_ref[...].astype(bf16)


def attend_back_kernel(
    score_scale,
    middle_ref,
    cot_ref,
    own_ref,
    other_ref,
    vector_ref,
    context_ref,
    mixed_ref,
    log_ref,
    weight_ref,
    segment_ref,
    normed_ref,
    rows_ref,
    hidden_sums_ref,
    fold_ref,
    block_ref,
    grad_middle_ref,
    grad_one_ref,
    keep_a_ref,
    send_a_ref,
    keep_b_ref,
    send_b_ref,
    keep_c_ref,
    send_c_ref,
    grad_context_ref,
    grad_mixed_ref,
    terms_ref,
    bias_ref,
):
    bf16, f32 = jnp.bfloat16, jnp.float32
    length = middle_ref.shape[0]
    width = context_ref.shape[1]
    half = length // 2
    unit, inverse = column_norm(middle_ref[...])
    grad_norm = own_ref[...].astype(f32) + other_ref[...].astype(f32)
    scaled = grad_norm * vector_ref[1:2]
    mean_grad = jnp.mean(scaled, axis=-1, keepdims=True)
    mean_cross = jnp.mean(scaled * unit, axis=-1, keepdims=True)
    cot = cot_ref[...].astype(f32)
    grad_middle = cot + inverse * (scaled - mean_grad - unit * mean_cross)
    grad_middle_ref[...] = grad_middle
    terms_ref[...] = jnp.zeros_like(terms_ref)
    terms_ref[1:2] = 0.5 * jnp.sum(grad_norm * unit, axis=0, keepdims=True)
    terms_ref[3:4] = 0.5 * jnp.sum(grad_norm, axis=0, keepdims=True)
    terms_ref[4:5] = 0.5 * jnp.sum(grad_middle, axis=0, keepdims=True)
    terms_ref[5:6] = 0.5 * jnp.sum(cot, axis=0, keepdims=True)
    hidden_width = hidden_sums_ref.shape[1]
    bias_ref[:, :hidden_width] = hidden_sums_ref[0:1]
    middle_rows = grad_middle.astype(bf16)
    third = keep_a_ref.shape[1]
    last = keep_c_ref.shape[1]
    store_blocks(
        nn(jnp.transpose(middle_rows), context_ref[...]),
        PLACE[TURNS[2][2]],
        keep_c_ref,
        send_c_ref,
        slice(third - width, third),
    )
    grad_context_ref[...] = nn(middle_rows, weight_ref[:, 3 * width : 4 * width]).astype(bf16)
    segment_row = segment_ref[...]
    spans = ((0, half, key_mask(segment_row, half, 0, half)), (half, length, key_mask(segment_row, length, half, half)))
    for two in range(width // 128):
        at = 128 * two
        query_two = mixed_ref[:, at : at + 128] * jnp.asarray(score_scale, bf16)
        key_two = mixed_ref[:, width + at : width + at + 128]
        value_two = mixed_ref[:, 2 * width + at : 2 * width + at + 128]
        grad_two = grad_context_ref[:, at : at + 128]
        key_turned = jnp.transpose(key_two)
        grad_queries = []
        grad_keys = [0.0, 0.0]
        grad_values = [0.0, 0.0]
        for which in range(2):
            query_rows = lane_half(query_two, which)
            grad_rows = lane_half(grad_two, which)
            key_rows = key_turned[HEAD_DIM * which : HEAD_DIM * (which + 1)]
            sides = []
            for side, (first, keys, mask) in enumerate(spans):
                query_side = query_rows[first : first + half]
                grad_side = grad_rows[first : first + half]
                log_side = log_ref[2 * two + which : 2 * two + which + 1, first : first + half]
                scores = inner_cols(key_two[:keys], query_side) + mask
                soft = jnp.exp(scores - log_side)
                grad_soft = inner_cols(value_two[:keys], grad_side)
                crossed = soft * grad_soft
                grad_scores = (
                    crossed - soft * jnp.sum(crossed, axis=0, keepdims=True)
                ).astype(bf16)
                grad_keys[side] += nn(grad_scores, query_side)
                grad_values[side] += nn(soft.astype(bf16), grad_side)
                sides.append(nn(key_rows[:, :keys], grad_scores))
            grad_queries.append(jnp.concatenate(sides, axis=1))
        queries_out = jnp.transpose(jnp.concatenate(grad_queries, axis=0)) * score_scale
        for place, value in enumerate((queries_out, grad_keys, grad_values)):
            columns = slice(place * width + at, place * width + at + 128)
            if place == 0:
                grad_mixed_ref[:, columns] = value.astype(bf16)
            else:
                grad_mixed_ref[:half, columns] = (value[0] + value[1][:half]).astype(bf16)
                grad_mixed_ref[half:, columns] = value[1][half:].astype(bf16)
            if place != 1:
                start = hidden_width + (place // 2) * width + at
                bias_ref[:, start : start + 128] = jnp.sum(
                    grad_mixed_ref[:, columns].astype(f32), axis=0, keepdims=True
                )
    unit, _ = column_norm(rows_ref[...].astype(f32))
    grad_one = inner_cols(grad_mixed_ref[...], weight_ref[:, : 3 * width])
    grad_one_ref[...] = grad_one.astype(bf16)
    terms_ref[0:1] = jnp.sum(grad_one * unit, axis=0, keepdims=True)
    terms_ref[2:3] = jnp.sum(grad_one, axis=0, keepdims=True)
    row = lax.broadcasted_iota(jnp.int32, (64, bias_ref.shape[1]), 0)
    lane = lax.broadcasted_iota(jnp.int32, (64, bias_ref.shape[1]), 1)
    inside = jnp.zeros(row.shape, jnp.bool_)
    for start, size in ((0, hidden_width), (hidden_width, width), (hidden_width + width, width)):
        first = row * (size // 64) + start
        inside = inside | ((lane >= first) & (lane < first + size // 64))
    spread = jnp.where(inside, bias_ref[...], 0.0)
    for matrix_ref in (fold_ref, block_ref):
        high = spread.astype(bf16)
        rest = (spread - high.astype(f32)).astype(bf16)
        if matrix_ref is fold_ref:
            spread = nn(high, matrix_ref[...]) + nn(rest, matrix_ref[...])
        else:
            spread = nn(matrix_ref[...], high) + nn(matrix_ref[...], rest)
    store_blocks(
        jnp.transpose(terms_ref[...]) + spread,
        PLACE[TURNS[2][2]],
        keep_c_ref,
        send_c_ref,
        slice(third, last),
    )
    turned = jnp.transpose(normed_ref[...])
    targets = ((keep_a_ref, send_a_ref), (keep_b_ref, send_b_ref), (keep_c_ref, send_c_ref))
    for i, (keep_ref, send_ref) in enumerate(targets):
        size = min(third, 3 * width - i * third)
        store_blocks(
            nn(turned, grad_mixed_ref[:, i * third : i * third + size]),
            PLACE[TURNS[i][2]],
            keep_ref,
            send_ref,
            slice(0, size),
        )


def token_kernel(
    core_ref,
    rows_ref,
    own_ref,
    other_ref,
    grad_middle_ref,
    vector_ref,
    order_ref,
    token_ref,
    token_full_ref,
):
    bf16, f32 = jnp.bfloat16, jnp.float32
    half = token_ref.shape[0]
    unit, inverse = column_norm(rows_ref[...].astype(f32))
    grad_norm = own_ref[...].astype(f32) + other_ref[...].astype(f32)
    scaled = grad_norm * vector_ref[0:1]
    mean_grad = jnp.mean(scaled, axis=-1, keepdims=True)
    mean_cross = jnp.mean(scaled * unit, axis=-1, keepdims=True)
    token_full_ref[...] = (
        grad_middle_ref[...] + inverse * (scaled - mean_grad - unit * mean_cross)
    )
    start = pl.multiple_of(core_ref[0] * half, half)
    token_rows = token_full_ref[pl.ds(start, half), :].astype(bf16)
    token_ref[...] = inner_cols(token_rows, order_ref[...]).astype(bf16)


def call(kernel, outs, scratch, *operands, smem=0):
    space = [pl.BlockSpec(memory_space=pltpu.SMEM)] * smem
    space += [pl.BlockSpec(memory_space=pltpu.VMEM)] * (len(operands) - smem)
    return pl.pallas_call(
        kernel,
        out_shape=[jax.ShapeDtypeStruct(shape, kind) for shape, kind in outs],
        in_specs=space,
        out_specs=[pl.BlockSpec(memory_space=pltpu.VMEM)] * len(outs),
        scratch_shapes=[pltpu.VMEM(shape, kind) for shape, kind in scratch],
        compiler_params=pltpu.CompilerParams(vmem_limit_bytes=56 * 1024 * 1024),
    )(*operands)


def local(
    tokens,
    cotangent,
    segments,
    input_weight,
    output_weight,
    up_weight,
    down_weight,
    head_bias,
    hidden_bias,
    norm_gains,
    shifts,
):
    bf16, f32 = jnp.bfloat16, jnp.float32
    half, width = tokens.shape
    length = segments.shape[1]
    block = input_weight.shape[0]
    heads_width = input_weight.shape[2]
    hidden_width = up_weight.shape[1]
    local_heads = heads_width // HEAD_DIM
    score_scale = 1.0 / math.sqrt(HEAD_DIM)
    core = lax.axis_index("c")

    first_end = 4 * heads_width + 128
    pack_width = first_end + 2 * hidden_width
    me = (
        (lax.axis_index("zh") * 4 + lax.axis_index("xh") * 2 + lax.axis_index("h"))
        .astype(jnp.int32)
        .reshape(1)
    )
    (shard,) = call(
        pack_kernel,
        [((block, pack_width), bf16)],
        [((128, block), f32)],
        input_weight,
        output_weight.T,
        up_weight,
        down_weight.T,
        norm_gains,
        shifts,
    )
    sources = source_blocks(width)
    order = lax.optimization_barrier(feature_order(sources, width))
    blocks = block_order(sources, width)
    folds = bias_fold(hidden_width, heads_width)

    def full_rows(rows):
        return nn(lax.all_gather(swap_roles(rows), "c", axis=0, tiled=True), order).astype(bf16)

    rows = full_rows(tokens)
    cot_rows = full_rows(cotangent)

    parts, order, blocks, folds, rows, cot_rows = lax.optimization_barrier(
        (gather_near(shard), order, blocks, folds, rows, cot_rows)
    )
    near = call(
        collect_kernel,
        [((8 * block, size), bf16) for size in (first_end, hidden_width, hidden_width)],
        [((8 * block, pack_width), f32)],
        me,
        *parts,
        smem=1,
    )
    small = swap_roles(
        jnp.concatenate(
            (head_bias.reshape(-1), hidden_bias, segments[0].astype(bf16))
        )
    )
    bias_rows = small[: 2 * heads_width].reshape(2, heads_width).astype(f32)
    hidden_row = small[2 * heads_width : 2 * heads_width + hidden_width].astype(f32)
    segment_row = small[2 * heads_width + hidden_width :].astype(f32).reshape(1, length)
    first_quarters, up_halves, down_halves = gather_far(near)

    def own_half(rows):
        return lax.dynamic_slice_in_dim(rows, core * half, half, axis=0)

    def other_half(rows):
        return lax.dynamic_slice_in_dim(rows, (1 - core) * half, half, axis=0)

    vectors, normed_one, mixed, log_sums, context, attended, first_weight = call(
        functools.partial(attend_kernel, score_scale),
        [
            ((8, width), f32),
            ((length, width), bf16),
            ((length, 3 * heads_width), bf16),
            ((8, length), f32),
            ((length, heads_width), bf16),
            ((length, width), bf16),
            ((width, first_end), bf16),
        ],
        [],
        rows,
        *first_quarters,
        bias_rows,
        segment_row,
    )
    third = hidden_width // 3

    def whole(*shape):
        return pl.BlockSpec(shape, lambda j: (0, 0))

    def cut(rows_of):
        return pl.BlockSpec((rows_of, third), lambda j: (0, j))

    def shaped(shape, kind):
        return jax.ShapeDtypeStruct(shape, kind)

    middle, feed, grad_two, up_keep, up_send, down_keep, down_send, hidden_sums = pl.pallas_call(
        feed_kernel,
        grid=(3,),
        out_shape=[
            shaped((length, width), f32),
            shaped((length, width), bf16),
            shaped((length, width), bf16),
        ]
        + [shaped((width // 2, hidden_width), bf16)] * 4
        + [shaped((8, hidden_width), f32)],
        in_specs=[whole(length, width)] * 3
        + [whole(8, width)]
        + [cut(width // 2)] * 4
        + [cut(1), whole(length, width)],
        out_specs=[whole(length, width)] * 3 + [cut(width // 2)] * 4 + [cut(8)],
        scratch_shapes=[
            pltpu.VMEM((length, width), bf16),
            pltpu.VMEM((width, length), bf16),
            pltpu.VMEM((width, length), bf16),
            pltpu.VMEM((width, third), bf16),
            pltpu.VMEM((width, third), bf16),
            pltpu.VMEM((length, width), f32),
            pltpu.VMEM((length, width), f32),
        ],
        compiler_params=pltpu.CompilerParams(vmem_limit_bytes=56 * 1024 * 1024),
    )(
        rows,
        attended,
        pair(attended),
        vectors,
        *up_halves,
        *down_halves,
        hidden_row.reshape(1, hidden_width),
        cot_rows,
    )
    down_other = step_along(down_send, TURNS[2][2])
    up_other = step_along(up_send, TURNS[1][2])
    grad_two_other, feed_other = lax.optimization_barrier((pair(grad_two), pair(other_half(feed))))
    grad_middle, grad_one, *first_grads = call(
        functools.partial(attend_back_kernel, score_scale),
        [
            ((length, width), f32),
            ((length, width), bf16),
        ]
        + [((width // 2, 4 * heads_width // 3), bf16)] * 4
        + [((width // 2, 4 * heads_width // 3 + 128), bf16)] * 2,
        [
            ((length, heads_width), bf16),
            ((length, 3 * heads_width), bf16),
            ((128, width), f32),
            ((1, hidden_width + 2 * heads_width), f32),
        ],
        middle,
        cot_rows,
        grad_two,
        grad_two_other,
        vectors,
        context,
        mixed,
        log_sums,
        first_weight,
        segment_row,
        normed_one,
        rows,
        hidden_sums,
        folds,
        blocks,
    )
    first_grads, grad_one, up_other, down_other = lax.optimization_barrier(
        (first_grads, grad_one, up_other, down_other)
    )
    turn_lists = TURNS + TURNS[1:]
    pieces = [
        (keep, step_along(send, turns[2]))
        for keep, send, turns in zip(first_grads[0::2], first_grads[1::2], TURNS)
    ]
    feeds = [
        fold_apart(up_keep, up_other, TURNS[1], 2),
        fold_apart(down_keep, down_other, TURNS[2], 2),
    ]
    grad_one_other = pair(grad_one)
    outcome = (
        own_half(middle)
        + own_half(feed).astype(f32)
        + feed_other.astype(f32)
        + vectors[5]
    )
    block_out = inner_cols(outcome.astype(bf16), order).astype(bf16)
    pieces, feeds, grad_one_other, block_out = lax.optimization_barrier(
        (pieces, feeds, grad_one_other, block_out)
    )
    pieces = fold(pieces, TURNS, (2, 2, 2))
    feeds = [(keep, step_along(send, turns[1])) for (keep, send), turns in zip(feeds, TURNS[1:])]
    (token_grad,) = call(
        token_kernel,
        [((half, width), bf16)],
        [((length, width), f32)],
        core.astype(jnp.int32).reshape(1),
        rows,
        grad_one,
        grad_one_other,
        grad_middle,
        vectors,
        order,
        smem=1,
    )
    pieces, feeds, token_grad = lax.optimization_barrier((pieces, feeds, token_grad))
    pieces = [
        (keep, step_along(send, turns[0]))
        for turns, (keep, send) in (
            (turns, fold_apart(*piece, turns, 1)) for piece, turns in zip(pieces + feeds, turn_lists)
        )
    ]
    operands = []
    for piece in pieces:
        operands += piece
    cross = pair(add_low(operands[4][:, -128:], operands[5][:, -128:]))
    shares = call(
        deal_kernel,
        [((2 * block, pack_width), bf16)] * 4,
        [],
        me,
        cross,
        *operands,
        smem=1,
    )
    shares, block_out, token_grad = lax.optimization_barrier((shares, block_out, token_grad))
    block_out, token_grad = swap_roles(block_out), swap_roles(token_grad)
    shares = scatter_near(shares)
    six = block // 2
    input_grad, output_grad, up_grad, down_grad, head_grad, hidden_grad, gain_grad, shift_grad = call(
        unpack_kernel,
        [
            ((block, 3, heads_width), f32),
            ((block, heads_width), f32),
            ((block, hidden_width), f32),
            ((block, hidden_width), f32),
            ((2, six), f32),
            ((1, 2 * block), f32),
            ((2, six), f32),
            ((4, six), f32),
        ],
        [],
        lax.axis_index("h").astype(jnp.int32).reshape(1),
        *shares,
        smem=1,
    )
    return (
        block_out,
        token_grad,
        input_grad,
        output_grad.T,
        up_grad,
        down_grad.T,
        head_grad,
        hidden_grad.reshape(2 * block),
        gain_grad,
        shift_grad,
    )


def solution(mesh):
    fine = Mesh(mesh.devices.reshape((2,) * 7), AXES)
    in_specs = (
        P(AXES, None),
        P(AXES, None),
        P(DP, None),
        P(DP, None, "h"),
        P("h", DP),
        P(DP, "h"),
        P("h", DP),
        P(None, "h"),
        P("h"),
        P(None, DP),
        P(None, DP),
    )
    out_specs = (
        P(AXES, None),
        P(AXES, None),
        P(DP, None, "h"),
        P("h", DP),
        P(DP, "h"),
        P("h", DP),
        P(None, ("h",) + DP),
        P(("h",) + DP),
        P(None, AXES),
        P(None, AXES),
    )
    return jax.shard_map(local, mesh=fine, in_specs=in_specs, out_specs=out_specs, check_vma=False)
```

```python
import functools
import itertools
import math

import jax
import jax.numpy as jnp
import numpy as np
from jax import lax
from jax.experimental import pallas as pl
from jax.experimental.pallas import tpu as pltpu
from jax.sharding import Mesh
from jax.sharding import PartitionSpec as P

HEAD_DIM = 64


norm_epsilon = 1e-05
masked_value = -1e30
gelu_factor = 0.7978845608028654


def inner_cols(left_side, right_side):
    return lax.dot_general(
        left_side, right_side, (((1,), (1,)), ((), ())), preferred_element_type=jnp.float32
    )


AXES = ("xh", "xl", "yl", "zh", "zl", "c", "h")
DP = AXES[:6]
RING = {"x": ("xh", "xl"), "y": ("h", "yl"), "z": ("zh", "zl")}
PLACE = {"z": 0, "y": 1, "x": 2}
TURNS = (("x", "y", "z"), ("y", "z", "x"), ("z", "x", "y"))


def swap_roles(values):
    return lax.ppermute(values, ("c", "h"), [(0, 0), (1, 2), (2, 1), (3, 3)])


def pair(values):
    return lax.ppermute(values, "c", [(0, 1), (1, 0)])


def step_along(values, axis):
    high, low = RING[axis]
    order = [name for name in AXES if name in (high, low, "c")]
    moves = []
    for place in itertools.product(range(2), repeat=3):
        target = dict(zip(order, place))
        target[low] ^= 1
        target[high] ^= target["c"]
        moves.append(
            (place[0] * 4 + place[1] * 2 + place[2], sum(target[n] << (2 - i) for i, n in enumerate(order)))
        )
    return lax.ppermute(values, tuple(order), moves)


def cross_roles(values, outward):
    moves = [(0, 1), (1, 3), (2, 0), (3, 2)]
    return lax.ppermute(values, ("c", "h"), moves if outward else [(b, a) for a, b in moves])


def flip(values, place):
    moves = []
    for xh, zh in itertools.product(range(2), repeat=2):
        moves.append((xh * 2 + zh, (xh ^ (place & 1)) * 2 + (zh ^ (place >> 1))))
    return lax.ppermute(values, ("xh", "zh"), moves)


def gather_near(shard):
    own = jnp.concatenate((swap_roles(shard), cross_roles(shard, True)), axis=0)
    return [own] + [flip(own, place) for place in range(1, 4)]


def add_low(left, right):
    return (left.astype(jnp.float32) + right.astype(jnp.float32)).astype(jnp.bfloat16)


def scatter_near(parts, span):
    others = [flip(part, place) for place, part in enumerate(parts) if place]
    total = parts[0].astype(jnp.float32)
    for other in others:
        total = total + other.astype(jnp.float32)
    total = total.astype(jnp.bfloat16)
    rows = total.shape[0] // 2
    small = total[:, span]
    crossed = cross_roles(small[:rows], True)
    others = lax.ppermute(small[rows:], ("c", "h"), [(0, 3), (1, 1), (2, 2), (3, 0)])
    return swap_roles(total[:rows]), cross_roles(total[rows:], False), crossed, others


def open_blocks(piece):
    return piece.reshape((1, 1, 1) + piece.shape)


def gather_far(pieces):
    pieces = [open_blocks(piece) for piece in pieces]

    def joined(piece, other, axis):
        return jnp.concatenate((piece, other), axis=PLACE[axis])

    def flat(piece):
        return piece.reshape(-1, piece.shape[4])

    others = [step_along(piece, TURNS[i][0]) for i, piece in enumerate(pieces)]
    others = lax.optimization_barrier(others)
    pieces = [joined(piece, other, TURNS[i][0]) for i, (piece, other) in enumerate(zip(pieces, others))]
    others = [step_along(piece, TURNS[i][1]) for i, piece in enumerate(pieces)]
    first = [flat(pieces[0]), flat(others[0])]
    first += [step_along(part, TURNS[0][2]) for part in first]
    wholes = [joined(pieces[i], others[i], TURNS[i][1]) for i in (1, 2)]
    others = [flat(step_along(whole, TURNS[i][2])) for i, whole in zip((1, 2), wholes)]
    first, wholes = lax.optimization_barrier((first, wholes))
    return first, (flat(wholes[0]), others[0]), (flat(wholes[1]), others[1])


def source_blocks(width):
    place = np.arange(width, dtype=np.int32) // (width // 64)
    near, far = place % 8, place // 8
    fixed = ((near >> 1) & 1) * 32 + (near >> 2) * 4 + (near & 1)
    xl = lax.axis_index("xl") ^ (far & 1)
    yl = lax.axis_index("yl") ^ ((far >> 1) & 1)
    zl = lax.axis_index("zl") ^ (far >> 2)
    return lax.optimization_barrier(fixed + xl * 16 + yl * 8 + zl * 2)


def feature_order(sources, width):
    block = width // 64
    inner = np.arange(width, dtype=np.int32) % block
    source = lax.optimization_barrier(sources * block + inner)
    return (lax.broadcasted_iota(jnp.int32, (width, width), 0) == source[None]).astype(jnp.bfloat16)


def block_order(sources, width):
    return (lax.broadcasted_iota(jnp.int32, (width, 64), 1) == sources[:, None]).astype(jnp.bfloat16)


def bias_fold(hidden_width, width):
    many, few = hidden_width // 64, width // 64
    target = np.concatenate(
        (
            np.arange(hidden_width) % many,
            np.arange(width) % few + many,
            np.arange(width) % few + many + few,
        )
    )
    return jnp.asarray(np.arange(128)[None] == target[:, None] + 8, jnp.bfloat16)


def place_rows(rows, me):
    block = rows // 8
    row = lax.broadcasted_iota(jnp.int32, (rows, rows), 0)
    column = lax.broadcasted_iota(jnp.int32, (rows, rows), 1)
    found = jnp.zeros((rows, rows), jnp.float32)
    for k in range(8):
        inside = (row >= k * block) & (row < (k + 1) * block)
        same = column - (me ^ k) * block == row - k * block
        found = jnp.where(inside & same, 1.0, found)
    return found.astype(jnp.bfloat16)


def eye(size):
    row = lax.broadcasted_iota(jnp.int32, (size, size), 0)
    column = lax.broadcasted_iota(jnp.int32, (size, size), 1)
    return (row == column).astype(jnp.float32).astype(jnp.bfloat16)


def pack_kernel(input_ref, output_ref, up_ref, down_ref, gains_ref, shifts_ref, shard_ref, small_ref):
    bf16 = jnp.bfloat16
    block, width = output_ref.shape
    hidden_width = up_ref.shape[1]
    for i in range(3):
        shard_ref[:, i * width : (i + 1) * width] = input_ref[:, i, :]
    shard_ref[:, 3 * width : 4 * width] = output_ref[...]
    small_ref[...] = jnp.zeros_like(small_ref)
    small_ref[0:2] = gains_ref[...].astype(jnp.float32)
    small_ref[2:6] = shifts_ref[...].astype(jnp.float32)
    at = 4 * width + 128
    shard_ref[:, 4 * width : at] = inner_cols(eye(block), small_ref[...].astype(bf16)).astype(bf16)
    shard_ref[:, at : at + hidden_width] = up_ref[...]
    shard_ref[:, at + hidden_width :] = down_ref[...]


def collect_kernel(me_ref, *refs):
    parts, outs, held_ref = refs[:4], refs[4:-1], refs[-1]
    rows = held_ref.shape[0]
    for i, part in enumerate(parts):
        held_ref[i * rows // 4 : (i + 1) * rows // 4] = part[...].astype(jnp.float32)
    moved = place_rows(rows, me_ref[0])
    at = 0
    for out in outs:
        columns = out.shape[1]
        held = held_ref[:, at : at + columns].astype(jnp.bfloat16)
        out[...] = nn(moved, held).astype(jnp.bfloat16)
        at += columns


def deal_kernel(me_ref, *refs):
    parts, outs = refs[:-4], refs[-4:]
    rows = parts[0].shape[0]
    moved = place_rows(rows, me_ref[0])
    at = 0
    for keep, other in zip(parts[::2], parts[1::2]):
        columns = keep.shape[1]
        total = add_low(keep[...], other[...])
        total = nn(moved, total)
        for i, out in enumerate(outs):
            part = total[i * rows // 4 : (i + 1) * rows // 4]
            out[:, at : at + columns] = part.astype(jnp.bfloat16)
        at += columns


def unpack_kernel(half_ref, *refs):
    parts = refs[:2]
    input_ref, output_ref, up_ref, down_ref, head_ref, hidden_ref, gain_ref, shift_ref = refs[4:]
    f32 = jnp.float32
    block, width = output_ref.shape
    hidden_width = up_ref.shape[1]
    six = block // 2

    def total(start, size):
        columns = slice(start, start + size)
        value = parts[0][:, columns].astype(f32)
        for part in parts[1:]:
            value = value + part[:, columns].astype(f32)
        return value

    def pick(rows, columns, offset):
        row = lax.broadcasted_iota(jnp.int32, (rows, columns), 0)
        column = lax.broadcasted_iota(jnp.int32, (rows, columns), 1)
        return (row == column + offset).astype(f32)

    def exact(left, right, dims):
        return lax.dot_general(
            left, right, (dims, ((), ())), precision=lax.Precision.HIGHEST, preferred_element_type=f32
        )

    for i in range(3):
        input_ref[:, i, :] = total(i * width, width)
    output_ref[...] = total(3 * width, width)
    at = 4 * width + 128
    up_ref[...] = total(at, hidden_width)
    down_ref[...] = total(at + hidden_width, hidden_width)
    small = total(4 * width, 128)
    lane = lax.broadcasted_iota(jnp.int32, small.shape, 1)
    small = small + jnp.where(lane < 8, refs[2][...].astype(f32) + refs[3][...].astype(f32), 0.0)
    norm_terms = exact(small, pick(block, six, half_ref[0] * six), ((0,), (0,)))
    gain_ref[...] = norm_terms[0:2]
    shift_ref[...] = norm_terms[2:6]
    hidden_ref[...] = exact(small[0:1], pick(128, 2 * block, 8), ((1,), (0,)))
    head_ref[0:1] = exact(small[0:1], pick(128, six, 8 + 2 * block), ((1,), (0,)))
    head_ref[1:2] = exact(small[0:1], pick(128, six, 8 + 2 * block + six), ((1,), (0,)))


def fold_kernel(layouts, *refs):
    ins, outs = refs[: 2 * len(layouts)], refs[2 * len(layouts) :]
    for i, (bits, place) in enumerate(layouts):
        keep_ref, other_ref = ins[2 * i : 2 * i + 2]
        rows = keep_ref.shape[0] >> bits
        counts = [0, 0]
        for block in range(1 << bits):
            which = (block >> (bits - 1 - place)) & 1
            at = counts[which] * rows
            counts[which] += 1
            span = slice(block * rows, (block + 1) * rows)
            outs[2 * i + which][at : at + rows] = add_low(keep_ref[span], other_ref[span])


def fold_apart(keep, other, turns, left):
    place = sorted(turns[:left], key=PLACE.get).index(turns[left - 1])
    rows, columns = keep.shape
    shape = (2,) * left + (rows >> left, columns)
    keep, other = keep.reshape(shape), other.reshape(shape)
    sums = []
    for i in range(2):
        part = add_low(
            lax.slice_in_dim(keep, i, i + 1, axis=place), lax.slice_in_dim(other, i, i + 1, axis=place)
        )
        sums.append(part.reshape(rows // 2, columns))
    return sums


def fold(pairs, turn_lists, turns_left):
    layouts = []
    for turns, left in zip(turn_lists, turns_left):
        place = sorted(turns[:left], key=PLACE.get).index(turns[left - 1])
        layouts.append((left, place))
    outs = []
    for keep, _ in pairs:
        outs += [((keep.shape[0] // 2, keep.shape[1]), jnp.bfloat16)] * 2
    parts = call(functools.partial(fold_kernel, layouts), outs, [], *[x for pair_of in pairs for x in pair_of])
    return [
        (keep, step_along(send, turns[left - 1]))
        for keep, send, turns, left in zip(parts[0::2], parts[1::2], turn_lists, turns_left)
    ]


def column_norm(values):
    mean_val = jnp.mean(values, axis=-1, keepdims=True)
    centered = values - mean_val
    variance = jnp.mean(centered * centered, axis=-1, keepdims=True)
    inverse = lax.rsqrt(variance + norm_epsilon)
    return centered * inverse, inverse


def nn(left, right):
    return jnp.dot(left, right, preferred_element_type=jnp.float32)


def key_mask(segment_row, keys, first, queries):
    column = jnp.transpose(jnp.broadcast_to(segment_row, (8, segment_row.shape[1])))[:keys, :1]
    row = segment_row[:, first : first + queries]
    key_pos = lax.broadcasted_iota(jnp.int32, (keys, queries), 0)
    query_pos = lax.broadcasted_iota(jnp.int32, (keys, queries), 1) + first
    return jnp.where((column == row) & (key_pos <= query_pos), 0.0, masked_value)


def lane_half(values, which):
    lane = lax.broadcasted_iota(jnp.int32, values.shape, 1)
    inside = (lane >= HEAD_DIM) if which else (lane < HEAD_DIM)
    return jnp.where(inside, values, jnp.zeros_like(values))


def attend_kernel(
    score_scale,
    rows_ref,
    quarter_0_ref,
    quarter_1_ref,
    quarter_2_ref,
    quarter_3_ref,
    bias_ref,
    segment_ref,
    vector_ref,
    normed_ref,
    mixed_ref,
    log_ref,
    context_ref,
    attended_ref,
    weight_ref,
):
    bf16 = jnp.bfloat16
    length = rows_ref.shape[0]
    width = context_ref.shape[1]
    join_blocks(TURNS[0], (quarter_0_ref, quarter_1_ref, quarter_2_ref, quarter_3_ref), weight_ref)
    vector_ref[...] = jnp.transpose(weight_ref[:, 4 * width : 4 * width + 128].astype(jnp.float32))[:8]
    half = length // 2
    unit, _ = column_norm(rows_ref[...].astype(jnp.float32))
    normed_ref[...] = (unit * vector_ref[0:1] + vector_ref[2:3]).astype(bf16)
    mixed = nn(normed_ref[...], weight_ref[:, : 3 * width])
    mixed_ref[:, :width] = (mixed[:, :width] + bias_ref[0:1]).astype(bf16)
    mixed_ref[:, width : 2 * width] = mixed[:, width : 2 * width].astype(bf16)
    mixed_ref[:, 2 * width :] = (mixed[:, 2 * width :] + bias_ref[1:2]).astype(bf16)
    segment_row = segment_ref[...]
    spans = ((0, half, key_mask(segment_row, half, 0, half)), (half, length, key_mask(segment_row, length, half, half)))
    log_ref[...] = jnp.zeros_like(log_ref)
    for two in range(width // 128):
        at = 128 * two
        query_two = mixed_ref[:, at : at + 128] * jnp.asarray(score_scale, bf16)
        key_two = mixed_ref[:, width + at : width + at + 128]
        value_turned = jnp.transpose(mixed_ref[:, 2 * width + at : 2 * width + at + 128])
        parts = []
        for which in range(2):
            query_rows = lane_half(query_two, which)
            value_rows = value_turned[HEAD_DIM * which : HEAD_DIM * (which + 1)]
            sides = []
            for first, keys, mask in spans:
                scores = inner_cols(key_two[:keys], query_rows[first : first + half]) + mask
                top = jnp.max(scores, axis=0, keepdims=True)
                exponent = jnp.exp(scores - top)
                total = jnp.sum(exponent, axis=0, keepdims=True)
                log_ref[2 * two + which : 2 * two + which + 1, first : first + half] = top + jnp.log(total)
                sides.append(nn(value_rows[:, :keys], exponent.astype(bf16)) / total)
            parts.append(jnp.concatenate(sides, axis=1))
        context_ref[:, at : at + 128] = jnp.transpose(jnp.concatenate(parts, axis=0)).astype(bf16)
    attended_ref[...] = inner_cols(
        context_ref[...], weight_ref[:, 3 * width : 4 * width]
    ).astype(bf16)


def store_blocks(value, place, keep_ref, send_ref, columns):
    rows = value.shape[0] // 8
    counts = [0, 0]
    for block in range(8):
        which = (block >> (2 - place)) & 1
        target = send_ref if which else keep_ref
        at = counts[which] * rows
        counts[which] += 1
        target[at : at + rows, columns] = value[block * rows : (block + 1) * rows].astype(target.dtype)


def join_blocks(turns, quarter_refs, whole_ref):
    rows = whole_ref.shape[0] // 8
    bit = [2 - PLACE[axis] for axis in turns]
    for block in range(8):
        which = ((block >> bit[1]) & 1) + 2 * ((block >> bit[2]) & 1)
        at = ((block >> bit[0]) & 1) * rows
        whole_ref[block * rows : (block + 1) * rows] = quarter_refs[which][at : at + rows]


def join_halves(place, half_refs, whole_ref):
    rows = whole_ref.shape[0] // 8
    counts = [0, 0]
    for block in range(8):
        which = (block >> (2 - place)) & 1
        at = counts[which] * rows
        counts[which] += 1
        whole_ref[block * rows : (block + 1) * rows] = half_refs[which][at : at + rows]


def feed_kernel(
    rows_ref,
    own_ref,
    other_ref,
    vector_ref,
    up_mine_ref,
    up_other_ref,
    down_mine_ref,
    down_other_ref,
    bias_ref,
    cot_ref,
    middle_ref,
    feed_ref,
    grad_two_ref,
    up_keep_ref,
    up_send_ref,
    down_keep_ref,
    down_send_ref,
    bias_grad_ref,
    normed_ref,
    normed_turned_ref,
    cot_turned_ref,
    up_ref,
    down_ref,
    feed_sum_ref,
    grad_two_sum_ref,
):
    bf16, f32 = jnp.bfloat16, jnp.float32

    @pl.when(pl.program_id(0) == 0)
    def _():
        middle = (
            rows_ref[...].astype(f32)
            + (own_ref[...].astype(f32) + other_ref[...].astype(f32))
            + vector_ref[4:5]
        )
        middle_ref[...] = middle
        unit, _ = column_norm(middle)
        normed_ref[...] = (unit * vector_ref[1:2] + vector_ref[3:4]).astype(bf16)
        normed_turned_ref[...] = jnp.transpose(normed_ref[...])
        cot_turned_ref[...] = jnp.transpose(cot_ref[...])
        feed_sum_ref[...] = jnp.zeros_like(feed_sum_ref)
        grad_two_sum_ref[...] = jnp.zeros_like(grad_two_sum_ref)

    join_halves(PLACE[TURNS[1][2]], (up_mine_ref, up_other_ref), up_ref)
    join_halves(PLACE[TURNS[2][2]], (down_mine_ref, down_other_ref), down_ref)
    before = nn(normed_ref[...], up_ref[...]) + bias_ref[...]
    square = before * before
    bend = jnp.tanh(gelu_factor * (before + 0.044715 * before * square))
    opened = 0.5 * (1.0 + bend)
    hidden = (before * opened).astype(bf16)
    slope = opened + 0.5 * before * (1.0 - bend * bend) * (
        gelu_factor * (1.0 + 3.0 * 0.044715 * square)
    )
    grad_before = (nn(cot_ref[...], down_ref[...]) * slope).astype(bf16)
    feed_sum_ref[...] += inner_cols(hidden, down_ref[...])
    grad_two_sum_ref[...] += inner_cols(grad_before, up_ref[...])
    bias_grad_ref[...] = jnp.broadcast_to(
        jnp.sum(grad_before.astype(f32), axis=0, keepdims=True), bias_grad_ref.shape
    )
    columns = slice(0, up_ref.shape[1])
    store_blocks(nn(cot_turned_ref[...], hidden), PLACE[TURNS[2][2]], down_keep_ref, down_send_ref, columns)
    store_blocks(nn(normed_turned_ref[...], grad_before), PLACE[TURNS[1][2]], up_keep_ref, up_send_ref, columns)

    @pl.when(pl.program_id(0) == pl.num_programs(0) - 1)
    def _():
        feed_ref[...] = feed_sum_ref[...].astype(bf16)
        grad_two_ref[...] = grad_two_sum_ref[...].astype(bf16)


def attend_back_kernel(
    score_scale,
    middle_ref,
    cot_ref,
    own_ref,
    other_ref,
    vector_ref,
    context_ref,
    mixed_ref,
    log_ref,
    weight_ref,
    segment_ref,
    normed_ref,
    rows_ref,
    hidden_sums_ref,
    fold_ref,
    block_ref,
    grad_middle_ref,
    grad_one_ref,
    keep_a_ref,
    send_a_ref,
    keep_b_ref,
    send_b_ref,
    keep_c_ref,
    send_c_ref,
    grad_context_ref,
    grad_mixed_ref,
    terms_ref,
    bias_ref,
):
    bf16, f32 = jnp.bfloat16, jnp.float32
    length = middle_ref.shape[0]
    width = context_ref.shape[1]
    half = length // 2
    unit, inverse = column_norm(middle_ref[...])
    grad_norm = own_ref[...].astype(f32) + other_ref[...].astype(f32)
    scaled = grad_norm * vector_ref[1:2]
    mean_grad = jnp.mean(scaled, axis=-1, keepdims=True)
    mean_cross = jnp.mean(scaled * unit, axis=-1, keepdims=True)
    cot = cot_ref[...].astype(f32)
    grad_middle = cot + inverse * (scaled - mean_grad - unit * mean_cross)
    grad_middle_ref[...] = grad_middle
    terms_ref[...] = jnp.zeros_like(terms_ref)
    terms_ref[1:2] = 0.5 * jnp.sum(grad_norm * unit, axis=0, keepdims=True)
    terms_ref[3:4] = 0.5 * jnp.sum(grad_norm, axis=0, keepdims=True)
    terms_ref[4:5] = 0.5 * jnp.sum(grad_middle, axis=0, keepdims=True)
    terms_ref[5:6] = 0.5 * jnp.sum(cot, axis=0, keepdims=True)
    hidden_width = hidden_sums_ref.shape[1]
    bias_ref[:, :hidden_width] = hidden_sums_ref[0:1]
    middle_rows = grad_middle.astype(bf16)
    third = keep_a_ref.shape[1]
    last = keep_c_ref.shape[1]
    store_blocks(
        nn(jnp.transpose(middle_rows), context_ref[...]),
        PLACE[TURNS[2][2]],
        keep_c_ref,
        send_c_ref,
        slice(third - width, third),
    )
    grad_context_ref[...] = nn(middle_rows, weight_ref[:, 3 * width : 4 * width]).astype(bf16)
    segment_row = segment_ref[...]
    spans = ((0, half, key_mask(segment_row, half, 0, half)), (half, length, key_mask(segment_row, length, half, half)))
    for two in range(width // 128):
        at = 128 * two
        query_two = mixed_ref[:, at : at + 128] * jnp.asarray(score_scale, bf16)
        key_two = mixed_ref[:, width + at : width + at + 128]
        value_two = mixed_ref[:, 2 * width + at : 2 * width + at + 128]
        grad_two = grad_context_ref[:, at : at + 128]
        key_turned = jnp.transpose(key_two)
        grad_queries = []
        grad_keys = [0.0, 0.0]
        grad_values = [0.0, 0.0]
        for which in range(2):
            query_rows = lane_half(query_two, which)
            grad_rows = lane_half(grad_two, which)
            key_rows = key_turned[HEAD_DIM * which : HEAD_DIM * (which + 1)]
            sides = []
            for side, (first, keys, mask) in enumerate(spans):
                query_side = query_rows[first : first + half]
                grad_side = grad_rows[first : first + half]
                log_side = log_ref[2 * two + which : 2 * two + which + 1, first : first + half]
                scores = inner_cols(key_two[:keys], query_side) + mask
                soft = jnp.exp(scores - log_side)
                grad_soft = inner_cols(value_two[:keys], grad_side)
                crossed = soft * grad_soft
                grad_scores = (
                    crossed - soft * jnp.sum(crossed, axis=0, keepdims=True)
                ).astype(bf16)
                grad_keys[side] += nn(grad_scores, query_side)
                grad_values[side] += nn(soft.astype(bf16), grad_side)
                sides.append(nn(key_rows[:, :keys], grad_scores))
            grad_queries.append(jnp.concatenate(sides, axis=1))
        queries_out = jnp.transpose(jnp.concatenate(grad_queries, axis=0)) * score_scale
        for place, value in enumerate((queries_out, grad_keys, grad_values)):
            columns = slice(place * width + at, place * width + at + 128)
            if place == 0:
                grad_mixed_ref[:, columns] = value.astype(bf16)
            else:
                grad_mixed_ref[:half, columns] = (value[0] + value[1][:half]).astype(bf16)
                grad_mixed_ref[half:, columns] = value[1][half:].astype(bf16)
            if place != 1:
                start = hidden_width + (place // 2) * width + at
                bias_ref[:, start : start + 128] = jnp.sum(
                    grad_mixed_ref[:, columns].astype(f32), axis=0, keepdims=True
                )
    unit, _ = column_norm(rows_ref[...].astype(f32))
    grad_one = inner_cols(grad_mixed_ref[...], weight_ref[:, : 3 * width])
    grad_one_ref[...] = grad_one.astype(bf16)
    terms_ref[0:1] = jnp.sum(grad_one * unit, axis=0, keepdims=True)
    terms_ref[2:3] = jnp.sum(grad_one, axis=0, keepdims=True)
    row = lax.broadcasted_iota(jnp.int32, (64, bias_ref.shape[1]), 0)
    lane = lax.broadcasted_iota(jnp.int32, (64, bias_ref.shape[1]), 1)
    inside = jnp.zeros(row.shape, jnp.bool_)
    for start, size in ((0, hidden_width), (hidden_width, width), (hidden_width + width, width)):
        first = row * (size // 64) + start
        inside = inside | ((lane >= first) & (lane < first + size // 64))
    spread = jnp.where(inside, bias_ref[...], 0.0)
    for matrix_ref in (fold_ref, block_ref):
        high = spread.astype(bf16)
        rest = (spread - high.astype(f32)).astype(bf16)
        if matrix_ref is fold_ref:
            spread = nn(high, matrix_ref[...]) + nn(rest, matrix_ref[...])
        else:
            spread = nn(matrix_ref[...], high) + nn(matrix_ref[...], rest)
    store_blocks(
        jnp.transpose(terms_ref[...]) + spread,
        PLACE[TURNS[2][2]],
        keep_c_ref,
        send_c_ref,
        slice(third, last),
    )
    turned = jnp.transpose(normed_ref[...])
    targets = ((keep_a_ref, send_a_ref), (keep_b_ref, send_b_ref), (keep_c_ref, send_c_ref))
    for i, (keep_ref, send_ref) in enumerate(targets):
        size = min(third, 3 * width - i * third)
        store_blocks(
            nn(turned, grad_mixed_ref[:, i * third : i * third + size]),
            PLACE[TURNS[i][2]],
            keep_ref,
            send_ref,
            slice(0, size),
        )


def token_kernel(
    core_ref,
    rows_ref,
    own_ref,
    other_ref,
    grad_middle_ref,
    vector_ref,
    order_ref,
    token_ref,
    token_full_ref,
):
    bf16, f32 = jnp.bfloat16, jnp.float32
    half = token_ref.shape[0]
    unit, inverse = column_norm(rows_ref[...].astype(f32))
    grad_norm = own_ref[...].astype(f32) + other_ref[...].astype(f32)
    scaled = grad_norm * vector_ref[0:1]
    mean_grad = jnp.mean(scaled, axis=-1, keepdims=True)
    mean_cross = jnp.mean(scaled * unit, axis=-1, keepdims=True)
    token_full_ref[...] = (
        grad_middle_ref[...] + inverse * (scaled - mean_grad - unit * mean_cross)
    )
    start = pl.multiple_of(core_ref[0] * half, half)
    token_rows = token_full_ref[pl.ds(start, half), :].astype(bf16)
    token_ref[...] = inner_cols(token_rows, order_ref[...]).astype(bf16)


def call(kernel, outs, scratch, *operands, smem=0):
    space = [pl.BlockSpec(memory_space=pltpu.SMEM)] * smem
    space += [pl.BlockSpec(memory_space=pltpu.VMEM)] * (len(operands) - smem)
    return pl.pallas_call(
        kernel,
        out_shape=[jax.ShapeDtypeStruct(shape, kind) for shape, kind in outs],
        in_specs=space,
        out_specs=[pl.BlockSpec(memory_space=pltpu.VMEM)] * len(outs),
        scratch_shapes=[pltpu.VMEM(shape, kind) for shape, kind in scratch],
        compiler_params=pltpu.CompilerParams(vmem_limit_bytes=56 * 1024 * 1024),
    )(*operands)


def local(
    tokens,
    cotangent,
    segments,
    input_weight,
    output_weight,
    up_weight,
    down_weight,
    head_bias,
    hidden_bias,
    norm_gains,
    shifts,
):
    bf16, f32 = jnp.bfloat16, jnp.float32
    half, width = tokens.shape
    length = segments.shape[1]
    block = input_weight.shape[0]
    heads_width = input_weight.shape[2]
    hidden_width = up_weight.shape[1]
    local_heads = heads_width // HEAD_DIM
    score_scale = 1.0 / math.sqrt(HEAD_DIM)
    core = lax.axis_index("c")

    first_end = 4 * heads_width + 128
    pack_width = first_end + 2 * hidden_width
    me = (
        (lax.axis_index("zh") * 4 + lax.axis_index("xh") * 2 + lax.axis_index("h"))
        .astype(jnp.int32)
        .reshape(1)
    )
    (shard,) = call(
        pack_kernel,
        [((block, pack_width), bf16)],
        [((128, block), f32)],
        input_weight,
        output_weight.T,
        up_weight,
        down_weight.T,
        norm_gains,
        shifts,
    )
    sources = source_blocks(width)
    order = lax.optimization_barrier(feature_order(sources, width))
    blocks = block_order(sources, width)
    folds = bias_fold(hidden_width, heads_width)

    def full_rows(rows):
        return nn(lax.all_gather(swap_roles(rows), "c", axis=0, tiled=True), order).astype(bf16)

    rows = full_rows(tokens)
    cot_rows = full_rows(cotangent)

    parts, order, blocks, folds, rows, cot_rows = lax.optimization_barrier(
        (gather_near(shard), order, blocks, folds, rows, cot_rows)
    )
    near = call(
        collect_kernel,
        [((8 * block, size), bf16) for size in (first_end, hidden_width, hidden_width)],
        [((8 * block, pack_width), f32)],
        me,
        *parts,
        smem=1,
    )
    small = swap_roles(
        jnp.concatenate(
            (head_bias.reshape(-1), hidden_bias, segments[0].astype(bf16))
        )
    )
    bias_rows = small[: 2 * heads_width].reshape(2, heads_width).astype(f32)
    hidden_row = small[2 * heads_width : 2 * heads_width + hidden_width].astype(f32)
    segment_row = small[2 * heads_width + hidden_width :].astype(f32).reshape(1, length)
    first_quarters, up_halves, down_halves = gather_far(near)

    def own_half(rows):
        return lax.dynamic_slice_in_dim(rows, core * half, half, axis=0)

    def other_half(rows):
        return lax.dynamic_slice_in_dim(rows, (1 - core) * half, half, axis=0)

    vectors, normed_one, mixed, log_sums, context, attended, first_weight = call(
        functools.partial(attend_kernel, score_scale),
        [
            ((8, width), f32),
            ((length, width), bf16),
            ((length, 3 * heads_width), bf16),
            ((8, length), f32),
            ((length, heads_width), bf16),
            ((length, width), bf16),
            ((width, first_end), bf16),
        ],
        [],
        rows,
        *first_quarters,
        bias_rows,
        segment_row,
    )
    third = hidden_width // 3

    def whole(*shape):
        return pl.BlockSpec(shape, lambda j: (0, 0))

    def cut(rows_of):
        return pl.BlockSpec((rows_of, third), lambda j: (0, j))

    def shaped(shape, kind):
        return jax.ShapeDtypeStruct(shape, kind)

    middle, feed, grad_two, up_keep, up_send, down_keep, down_send, hidden_sums = pl.pallas_call(
        feed_kernel,
        grid=(3,),
        out_shape=[
            shaped((length, width), f32),
            shaped((length, width), bf16),
            shaped((length, width), bf16),
        ]
        + [shaped((width // 2, hidden_width), bf16)] * 4
        + [shaped((8, hidden_width), f32)],
        in_specs=[whole(length, width)] * 3
        + [whole(8, width)]
        + [cut(width // 2)] * 4
        + [cut(1), whole(length, width)],
        out_specs=[whole(length, width)] * 3 + [cut(width // 2)] * 4 + [cut(8)],
        scratch_shapes=[
            pltpu.VMEM((length, width), bf16),
            pltpu.VMEM((width, length), bf16),
            pltpu.VMEM((width, length), bf16),
            pltpu.VMEM((width, third), bf16),
            pltpu.VMEM((width, third), bf16),
            pltpu.VMEM((length, width), f32),
            pltpu.VMEM((length, width), f32),
        ],
        compiler_params=pltpu.CompilerParams(vmem_limit_bytes=56 * 1024 * 1024),
    )(
        rows,
        attended,
        pair(attended),
        vectors,
        *up_halves,
        *down_halves,
        hidden_row.reshape(1, hidden_width),
        cot_rows,
    )
    down_other = step_along(down_send, TURNS[2][2])
    up_other = step_along(up_send, TURNS[1][2])
    grad_two_other, feed_other = lax.optimization_barrier((pair(grad_two), pair(other_half(feed))))
    grad_middle, grad_one, *first_grads = call(
        functools.partial(attend_back_kernel, score_scale),
        [
            ((length, width), f32),
            ((length, width), bf16),
        ]
        + [((width // 2, 4 * heads_width // 3), bf16)] * 4
        + [((width // 2, 4 * heads_width // 3 + 128), bf16)] * 2,
        [
            ((length, heads_width), bf16),
            ((length, 3 * heads_width), bf16),
            ((128, width), f32),
            ((1, hidden_width + 2 * heads_width), f32),
        ],
        middle,
        cot_rows,
        grad_two,
        grad_two_other,
        vectors,
        context,
        mixed,
        log_sums,
        first_weight,
        segment_row,
        normed_one,
        rows,
        hidden_sums,
        folds,
        blocks,
    )
    first_grads, grad_one, up_other, down_other = lax.optimization_barrier(
        (first_grads, grad_one, up_other, down_other)
    )
    turn_lists = TURNS + TURNS[1:]
    pieces = [
        (keep, step_along(send, turns[2]))
        for keep, send, turns in zip(first_grads[0::2], first_grads[1::2], TURNS)
    ]
    feeds = [
        fold_apart(up_keep, up_other, TURNS[1], 2),
        fold_apart(down_keep, down_other, TURNS[2], 2),
    ]
    grad_one_other = pair(grad_one)
    outcome = (
        own_half(middle)
        + own_half(feed).astype(f32)
        + feed_other.astype(f32)
        + vectors[5]
    )
    block_out = inner_cols(outcome.astype(bf16), order).astype(bf16)
    pieces, feeds, grad_one_other, block_out = lax.optimization_barrier(
        (pieces, feeds, grad_one_other, block_out)
    )
    pieces = fold(pieces, TURNS, (2, 2, 2))
    feeds = [(keep, step_along(send, turns[1])) for (keep, send), turns in zip(feeds, TURNS[1:])]
    (token_grad,) = call(
        token_kernel,
        [((half, width), bf16)],
        [((length, width), f32)],
        core.astype(jnp.int32).reshape(1),
        rows,
        grad_one,
        grad_one_other,
        grad_middle,
        vectors,
        order,
        smem=1,
    )
    pieces, feeds, token_grad = lax.optimization_barrier((pieces, feeds, token_grad))
    pieces = [
        (keep, step_along(send, turns[0]))
        for turns, (keep, send) in (
            (turns, fold_apart(*piece, turns, 1)) for piece, turns in zip(pieces + feeds, turn_lists)
        )
    ]
    operands = []
    for piece in pieces:
        operands += piece
    shares = call(
        deal_kernel,
        [((2 * block, pack_width), bf16)] * 4,
        [],
        me,
        *operands,
        smem=1,
    )
    shares, block_out, token_grad = lax.optimization_barrier((shares, block_out, token_grad))
    block_out, token_grad = swap_roles(block_out), swap_roles(token_grad)
    shares = scatter_near(shares, slice(4 * heads_width, first_end))
    six = block // 2
    input_grad, output_grad, up_grad, down_grad, head_grad, hidden_grad, gain_grad, shift_grad = call(
        unpack_kernel,
        [
            ((block, 3, heads_width), f32),
            ((block, heads_width), f32),
            ((block, hidden_width), f32),
            ((block, hidden_width), f32),
            ((2, six), f32),
            ((1, 2 * block), f32),
            ((2, six), f32),
            ((4, six), f32),
        ],
        [],
        lax.axis_index("h").astype(jnp.int32).reshape(1),
        *shares,
        smem=1,
    )
    return (
        block_out,
        token_grad,
        input_grad,
        output_grad.T,
        up_grad,
        down_grad.T,
        head_grad,
        hidden_grad.reshape(2 * block),
        gain_grad,
        shift_grad,
    )


def solution(mesh):
    fine = Mesh(mesh.devices.reshape((2,) * 7), AXES)
    in_specs = (
        P(AXES, None),
        P(AXES, None),
        P(DP, None),
        P(DP, None, "h"),
        P("h", DP),
        P(DP, "h"),
        P("h", DP),
        P(None, "h"),
        P("h"),
        P(None, DP),
        P(None, DP),
    )
    out_specs = (
        P(AXES, None),
        P(AXES, None),
        P(DP, None, "h"),
        P("h", DP),
        P(DP, "h"),
        P("h", DP),
        P(None, ("h",) + DP),
        P(("h",) + DP),
        P(None, AXES),
        P(None, AXES),
    )
    return jax.shard_map(local, mesh=fine, in_specs=in_specs, out_specs=out_specs, check_vma=False)
```
